32 devices in a mesh: dp: 16 (over z, y, core), seq: 2 (over x).
Axes of the slice: x: 2, y: 2, z: 4, core: 2. Of those that a mesh axis runs over, the one named last changes fastest.
Arguments:
- tokens: bfloat16 [32, 1024, 768], P('dp', 'seq'), may hold values from -6 to 6
- cotangent: bfloat16 [32, 1024, 768], P('dp', 'seq'), may hold values from -6 to 6
- time_index: int32 [32], P('dp'), may hold values from 0 to 999
- span_starts: int32 [32], P('dp'), may hold values from 0 to 511, as said below
- span_lengths: int32 [32], P('dp'), may hold values from 2 to 1024, as said below
- w_ada: bfloat16 [128, 4608], replicated, may hold values from -0.5 to 0.5
- b_ada: float32 [4608], replicated, may hold values from -3 to 3
- gain_one: float32 [768], replicated, may hold values from 0.5 to 1.5
- w_qkv: bfloat16 [768, 2304], replicated, may hold values from -0.21875 to 0.21875
- w_out: bfloat16 [768, 768], replicated, may hold values from -4 to 4
- gain_two: float32 [768], replicated, may hold values from 0.5 to 1.5
- w_up: bfloat16 [768, 3072], replicated, may hold values from -0.21875 to 0.21875
- b_up: float32 [3072], replicated, may hold values from -3 to 3
- w_down: bfloat16 [3072, 768], replicated, may hold values from -0.109375 to 0.109375
- b_down: float32 [768], replicated, may hold values from -3 to 3
Outputs:
- output: bfloat16 [32, 1024, 768], P('dp', 'seq')
- grad_tokens: float32 [32, 1024, 768], P('dp', 'seq')
- grad_w_ada: float32 [128, 4608], P('dp')
- grad_b_ada: float32 [4608], P('dp')
- grad_gain_one: float32 [768], P('dp')
- grad_w_qkv: float32 [768, 2304], P('dp')
- grad_w_out: float32 [768, 768], P('dp')
- grad_gain_two: float32 [768], P('dp')
- grad_w_up: float32 [768, 3072], P('dp')
- grad_b_up: float32 [3072], P('dp')
- grad_w_down: float32 [3072, 768], P('dp')
- grad_b_down: float32 [768], P('dp')
The draws below stay inside these ranges and needn't reach their ends.
Inputs may be any that keep to these rules, and one draw needn't show every extreme that they name: `span_starts`: each span starts in the first half of its sequence, before position 512. `span_lengths`: each span covers positions 511 and 512 and ends within its sequence.
All inputs are finite; a program needn't handle non-finite values.
Results may differ from the reference program's by a relative error of at most 0.015.
Values may be sent and summed in bfloat16 or wider, within the bound.
A program may use at most 256 MiB of HBM per device.

```python
import math
import jax
import jax.numpy as jnp
from jax import lax

D = 768
HEADS = 12
HD = 64
FF = 3072
COND = 128
LENGTH = 1024
SEQS = 32


def span_pair(key):
    start_key = jax.random.fold_in(key, 11)
    extent_key = jax.random.fold_in(key, 12)
    chosen_key = jax.random.fold_in(key, 13)
    span_start = jax.random.randint(start_key, (SEQS,), 0, LENGTH // 2)
    lowest = LENGTH // 2 - span_start + 1
    extent = lowest + jax.random.randint(extent_key, (SEQS,), 0, LENGTH // 2)
    chosen = jax.random.randint(chosen_key, (), 0, SEQS)
    neighbour = (chosen + 1) % SEQS
    places = jnp.arange(SEQS, dtype=jnp.int32)
    span_start = jnp.where(places == chosen, 0, span_start)
    extent = jnp.where(places == chosen, LENGTH, extent)
    span_start = jnp.where(places == neighbour, LENGTH // 2 - 1, span_start)
    extent = jnp.where(places == neighbour, 2, extent)
    return (span_start.astype(jnp.int32), extent.astype(jnp.int32))


def draw_span_starts(key, part):
    shared = span_pair(key)
    return shared[0]


def draw_span_lengths(key, part):
    shared = span_pair(key)
    return shared[1]


def touch_ends(values, own_key, smallest, largest):
    dims = values.shape
    spot = [jax.random.randint(jax.random.fold_in(own_key, axis), (), 0, dims[axis]) for axis in range(len(dims))]
    values = values.at[tuple(spot)].set(smallest)
    longest = dims.index(max(dims))
    spot[longest] = (spot[longest] + 1) % dims[longest]
    return values.at[tuple(spot)].set(largest)


def steps_of(own_key, dims, cuts, low, top_value):
    gain, own = 1.0, jax.random.fold_in(own_key, 6)
    for position, blocks in cuts:
        heights = jnp.exp(jax.random.uniform(jax.random.fold_in(own, position), (blocks,), jnp.float32, low / len(cuts), top_value / len(cuts)))
        gain = gain * jnp.repeat(heights, dims[position] // blocks).reshape([-1 if axis == position else 1 for axis in range(len(dims))])
    return gain


def centred(own_key, shape, deviation, bound, pieces=(), kind=jnp.bfloat16):
    gain = steps_of(own_key, shape, pieces, -0.22, 0.18) if pieces else 1.0
    drawn = jax.random.normal(own_key, shape, jnp.float32) * deviation * gain
    return jnp.minimum(jnp.maximum(drawn, -bound), bound).astype(kind)


def setup_inputs(seed: int = 0) -> dict:
    seeds = jax.random.split(jax.random.key(seed), 16)
    return {
        "tokens": centred(seeds[0], (SEQS, LENGTH, D), 1.0, 6.0, ((0, 16), (1, 2))),
        "cotangent": centred(seeds[1], (SEQS, LENGTH, D), 1.0, 6.0, ((0, 16), (1, 2))),
        "time_index": touch_ends(jax.random.randint(seeds[2], (SEQS,), 0, 1000), jax.random.fold_in(seeds[2], 1), 0, 999).astype(jnp.int32),
        "span_starts": draw_span_starts(jax.random.fold_in(seeds[15], 71), 0),
        "span_lengths": draw_span_lengths(jax.random.fold_in(seeds[15], 71), 0),
        "w_ada": centred(seeds[5], (COND, 6 * D), COND ** -0.5, 0.5),
        "b_ada": centred(seeds[6], (6 * D,), 0.5, 3.0, (), jnp.float32),
        "gain_one": jnp.clip(1.0 + 0.1 * jax.random.normal(seeds[7], (D,), jnp.float32), 0.5, 1.5),
        "w_qkv": centred(seeds[8], (D, 3 * D), D ** -0.5, 0.21875),
        "w_out": centred(seeds[9], (D, D), (max(D * 3 // LENGTH, 1)) ** -0.5, 4.0),
        "gain_two": jnp.clip(1.0 + 0.1 * jax.random.normal(seeds[10], (D,), jnp.float32), 0.5, 1.5),
        "w_up": centred(seeds[11], (D, FF), D ** -0.5, 0.21875),
        "b_up": centred(seeds[12], (FF,), 0.5, 3.0, (), jnp.float32),
        "w_down": centred(seeds[13], (FF, D), FF ** -0.5, 0.109375),
        "b_down": centred(seeds[14], (D,), 0.5, 3.0, (), jnp.float32),
    }


@jax.custom_vjp
def low(v):
    return lax.optimization_barrier(v.astype(jnp.bfloat16)).astype(jnp.float32)

@jax.custom_vjp
def low_back(v):
    return v

def low_keep(v):
    return (low(v), None)

def low_pass(kept, grad):
    return (grad,)

def back_keep(v):
    return (v, None)

def back_low(kept, grad):
    return (low(grad),)
low.defvjp(low_keep, low_pass)
low_back.defvjp(back_keep, back_low)
PRECISE = lax.Precision.HIGHEST
NORM_EPS = 1e-05

def layer_norm(values):
    centre = values - lax.optimization_barrier(jnp.mean(values, axis=-1, keepdims=True))
    spread = lax.optimization_barrier(jnp.mean(centre * centre, axis=-1, keepdims=True))
    return centre * lax.rsqrt(spread + NORM_EPS)

def time_features(time_steps):
    pair_count = COND // 2
    frequency = jnp.exp(-math.log(10000.0) * jnp.arange(pair_count, dtype=jnp.float32) / pair_count)
    angles = time_steps.astype(jnp.float32)[:, None] * frequency[None, :]
    return jnp.concatenate([jnp.cos(angles), jnp.sin(angles)], axis=-1)

def rotary_tables(positions):
    half_dim = HD // 2
    frequency = jnp.exp(-math.log(10000.0) * jnp.arange(half_dim, dtype=jnp.float32) / half_dim)
    angles = positions[:, None] * frequency[None, :]
    return (jnp.cos(angles), jnp.sin(angles))

def rotate(vectors, cos_table, sin_table):
    half_dim = vectors.shape[-1] // 2
    leading = vectors[..., :half_dim]
    trailing = vectors[..., half_dim:]
    cosine = cos_table[:, None, :]
    sine_part = sin_table[:, None, :]
    return jnp.concatenate([leading * cosine - trailing * sine_part, trailing * cosine + leading * sine_part], axis=-1)

def one_seq(params, resid_in, cond_act):
    w_ada, b_ada, gain_one, w_qkv, w_out, gain_two, w_up, b_up, w_down, b_down = params
    length, model_width = resid_in.shape
    modulation = jnp.dot(cond_act, w_ada, precision=PRECISE) + b_ada
    shift_one, scale_one, gate_one, shift_two, scale_two, gate_two = jnp.split(modulation, 6)
    act_one = low(layer_norm(resid_in) * gain_one * (1.0 + scale_one) + shift_one)
    projected = low_back(jnp.dot(act_one, w_qkv, precision=PRECISE))
    q_part, k_part, v_part = jnp.split(projected, 3, axis=-1)
    head_shape = (length, HEADS, HD)
    cos_table, sin_table = rotary_tables(jnp.arange(length, dtype=jnp.float32))
    queries = low_back(low(rotate(q_part.reshape(head_shape), cos_table, sin_table)))
    keys_all = low_back(low(rotate(k_part.reshape(head_shape), cos_table, sin_table)))
    values = low_back(low(v_part.reshape(head_shape)))
    scores = low_back(jnp.einsum('qhd,khd->hqk', queries, keys_all, precision=PRECISE) * HD ** (-0.5))
    soft_out = low(jax.nn.softmax(scores, axis=-1))
    mixture = jnp.einsum('hqk,khd->qhd', soft_out, values, precision=PRECISE).reshape(length, model_width)
    attended = low_back(low(mixture))
    branch = low_back(jnp.dot(attended, w_out, precision=PRECISE))
    x_one = resid_in + gate_one * branch
    act_two = low(layer_norm(x_one) * gain_two * (1.0 + scale_two) + shift_two)
    up_proj = low_back(jnp.dot(act_two, w_up, precision=PRECISE) + b_up)
    hidden = low(jax.nn.gelu(up_proj, approximate=True))
    down_proj = low_back(jnp.dot(hidden, w_down, precision=PRECISE) + b_down)
    return x_one + gate_two * down_proj

def reference(tokens, cotangent, time_index, span_starts, span_lengths, w_ada, b_ada, gain_one, w_qkv, w_out, gain_two, w_up, b_up, w_down, b_down):
    params = tuple((weight.astype(jnp.float32) for weight in (w_ada, b_ada, gain_one, w_qkv, w_out, gain_two, w_up, b_up, w_down, b_down)))
    cond_act = jax.nn.silu(time_features(time_index))
    positions = jnp.arange(LENGTH, dtype=jnp.int32)
    inside = (positions[None, :] >= span_starts[:, None]) & (positions[None, :] < (span_starts + span_lengths)[:, None])
    span_weight = jnp.where(inside, 2.0, 0.5).astype(jnp.float32)
    grad_out = cotangent.astype(jnp.float32) * span_weight[:, :, None]
    resid_in = tokens.astype(jnp.float32)

    def forward(inputs_all, params_all):

        def per_seq(entries):
            return one_seq(params_all, entries[0], entries[1])
        return lax.map(jax.checkpoint(per_seq), (inputs_all, cond_act))
    output, pull_back = jax.vjp(forward, resid_in, params)
    grad_in, weight_grads = pull_back(grad_out)
    return (output.astype(jnp.bfloat16), grad_in, weight_grads[0], weight_grads[1], weight_grads[2], weight_grads[3], weight_grads[4], weight_grads[5], weight_grads[6], weight_grads[7], weight_grads[8], weight_grads[9])
```

```python
import functools
import math

import jax
import jax.numpy as jnp
from jax import lax
from jax.experimental import pallas as pl
from jax.experimental.pallas import tpu as pltpu
from jax.sharding import PartitionSpec as P

HEADS = 12
HD = 64
PAIRS = HEADS // 2
NORM_EPS = 1e-05
LOG2E = math.log2(math.e)
BF = jnp.bfloat16
F32 = jnp.float32
MIB = 1 << 20

NN = (((1,), (0,)), ((), ()))
NT = (((1,), (1,)), ((), ()))
TN = (((0,), (0,)), ((), ()))


def mm(a, b, dims=NN):
    return lax.dot_general(a, b, dims, preferred_element_type=F32)


def norm_parts(x):
    centre = x - jnp.mean(x, axis=-1, keepdims=True)
    rstd = lax.rsqrt(jnp.mean(centre * centre, axis=-1, keepdims=True) + NORM_EPS)
    return centre * rstd, rstd


def norm_pull(n, rstd, dn):
    return rstd * (
        dn - jnp.mean(dn, axis=-1, keepdims=True) - n * jnp.mean(dn * n, axis=-1, keepdims=True)
    )


def col_sum(x):
    return jnp.sum(x, axis=0, keepdims=True)


def rows_of(size, index):
    return pl.ds(pl.multiple_of(index * size, size), size)


def params(mib=56):
    return pltpu.CompilerParams(vmem_limit_bytes=mib * MIB)


def whole(shape):
    zeros = (0,) * len(shape)
    return pl.BlockSpec(shape, lambda *_: zeros)


def project_kernel(own_ref, rem_ref, vec_ref, cos_ref, sin_ref, w_ref, act_ref, out_ref):
    step = pl.program_id(0)
    half, _ = own_ref.shape
    tile = 256

    @pl.when(step == 0)
    def _():
        scale = vec_ref[0:1, :]
        shift = vec_ref[1:2, :]
        for part, ref in enumerate((own_ref, rem_ref)):
            for t in range(half // tile):
                n, _ = norm_parts(ref[t * tile : (t + 1) * tile, :].astype(F32))
                act = (n * scale + shift).astype(BF)
                start = part * half + t * tile
                act_ref[:, start : start + tile] = act.T

    proj = mm(w_ref[...], act_ref[...])
    heads = proj.shape[0] // HD
    tokens = proj.shape[1]

    @pl.when(step < 4)
    def _():
        factor = jnp.where(step < 2, HD**-0.5, 1.0)
        cos = cos_ref[...] * factor
        sin = sin_ref[...] * factor
        for h in range(heads):
            a = proj[h * HD : h * HD + HD // 2]
            b = proj[h * HD + HD // 2 : (h + 1) * HD]
            out_ref[h * HD : h * HD + HD // 2, :] = (a * cos - b * sin).astype(BF)
            out_ref[h * HD + HD // 2 : (h + 1) * HD, :] = (b * cos + a * sin).astype(BF)

    @pl.when(step >= 4)
    def _():
        out_ref[...] = proj.astype(BF)


def project(own, rem, vec, cos_t, sin_t, w_qkv_t):
    half, width = own.shape
    tokens = 2 * half
    blk = width // 2
    return pl.pallas_call(
        project_kernel,
        grid=(6,),
        in_specs=[
            whole(own.shape),
            whole(rem.shape),
            whole(vec.shape),
            whole(cos_t.shape),
            whole(sin_t.shape),
            pl.BlockSpec((blk, width), lambda i: (i, 0)),
        ],
        out_specs=[
            whole((width, tokens)),
            pl.BlockSpec((blk, tokens), lambda i: (i, 0)),
        ],
        out_shape=[
            jax.ShapeDtypeStruct((width, tokens), BF),
            jax.ShapeDtypeStruct((3 * width, tokens), BF),
        ],
        compiler_params=params(),
        cost_estimate=pl.CostEstimate(
            flops=6 * tokens * width * width, bytes_accessed=14 << 20, transcendentals=0
        ),
        name="project",
    )(own, rem, vec, cos_t, sin_t, w_qkv_t)


def attend_kernel(q_ref, k_ref, v_ref, att_ref, e_ref, linv_ref, q_mask, v_ext):
    tokens = q_ref.shape[1]
    tile = 256
    zero = jnp.zeros((HD, tokens), BF)
    k_nat = k_ref[...].T
    q_mask[0, 0:HD, :] = q_ref[0:HD, :]
    q_mask[0, HD:, :] = zero
    q_mask[1, 0:HD, :] = zero
    q_mask[1, HD:, :] = q_ref[HD:, :]
    for h in range(2):
        v_ext[h, 0:HD, :] = v_ref[h * HD : (h + 1) * HD, :]
        v_ext[h, HD:, :] = jnp.ones((16, tokens), BF)
    for h in range(2):
        for t in range(tokens // tile):
            cols = slice(t * tile, (t + 1) * tile)
            s = mm(k_nat, q_mask[h, :, cols])
            top = jnp.max(s, axis=0, keepdims=True)
            e = jnp.exp(s - top).astype(BF)
            e_ref[h, :, cols] = e
            mix = mm(v_ext[h], e)
            linv = 1.0 / mix[HD : HD + 1, :]
            linv_ref[0, h : h + 1, cols] = linv
            att_ref[h * HD : (h + 1) * HD, cols] = (mix[0:HD, :] * linv).astype(BF)


def attend(qkv_t):
    tokens = qkv_t.shape[1]
    width = HEADS * HD

    def part(k):
        return pl.BlockSpec((2 * HD, tokens), lambda i: (i + k * PAIRS, 0))

    return pl.pallas_call(
        attend_kernel,
        grid=(PAIRS,),
        in_specs=[part(0), part(1), part(2)],
        out_specs=[
            part(0),
            pl.BlockSpec((2, tokens, tokens), lambda i: (i, 0, 0)),
            pl.BlockSpec((1, 8, tokens), lambda i: (i, 0, 0)),
        ],
        out_shape=[
            jax.ShapeDtypeStruct((width, tokens), BF),
            jax.ShapeDtypeStruct((HEADS, tokens, tokens), BF),
            jax.ShapeDtypeStruct((PAIRS, 8, tokens), F32),
        ],
        scratch_shapes=[
            pltpu.VMEM((2, 2 * HD, tokens), BF),
            pltpu.VMEM((2, HD + 16, tokens), BF),
        ],
        compiler_params=params(),
        cost_estimate=pl.CostEstimate(
            flops=16 * tokens * tokens * width,
            bytes_accessed=30 << 20,
            transcendentals=HEADS * tokens * tokens,
        ),
        name="attend",
    )(qkv_t, qkv_t, qkv_t)


def gelu_both(u):
    c = math.sqrt(2.0 / math.pi)
    u2 = u * u
    th = jnp.tanh(u * (c + (c * 0.044715) * u2))
    half = 0.5 * (1.0 + th)
    value = u * half
    slope = half + (0.5 * u) * (1.0 - th * th) * (c + (3.0 * c * 0.044715) * u2)
    return value, slope


def middle_kernel(
    att_ref,
    tok_own,
    tok_rem,
    cot_own,
    cot_rem,
    span_ref,
    vec_ref,
    b_up_ref,
    w_out_ref,
    w_up_ref,
    w_down_ref,
    out_own,
    out_rem,
    dx_ref,
    d_att_ref,
    g_out_ref,
    g_up_ref,
    g_down_ref,
    g_bup_ref,
    sums_ref,
    branch,
    x_one,
    act_two,
    d_down,
    down_acc,
    d_act,
    d_branch,
):
    step = pl.program_id(0)
    steps = pl.num_programs(0)
    tokens = att_ref.shape[1]
    half = tokens // 2
    tile = 256
    per_half = half // tile
    gate_one = vec_ref[0:1, :]
    mult_two = vec_ref[1:2, :]
    shift_two = vec_ref[2:3, :]
    gate_two = vec_ref[3:4, :]
    b_down = vec_ref[4:5, :]
    gain_two = vec_ref[5:6, :]
    scale_two = vec_ref[6:7, :]

    @pl.when(step == 0)
    def _():
        for part, (tok, cot) in enumerate(((tok_own, cot_own), (tok_rem, cot_rem))):
            for t in range(per_half):
                src = slice(t * tile, (t + 1) * tile)
                dst = slice(part * half + t * tile, part * half + (t + 1) * tile)
                br = mm(att_ref[:, dst], w_out_ref[...], TN)
                branch[dst, :] = br
                x = tok[src, :].astype(F32) + gate_one * br
                x_one[dst, :] = x
                n, _ = norm_parts(x)
                act_two[dst, :] = (n * mult_two + shift_two).astype(BF)
                grad_out = cot[src, :].astype(F32) * span_ref[dst, :]
                d_down[dst, :] = (gate_two * grad_out).astype(BF)

    up = mm(act_two[...], w_up_ref[...]) + b_up_ref[...]
    value, slope = gelu_both(up)
    hidden = value.astype(BF)
    d_hidden = mm(d_down[...], w_down_ref[...], NT)
    d_up_full = slope * d_hidden
    d_up = d_up_full.astype(BF)
    g_bup_ref[...] = col_sum(d_up.astype(F32))
    down_part = mm(hidden, w_down_ref[...])
    d_act_part = mm(d_up, w_up_ref[...], NT)
    g_down_ref[...] = mm(hidden, d_down[...], TN).astype(BF)
    g_up_ref[...] = mm(act_two[...], d_up, TN).astype(BF)

    @pl.when(step == 0)
    def _():
        down_acc[...] = down_part
        d_act[...] = d_act_part

    @pl.when(step > 0)
    def _():
        down_acc[...] += down_part
        d_act[...] += d_act_part

    @pl.when(step == steps - 1)
    def _():
        zero = jnp.zeros((1, gate_one.shape[1]), F32)
        s_gate_two, s_shift, s_pull, s_gate_one, s_bdown = zero, zero, zero, zero, zero
        for part, (cot, out) in enumerate(((cot_own, out_own), (cot_rem, out_rem))):
            for t in range(per_half):
                src = slice(t * tile, (t + 1) * tile)
                dst = slice(part * half + t * tile, part * half + (t + 1) * tile)
                x = x_one[dst, :]
                down = down_acc[dst, :] + b_down
                out[src, :] = (x + gate_two * down).astype(BF)
                grad_out = cot[src, :].astype(F32) * span_ref[dst, :]
                s_gate_two += col_sum(grad_out * down)
                s_bdown += col_sum(d_down[dst, :].astype(F32))
                n, rstd = norm_parts(x)
                da = d_act[dst, :]
                s_shift += col_sum(da)
                s_pull += col_sum(da * n)
                dx = grad_out + norm_pull(n, rstd, da * mult_two)
                dx_ref[dst, :] = dx
                s_gate_one += col_sum(dx * branch[dst, :])
                d_branch[dst, :] = (gate_one * dx).astype(BF)
        sums_ref[0:1, :] = s_gate_one
        sums_ref[1:2, :] = s_shift
        sums_ref[2:3, :] = s_pull * gain_two
        sums_ref[3:4, :] = s_gate_two
        sums_ref[4:5, :] = s_pull * (1.0 + scale_two)
        sums_ref[5:6, :] = s_bdown
        sums_ref[6:8, :] = jnp.zeros((2, gate_one.shape[1]), F32)
        g_out_ref[...] = mm(att_ref[...], d_branch[...]).astype(BF)
        d_att_ref[...] = mm(w_out_ref[...], d_branch[...], NT).astype(BF)


def middle(att_t, tok_own, tok_rem, cot_own, cot_rem, span, vec, b_up, w_out, w_up, w_down):
    width, tokens = att_t.shape
    half = tokens // 2
    ff = w_up.shape[1]
    tile = 512
    return pl.pallas_call(
        middle_kernel,
        grid=(ff // tile,),
        in_specs=[
            whole(att_t.shape),
            whole(tok_own.shape),
            whole(tok_rem.shape),
            whole(cot_own.shape),
            whole(cot_rem.shape),
            whole(span.shape),
            whole(vec.shape),
            pl.BlockSpec((1, tile), lambda i: (0, i)),
            whole(w_out.shape),
            pl.BlockSpec((width, tile), lambda i: (0, i)),
            pl.BlockSpec((tile, width), lambda i: (i, 0)),
        ],
        out_specs=[
            whole((half, width)),
            whole((half, width)),
            whole((tokens, width)),
            whole((width, tokens)),
            whole((width, width)),
            pl.BlockSpec((width, tile), lambda i: (0, i)),
            pl.BlockSpec((tile, width), lambda i: (i, 0)),
            pl.BlockSpec((1, tile), lambda i: (0, i)),
            whole((8, width)),
        ],
        out_shape=[
            jax.ShapeDtypeStruct((half, width), BF),
            jax.ShapeDtypeStruct((half, width), BF),
            jax.ShapeDtypeStruct((tokens, width), F32),
            jax.ShapeDtypeStruct((width, tokens), BF),
            jax.ShapeDtypeStruct((width, width), BF),
            jax.ShapeDtypeStruct((width, ff), BF),
            jax.ShapeDtypeStruct((ff, width), BF),
            jax.ShapeDtypeStruct((1, ff), F32),
            jax.ShapeDtypeStruct((8, width), F32),
        ],
        scratch_shapes=[
            pltpu.VMEM((tokens, width), F32),
            pltpu.VMEM((tokens, width), F32),
            pltpu.VMEM((tokens, width), BF),
            pltpu.VMEM((tokens, width), BF),
            pltpu.VMEM((tokens, width), F32),
            pltpu.VMEM((tokens, width), F32),
            pltpu.VMEM((tokens, width), BF),
        ],
        compiler_params=params(),
        cost_estimate=pl.CostEstimate(
            flops=12 * tokens * width * ff + 6 * tokens * width * width,
            bytes_accessed=40 << 20,
            transcendentals=tokens * ff,
        ),
        name="middle",
    )(att_t, tok_own, tok_rem, cot_own, cot_rem, span, vec, b_up, w_out, w_up, w_down)


def attend_back_kernel(
    q_ref, k_ref, v_ref, att_ref, d_att_ref, e_ref, linv_ref, cos_ref, sin_ref, out_ref, do_mask
):
    tokens = q_ref.shape[1]
    tile = 256
    zero = jnp.zeros((HD, tokens), BF)
    v_nat = v_ref[...].T
    cos = cos_ref[...]
    sin = sin_ref[...]

    def unrotate(x):
        low = x.astype(BF).astype(F32)
        a, b = low[0 : HD // 2], low[HD // 2 :]
        return a * cos + b * sin, b * cos - a * sin

    for h in range(2):
        rows = slice(h * HD, (h + 1) * HD)
        linv = linv_ref[0, h : h + 1, :]
        d_o = d_att_ref[rows, :].astype(F32)
        d_os = (d_o * linv).astype(BF)
        do_mask[h, rows, :] = d_os
        do_mask[h, (1 - h) * HD : (2 - h) * HD, :] = zero
        inner = col_sum(d_o * att_ref[rows, :].astype(F32)) * linv
        d_values = mm(d_os, e_ref[h], NT)
        out_ref[2, rows, :] = d_values.astype(BF)
        d_keys = jnp.zeros((HD, tokens), F32)
        d_queries = []
        for t in range(tokens // tile):
            cols = slice(t * tile, (t + 1) * tile)
            d_probs = mm(v_nat, do_mask[h, :, cols])
            d_s = (e_ref[h, :, cols].astype(F32) * (d_probs - inner[:, cols])).astype(BF)
            d_queries.append(mm(k_ref[rows, :], d_s))
            d_keys += mm(q_ref[rows, cols], d_s, NT)
        dq = jnp.concatenate(d_queries, axis=1) * HD**-0.5
        lead, trail = unrotate(dq)
        out_ref[0, h * HD : h * HD + HD // 2, :] = lead.astype(BF)
        out_ref[0, h * HD + HD // 2 : (h + 1) * HD, :] = trail.astype(BF)
        lead, trail = unrotate(d_keys)
        out_ref[1, h * HD : h * HD + HD // 2, :] = lead.astype(BF)
        out_ref[1, h * HD + HD // 2 : (h + 1) * HD, :] = trail.astype(BF)


def attend_back(qkv_t, att_t, d_att_t, e, linv, cos_t, sin_t):
    tokens = qkv_t.shape[1]
    width = HEADS * HD

    def part(k):
        return pl.BlockSpec((2 * HD, tokens), lambda i: (i + k * PAIRS, 0))

    return pl.pallas_call(
        attend_back_kernel,
        grid=(PAIRS,),
        in_specs=[
            part(0),
            part(1),
            part(2),
            part(0),
            part(0),
            pl.BlockSpec((2, tokens, tokens), lambda i: (i, 0, 0)),
            pl.BlockSpec((1, 8, tokens), lambda i: (i, 0, 0)),
            whole(cos_t.shape),
            whole(sin_t.shape),
        ],
        out_specs=pl.BlockSpec((3, 2 * HD, tokens), lambda i: (0, i, 0)),
        out_shape=jax.ShapeDtypeStruct((3, width, tokens), BF),
        scratch_shapes=[pltpu.VMEM((2, 2 * HD, tokens), BF)],
        compiler_params=params(),
        cost_estimate=pl.CostEstimate(
            flops=32 * tokens * tokens * width, bytes_accessed=36 << 20, transcendentals=0
        ),
        name="attend_back",
    )(qkv_t, qkv_t, qkv_t, att_t, d_att_t, e, linv, cos_t, sin_t)


def tail_kernel(tok_own, tok_rem, d_proj_ref, w_ref, dx_ref, vec_ref, own_ref, rem_ref, sums_ref):
    step = pl.program_id(0)
    steps = pl.num_programs(0)
    mult_one = vec_ref[0:1, :]
    gain_one = vec_ref[2:3, :]
    scale_one = vec_ref[3:4, :]
    d_act = mm(d_proj_ref[...], w_ref[...], TN)

    def finish(tok, out):
        n, rstd = norm_parts(tok[...].astype(F32))
        grad = dx_ref[...] + norm_pull(n, rstd, d_act * mult_one)
        out[...] = grad.astype(out.dtype)
        return col_sum(d_act), col_sum(d_act * n)

    @pl.when(step == 0)
    def _():
        shift, pull = finish(tok_rem, rem_ref)
        sums_ref[0:1, :] = shift
        sums_ref[1:2, :] = pull
        sums_ref[2:, :] = jnp.zeros((6, shift.shape[1]), F32)

    @pl.when(step == steps - 1)
    def _():
        shift, pull = finish(tok_own, own_ref)
        shift = sums_ref[0:1, :] + shift
        pull = sums_ref[1:2, :] + pull
        sums_ref[0:1, :] = shift
        sums_ref[1:2, :] = pull * gain_one
        sums_ref[2:3, :] = pull * (1.0 + scale_one)


def tail(tok_own, tok_rem, d_proj_t, w_qkv_t, dx, vec):
    half, width = tok_own.shape
    return pl.pallas_call(
        tail_kernel,
        grid=(2,),
        in_specs=[
            whole(tok_own.shape),
            whole(tok_rem.shape),
            pl.BlockSpec((3 * width, half), lambda i: (0, 1 - i)),
            whole(w_qkv_t.shape),
            pl.BlockSpec((half, width), lambda i: (1 - i, 0)),
            whole(vec.shape),
        ],
        out_specs=[whole((half, width)), whole((half, width)), whole((8, width))],
        out_shape=[
            jax.ShapeDtypeStruct((half, width), F32),
            jax.ShapeDtypeStruct((half, width), BF),
            jax.ShapeDtypeStruct((8, width), F32),
        ],
        compiler_params=params(),
        cost_estimate=pl.CostEstimate(
            flops=12 * half * width * width, bytes_accessed=20 << 20, transcendentals=0
        ),
        name="tail",
    )(tok_own, tok_rem, d_proj_t, w_qkv_t, dx, vec)


def weight_grad_kernel(act_ref, d_proj_ref, out_ref):
    out_ref[...] = mm(act_ref[...], d_proj_ref[...], NT).astype(BF)


def weight_grad(act_t, d_proj_t):
    width, tokens = act_t.shape
    cols = d_proj_t.shape[0]
    tile = 768
    return pl.pallas_call(
        weight_grad_kernel,
        grid=(cols // tile,),
        in_specs=[whole(act_t.shape), pl.BlockSpec((tile, tokens), lambda i: (i, 0))],
        out_specs=pl.BlockSpec((width, tile), lambda i: (0, i)),
        out_shape=jax.ShapeDtypeStruct((width, cols), BF),
        compiler_params=params(),
        cost_estimate=pl.CostEstimate(
            flops=2 * cols * width * tokens, bytes_accessed=12 << 20, transcendentals=0
        ),
        name="weight_grad",
    )(act_t, d_proj_t)


def time_features(time_steps, pair_count):
    frequency = jnp.exp(-math.log(10000.0) * jnp.arange(pair_count, dtype=F32) / pair_count)
    angles = time_steps.astype(F32)[:, None] * frequency[None, :]
    return jnp.concatenate([jnp.cos(angles), jnp.sin(angles)], axis=-1)


def per_device(
    tokens,
    cotangent,
    time_index,
    span_starts,
    span_lengths,
    w_ada,
    b_ada,
    gain_one,
    w_qkv,
    w_out,
    gain_two,
    w_up,
    b_up,
    w_down,
    b_down,
):
    seqs_dev, half, width = tokens.shape
    length = 2 * half
    rank = lax.axis_index("seq")
    swap = [(0, 1), (1, 0)]

    def pick(x, i):
        return lax.dynamic_index_in_dim(x, i, 0, keepdims=False)

    tok_own, tok_send = pick(tokens, rank), pick(tokens, 1 - rank)
    cot_own, cot_send = pick(cotangent, rank), pick(cotangent, 1 - rank)
    tok_rem = lax.ppermute(tok_send, "seq", swap)
    cot_rem = lax.ppermute(cot_send, "seq", swap)

    here = jnp.arange(half, dtype=jnp.int32)
    place = jnp.concatenate([rank * half + here, (1 - rank) * half + here])
    frequency = jnp.exp(-math.log(10000.0) * jnp.arange(HD // 2, dtype=F32) / (HD // 2))
    angles = frequency[:, None] * place.astype(F32)[None, :]
    cos_t, sin_t = jnp.cos(angles), jnp.sin(angles)
    start, extent = pick(span_starts, rank), pick(span_lengths, rank)
    span = jnp.where((place >= start) & (place < start + extent), 2.0, 0.5).astype(F32)[:, None]

    time_own = lax.dynamic_slice_in_dim(time_index, rank, 1)
    cond_act = jax.nn.silu(time_features(time_own, w_ada.shape[0] // 2))
    modulation = (
        jnp.dot(cond_act, w_ada.astype(F32), precision=lax.Precision.HIGHEST)[0] + b_ada
    )
    shift_one, scale_one, gate_one, shift_two, scale_two, gate_two = jnp.split(modulation, 6)
    zeros = jnp.zeros_like(shift_one)
    vec_one = jnp.stack(
        [gain_one * (1.0 + scale_one), shift_one, gain_one, scale_one, zeros, zeros, zeros, zeros]
    )
    vec_two = jnp.stack(
        [
            gate_one,
            gain_two * (1.0 + scale_two),
            shift_two,
            gate_two,
            b_down,
            gain_two,
            scale_two,
            zeros,
        ]
    )
    w_qkv_t = w_qkv.T

    act_t, qkv_t = project(tok_own, tok_rem, vec_one, cos_t, sin_t, w_qkv_t)
    att_t, e, linv = attend(qkv_t)
    out_own, out_rem, dx, d_att_t, g_out, g_up, g_down, g_bup, sums_two = middle(
        att_t, tok_own, tok_rem, cot_own, cot_rem, span, vec_two, b_up[None], w_out, w_up, w_down
    )
    d_proj = attend_back(qkv_t, att_t, d_att_t, e, linv, cos_t, sin_t)
    d_proj_t = d_proj.reshape(3 * width, length)
    g_own, g_rem, sums_one = tail(tok_own, tok_rem, d_proj_t, w_qkv_t, dx, vec_one)
    g_qkv = weight_grad(act_t, d_proj_t)

    def spread(own, other):
        first = jnp.where(rank == 0, own, other)
        second = jnp.where(rank == 0, other, own)
        return jnp.stack([first, second])

    output = spread(out_own, lax.ppermute(out_rem, "seq", swap))
    grad_tokens = spread(g_own, lax.ppermute(g_rem, "seq", swap).astype(F32))

    gate_sums = jnp.concatenate([sums_two[:6].reshape(-1), g_bup[0], time_own.astype(F32)])
    early = lax.all_gather(gate_sums, ("dp", "seq"))
    late = lax.all_gather(sums_one[:3].reshape(-1), ("dp", "seq"))
    everyone = early[:, -1]
    ff = w_up.shape[1]
    features = jax.nn.silu(time_features(everyone, w_ada.shape[0] // 2))
    d_mod = jnp.concatenate([late[:, : 2 * width], early[:, : 4 * width]], axis=1)
    dp = lax.axis_index("dp")

    def mine(x, axis=0):
        size = x.shape[axis] // lax.axis_size("dp")
        return lax.dynamic_slice_in_dim(x, dp * size, size, axis)

    s_w_ada = jnp.dot(mine(features, 1).T, d_mod, precision=lax.Precision.HIGHEST)
    s_b_ada = jnp.sum(mine(d_mod, 1), axis=0)
    s_gain_one = jnp.sum(mine(late[:, 2 * width :], 1), axis=0)
    s_gain_two = jnp.sum(mine(early[:, 4 * width : 5 * width], 1), axis=0)
    s_b_down = jnp.sum(mine(early[:, 5 * width : 6 * width], 1), axis=0)
    s_b_up = jnp.sum(mine(early[:, 6 * width : 6 * width + ff], 1), axis=0)

    def reduce_rows(g):
        part = lax.psum_scatter(g, "dp", scatter_dimension=0, tiled=True)
        return lax.psum(part, "seq").astype(F32)

    return (
        output,
        grad_tokens,
        s_w_ada,
        s_b_ada,
        s_gain_one,
        reduce_rows(g_qkv),
        reduce_rows(g_out),
        s_gain_two,
        reduce_rows(g_up),
        s_b_up,
        reduce_rows(g_down),
        s_b_down,
    )


def solution(mesh):
    rows = P("dp", "seq", None)
    return jax.shard_map(
        per_device,
        mesh=mesh,
        in_specs=(rows, rows, P("dp"), P("dp"), P("dp")) + (P(),) * 10,
        out_specs=(
            rows,
            rows,
            P("dp", None),
            P("dp"),
            P("dp"),
            P("dp", None),
            P("dp", None),
            P("dp"),
            P("dp", None),
            P("dp"),
            P("dp", None),
            P("dp"),
        ),
        check_vma=False,
    )
```

```python
import functools
import math

import jax
import jax.numpy as jnp
from jax import lax
from jax.experimental import pallas as pl
from jax.experimental.pallas import tpu as pltpu
from jax.sharding import PartitionSpec as P

HEADS = 12
HD = 64
PAIRS = HEADS // 2
NORM_EPS = 1e-05
LOG2E = math.log2(math.e)
BF = jnp.bfloat16
F32 = jnp.float32
MIB = 1 << 20

NN = (((1,), (0,)), ((), ()))
NT = (((1,), (1,)), ((), ()))
TN = (((0,), (0,)), ((), ()))


def mm(a, b, dims=NN):
    return lax.dot_general(a, b, dims, preferred_element_type=F32)


def norm_parts(x):
    centre = x - jnp.mean(x, axis=-1, keepdims=True)
    rstd = lax.rsqrt(jnp.mean(centre * centre, axis=-1, keepdims=True) + NORM_EPS)
    return centre * rstd, rstd


def norm_pull(n, rstd, dn):
    return rstd * (
        dn - jnp.mean(dn, axis=-1, keepdims=True) - n * jnp.mean(dn * n, axis=-1, keepdims=True)
    )


def col_sum(x):
    return jnp.sum(x, axis=0, keepdims=True)


def rows_of(size, index):
    return pl.ds(pl.multiple_of(index * size, size), size)


def params(mib=56, collective_id=None):
    if collective_id is None:
        return pltpu.CompilerParams(vmem_limit_bytes=mib * MIB)
    return pltpu.CompilerParams(
        vmem_limit_bytes=mib * MIB, collective_id=collective_id, has_side_effects=True
    )


def whole(shape):
    zeros = (0,) * len(shape)
    return pl.BlockSpec(shape, lambda *_: zeros)


MESH = pl.DeviceIdType.MESH
ANY = pl.BlockSpec(memory_space=pl.ANY)
SEMS = [pltpu.SemaphoreType.DMA, pltpu.SemaphoreType.DMA]


def greet(*partners):
    barrier = pltpu.get_barrier_semaphore()
    for partner in partners:
        pl.semaphore_signal(barrier, inc=1, device_id=partner, device_id_type=MESH)
    pl.semaphore_wait(barrier, len(partners))


def remote(src, dst, send, recv, device):
    return pltpu.make_async_remote_copy(
        src_ref=src, dst_ref=dst, send_sem=send, recv_sem=recv, device_id=device, device_id_type=MESH
    )


def seq_partner():
    return (lax.axis_index("dp"), 1 - lax.axis_index("seq"))


def swap_start(src, dst, send, recv):
    partner = seq_partner()
    greet(partner)
    remote(src, dst, send, recv, partner).start()


def swap_wait(src, dst, send, recv):
    remote(src, dst, send, recv, seq_partner()).wait()


def project_kernel(own_ref, rem_ref, vec_ref, cos_ref, sin_ref, w_ref, act_ref, out_ref):
    step = pl.program_id(0)
    half, _ = own_ref.shape
    tile = 256

    @pl.when(step == 0)
    def _():
        scale = vec_ref[0:1, :]
        shift = vec_ref[1:2, :]
        for part, ref in enumerate((own_ref, rem_ref)):
            for t in range(half // tile):
                n, _ = norm_parts(ref[t * tile : (t + 1) * tile, :].astype(F32))
                act = (n * scale + shift).astype(BF)
                start = part * half + t * tile
                act_ref[:, start : start + tile] = act.T

    proj = mm(w_ref[...], act_ref[...])
    heads = proj.shape[0] // HD
    tokens = proj.shape[1]

    @pl.when(step < 4)
    def _():
        factor = jnp.where(step < 2, HD**-0.5, 1.0)
        cos = cos_ref[...] * factor
        sin = sin_ref[...] * factor
        for h in range(heads):
            a = proj[h * HD : h * HD + HD // 2]
            b = proj[h * HD + HD // 2 : (h + 1) * HD]
            out_ref[h * HD : h * HD + HD // 2, :] = (a * cos - b * sin).astype(BF)
            out_ref[h * HD + HD // 2 : (h + 1) * HD, :] = (b * cos + a * sin).astype(BF)

    @pl.when(step >= 4)
    def _():
        out_ref[...] = proj.astype(BF)


def project(own, rem, vec, cos_t, sin_t, w_qkv_t):
    half, width = own.shape
    tokens = 2 * half
    blk = width // 2
    return pl.pallas_call(
        project_kernel,
        grid=(6,),
        in_specs=[
            whole(own.shape),
            whole(rem.shape),
            whole(vec.shape),
            whole(cos_t.shape),
            whole(sin_t.shape),
            pl.BlockSpec((blk, width), lambda i: (i, 0)),
        ],
        out_specs=[
            whole((width, tokens)),
            pl.BlockSpec((blk, tokens), lambda i: (i, 0)),
        ],
        out_shape=[
            jax.ShapeDtypeStruct((width, tokens), BF),
            jax.ShapeDtypeStruct((3 * width, tokens), BF),
        ],
        compiler_params=params(),
        cost_estimate=pl.CostEstimate(
            flops=6 * tokens * width * width, bytes_accessed=14 << 20, transcendentals=0
        ),
        name="project",
    )(own, rem, vec, cos_t, sin_t, w_qkv_t)


def attend_kernel(
    q_ref, k_ref, v_ref, cot_ref, att_ref, e_ref, linv_ref, cot_rem, q_mask, v_ext, send, recv
):
    step = pl.program_id(0)
    cot_send = cot_ref.at[1 - lax.axis_index("seq")]

    @pl.when(step == 0)
    def _():
        swap_start(cot_send, cot_rem, send, recv)

    tokens = q_ref.shape[1]
    tile = 256
    zero = jnp.zeros((HD, tokens), BF)
    k_nat = k_ref[...].T
    q_mask[0, 0:HD, :] = q_ref[0:HD, :]
    q_mask[0, HD:, :] = zero
    q_mask[1, 0:HD, :] = zero
    q_mask[1, HD:, :] = q_ref[HD:, :]
    for h in range(2):
        v_ext[h, 0:HD, :] = v_ref[h * HD : (h + 1) * HD, :]
        v_ext[h, HD:, :] = jnp.ones((16, tokens), BF)
    for h in range(2):
        for t in range(tokens // tile):
            cols = slice(t * tile, (t + 1) * tile)
            s = mm(k_nat, q_mask[h, :, cols])
            top = jnp.max(s, axis=0, keepdims=True)
            e = jnp.exp(s - top).astype(BF)
            e_ref[h, :, cols] = e
            mix = mm(v_ext[h], e)
            linv = 1.0 / mix[HD : HD + 1, :]
            linv_ref[0, h : h + 1, cols] = linv
            att_ref[h * HD : (h + 1) * HD, cols] = (mix[0:HD, :] * linv).astype(BF)

    @pl.when(step == pl.num_programs(0) - 1)
    def _():
        swap_wait(cot_send, cot_rem, send, recv)


def attend(qkv_t, cotangent):
    tokens = qkv_t.shape[1]
    width = HEADS * HD

    def part(k):
        return pl.BlockSpec((2 * HD, tokens), lambda i: (i + k * PAIRS, 0))

    return pl.pallas_call(
        attend_kernel,
        grid=(PAIRS,),
        in_specs=[part(0), part(1), part(2), ANY],
        out_specs=[
            part(0),
            pl.BlockSpec((2, tokens, tokens), lambda i: (i, 0, 0)),
            pl.BlockSpec((1, 8, tokens), lambda i: (i, 0, 0)),
            ANY,
        ],
        out_shape=[
            jax.ShapeDtypeStruct((width, tokens), BF),
            jax.ShapeDtypeStruct((HEADS, tokens, tokens), BF),
            jax.ShapeDtypeStruct((PAIRS, 8, tokens), F32),
            jax.ShapeDtypeStruct(cotangent.shape[1:], BF),
        ],
        scratch_shapes=[
            pltpu.VMEM((2, 2 * HD, tokens), BF),
            pltpu.VMEM((2, HD + 16, tokens), BF),
        ]
        + SEMS,
        compiler_params=params(collective_id=1),
        cost_estimate=pl.CostEstimate(
            flops=16 * tokens * tokens * width,
            bytes_accessed=30 << 20,
            transcendentals=HEADS * tokens * tokens,
        ),
        name="attend",
    )(qkv_t, qkv_t, qkv_t, cotangent)


def gelu_both(u):
    c = math.sqrt(2.0 / math.pi)
    u2 = u * u
    th = jnp.tanh(u * (c + (c * 0.044715) * u2))
    half = 0.5 * (1.0 + th)
    value = u * half
    slope = half + (0.5 * u) * (1.0 - th * th) * (c + (3.0 * c * 0.044715) * u2)
    return value, slope


def middle_kernel(
    att_ref,
    tok_own,
    tok_rem,
    cot_own,
    cot_rem,
    span_ref,
    vec_ref,
    b_up_ref,
    w_out_ref,
    w_up_ref,
    w_down_ref,
    out_own,
    out_rem,
    dx_ref,
    d_att_ref,
    g_out_ref,
    g_up_ref,
    g_down_ref,
    g_bup_ref,
    sums_ref,
    branch,
    x_one,
    act_two,
    d_down,
    down_acc,
    d_act,
    d_branch,
):
    step = pl.program_id(0)
    steps = pl.num_programs(0)
    tokens = att_ref.shape[1]
    half = tokens // 2
    tile = 256
    per_half = half // tile
    gate_one = vec_ref[0:1, :]
    mult_two = vec_ref[1:2, :]
    shift_two = vec_ref[2:3, :]
    gate_two = vec_ref[3:4, :]
    b_down = vec_ref[4:5, :]
    gain_two = vec_ref[5:6, :]
    scale_two = vec_ref[6:7, :]

    @pl.when(step == 0)
    def _():
        for part, (tok, cot) in enumerate(((tok_own, cot_own), (tok_rem, cot_rem))):
            for t in range(per_half):
                src = slice(t * tile, (t + 1) * tile)
                dst = slice(part * half + t * tile, part * half + (t + 1) * tile)
                br = mm(att_ref[:, dst], w_out_ref[...], TN)
                branch[dst, :] = br
                x = tok[src, :].astype(F32) + gate_one * br
                x_one[dst, :] = x
                n, _ = norm_parts(x)
                act_two[dst, :] = (n * mult_two + shift_two).astype(BF)
                grad_out = cot[src, :].astype(F32) * span_ref[dst, :]
                d_down[dst, :] = (gate_two * grad_out).astype(BF)

    up = mm(act_two[...], w_up_ref[...]) + b_up_ref[...]
    value, slope = gelu_both(up)
    hidden = value.astype(BF)
    d_hidden = mm(d_down[...], w_down_ref[...], NT)
    d_up_full = slope * d_hidden
    d_up = d_up_full.astype(BF)
    g_bup_ref[...] = col_sum(d_up.astype(F32))
    down_part = mm(hidden, w_down_ref[...])
    d_act_part = mm(d_up, w_up_ref[...], NT)
    g_down_ref[...] = mm(hidden, d_down[...], TN).astype(BF)
    g_up_ref[...] = mm(act_two[...], d_up, TN).astype(BF)

    @pl.when(step == 0)
    def _():
        down_acc[...] = down_part
        d_act[...] = d_act_part

    @pl.when(step > 0)
    def _():
        down_acc[...] += down_part
        d_act[...] += d_act_part

    @pl.when(step == steps - 1)
    def _():
        zero = jnp.zeros((1, gate_one.shape[1]), F32)
        s_gate_two, s_shift, s_pull, s_gate_one, s_bdown = zero, zero, zero, zero, zero
        for part, (cot, out) in enumerate(((cot_own, out_own), (cot_rem, out_rem))):
            for t in range(per_half):
                src = slice(t * tile, (t + 1) * tile)
                dst = slice(part * half + t * tile, part * half + (t + 1) * tile)
                x = x_one[dst, :]
                down = down_acc[dst, :] + b_down
                out[src, :] = (x + gate_two * down).astype(BF)
                grad_out = cot[src, :].astype(F32) * span_ref[dst, :]
                s_gate_two += col_sum(grad_out * down)
                s_bdown += col_sum(d_down[dst, :].astype(F32))
                n, rstd = norm_parts(x)
                da = d_act[dst, :]
                s_shift += col_sum(da)
                s_pull += col_sum(da * n)
                dx = grad_out + norm_pull(n, rstd, da * mult_two)
                dx_ref[dst, :] = dx
                s_gate_one += col_sum(dx * branch[dst, :])
                d_branch[dst, :] = (gate_one * dx).astype(BF)
        sums_ref[0:1, :] = s_gate_one
        sums_ref[1:2, :] = s_shift
        sums_ref[2:3, :] = s_pull * gain_two
        sums_ref[3:4, :] = s_gate_two
        sums_ref[4:5, :] = s_pull * (1.0 + scale_two)
        sums_ref[5:6, :] = s_bdown
        sums_ref[6:8, :] = jnp.zeros((2, gate_one.shape[1]), F32)
        g_out_ref[...] = mm(att_ref[...], d_branch[...]).astype(BF)
        d_att_ref[...] = mm(w_out_ref[...], d_branch[...], NT).astype(BF)


def middle(att_t, tok_own, tok_rem, cot_own, cot_rem, span, vec, b_up, w_out, w_up, w_down):
    width, tokens = att_t.shape
    half = tokens // 2
    ff = w_up.shape[1]
    tile = 512
    return pl.pallas_call(
        middle_kernel,
        grid=(ff // tile,),
        in_specs=[
            whole(att_t.shape),
            whole(tok_own.shape),
            whole(tok_rem.shape),
            whole(cot_own.shape),
            whole(cot_rem.shape),
            whole(span.shape),
            whole(vec.shape),
            pl.BlockSpec((1, tile), lambda i: (0, i)),
            whole(w_out.shape),
            pl.BlockSpec((width, tile), lambda i: (0, i)),
            pl.BlockSpec((tile, width), lambda i: (i, 0)),
        ],
        out_specs=[
            whole((half, width)),
            whole((half, width)),
            whole((tokens, width)),
            whole((width, tokens)),
            whole((width, width)),
            pl.BlockSpec((width, tile), lambda i: (0, i)),
            pl.BlockSpec((tile, width), lambda i: (i, 0)),
            pl.BlockSpec((1, tile), lambda i: (0, i)),
            whole((8, width)),
        ],
        out_shape=[
            jax.ShapeDtypeStruct((half, width), BF),
            jax.ShapeDtypeStruct((half, width), BF),
            jax.ShapeDtypeStruct((tokens, width), F32),
            jax.ShapeDtypeStruct((width, tokens), BF),
            jax.ShapeDtypeStruct((width, width), BF),
            jax.ShapeDtypeStruct((width, ff), BF),
            jax.ShapeDtypeStruct((ff, width), BF),
            jax.ShapeDtypeStruct((1, ff), F32),
            jax.ShapeDtypeStruct((8, width), F32),
        ],
        scratch_shapes=[
            pltpu.VMEM((tokens, width), F32),
            pltpu.VMEM((tokens, width), F32),
            pltpu.VMEM((tokens, width), BF),
            pltpu.VMEM((tokens, width), BF),
            pltpu.VMEM((tokens, width), F32),
            pltpu.VMEM((tokens, width), F32),
            pltpu.VMEM((tokens, width), BF),
        ],
        compiler_params=params(),
        cost_estimate=pl.CostEstimate(
            flops=12 * tokens * width * ff + 6 * tokens * width * width,
            bytes_accessed=40 << 20,
            transcendentals=tokens * ff,
        ),
        name="middle",
    )(att_t, tok_own, tok_rem, cot_own, cot_rem, span, vec, b_up, w_out, w_up, w_down)


def attend_back_kernel(
    q_ref,
    k_ref,
    v_ref,
    att_ref,
    d_att_ref,
    e_ref,
    linv_ref,
    cos_ref,
    sin_ref,
    give_ref,
    out_ref,
    take_ref,
    do_mask,
    send,
    recv,
):
    step = pl.program_id(0)

    @pl.when(step == 0)
    def _():
        swap_start(give_ref, take_ref, send, recv)

    tokens = q_ref.shape[1]
    tile = 256
    zero = jnp.zeros((HD, tokens), BF)
    v_nat = v_ref[...].T
    cos = cos_ref[...]
    sin = sin_ref[...]

    def unrotate(x):
        low = x.astype(BF).astype(F32)
        a, b = low[0 : HD // 2], low[HD // 2 :]
        return a * cos + b * sin, b * cos - a * sin

    for h in range(2):
        rows = slice(h * HD, (h + 1) * HD)
        linv = linv_ref[0, h : h + 1, :]
        d_o = d_att_ref[rows, :].astype(F32)
        d_os = (d_o * linv).astype(BF)
        do_mask[h, rows, :] = d_os
        do_mask[h, (1 - h) * HD : (2 - h) * HD, :] = zero
        inner = col_sum(d_o * att_ref[rows, :].astype(F32)) * linv
        d_values = mm(d_os, e_ref[h], NT)
        out_ref[2, rows, :] = d_values.astype(BF)
        d_keys = jnp.zeros((HD, tokens), F32)
        d_queries = []
        for t in range(tokens // tile):
            cols = slice(t * tile, (t + 1) * tile)
            d_probs = mm(v_nat, do_mask[h, :, cols])
            d_s = (e_ref[h, :, cols].astype(F32) * (d_probs - inner[:, cols])).astype(BF)
            d_queries.append(mm(k_ref[rows, :], d_s))
            d_keys += mm(q_ref[rows, cols], d_s, NT)
        dq = jnp.concatenate(d_queries, axis=1) * HD**-0.5
        lead, trail = unrotate(dq)
        out_ref[0, h * HD : h * HD + HD // 2, :] = lead.astype(BF)
        out_ref[0, h * HD + HD // 2 : (h + 1) * HD, :] = trail.astype(BF)
        lead, trail = unrotate(d_keys)
        out_ref[1, h * HD : h * HD + HD // 2, :] = lead.astype(BF)
        out_ref[1, h * HD + HD // 2 : (h + 1) * HD, :] = trail.astype(BF)

    @pl.when(step == pl.num_programs(0) - 1)
    def _():
        swap_wait(give_ref, take_ref, send, recv)


def attend_back(qkv_t, att_t, d_att_t, e, linv, cos_t, sin_t, give):
    tokens = qkv_t.shape[1]
    width = HEADS * HD

    def part(k):
        return pl.BlockSpec((2 * HD, tokens), lambda i: (i + k * PAIRS, 0))

    return pl.pallas_call(
        attend_back_kernel,
        grid=(PAIRS,),
        in_specs=[
            part(0),
            part(1),
            part(2),
            part(0),
            part(0),
            pl.BlockSpec((2, tokens, tokens), lambda i: (i, 0, 0)),
            pl.BlockSpec((1, 8, tokens), lambda i: (i, 0, 0)),
            whole(cos_t.shape),
            whole(sin_t.shape),
            ANY,
        ],
        out_specs=[pl.BlockSpec((3, 2 * HD, tokens), lambda i: (0, i, 0)), ANY],
        out_shape=[
            jax.ShapeDtypeStruct((3, width, tokens), BF),
            jax.ShapeDtypeStruct(give.shape, give.dtype),
        ],
        scratch_shapes=[pltpu.VMEM((2, 2 * HD, tokens), BF)] + SEMS,
        compiler_params=params(collective_id=2),
        cost_estimate=pl.CostEstimate(
            flops=32 * tokens * tokens * width, bytes_accessed=36 << 20, transcendentals=0
        ),
        name="attend_back",
    )(qkv_t, qkv_t, qkv_t, att_t, d_att_t, e, linv, cos_t, sin_t, give)


def tail_kernel(tok_own, tok_rem, d_proj_ref, w_ref, dx_ref, vec_ref, own_ref, rem_ref, sums_ref):
    step = pl.program_id(0)
    steps = pl.num_programs(0)
    mult_one = vec_ref[0:1, :]
    gain_one = vec_ref[2:3, :]
    scale_one = vec_ref[3:4, :]
    d_act = mm(d_proj_ref[...], w_ref[...], TN)

    def finish(tok, out):
        n, rstd = norm_parts(tok[...].astype(F32))
        grad = dx_ref[...] + norm_pull(n, rstd, d_act * mult_one)
        out[...] = grad.astype(out.dtype)
        return col_sum(d_act), col_sum(d_act * n)

    @pl.when(step == 0)
    def _():
        shift, pull = finish(tok_rem, rem_ref)
        sums_ref[0:1, :] = shift
        sums_ref[1:2, :] = pull
        sums_ref[2:, :] = jnp.zeros((6, shift.shape[1]), F32)

    @pl.when(step == steps - 1)
    def _():
        shift, pull = finish(tok_own, own_ref)
        shift = sums_ref[0:1, :] + shift
        pull = sums_ref[1:2, :] + pull
        sums_ref[0:1, :] = shift
        sums_ref[1:2, :] = pull * gain_one
        sums_ref[2:3, :] = pull * (1.0 + scale_one)


def tail(tok_own, tok_rem, d_proj_t, w_qkv_t, dx, vec):
    half, width = tok_own.shape
    return pl.pallas_call(
        tail_kernel,
        grid=(2,),
        in_specs=[
            whole(tok_own.shape),
            whole(tok_rem.shape),
            pl.BlockSpec((3 * width, half), lambda i: (0, 1 - i)),
            whole(w_qkv_t.shape),
            pl.BlockSpec((half, width), lambda i: (1 - i, 0)),
            whole(vec.shape),
        ],
        out_specs=[whole((half, width)), whole((half, width)), whole((8, width))],
        out_shape=[
            jax.ShapeDtypeStruct((half, width), F32),
            jax.ShapeDtypeStruct((half, width), BF),
            jax.ShapeDtypeStruct((8, width), F32),
        ],
        compiler_params=params(),
        cost_estimate=pl.CostEstimate(
            flops=12 * half * width * width, bytes_accessed=20 << 20, transcendentals=0
        ),
        name="tail",
    )(tok_own, tok_rem, d_proj_t, w_qkv_t, dx, vec)


def weight_grad_kernel(act_ref, d_proj_ref, out_ref):
    out_ref[...] = mm(act_ref[...], d_proj_ref[...], NT).astype(BF)


def weight_grad(act_t, d_proj_t):
    width, tokens = act_t.shape
    cols = d_proj_t.shape[0]
    tile = 768
    return pl.pallas_call(
        weight_grad_kernel,
        grid=(cols // tile,),
        in_specs=[whole(act_t.shape), pl.BlockSpec((tile, tokens), lambda i: (i, 0))],
        out_specs=pl.BlockSpec((width, tile), lambda i: (0, i)),
        out_shape=jax.ShapeDtypeStruct((width, cols), BF),
        compiler_params=params(),
        cost_estimate=pl.CostEstimate(
            flops=2 * cols * width * tokens, bytes_accessed=12 << 20, transcendentals=0
        ),
        name="weight_grad",
    )(act_t, d_proj_t)


def reduce_kernel(count, *refs):
    grads, mod_ref, sum_ref = refs[:count], refs[count], refs[count + 1]
    refs = refs[count + 2 :]
    outs, mod_out, sum_out = refs[:count], refs[count], refs[count + 1]
    refs = refs[count + 2 :]
    own, from_core, from_y, from_z, last, from_x = (
        refs[k * count : (k + 1) * count] for k in range(6)
    )
    sum_own, sum_core, sum_y, sum_z, sum_x, mod_all, sems, z_send, z_recv = refs[6 * count :]
    dp, x = lax.axis_index("dp"), lax.axis_index("seq")
    z, y, c = dp // 4, lax.rem(dp // 2, 2), lax.rem(dp, 2)
    zs = mod_all.shape[0]
    core = (dp + 1 - 2 * c, x)
    across = (dp + 2 - 4 * y, x)
    facing = (dp, 1 - x)
    far = [lax.rem(z + k, zs) for k in range(1, zs)]
    far_devices = [(f * 4 + 2 * y + c, x) for f in far]

    for i in range(count):
        pltpu.make_async_copy(grads[i].at[:, :, c], own[i], sems.at[i, 8]).start()
    mine = (z, y, c, x)
    pltpu.make_async_copy(mod_ref, mod_all.at[mine], sems.at[count, 8]).start()
    pltpu.make_async_copy(sum_ref, sum_own, sems.at[count + 1, 8]).start()

    greet(core, across, facing, *far_devices)

    def over(stage, i, src, dst, device):
        return remote(src, dst, sems.at[i, 2 * stage], sems.at[i, 2 * stage + 1], device)

    def to_core(i):
        return over(0, i, grads[i].at[:, :, 1 - c], from_core[i], core)

    def to_across(i):
        return over(1, i, own[i].at[:, 1 - y], from_y[i], across)

    def to_facing(i):
        return over(2, i, last[i], from_x[i], facing)

    def to_far(i, k, incoming):
        f = far[k]
        return remote(
            own[i].at[f, y] if i < count else sum_own if i > count else mod_all.at[z, :, :, x],
            (from_z[i] if i < count else sum_z).at[f if incoming else z]
            if i != count
            else mod_all.at[f if incoming else z, :, :, x],
            z_send.at[i, k],
            z_recv.at[i, f if incoming else z],
            far_devices[k],
        )

    def far_start(i):
        for k in range(zs - 1):
            to_far(i, k, False).start()

    def far_wait(i):
        for k in range(zs - 1):
            to_far(i, k, False).wait_send()
            to_far(i, k, True).wait_recv()

    def mod_core():
        return over(0, count, mod_all.at[mine], mod_all.at[mine], core)

    def mod_core_in():
        slot = mod_all.at[z, y, 1 - c, x]
        return over(0, count, slot, slot, core)

    def mod_across(row):
        slot = mod_all.at[z, row, :, x]
        return over(1, count, slot, slot, across)

    def mod_facing(side):
        slot = mod_all.at[:, :, :, side]
        return over(2, count, slot, slot, facing)

    def sum_swap(stage, dst, device):
        return over(stage, count + 1, sum_own, dst, device)

    for i in range(count):
        to_core(i).start()
    pltpu.make_async_copy(mod_ref, mod_all.at[mine], sems.at[count, 8]).wait()
    pltpu.make_async_copy(sum_ref, sum_own, sems.at[count + 1, 8]).wait()
    mod_core().start()
    sum_swap(0, sum_core, core).start()

    for i in range(count):
        pltpu.make_async_copy(grads[i].at[:, :, c], own[i], sems.at[i, 8]).wait()
        to_core(i).wait()
        for a in range(zs):
            for b in range(2):
                own[i][a, b] = own[i][a, b] + from_core[i][a, b]
        to_across(i).start()
    mod_core().wait_send()
    mod_core_in().wait_recv()
    mod_across(y).start()
    sum_swap(0, sum_core, core).wait()
    sum_own[...] += sum_core[...]
    sum_swap(1, sum_y, across).start()

    mod_across(y).wait_send()
    mod_across(1 - y).wait_recv()
    far_start(count)
    sum_swap(1, sum_y, across).wait()
    sum_own[...] += sum_y[...]
    far_start(count + 1)
    for i in range(count):
        to_across(i).wait()
        for a in range(zs):
            own[i][a, y] = own[i][a, y] + from_y[i][a]
        far_start(i)
    far_wait(count)
    mod_facing(x).start()
    far_wait(count + 1)
    sum_z[z] = sum_own[...]
    total = sum_z[0]
    for a in range(1, zs):
        total += sum_z[a]
    sum_own[...] = total
    sum_swap(2, sum_x, facing).start()
    for i in range(count):
        far_wait(i)
        from_z[i][z] = own[i][z, y]
        total = from_z[i][0].astype(F32)
        for a in range(1, zs):
            total += from_z[i][a].astype(F32)
        last[i][...] = total.astype(BF)
        to_facing(i).start()
    mod_facing(x).wait_send()
    mod_facing(1 - x).wait_recv()
    mod_out[...] = mod_all[...]
    sum_swap(2, sum_x, facing).wait()
    sum_out[...] = sum_own[...] + sum_x[...]
    for i in range(count):
        to_facing(i).wait()
        outs[i][...] = last[i][...].astype(F32) + from_x[i][...].astype(F32)


def reduce_all(grads, mod, sums, dp):
    zs = dp // 4
    grads = [g.reshape(zs, 2, 2, g.shape[0] // dp, g.shape[1]) for g in grads]
    tails = [g.shape[3:] for g in grads]
    count = len(grads)

    def scratch(*lead):
        return [pltpu.VMEM(lead + t, BF) for t in tails]

    everyone = (zs, 2, 2, 2) + mod.shape
    return pl.pallas_call(
        functools.partial(reduce_kernel, count),
        in_specs=[ANY] * (count + 2),
        out_specs=[pl.BlockSpec(memory_space=pltpu.VMEM)] * (count + 2),
        out_shape=[jax.ShapeDtypeStruct(t, F32) for t in tails]
        + [jax.ShapeDtypeStruct(everyone, BF), jax.ShapeDtypeStruct(sums.shape, F32)],
        scratch_shapes=scratch(zs, 2)
        + scratch(zs, 2)
        + scratch(zs)
        + scratch(zs)
        + scratch()
        + scratch()
        + [pltpu.VMEM(sums.shape, F32)] * 3
        + [
            pltpu.VMEM((zs,) + sums.shape, F32),
            pltpu.VMEM(sums.shape, F32),
            pltpu.VMEM(everyone, BF),
            pltpu.SemaphoreType.DMA((count + 2, 9)),
            pltpu.SemaphoreType.DMA((count + 2, zs)),
            pltpu.SemaphoreType.DMA((count + 2, zs)),
        ],
        compiler_params=params(collective_id=3),
        name="reduce_all",
    )(*grads, mod, sums)


def time_features(time_steps, pair_count):
    frequency = jnp.exp(-math.log(10000.0) * jnp.arange(pair_count, dtype=F32) / pair_count)
    angles = time_steps.astype(F32)[:, None] * frequency[None, :]
    return jnp.concatenate([jnp.cos(angles), jnp.sin(angles)], axis=-1)


def per_device(
    tokens,
    cotangent,
    time_index,
    span_starts,
    span_lengths,
    w_ada,
    b_ada,
    gain_one,
    w_qkv,
    w_out,
    gain_two,
    w_up,
    b_up,
    w_down,
    b_down,
):
    seqs_dev, half, width = tokens.shape
    length = 2 * half
    rank = lax.axis_index("seq")
    swap = [(0, 1), (1, 0)]

    def pick(x, i):
        return lax.dynamic_index_in_dim(x, i, 0, keepdims=False)

    tok_own, tok_send = pick(tokens, rank), pick(tokens, 1 - rank)
    cot_own = pick(cotangent, rank)
    tok_rem = lax.ppermute(tok_send, "seq", swap)

    here = jnp.arange(half, dtype=jnp.int32)
    place = jnp.concatenate([rank * half + here, (1 - rank) * half + here])
    frequency = jnp.exp(-math.log(10000.0) * jnp.arange(HD // 2, dtype=F32) / (HD // 2))
    angles = frequency[:, None] * place.astype(F32)[None, :]
    cos_t, sin_t = jnp.cos(angles), jnp.sin(angles)
    start, extent = pick(span_starts, rank), pick(span_lengths, rank)
    span = jnp.where((place >= start) & (place < start + extent), 2.0, 0.5).astype(F32)[:, None]

    time_own = lax.dynamic_slice_in_dim(time_index, rank, 1)
    cond_act = jax.nn.silu(time_features(time_own, w_ada.shape[0] // 2))
    modulation = (
        jnp.dot(cond_act, w_ada.astype(F32), precision=lax.Precision.HIGHEST)[0] + b_ada
    )
    shift_one, scale_one, gate_one, shift_two, scale_two, gate_two = jnp.split(modulation, 6)
    zeros = jnp.zeros_like(shift_one)
    vec_one = jnp.stack(
        [gain_one * (1.0 + scale_one), shift_one, gain_one, scale_one, zeros, zeros, zeros, zeros]
    )
    vec_two = jnp.stack(
        [
            gate_one,
            gain_two * (1.0 + scale_two),
            shift_two,
            gate_two,
            b_down,
            gain_two,
            scale_two,
            zeros,
        ]
    )
    w_qkv_t = w_qkv.T

    act_t, qkv_t = project(tok_own, tok_rem, vec_one, cos_t, sin_t, w_qkv_t)
    att_t, e, linv, cot_rem = attend(qkv_t, cotangent)
    out_own, out_rem, dx, d_att_t, g_out, g_up, g_down, g_bup, sums_two = middle(
        att_t, tok_own, tok_rem, cot_own, cot_rem, span, vec_two, b_up[None], w_out, w_up, w_down
    )
    d_proj, out_back = attend_back(qkv_t, att_t, d_att_t, e, linv, cos_t, sin_t, out_rem)
    d_proj_t = d_proj.reshape(3 * width, length)
    g_own, g_rem, sums_one = tail(tok_own, tok_rem, d_proj_t, w_qkv_t, dx, vec_one)
    g_qkv = weight_grad(act_t, d_proj_t)

    def spread(own, other):
        first = jnp.where(rank == 0, own, other)
        second = jnp.where(rank == 0, other, own)
        return jnp.stack([first, second])

    output = spread(out_own, out_back)
    grad_tokens = spread(g_own, lax.ppermute(g_rem, "seq", swap).astype(F32))

    dp, dps = lax.axis_index("dp"), lax.axis_size("dp")
    ff = w_up.shape[1]
    d_mod = jnp.concatenate([sums_one[:2].reshape(-1), sums_two[:4].reshape(-1)])
    small = jnp.concatenate([sums_one[2], sums_two[4], sums_two[5], g_bup[0]])
    grads = (g_qkv, g_out, g_up, g_down)
    if dps % 4 == 0 and all(g.shape[0] % (16 * dps) == 0 for g in grads):
        time_parts = jnp.concatenate([time_own // 32, time_own % 32]).astype(F32)
        mod_rows = -(-(d_mod.size + 2) // 2048) * 16
        mod = jnp.concatenate([d_mod, time_parts])
        mod = jnp.pad(mod, (0, mod_rows * 128 - mod.size)).astype(BF).reshape(mod_rows, 128)
        sum_rows = -(-small.size // 1024) * 8
        sums = jnp.pad(small, (0, sum_rows * 128 - small.size)).reshape(sum_rows, 128)
        *shards, mod_all, sums = reduce_all(grads, mod, sums, dps)
        mod_all = mod_all.reshape(-1, mod_rows * 128).astype(F32)
        d_mod_all = mod_all[:, : d_mod.size]
        time_all = 32.0 * mod_all[:, d_mod.size] + mod_all[:, d_mod.size + 1]
        small = sums.reshape(-1)[: small.size]
    else:
        shards = [
            lax.psum(lax.psum_scatter(g, "dp", scatter_dimension=0, tiled=True), "seq").astype(F32)
            for g in grads
        ]
        d_mod_all = lax.all_gather(d_mod, ("dp", "seq"))
        time_all = lax.all_gather(time_own[0].astype(F32), ("dp", "seq"))
        small = lax.psum(small, ("dp", "seq"))

    def mine(x, axis=0):
        size = x.shape[axis] // dps
        return lax.dynamic_slice_in_dim(x, dp * size, size, axis)

    features = jax.nn.silu(time_features(time_all, w_ada.shape[0] // 2))
    s_w_ada = jnp.dot(mine(features, 1).T, d_mod_all, precision=lax.Precision.HIGHEST)
    s_b_ada = jnp.sum(mine(d_mod_all, 1), axis=0)
    s_gain_one = mine(small[:width])
    s_gain_two = mine(small[width : 2 * width])
    s_b_down = mine(small[2 * width : 3 * width])
    s_b_up = mine(small[3 * width :])
    s_qkv, s_out, s_up, s_down = shards

    return (
        output,
        grad_tokens,
        s_w_ada,
        s_b_ada,
        s_gain_one,
        s_qkv,
        s_out,
        s_gain_two,
        s_up,
        s_b_up,
        s_down,
        s_b_down,
    )


def solution(mesh):
    rows = P("dp", "seq", None)
    return jax.shard_map(
        per_device,
        mesh=mesh,
        in_specs=(rows, rows, P("dp"), P("dp"), P("dp")) + (P(),) * 10,
        out_specs=(
            rows,
            rows,
            P("dp", None),
            P("dp"),
            P("dp"),
            P("dp", None),
            P("dp", None),
            P("dp"),
            P("dp", None),
            P("dp"),
            P("dp", None),
            P("dp"),
        ),
        check_vma=False,
    )
```

```python
import functools
import math

import jax
import jax.numpy as jnp
from jax import lax
from jax.experimental import pallas as pl
from jax.experimental.pallas import tpu as pltpu
from jax.sharding import PartitionSpec as P

HEADS = 12
HD = 64
PAIRS = HEADS // 2
NORM_EPS = 1e-05
LOG2E = math.log2(math.e)
BF = jnp.bfloat16
F32 = jnp.float32
MIB = 1 << 20

NN = (((1,), (0,)), ((), ()))
NT = (((1,), (1,)), ((), ()))
TN = (((0,), (0,)), ((), ()))


def mm(a, b, dims=NN):
    return lax.dot_general(a, b, dims, preferred_element_type=F32)


def norm_parts(x):
    centre = x - jnp.mean(x, axis=-1, keepdims=True)
    rstd = lax.rsqrt(jnp.mean(centre * centre, axis=-1, keepdims=True) + NORM_EPS)
    return centre * rstd, rstd


def norm_pull(n, rstd, dn):
    return rstd * (
        dn - jnp.mean(dn, axis=-1, keepdims=True) - n * jnp.mean(dn * n, axis=-1, keepdims=True)
    )


def col_sum(x):
    return jnp.sum(x, axis=0, keepdims=True)


def rows_of(size, index):
    return pl.ds(pl.multiple_of(index * size, size), size)


def params(mib=56, collective_id=None):
    if collective_id is None:
        return pltpu.CompilerParams(vmem_limit_bytes=mib * MIB)
    return pltpu.CompilerParams(
        vmem_limit_bytes=mib * MIB, collective_id=collective_id, has_side_effects=True
    )


def whole(shape):
    zeros = (0,) * len(shape)
    return pl.BlockSpec(shape, lambda *_: zeros)


MESH = pl.DeviceIdType.MESH
ANY = pl.BlockSpec(memory_space=pl.ANY)
SEMS = [pltpu.SemaphoreType.DMA, pltpu.SemaphoreType.DMA]


def greet(*partners):
    barrier = pltpu.get_barrier_semaphore()
    for partner in partners:
        pl.semaphore_signal(barrier, inc=1, device_id=partner, device_id_type=MESH)
    pl.semaphore_wait(barrier, len(partners))


def remote(src, dst, send, recv, device):
    return pltpu.make_async_remote_copy(
        src_ref=src, dst_ref=dst, send_sem=send, recv_sem=recv, device_id=device, device_id_type=MESH
    )


def seq_partner():
    return (lax.axis_index("dp"), 1 - lax.axis_index("seq"))


def swap_start(src, dst, send, recv):
    partner = seq_partner()
    greet(partner)
    remote(src, dst, send, recv, partner).start()


def swap_wait(src, dst, send, recv):
    remote(src, dst, send, recv, seq_partner()).wait()


class Links:
    def __init__(self, sems, zs):
        self.sems, self.used, self.zs = sems, 0, zs
        dp, self.x = lax.axis_index("dp"), lax.axis_index("seq")
        self.z, self.y, self.c = dp // 4, lax.rem(dp // 2, 2), lax.rem(dp, 2)
        self.core = (dp + 1 - 2 * self.c, self.x)
        self.across = (dp + 2 - 4 * self.y, self.x)
        self.facing = (dp, 1 - self.x)
        self.far = [lax.rem(self.z + k, zs) for k in range(1, zs)]

    def at_z(self, f):
        return (f * 4 + 2 * self.y + self.c, self.x)

    def take(self, count):
        self.used += count
        return self.used - count

    def local(self, src, dst):
        sem = self.take(1)
        return lambda: pltpu.make_async_copy(src(), dst(), self.sems.at[sem])

    def swap(self, src, dst, device):
        sem = self.take(2)
        return lambda: remote(src(), dst(), self.sems.at[sem], self.sems.at[sem + 1], device)

    def spread(self, src, dst):
        sem = self.take(2 * self.zs)

        def make(f, slot):
            return remote(
                src(f), dst(slot), self.sems.at[sem + f], self.sems.at[sem + self.zs + slot], self.at_z(f)
            )

        def start():
            for f in self.far:
                make(f, self.z).start()

        def wait():
            for f in self.far:
                make(f, self.z).wait_send()
                make(f, f).wait_recv()

        return start, wait

    def gather(self, src, dst, goal):
        sem = self.take(1 + self.zs)

        def make(slot):
            return remote(
                src(), dst(slot), self.sems.at[sem], self.sems.at[sem + 1 + slot], self.at_z(goal)
            )

        def start():
            pl.when(self.z != goal)(lambda: make(self.z).start())

        def wait():
            pl.when(self.z != goal)(lambda: make(self.z).wait_send())

            @pl.when(self.z == goal)
            def _():
                for f in self.far:
                    make(f).wait_recv()

        return start, wait


def add_to(dst, src, lead):
    for index in lead:
        dst[index] = dst[index] + src[index]


def grid_of(*sizes):
    return [()] if not sizes else [(i,) + r for i in range(sizes[0]) for r in grid_of(*sizes[1:])]


def round_up(value, unit):
    return -(-value // unit) * unit


def early_mod_rows(width):
    return round_up(4 * width // 128 + 1, 16)


def early_sum_rows(width, ff):
    return round_up((2 * width + ff) // 128, 8)


def put_rows(ref, start, row):
    for k in range(row.shape[1] // 128):
        ref[start + k : start + k + 1, :] = row[:, k * 128 : (k + 1) * 128].astype(ref.dtype)


def once(shape):
    zeros = (0,) * len(shape)
    return pl.BlockSpec(shape, lambda *_: zeros, pipeline_mode=pl.Buffered(1))


def project_kernel(own_ref, rem_ref, vec_ref, cos_ref, sin_ref, w_ref, act_ref, out_ref):
    step = pl.program_id(0)
    half, _ = own_ref.shape
    tile = 256

    @pl.when(step == 0)
    def _():
        scale = vec_ref[0:1, :]
        shift = vec_ref[1:2, :]
        for part, ref in enumerate((own_ref, rem_ref)):
            for t in range(half // tile):
                n, _ = norm_parts(ref[t * tile : (t + 1) * tile, :].astype(F32))
                act = (n * scale + shift).astype(BF)
                start = part * half + t * tile
                act_ref[:, start : start + tile] = act.T

    proj = mm(w_ref[...], act_ref[...])
    heads = proj.shape[0] // HD
    tokens = proj.shape[1]

    @pl.when(step < 4)
    def _():
        factor = jnp.where(step < 2, HD**-0.5, 1.0)
        cos = cos_ref[...] * factor
        sin = sin_ref[...] * factor
        for h in range(heads):
            a = proj[h * HD : h * HD + HD // 2]
            b = proj[h * HD + HD // 2 : (h + 1) * HD]
            out_ref[h * HD : h * HD + HD // 2, :] = (a * cos - b * sin).astype(BF)
            out_ref[h * HD + HD // 2 : (h + 1) * HD, :] = (b * cos + a * sin).astype(BF)

    @pl.when(step >= 4)
    def _():
        out_ref[...] = proj.astype(BF)


def project(own, rem, vec, cos_t, sin_t, w_qkv_t):
    half, width = own.shape
    tokens = 2 * half
    blk = width // 2
    return pl.pallas_call(
        project_kernel,
        grid=(6,),
        in_specs=[
            whole(own.shape),
            whole(rem.shape),
            whole(vec.shape),
            whole(cos_t.shape),
            whole(sin_t.shape),
            pl.BlockSpec((blk, width), lambda i: (i, 0)),
        ],
        out_specs=[
            whole((width, tokens)),
            pl.BlockSpec((blk, tokens), lambda i: (i, 0)),
        ],
        out_shape=[
            jax.ShapeDtypeStruct((width, tokens), BF),
            jax.ShapeDtypeStruct((3 * width, tokens), BF),
        ],
        compiler_params=params(),
        cost_estimate=pl.CostEstimate(
            flops=6 * tokens * width * width, bytes_accessed=14 << 20, transcendentals=0
        ),
        name="project",
    )(own, rem, vec, cos_t, sin_t, w_qkv_t)


def attend_kernel(
    q_ref, k_ref, v_ref, cot_ref, att_ref, e_ref, linv_ref, cot_rem, q_mask, v_ext, send, recv
):
    step = pl.program_id(0)
    cot_send = cot_ref.at[1 - lax.axis_index("seq")]

    @pl.when(step == 0)
    def _():
        swap_start(cot_send, cot_rem, send, recv)

    tokens = q_ref.shape[1]
    tile = 256
    zero = jnp.zeros((HD, tokens), BF)
    k_nat = k_ref[...].T
    q_mask[0, 0:HD, :] = q_ref[0:HD, :]
    q_mask[0, HD:, :] = zero
    q_mask[1, 0:HD, :] = zero
    q_mask[1, HD:, :] = q_ref[HD:, :]
    for h in range(2):
        v_ext[h, 0:HD, :] = v_ref[h * HD : (h + 1) * HD, :]
        v_ext[h, HD:, :] = jnp.ones((16, tokens), BF)
    for h in range(2):
        for t in range(tokens // tile):
            cols = slice(t * tile, (t + 1) * tile)
            s = mm(k_nat, q_mask[h, :, cols])
            top = jnp.max(s, axis=0, keepdims=True)
            e = jnp.exp(s - top).astype(BF)
            e_ref[h, :, cols] = e
            mix = mm(v_ext[h], e)
            linv = 1.0 / mix[HD : HD + 1, :]
            linv_ref[0, h : h + 1, cols] = linv
            att_ref[h * HD : (h + 1) * HD, cols] = (mix[0:HD, :] * linv).astype(BF)

    @pl.when(step == pl.num_programs(0) - 1)
    def _():
        swap_wait(cot_send, cot_rem, send, recv)


def attend(qkv_t, cotangent):
    tokens = qkv_t.shape[1]
    width = HEADS * HD

    def part(k):
        return pl.BlockSpec((2 * HD, tokens), lambda i: (i + k * PAIRS, 0))

    return pl.pallas_call(
        attend_kernel,
        grid=(PAIRS,),
        in_specs=[part(0), part(1), part(2), ANY],
        out_specs=[
            part(0),
            pl.BlockSpec((2, tokens, tokens), lambda i: (i, 0, 0)),
            pl.BlockSpec((1, 8, tokens), lambda i: (i, 0, 0)),
            ANY,
        ],
        out_shape=[
            jax.ShapeDtypeStruct((width, tokens), BF),
            jax.ShapeDtypeStruct((HEADS, tokens, tokens), BF),
            jax.ShapeDtypeStruct((PAIRS, 8, tokens), F32),
            jax.ShapeDtypeStruct(cotangent.shape[1:], BF),
        ],
        scratch_shapes=[
            pltpu.VMEM((2, 2 * HD, tokens), BF),
            pltpu.VMEM((2, HD + 16, tokens), BF),
        ]
        + SEMS,
        compiler_params=params(collective_id=1),
        cost_estimate=pl.CostEstimate(
            flops=16 * tokens * tokens * width,
            bytes_accessed=30 << 20,
            transcendentals=HEADS * tokens * tokens,
        ),
        name="attend",
    )(qkv_t, qkv_t, qkv_t, cotangent)


def gelu_both(u):
    c = math.sqrt(2.0 / math.pi)
    u2 = u * u
    th = jnp.tanh(u * (c + (c * 0.044715) * u2))
    half = 0.5 * (1.0 + th)
    value = u * half
    slope = half + (0.5 * u) * (1.0 - th * th) * (c + (3.0 * c * 0.044715) * u2)
    return value, slope


def middle_kernel(
    att_ref,
    tok_own,
    tok_rem,
    cot_own,
    cot_rem,
    span_ref,
    vec_ref,
    b_up_ref,
    w_out_ref,
    w_up_ref,
    w_down_ref,
    out_own,
    out_rem,
    dx_ref,
    d_att_ref,
    g_out_ref,
    g_up_ref,
    g_down_ref,
    g_bup_ref,
    sums_ref,
    branch,
    x_one,
    act_two,
    d_down,
    down_acc,
    d_act,
    d_branch,
):
    step = pl.program_id(0)
    steps = pl.num_programs(0)
    tokens = att_ref.shape[1]
    half = tokens // 2
    tile = 256
    per_half = half // tile
    gate_one = vec_ref[0:1, :]
    mult_two = vec_ref[1:2, :]
    shift_two = vec_ref[2:3, :]
    gate_two = vec_ref[3:4, :]
    b_down = vec_ref[4:5, :]
    gain_two = vec_ref[5:6, :]
    scale_two = vec_ref[6:7, :]

    @pl.when(step == 0)
    def _():
        for part, (tok, cot) in enumerate(((tok_own, cot_own), (tok_rem, cot_rem))):
            for t in range(per_half):
                src = slice(t * tile, (t + 1) * tile)
                dst = slice(part * half + t * tile, part * half + (t + 1) * tile)
                br = mm(att_ref[:, dst], w_out_ref[...], TN)
                branch[dst, :] = br
                x = tok[src, :].astype(F32) + gate_one * br
                x_one[dst, :] = x
                n, _ = norm_parts(x)
                act_two[dst, :] = (n * mult_two + shift_two).astype(BF)
                grad_out = cot[src, :].astype(F32) * span_ref[dst, :]
                d_down[dst, :] = (gate_two * grad_out).astype(BF)

    up = mm(act_two[...], w_up_ref[...]) + b_up_ref[...]
    value, slope = gelu_both(up)
    hidden = value.astype(BF)
    d_hidden = mm(d_down[...], w_down_ref[...], NT)
    d_up_full = slope * d_hidden
    d_up = d_up_full.astype(BF)
    g_bup_ref[...] = col_sum(d_up.astype(F32))
    down_part = mm(hidden, w_down_ref[...])
    d_act_part = mm(d_up, w_up_ref[...], NT)
    g_down_ref[...] = mm(hidden, d_down[...], TN).astype(BF)
    g_up_ref[...] = mm(act_two[...], d_up, TN).astype(BF)

    @pl.when(step == 0)
    def _():
        down_acc[...] = down_part
        d_act[...] = d_act_part

    @pl.when(step > 0)
    def _():
        down_acc[...] += down_part
        d_act[...] += d_act_part

    @pl.when(step == steps - 1)
    def _():
        zero = jnp.zeros((1, gate_one.shape[1]), F32)
        s_gate_two, s_shift, s_pull, s_gate_one, s_bdown = zero, zero, zero, zero, zero
        for part, (cot, out) in enumerate(((cot_own, out_own), (cot_rem, out_rem))):
            for t in range(per_half):
                src = slice(t * tile, (t + 1) * tile)
                dst = slice(part * half + t * tile, part * half + (t + 1) * tile)
                x = x_one[dst, :]
                down = down_acc[dst, :] + b_down
                out[src, :] = (x + gate_two * down).astype(BF)
                grad_out = cot[src, :].astype(F32) * span_ref[dst, :]
                s_gate_two += col_sum(grad_out * down)
                s_bdown += col_sum(d_down[dst, :].astype(F32))
                n, rstd = norm_parts(x)
                da = d_act[dst, :]
                s_shift += col_sum(da)
                s_pull += col_sum(da * n)
                dx = grad_out + norm_pull(n, rstd, da * mult_two)
                dx_ref[dst, :] = dx
                s_gate_one += col_sum(dx * branch[dst, :])
                d_branch[dst, :] = (gate_one * dx).astype(BF)
        sums_ref[0:1, :] = s_gate_one
        sums_ref[1:2, :] = s_shift
        sums_ref[2:3, :] = s_pull * gain_two
        sums_ref[3:4, :] = s_gate_two
        sums_ref[4:5, :] = s_pull * (1.0 + scale_two)
        sums_ref[5:6, :] = s_bdown
        sums_ref[6:8, :] = jnp.zeros((2, gate_one.shape[1]), F32)
        g_out_ref[...] = mm(att_ref[...], d_branch[...]).astype(BF)
        d_att_ref[...] = mm(w_out_ref[...], d_branch[...], NT).astype(BF)


def middle(att_t, tok_own, tok_rem, cot_own, cot_rem, span, vec, b_up, w_out, w_up, w_down):
    width, tokens = att_t.shape
    half = tokens // 2
    ff = w_up.shape[1]
    tile = 512
    return pl.pallas_call(
        middle_kernel,
        grid=(ff // tile,),
        in_specs=[
            whole(att_t.shape),
            whole(tok_own.shape),
            whole(tok_rem.shape),
            whole(cot_own.shape),
            whole(cot_rem.shape),
            whole(span.shape),
            whole(vec.shape),
            pl.BlockSpec((1, tile), lambda i: (0, i)),
            whole(w_out.shape),
            pl.BlockSpec((width, tile), lambda i: (0, i)),
            pl.BlockSpec((tile, width), lambda i: (i, 0)),
        ],
        out_specs=[
            whole((half, width)),
            whole((half, width)),
            whole((tokens, width)),
            whole((width, tokens)),
            whole((width, width)),
            pl.BlockSpec((width, tile), lambda i: (0, i)),
            pl.BlockSpec((tile, width), lambda i: (i, 0)),
            pl.BlockSpec((1, tile), lambda i: (0, i)),
            whole((8, width)),
        ],
        out_shape=[
            jax.ShapeDtypeStruct((half, width), BF),
            jax.ShapeDtypeStruct((half, width), BF),
            jax.ShapeDtypeStruct((tokens, width), F32),
            jax.ShapeDtypeStruct((width, tokens), BF),
            jax.ShapeDtypeStruct((width, width), BF),
            jax.ShapeDtypeStruct((width, ff), BF),
            jax.ShapeDtypeStruct((ff, width), BF),
            jax.ShapeDtypeStruct((1, ff), F32),
            jax.ShapeDtypeStruct((8, width), F32),
        ],
        scratch_shapes=[
            pltpu.VMEM((tokens, width), F32),
            pltpu.VMEM((tokens, width), F32),
            pltpu.VMEM((tokens, width), BF),
            pltpu.VMEM((tokens, width), BF),
            pltpu.VMEM((tokens, width), F32),
            pltpu.VMEM((tokens, width), F32),
            pltpu.VMEM((tokens, width), BF),
        ],
        compiler_params=params(),
        cost_estimate=pl.CostEstimate(
            flops=12 * tokens * width * ff + 6 * tokens * width * width,
            bytes_accessed=40 << 20,
            transcendentals=tokens * ff,
        ),
        name="middle",
    )(att_t, tok_own, tok_rem, cot_own, cot_rem, span, vec, b_up, w_out, w_up, w_down)


def middle_links_kernel(
    zs,
    att_ref,
    tok_own,
    tok_rem,
    cot_own,
    cot_rem,
    span_ref,
    vec_ref,
    b_up_ref,
    w_out_ref,
    w_up_ref,
    w_down_ref,
    out_own,
    out_rem,
    dx_ref,
    d_att_ref,
    g_out_ref,
    g_up_ref,
    g_down_ref,
    up_ref,
    down_ref,
    mod_ref,
    sum_ref,
    branch,
    x_one,
    act_two,
    d_down,
    down_acc,
    d_act,
    d_branch,
    hidden,
    d_up,
    up_core,
    up_side,
    down_core,
    down_y,
    sems,
):
    step = pl.program_id(0)
    steps = zs
    tokens = att_ref.shape[1]
    width = att_ref.shape[0]
    half = tokens // 2
    cut = width // 2
    tile = 256
    per_half = half // tile
    gate_one = vec_ref[0:1, :]
    mult_two = vec_ref[1:2, :]
    shift_two = vec_ref[2:3, :]
    gate_two = vec_ref[3:4, :]
    b_down = vec_ref[4:5, :]
    gain_two = vec_ref[5:6, :]
    scale_two = vec_ref[6:7, :]

    links = Links(sems, zs)
    x, y, c = links.x, links.y, links.c
    up_to_core = [
        links.swap(lambda: g_up_ref.at[:, :, :, 1 - c], lambda j=j: up_core.at[j], links.core)
        for j in range(steps - 1)
    ]
    down_to_core = [
        links.swap(lambda: g_down_ref.at[:, 1 - c], lambda j=j: down_core.at[j], links.core)
        for j in range(steps - 1)
    ]
    up_to_side = [
        links.swap(lambda j=j: up_core.at[j, 1 - x], lambda j=j: up_side.at[j], links.facing)
        for j in range(steps - 1)
    ]
    down_to_y = [
        links.swap(lambda j=j: down_core.at[j, 1 - y], lambda j=j: down_y.at[j], links.across)
        for j in range(steps - 1)
    ]

    @pl.when(step == 0)
    def _():
        greet(links.core, links.across, links.facing)
        for part, (tok, cot) in enumerate(((tok_own, cot_own), (tok_rem, cot_rem))):
            for t in range(per_half):
                src = slice(t * tile, (t + 1) * tile)
                dst = slice(part * half + t * tile, part * half + (t + 1) * tile)
                br = mm(att_ref[:, dst], w_out_ref[...], TN)
                branch[dst, :] = br
                xv = tok[src, :].astype(F32) + gate_one * br
                x_one[dst, :] = xv
                n, _ = norm_parts(xv)
                act_two[dst, :] = (n * mult_two + shift_two).astype(BF)
                grad_out = cot[src, :].astype(F32) * span_ref[dst, :]
                d_down[dst, :] = (gate_two * grad_out).astype(BF)
                down_acc[dst, :] = jnp.zeros((tile, width), F32)
                d_act[dst, :] = jnp.zeros((tile, width), F32)

    bup = jnp.zeros((1, w_up_ref.shape[1]), F32)
    for part in range(2):
        rows = slice(part * half, (part + 1) * half)
        up = mm(act_two[rows, :], w_up_ref[...]) + b_up_ref[...]
        value, slope = gelu_both(up)
        hidden[rows, :] = value.astype(BF)
        d_up_low = (slope * mm(d_down[rows, :], w_down_ref[...], NT)).astype(BF)
        bup += col_sum(d_up_low.astype(F32))
        d_up[rows, :] = d_up_low
    for j in range(steps):
        pl.when(step == j)(lambda j=j: put_rows(sum_ref, 2 * width // 128 + j * bup.shape[1] // 128, bup))

    for j in range(steps - 1):

        @pl.when(step == j + 1)
        def _(j=j):
            up_to_core[j]().wait()
            for h, a, b in grid_of(2, zs, 2):
                up_core[j, h, a, b] = up_core[j, h, a, b] + g_up_ref[h, a, b, c]
            up_to_side[j]().start()
            down_to_core[j]().wait()
            for b in range(2):
                down_core[j, b] = down_core[j, b] + g_down_ref[b, c]
            down_to_y[j]().start()

    down_acc[...] += mm(hidden[...], w_down_ref[...])
    d_act[...] += mm(d_up[...], w_up_ref[...], NT)
    g_down = mm(hidden[...], d_down[...], TN).astype(BF)
    g_down_ref[...] = g_down.reshape(g_down_ref.shape)
    g_up = mm(act_two[...], d_up[...], TN).astype(BF)
    for h in range(2):
        g_up_ref[h] = g_up[:, h * cut : (h + 1) * cut].reshape(g_up_ref.shape[1:])

    for j in range(steps - 1):

        @pl.when(step == j)
        def _(j=j):
            up_to_core[j]().start()
            down_to_core[j]().start()

    @pl.when(step == steps - 1)
    def _():
        zero = jnp.zeros((1, width), F32)
        s_gate_two, s_shift, s_pull, s_gate_one, s_bdown = zero, zero, zero, zero, zero
        for part, (cot, out) in enumerate(((cot_own, out_own), (cot_rem, out_rem))):
            for t in range(per_half):
                src = slice(t * tile, (t + 1) * tile)
                dst = slice(part * half + t * tile, part * half + (t + 1) * tile)
                xv = x_one[dst, :]
                down = down_acc[dst, :] + b_down
                out[src, :] = (xv + gate_two * down).astype(BF)
                grad_out = cot[src, :].astype(F32) * span_ref[dst, :]
                s_gate_two += col_sum(grad_out * down)
                s_bdown += col_sum(d_down[dst, :].astype(F32))
                n, rstd = norm_parts(xv)
                da = d_act[dst, :]
                s_shift += col_sum(da)
                s_pull += col_sum(da * n)
                dx = grad_out + norm_pull(n, rstd, da * mult_two)
                dx_ref[dst, :] = dx
                s_gate_one += col_sum(dx * branch[dst, :])
                d_branch[dst, :] = (gate_one * dx).astype(BF)
        lines = width // 128
        mod_ref[4 * lines :, :] = jnp.zeros((mod_ref.shape[0] - 4 * lines, 128), BF)
        for k, row in enumerate((s_gate_one, s_shift, s_pull * gain_two, s_gate_two)):
            put_rows(mod_ref, k * lines, row)
        put_rows(mod_ref, 4 * lines, vec_ref[7:8, 0:128])
        put_rows(sum_ref, 0, s_pull * (1.0 + scale_two))
        put_rows(sum_ref, lines, s_bdown)
        g_out = mm(att_ref[...], d_branch[...]).astype(BF)
        for h in range(2):
            g_out_ref[h] = g_out[:, h * cut : (h + 1) * cut].reshape(g_out_ref.shape[1:])
        d_att_ref[...] = mm(w_out_ref[...], d_branch[...], NT).astype(BF)
        for j in range(steps - 1):
            up_to_side[j]().wait()
            for a, b in grid_of(zs, 2):
                up_ref[j, a, b] = up_core[j, x, a, b] + up_side[j, a, b]
            down_to_y[j]().wait()
            down_ref[j] = down_core[j, y] + down_y[j]


def middle_links(
    att_t, tok_own, tok_rem, cot_own, cot_rem, span, vec, b_up, w_out, w_up, w_down, zs
):
    width, tokens = att_t.shape
    half = tokens // 2
    cut = width // 2
    ff = w_up.shape[1]
    tile = ff // zs
    rows = width // (4 * zs)
    down_rows = tile // 4
    halves = (2, zs, 2, 2, rows, cut)
    owned = (2, 2, down_rows, width)
    outs = [
        ((half, width), BF),
        ((half, width), BF),
        ((tokens, width), F32),
        ((width, tokens), BF),
        (halves, BF),
        (halves, BF),
        (owned, BF),
        ((zs - 1, zs, 2, rows, cut), BF),
        ((zs - 1, down_rows, width), BF),
        ((early_mod_rows(width), 128), BF),
        ((early_sum_rows(width, ff), 128), F32),
    ]
    return pl.pallas_call(
        functools.partial(middle_links_kernel, zs),
        grid=(zs,),
        in_specs=[
            once(att_t.shape),
            once(tok_own.shape),
            once(tok_rem.shape),
            once(cot_own.shape),
            once(cot_rem.shape),
            once(span.shape),
            once(vec.shape),
            pl.BlockSpec((1, tile), lambda i: (0, i)),
            once(w_out.shape),
            pl.BlockSpec((width, tile), lambda i: (0, i)),
            pl.BlockSpec((tile, width), lambda i: (i, 0)),
        ],
        out_specs=[once(shape) for shape, _ in outs],
        out_shape=[jax.ShapeDtypeStruct(*o) for o in outs],
        scratch_shapes=[
            pltpu.VMEM((tokens, width), F32),
            pltpu.VMEM((tokens, width), F32),
            pltpu.VMEM((tokens, width), BF),
            pltpu.VMEM((tokens, width), BF),
            pltpu.VMEM((tokens, width), F32),
            pltpu.VMEM((tokens, width), F32),
            pltpu.VMEM((tokens, width), BF),
            pltpu.VMEM((tokens, tile), BF),
            pltpu.VMEM((tokens, tile), BF),
            pltpu.VMEM((zs - 1, 2, zs, 2, rows, cut), BF),
            pltpu.VMEM((zs - 1, zs, 2, rows, cut), BF),
            pltpu.VMEM((zs - 1, 2, down_rows, width), BF),
            pltpu.VMEM((zs - 1, down_rows, width), BF),
            pltpu.SemaphoreType.DMA((8 * (zs - 1),)),
        ],
        compiler_params=params(62, collective_id=4),
        cost_estimate=pl.CostEstimate(
            flops=12 * tokens * width * ff + 6 * tokens * width * width,
            bytes_accessed=40 << 20,
            transcendentals=tokens * ff,
        ),
        name="middle_links",
    )(att_t, tok_own, tok_rem, cot_own, cot_rem, span, vec, b_up, w_out, w_up, w_down)


def attend_back_kernel(
    q_ref,
    k_ref,
    v_ref,
    att_ref,
    d_att_ref,
    e_ref,
    linv_ref,
    cos_ref,
    sin_ref,
    give_ref,
    out_ref,
    take_ref,
    do_mask,
    send,
    recv,
):
    step = pl.program_id(0)

    @pl.when(step == 0)
    def _():
        swap_start(give_ref, take_ref, send, recv)

    tokens = q_ref.shape[1]
    tile = 256
    zero = jnp.zeros((HD, tokens), BF)
    v_nat = v_ref[...].T
    cos = cos_ref[...]
    sin = sin_ref[...]

    def unrotate(x):
        low = x.astype(BF).astype(F32)
        a, b = low[0 : HD // 2], low[HD // 2 :]
        return a * cos + b * sin, b * cos - a * sin

    for h in range(2):
        rows = slice(h * HD, (h + 1) * HD)
        linv = linv_ref[0, h : h + 1, :]
        d_o = d_att_ref[rows, :].astype(F32)
        d_os = (d_o * linv).astype(BF)
        do_mask[h, rows, :] = d_os
        do_mask[h, (1 - h) * HD : (2 - h) * HD, :] = zero
        inner = col_sum(d_o * att_ref[rows, :].astype(F32)) * linv
        d_values = mm(d_os, e_ref[h], NT)
        out_ref[2, rows, :] = d_values.astype(BF)
        d_keys = jnp.zeros((HD, tokens), F32)
        d_queries = []
        for t in range(tokens // tile):
            cols = slice(t * tile, (t + 1) * tile)
            d_probs = mm(v_nat, do_mask[h, :, cols])
            d_s = (e_ref[h, :, cols].astype(F32) * (d_probs - inner[:, cols])).astype(BF)
            d_queries.append(mm(k_ref[rows, :], d_s))
            d_keys += mm(q_ref[rows, cols], d_s, NT)
        dq = jnp.concatenate(d_queries, axis=1) * HD**-0.5
        lead, trail = unrotate(dq)
        out_ref[0, h * HD : h * HD + HD // 2, :] = lead.astype(BF)
        out_ref[0, h * HD + HD // 2 : (h + 1) * HD, :] = trail.astype(BF)
        lead, trail = unrotate(d_keys)
        out_ref[1, h * HD : h * HD + HD // 2, :] = lead.astype(BF)
        out_ref[1, h * HD + HD // 2 : (h + 1) * HD, :] = trail.astype(BF)

    @pl.when(step == pl.num_programs(0) - 1)
    def _():
        swap_wait(give_ref, take_ref, send, recv)


def attend_back(qkv_t, att_t, d_att_t, e, linv, cos_t, sin_t, give):
    tokens = qkv_t.shape[1]
    width = HEADS * HD

    def part(k):
        return pl.BlockSpec((2 * HD, tokens), lambda i: (i + k * PAIRS, 0))

    return pl.pallas_call(
        attend_back_kernel,
        grid=(PAIRS,),
        in_specs=[
            part(0),
            part(1),
            part(2),
            part(0),
            part(0),
            pl.BlockSpec((2, tokens, tokens), lambda i: (i, 0, 0)),
            pl.BlockSpec((1, 8, tokens), lambda i: (i, 0, 0)),
            whole(cos_t.shape),
            whole(sin_t.shape),
            ANY,
        ],
        out_specs=[pl.BlockSpec((3, 2 * HD, tokens), lambda i: (0, i, 0)), ANY],
        out_shape=[
            jax.ShapeDtypeStruct((3, width, tokens), BF),
            jax.ShapeDtypeStruct(give.shape, give.dtype),
        ],
        scratch_shapes=[pltpu.VMEM((2, 2 * HD, tokens), BF)] + SEMS,
        compiler_params=params(collective_id=2),
        cost_estimate=pl.CostEstimate(
            flops=32 * tokens * tokens * width, bytes_accessed=36 << 20, transcendentals=0
        ),
        name="attend_back",
    )(qkv_t, qkv_t, qkv_t, att_t, d_att_t, e, linv, cos_t, sin_t, give)


def tail_kernel(tok_own, tok_rem, d_proj_ref, w_ref, dx_ref, vec_ref, own_ref, rem_ref, sums_ref):
    step = pl.program_id(0)
    steps = pl.num_programs(0)
    mult_one = vec_ref[0:1, :]
    gain_one = vec_ref[2:3, :]
    scale_one = vec_ref[3:4, :]
    d_act = mm(d_proj_ref[...], w_ref[...], TN)

    def finish(tok, out):
        n, rstd = norm_parts(tok[...].astype(F32))
        grad = dx_ref[...] + norm_pull(n, rstd, d_act * mult_one)
        out[...] = grad.astype(out.dtype)
        return col_sum(d_act), col_sum(d_act * n)

    @pl.when(step == 0)
    def _():
        shift, pull = finish(tok_rem, rem_ref)
        sums_ref[0:1, :] = shift
        sums_ref[1:2, :] = pull
        sums_ref[2:, :] = jnp.zeros((6, shift.shape[1]), F32)

    @pl.when(step == steps - 1)
    def _():
        shift, pull = finish(tok_own, own_ref)
        shift = sums_ref[0:1, :] + shift
        pull = sums_ref[1:2, :] + pull
        sums_ref[0:1, :] = shift
        sums_ref[1:2, :] = pull * gain_one
        sums_ref[2:3, :] = pull * (1.0 + scale_one)


def tail(tok_own, tok_rem, d_proj_t, w_qkv_t, dx, vec):
    half, width = tok_own.shape
    return pl.pallas_call(
        tail_kernel,
        grid=(2,),
        in_specs=[
            whole(tok_own.shape),
            whole(tok_rem.shape),
            pl.BlockSpec((3 * width, half), lambda i: (0, 1 - i)),
            whole(w_qkv_t.shape),
            pl.BlockSpec((half, width), lambda i: (1 - i, 0)),
            whole(vec.shape),
        ],
        out_specs=[whole((half, width)), whole((half, width)), whole((8, width))],
        out_shape=[
            jax.ShapeDtypeStruct((half, width), F32),
            jax.ShapeDtypeStruct((half, width), BF),
            jax.ShapeDtypeStruct((8, width), F32),
        ],
        compiler_params=params(),
        cost_estimate=pl.CostEstimate(
            flops=12 * half * width * width, bytes_accessed=20 << 20, transcendentals=0
        ),
        name="tail",
    )(tok_own, tok_rem, d_proj_t, w_qkv_t, dx, vec)


def weight_grad_kernel(act_ref, d_proj_ref, out_ref):
    out_ref[...] = mm(act_ref[...], d_proj_ref[...], NT).astype(BF)


def weight_grad(act_t, d_proj_t):
    width, tokens = act_t.shape
    cols = d_proj_t.shape[0]
    tile = 768
    return pl.pallas_call(
        weight_grad_kernel,
        grid=(cols // tile,),
        in_specs=[whole(act_t.shape), pl.BlockSpec((tile, tokens), lambda i: (i, 0))],
        out_specs=pl.BlockSpec((width, tile), lambda i: (0, i)),
        out_shape=jax.ShapeDtypeStruct((width, cols), BF),
        compiler_params=params(),
        cost_estimate=pl.CostEstimate(
            flops=2 * cols * width * tokens, bytes_accessed=12 << 20, transcendentals=0
        ),
        name="weight_grad",
    )(act_t, d_proj_t)


def gather_stages(links, ref):
    z, y, c, x = links.z, links.y, links.c, links.x

    def pair(mine, theirs, device):
        sem = links.take(2)

        def make(slot):
            return remote(slot(), slot(), links.sems.at[sem], links.sems.at[sem + 1], device)

        def wait():
            make(mine).wait_send()
            make(theirs).wait_recv()

        return (lambda: make(mine).start()), wait

    sem = links.take(2 * links.zs)

    def make(f, slot):
        block = ref.at[slot, :, :, x]
        return remote(
            block, block, links.sems.at[sem + f], links.sems.at[sem + links.zs + slot], links.at_z(f)
        )

    def far_start():
        for f in links.far:
            make(f, z).start()

    def far_wait():
        for f in links.far:
            make(f, z).wait_send()
            make(f, f).wait_recv()

    return [
        pair(lambda: ref.at[z, y, c, x], lambda: ref.at[z, y, 1 - c, x], links.core),
        pair(lambda: ref.at[z, y, :, x], lambda: ref.at[z, 1 - y, :, x], links.across),
        (far_start, far_wait),
        pair(lambda: ref.at[:, :, :, x], lambda: ref.at[:, :, :, 1 - x], links.facing),
    ]


def sum_stages(links, ref, take, far):
    swaps = [
        links.swap(lambda: ref, lambda k=k: take.at[k], device)
        for k, device in enumerate((links.core, links.across, links.facing))
    ]
    far_start, far_wait = links.spread(lambda f: ref, lambda slot: far.at[slot])

    def finish(k):
        swaps[k]().wait()
        ref[...] += take[k]

    def far_finish():
        far_wait()
        far[links.z] = ref[...]
        total = far[0]
        for f in range(1, links.zs):
            total += far[f]
        ref[...] = total

    return [
        (lambda: swaps[0]().start(), lambda: finish(0)),
        (lambda: swaps[1]().start(), lambda: finish(1)),
        (far_start, far_finish),
        (lambda: swaps[2]().start(), lambda: finish(2)),
    ]


def back_kernel(zs, split, ins, outs, scratch):
    (
        q_ref,
        k_ref,
        v_ref,
        att_ref,
        d_att_ref,
        e_ref,
        linv_ref,
        cos_ref,
        sin_ref,
        own_ref,
        give_ref,
        up_ref,
        down_ref,
        raw_up,
        raw_out,
        raw_down,
        mod_ref,
        sum_ref,
        act_ref,
        w_ref,
        tok_own,
        tok_rem,
        dx_ref,
        vec_ref,
    ) = ins
    result, grad_ref, s_qkv, s_out, s_up, s_down, *small_outs = outs
    (
        do_mask,
        d_proj,
        sems,
        u_own,
        u_core,
        u_side,
        u_sum,
        u_y,
        u_z,
        u_last,
        u_facing,
        d_own,
        d_core,
        d_y,
        d_sum,
        d_z,
        d_last,
        d_facing,
        q_raws,
        q_cores,
        q_ys,
        q_zs,
        q_lasts,
        q_facings,
        g_send,
        g_take,
        early_take,
        early_far,
        late_take,
        late_far,
        mod_early,
        mod_late,
        sum_early,
        sum_late,
    ) = scratch
    step = pl.program_id(0)
    tokens = q_ref.shape[1]
    width = act_ref.shape[0]
    half = tokens // 2
    cut = width // 2
    pieces = zs + 1
    links = Links(sems, zs)
    x, y, z, c = links.x, links.y, links.z, links.c

    def at(k):
        return pl.when(step == k)

    raws = (raw_up, raw_out)
    u_keep = [links.local(lambda r=r: r.at[:, :, :, c], lambda k=k: u_own.at[k]) for k, r in enumerate(raws)]
    u_to_core = [
        links.swap(lambda r=r: r.at[:, :, :, 1 - c], lambda k=k: u_core.at[k], links.core)
        for k, r in enumerate(raws)
    ]
    u_to_side = [
        links.swap(lambda k=k: u_own.at[k, 1 - x], lambda k=k: u_side.at[k], links.facing)
        for k in range(2)
    ]
    u_load = [links.local(lambda j=j: up_ref.at[j, :, y], lambda j=j: u_sum.at[j, :, y]) for j in range(zs - 1)]

    def u_y_src(j):
        if j < zs - 1:
            return up_ref.at[j, :, 1 - y]
        return u_sum.at[j, :, 1 - y]

    u_to_y = [
        links.swap(lambda j=j: u_y_src(j), lambda j=j: u_y.at[j], links.across) for j in range(pieces)
    ]
    u_far = [
        links.spread(lambda f, j=j: u_sum.at[j, f, y], lambda slot, j=j: u_z.at[j, slot])
        for j in range(pieces)
    ]
    u_to_facing = [
        links.swap(lambda j=j: u_last.at[j], lambda j=j: u_facing.at[j], links.facing)
        for j in range(pieces)
    ]
    d_keep = links.local(lambda: raw_down.at[:, c], lambda: d_own)
    d_to_core = links.swap(lambda: raw_down.at[:, 1 - c], lambda: d_core, links.core)
    d_to_y = links.swap(lambda: d_own.at[1 - y], lambda: d_y, links.across)
    d_load = links.local(lambda: down_ref, lambda: d_sum.at[0 : zs - 1])
    d_far = [
        links.gather(
            lambda j=j: down_ref.at[j] if j < zs - 1 else d_sum.at[j], lambda slot: d_z.at[slot], j
        )
        for j in range(zs)
    ]
    d_to_facing = links.swap(lambda: d_last, lambda: d_facing, links.facing)
    groups = range(len(split))
    q_to_core = [
        links.swap(lambda g=g: q_raws[g].at[:, :, 1 - c], lambda g=g: q_cores[g], links.core)
        for g in groups
    ]
    q_to_y = [
        links.swap(lambda g=g: q_cores[g].at[:, 1 - y], lambda g=g: q_ys[g], links.across)
        for g in groups
    ]
    q_far = [
        links.spread(lambda f, g=g: q_cores[g].at[f, y], lambda slot, g=g: q_zs[g].at[slot])
        for g in groups
    ]
    q_to_facing = [
        links.swap(lambda g=g: q_lasts[g], lambda g=g: q_facings[g], links.facing) for g in groups
    ]
    keep_out = links.local(lambda: own_ref, lambda: result.at[x])
    out_sem = links.take(2)

    def cross_out(slot):
        return remote(give_ref, result.at[slot], sems.at[out_sem], sems.at[out_sem + 1], links.facing)

    give_grad = links.swap(lambda: g_send, lambda: g_take, links.facing)
    early = [
        gather_stages(links, mod_early),
        sum_stages(links, sum_early, early_take, early_far),
    ]
    late = [gather_stages(links, mod_late), sum_stages(links, sum_late, late_take, late_far)]

    def begin(arrays, stage):
        for stages in arrays:
            stages[stage][0]()

    def end(arrays, stage):
        for stages in arrays:
            stages[stage][1]()

    def u_y_done(j):
        u_to_y[j]().wait()
        for a in range(zs):
            u_sum[j, a, y] = u_sum[j, a, y] + u_y[j, a]
        u_far[j][0]()

    def u_z_done(j):
        u_far[j][1]()
        total = u_sum[j, z, y].astype(F32)
        for f in links.far:
            total += u_z[j, f].astype(F32)
        u_last[j] = total.astype(BF)
        u_to_facing[j]().start()

    def u_done(j):
        u_to_facing[j]().wait()
        mine, other = u_last[j].astype(F32), u_facing[j].astype(F32)
        out, start = (s_up, j * width) if j < zs else (s_out, 0)
        out[:, start : start + cut] = jnp.where(x == 0, mine, other)
        out[:, start + cut : start + width] = jnp.where(x == 0, other, mine)

    def q_core_done(g):
        q_to_core[g]().wait()
        for a, b in grid_of(zs, 2):
            q_cores[g][a, b] = q_cores[g][a, b] + q_raws[g][a, b, c]
        q_to_y[g]().start()

    def q_y_done(g):
        q_to_y[g]().wait()
        for a in range(zs):
            q_cores[g][a, y] = q_cores[g][a, y] + q_ys[g][a]
        q_far[g][0]()

    def q_z_done(g):
        q_far[g][1]()
        total = q_cores[g][z, y].astype(F32)
        for f in links.far:
            total += q_zs[g][f].astype(F32)
        q_lasts[g][...] = total.astype(BF)
        q_to_facing[g]().start()

    def q_done(g):
        q_to_facing[g]().wait()
        total = q_lasts[g][...].astype(F32) + q_facings[g][...].astype(F32)
        first, size = split[g][0] * HD, (split[g][1] - split[g][0]) * HD
        for p in range(3):
            s_qkv[:, p * width + first : p * width + first + size] = total[:, p * size : (p + 1) * size]

    def weight_grad_of(g):
        first, size = split[g][0] * HD, (split[g][1] - split[g][0]) * HD
        for p in range(3):
            rows = slice(p * width + first, p * width + first + size)
            part = mm(act_ref[...], d_proj[rows, :], NT).astype(BF)
            q_raws[g][:, :, :, :, p * size : (p + 1) * size] = part.reshape(
                q_raws[g].shape[:4] + (size,)
            )
        q_to_core[g]().start()


    @at(0)
    def _():
        greet(links.core, links.across, links.facing, *[links.at_z(f) for f in links.far])
        for k in range(2):
            u_to_core[k]().start()
            u_keep[k]().start()
        d_to_core().start()
        d_keep().start()
        d_load().start()
        for j in range(zs - 1):
            u_load[j]().start()
            u_to_y[j]().start()
            d_far[j][0]()
        mod_early[z, y, c, x] = mod_ref[...]
        sum_early[...] = sum_ref[...]
        begin(early, 0)
        keep_out().start()
        cross_out(x).start()

    @at(1)
    def _():
        for k in range(2):
            u_keep[k]().wait()
            u_to_core[k]().wait()
            for h, a, b in grid_of(2, zs, 2):
                u_own[k, h, a, b] = u_own[k, h, a, b] + u_core[k, h, a, b]
            u_to_side[k]().start()
        d_keep().wait()
        d_to_core().wait()
        for b in range(2):
            d_own[b] = d_own[b] + d_core[b]
        d_to_y().start()
        end(early, 0)
        begin(early, 1)

    @at(2)
    def _():
        for j in range(zs - 1):
            u_load[j]().wait()
            u_y_done(j)
        end(early, 1)
        begin(early, 2)

    @at(3)
    def _():
        d_to_y().wait()
        d_sum[zs - 1] = d_own[y] + d_y[...]
        d_far[zs - 1][0]()
        end(early, 2)
        begin(early, 3)

    @at(4)
    def _():
        weight_grad_of(0)
        for k in range(2):
            u_to_side[k]().wait()
            for a, b in grid_of(zs, 2):
                u_sum[zs - 1 + k, a, b] = u_own[k, x, a, b] + u_side[k, a, b]
            u_to_y[zs - 1 + k]().start()
        for j in range(zs - 1):
            u_z_done(j)

    @at(5)
    def _():
        q_core_done(0)
        end(early, 3)
        for k in range(2):
            u_y_done(zs - 1 + k)
        d_load().wait()
        for j in range(zs):
            d_far[j][1]()
        total = d_sum[z].astype(F32)
        for f in links.far:
            total += d_z[f].astype(F32)
        d_last[...] = total.astype(BF)
        d_to_facing().start()


    @pl.when(step < PAIRS)
    def _():
        tile = 256
        zero = jnp.zeros((HD, tokens), BF)
        v_nat = v_ref[...].T
        cos = cos_ref[...]
        sin = sin_ref[...]

        def put(part, h, value):
            low = value.astype(BF).astype(F32)
            a, b = low[0 : HD // 2], low[HD // 2 :]
            start = part * width + step * 2 * HD + h * HD
            d_proj[pl.ds(pl.multiple_of(start, 32), 32), :] = (a * cos + b * sin).astype(BF)
            d_proj[pl.ds(pl.multiple_of(start + 32, 32), 32), :] = (b * cos - a * sin).astype(BF)

        for h in range(2):
            rows = slice(h * HD, (h + 1) * HD)
            linv = linv_ref[0, h : h + 1, :]
            d_o = d_att_ref[rows, :].astype(F32)
            d_os = (d_o * linv).astype(BF)
            do_mask[h, rows, :] = d_os
            do_mask[h, (1 - h) * HD : (2 - h) * HD, :] = zero
            inner = col_sum(d_o * att_ref[rows, :].astype(F32)) * linv
            d_values = mm(d_os, e_ref[h], NT)
            start = 2 * width + step * 2 * HD + h * HD
            d_proj[pl.ds(pl.multiple_of(start, HD), HD), :] = d_values.astype(BF)
            d_keys = jnp.zeros((HD, tokens), F32)
            d_queries = []
            for t in range(tokens // tile):
                cols = slice(t * tile, (t + 1) * tile)
                d_probs = mm(v_nat, do_mask[h, :, cols])
                d_s = (e_ref[h, :, cols].astype(F32) * (d_probs - inner[:, cols])).astype(BF)
                d_queries.append(mm(k_ref[rows, :], d_s))
                d_keys += mm(q_ref[rows, cols], d_s, NT)
            put(0, h, jnp.concatenate(d_queries, axis=1) * HD**-0.5)
            put(1, h, d_keys)


    def finish(tok, cols):
        d_act = mm(d_proj[:, cols], w_ref[...], TN)
        n, rstd = norm_parts(tok[...].astype(F32))
        grad = dx_ref[cols, :] + norm_pull(n, rstd, d_act * vec_ref[0:1, :])
        return grad, col_sum(d_act), col_sum(d_act * n)

    @at(PAIRS)
    def _():
        weight_grad_of(1)
        for k in range(2):
            u_z_done(zs - 1 + k)
        q_y_done(0)
        grad, shift, pull = finish(tok_rem, slice(half, 2 * half))
        g_send[...] = grad.astype(BF)
        give_grad().start()
        q_core_done(1)
        grad, shift_own, pull_own = finish(tok_own, slice(0, half))
        grad_ref[x] = grad
        shift += shift_own
        pull += pull_own
        lines = width // 128
        mine = mod_late.at[z, y, c, x]
        mine[2 * lines :, :] = jnp.zeros((mod_late.shape[4] - 2 * lines, 128), BF)
        put_rows(mine, 0, shift)
        put_rows(mine, lines, pull * vec_ref[2:3, :])
        sum_late[lines:, :] = jnp.zeros((sum_late.shape[0] - lines, 128), F32)
        put_rows(sum_late, 0, pull * (1.0 + vec_ref[3:4, :]))
        begin(late, 0)
        d_to_facing().wait()
        s_down[...] = d_last[...].astype(F32) + d_facing[...].astype(F32)
        end(late, 0)
        begin(late, 1)
        for j in range(pieces):
            u_done(j)
        q_z_done(0)
        end(late, 1)
        begin(late, 2)
        q_y_done(1)
        end(late, 2)
        begin(late, 3)
        keep_out().wait()
        cross_out(x).wait_send()
        cross_out(1 - x).wait_recv()
        q_done(0)
        q_z_done(1)
        end(late, 3)
        give_grad().wait()
        grad_ref[1 - x] = g_take[...].astype(F32)
        q_done(1)
        for out, value in zip(small_outs, (mod_early, mod_late, sum_early, sum_late)):
            out[...] = value[...]


def back(ins, zs, ff):
    (q, att, d_att, e, linv, cos_t, sin_t, own, give, up, down, raw_up, raw_out, raw_down) = ins[:14]
    mod, sums, act_t, w_qkv_t, tok_own, tok_rem, dx, vec = ins[14:]
    width, tokens = att.shape
    half = tokens // 2
    cut = width // 2
    rows = width // (4 * zs)
    down_rows = ff // (4 * zs)
    pieces = zs + 1
    split = ((0, 8), (8, HEADS))
    sizes = [3 * (b - a) * HD for a, b in split]
    last = PAIRS - 1

    def part(k):
        return pl.BlockSpec((2 * HD, tokens), lambda i: (jnp.minimum(i, last) + k * PAIRS, 0))

    def vm(*shape, kind=BF):
        return pltpu.VMEM(shape, kind)

    lines = width // 128
    mod_early = (zs, 2, 2, 2) + mod.shape
    mod_late = (zs, 2, 2, 2, round_up(2 * lines, 16), 128)
    sum_late = (round_up(lines, 8), 128)
    outs = [
        ((half, width), F32),
        ((rows, 3 * width), F32),
        ((rows, width), F32),
        ((rows, ff), F32),
        ((down_rows, width), F32),
        (mod_early, BF),
        (mod_late, BF),
        (sums.shape, F32),
        (sum_late, F32),
    ]
    outs[0] = ((2, half, width), F32)
    in_specs = (
        [part(0), part(1), part(2), part(0), part(0)]
        + [
            pl.BlockSpec((2, tokens, tokens), lambda i: (jnp.minimum(i, last), 0, 0)),
            pl.BlockSpec((1, 8, tokens), lambda i: (jnp.minimum(i, last), 0, 0)),
            once(cos_t.shape),
            once(sin_t.shape),
        ]
        + [ANY] * 7
        + [once(a.shape) for a in (mod, sums, act_t, w_qkv_t, tok_own, tok_rem, dx, vec)]
    )
    out_specs = [ANY] + [once(shape) for shape, _ in outs]
    out_shape = [jax.ShapeDtypeStruct((2, half, width), BF)] + [
        jax.ShapeDtypeStruct(*o) for o in outs
    ]
    scratch = [
        vm(2, 2 * HD, tokens),
        vm(3 * width, tokens),
        pltpu.SemaphoreType.DMA((250,)),
        vm(2, 2, zs, 2, rows, cut),
        vm(2, 2, zs, 2, rows, cut),
        vm(2, zs, 2, rows, cut),
        vm(pieces, zs, 2, rows, cut),
        vm(pieces, zs, rows, cut),
        vm(pieces, zs, rows, cut),
        vm(pieces, rows, cut),
        vm(pieces, rows, cut),
        vm(2, down_rows, width),
        vm(2, down_rows, width),
        vm(down_rows, width),
        vm(zs, down_rows, width),
        vm(zs, down_rows, width),
        vm(down_rows, width),
        vm(down_rows, width),
        [vm(zs, 2, 2, rows, s) for s in sizes],
        [vm(zs, 2, rows, s) for s in sizes],
        [vm(zs, rows, s) for s in sizes],
        [vm(zs, rows, s) for s in sizes],
        [vm(rows, s) for s in sizes],
        [vm(rows, s) for s in sizes],
        vm(half, width),
        vm(half, width),
        vm(3, *sums.shape, kind=F32),
        vm(zs, *sums.shape, kind=F32),
        vm(3, *sum_late, kind=F32),
        vm(zs, *sum_late, kind=F32),
        vm(*mod_early),
        vm(*mod_late),
        vm(*sums.shape, kind=F32),
        vm(*sum_late, kind=F32),
    ]
    flat, tree = jax.tree.flatten(scratch)
    n_in, n_out = len(in_specs), len(out_specs)

    def kernel(*refs):
        back_kernel(
            zs,
            split,
            refs[:n_in],
            refs[n_in : n_in + n_out],
            jax.tree.unflatten(tree, refs[n_in + n_out :]),
        )

    return pl.pallas_call(
        kernel,
        grid=(PAIRS + 1,),
        in_specs=in_specs,
        out_specs=out_specs,
        out_shape=out_shape,
        scratch_shapes=flat,
        compiler_params=params(62, collective_id=5),
        cost_estimate=pl.CostEstimate(
            flops=32 * tokens * tokens * width + 12 * tokens * width * width,
            bytes_accessed=60 << 20,
            transcendentals=0,
        ),
        name="back",
    )(q, q, q, att, d_att, e, linv, cos_t, sin_t, *ins[7:])


def time_features(time_steps, pair_count):
    frequency = jnp.exp(-math.log(10000.0) * jnp.arange(pair_count, dtype=F32) / pair_count)
    angles = time_steps.astype(F32)[:, None] * frequency[None, :]
    return jnp.concatenate([jnp.cos(angles), jnp.sin(angles)], axis=-1)


def per_device(
    tokens,
    cotangent,
    time_index,
    span_starts,
    span_lengths,
    w_ada,
    b_ada,
    gain_one,
    w_qkv,
    w_out,
    gain_two,
    w_up,
    b_up,
    w_down,
    b_down,
):
    seqs_dev, half, width = tokens.shape
    length = 2 * half
    rank = lax.axis_index("seq")
    swap = [(0, 1), (1, 0)]

    def pick(x, i):
        return lax.dynamic_index_in_dim(x, i, 0, keepdims=False)

    tok_own, tok_send = pick(tokens, rank), pick(tokens, 1 - rank)
    cot_own = pick(cotangent, rank)
    tok_rem = lax.ppermute(tok_send, "seq", swap)

    here = jnp.arange(half, dtype=jnp.int32)
    place = jnp.concatenate([rank * half + here, (1 - rank) * half + here])
    frequency = jnp.exp(-math.log(10000.0) * jnp.arange(HD // 2, dtype=F32) / (HD // 2))
    angles = frequency[:, None] * place.astype(F32)[None, :]
    cos_t, sin_t = jnp.cos(angles), jnp.sin(angles)
    start, extent = pick(span_starts, rank), pick(span_lengths, rank)
    span = jnp.where((place >= start) & (place < start + extent), 2.0, 0.5).astype(F32)[:, None]

    time_own = lax.dynamic_slice_in_dim(time_index, rank, 1)
    cond_act = jax.nn.silu(time_features(time_own, w_ada.shape[0] // 2))
    modulation = (
        jnp.dot(cond_act, w_ada.astype(F32), precision=lax.Precision.HIGHEST)[0] + b_ada
    )
    shift_one, scale_one, gate_one, shift_two, scale_two, gate_two = jnp.split(modulation, 6)
    zeros = jnp.zeros_like(shift_one)
    vec_one = jnp.stack(
        [gain_one * (1.0 + scale_one), shift_one, gain_one, scale_one, zeros, zeros, zeros, zeros]
    )
    vec_two = jnp.stack(
        [
            gate_one,
            gain_two * (1.0 + scale_two),
            shift_two,
            gate_two,
            b_down,
            gain_two,
            scale_two,
            jnp.pad(jnp.concatenate([time_own // 32, time_own % 32]).astype(F32), (0, width - 2)),
        ]
    )
    w_qkv_t = w_qkv.T

    dp, dps = lax.axis_index("dp"), lax.axis_size("dp")
    ff = w_up.shape[1]
    zs = dps // 4
    linked = dps % 4 == 0 and width % (64 * zs) == 0 and ff == zs * width

    act_t, qkv_t = project(tok_own, tok_rem, vec_one, cos_t, sin_t, w_qkv_t)
    att_t, e, linv, cot_rem = attend(qkv_t, cotangent)
    if linked:
        out_own, out_rem, dx, d_att_t, raw_out, raw_up, raw_down, up, down, mod, sums = middle_links(
            att_t, tok_own, tok_rem, cot_own, cot_rem, span, vec_two, b_up[None], w_out, w_up, w_down, zs
        )
        ins = (qkv_t, att_t, d_att_t, e, linv, cos_t, sin_t, out_own, out_rem, up, down)
        ins += (raw_up, raw_out, raw_down, mod, sums, act_t, w_qkv_t, tok_own, tok_rem, dx, vec_one)
        output, grad_tokens, *shards, mod_early, mod_late, sum_early, sum_late = back(ins, zs, ff)
        mod_early = mod_early.reshape(2 * dps, -1).astype(F32)
        mod_late = mod_late.reshape(2 * dps, -1).astype(F32)
        d_mod_all = jnp.concatenate([mod_late[:, : 2 * width], mod_early[:, : 4 * width]], axis=1)
        time_all = 32.0 * mod_early[:, 4 * width] + mod_early[:, 4 * width + 1]
        small = jnp.concatenate(
            [sum_late.reshape(-1)[:width], sum_early.reshape(-1)[: 2 * width + ff]]
        )
    else:
        out_own, out_rem, dx, d_att_t, g_out, g_up, g_down, g_bup, sums_two = middle(
            att_t, tok_own, tok_rem, cot_own, cot_rem, span, vec_two, b_up[None], w_out, w_up, w_down
        )
        d_proj, out_back = attend_back(qkv_t, att_t, d_att_t, e, linv, cos_t, sin_t, out_rem)
        d_proj_t = d_proj.reshape(3 * width, length)
        g_own, g_rem, sums_one = tail(tok_own, tok_rem, d_proj_t, w_qkv_t, dx, vec_one)
        g_qkv = weight_grad(act_t, d_proj_t)

        def spread(own, other):
            first = jnp.where(rank == 0, own, other)
            second = jnp.where(rank == 0, other, own)
            return jnp.stack([first, second])

        output = spread(out_own, out_back)
        grad_tokens = spread(g_own, lax.ppermute(g_rem, "seq", swap).astype(F32))
        shards = [
            lax.psum(lax.psum_scatter(g, "dp", scatter_dimension=0, tiled=True), "seq").astype(F32)
            for g in (g_qkv, g_out, g_up, g_down)
        ]
        d_mod = jnp.concatenate([sums_one[:2].reshape(-1), sums_two[:4].reshape(-1)])
        small = jnp.concatenate([sums_one[2], sums_two[4], sums_two[5], g_bup[0]])
        d_mod_all = lax.all_gather(d_mod, ("dp", "seq"))
        time_all = lax.all_gather(time_own[0].astype(F32), ("dp", "seq"))
        small = lax.psum(small, ("dp", "seq"))

    def mine(x, axis=0):
        size = x.shape[axis] // dps
        return lax.dynamic_slice_in_dim(x, dp * size, size, axis)

    features = jax.nn.silu(time_features(time_all, w_ada.shape[0] // 2))
    s_w_ada = jnp.dot(mine(features, 1).T, d_mod_all, precision=lax.Precision.HIGHEST)
    s_b_ada = jnp.sum(mine(d_mod_all, 1), axis=0)
    s_gain_one = mine(small[:width])
    s_gain_two = mine(small[width : 2 * width])
    s_b_down = mine(small[2 * width : 3 * width])
    s_b_up = mine(small[3 * width :])
    s_qkv, s_out, s_up, s_down = shards

    return (
        output,
        grad_tokens,
        s_w_ada,
        s_b_ada,
        s_gain_one,
        s_qkv,
        s_out,
        s_gain_two,
        s_up,
        s_b_up,
        s_down,
        s_b_down,
    )


def solution(mesh):
    rows = P("dp", "seq", None)
    return jax.shard_map(
        per_device,
        mesh=mesh,
        in_specs=(rows, rows, P("dp"), P("dp"), P("dp")) + (P(),) * 10,
        out_specs=(
            rows,
            rows,
            P("dp", None),
            P("dp"),
            P("dp"),
            P("dp", None),
            P("dp", None),
            P("dp"),
            P("dp", None),
            P("dp"),
            P("dp", None),
            P("dp"),
        ),
        check_vma=False,
    )
```

```python
import functools
import math

import jax
import jax.numpy as jnp
from jax import lax
from jax.experimental import pallas as pl
from jax.experimental.pallas import tpu as pltpu
from jax.sharding import PartitionSpec as P

HEADS = 12
HD = 64
PAIRS = HEADS // 2
NORM_EPS = 1e-05
LOG2E = math.log2(math.e)
BF = jnp.bfloat16
F32 = jnp.float32
MIB = 1 << 20

NN = (((1,), (0,)), ((), ()))
NT = (((1,), (1,)), ((), ()))
TN = (((0,), (0,)), ((), ()))


def mm(a, b, dims=NN):
    return lax.dot_general(a, b, dims, preferred_element_type=F32)


def norm_parts(x):
    centre = x - jnp.mean(x, axis=-1, keepdims=True)
    rstd = lax.rsqrt(jnp.mean(centre * centre, axis=-1, keepdims=True) + NORM_EPS)
    return centre * rstd, rstd


def norm_pull(n, rstd, dn):
    return rstd * (
        dn - jnp.mean(dn, axis=-1, keepdims=True) - n * jnp.mean(dn * n, axis=-1, keepdims=True)
    )


def col_sum(x):
    return jnp.sum(x, axis=0, keepdims=True)


def rows_of(size, index):
    return pl.ds(pl.multiple_of(index * size, size), size)


def params(mib=56, collective_id=None):
    if collective_id is None:
        return pltpu.CompilerParams(vmem_limit_bytes=mib * MIB)
    return pltpu.CompilerParams(
        vmem_limit_bytes=mib * MIB, collective_id=collective_id, has_side_effects=True
    )


def whole(shape):
    zeros = (0,) * len(shape)
    return pl.BlockSpec(shape, lambda *_: zeros)


MESH = pl.DeviceIdType.MESH
ANY = pl.BlockSpec(memory_space=pl.ANY)
SEMS = [pltpu.SemaphoreType.DMA, pltpu.SemaphoreType.DMA]


def greet(*partners):
    barrier = pltpu.get_barrier_semaphore()
    for partner in partners:
        pl.semaphore_signal(barrier, inc=1, device_id=partner, device_id_type=MESH)
    pl.semaphore_wait(barrier, len(partners))


def remote(src, dst, send, recv, device):
    return pltpu.make_async_remote_copy(
        src_ref=src, dst_ref=dst, send_sem=send, recv_sem=recv, device_id=device, device_id_type=MESH
    )


def seq_partner():
    return (lax.axis_index("dp"), 1 - lax.axis_index("seq"))


def swap_start(src, dst, send, recv):
    partner = seq_partner()
    greet(partner)
    remote(src, dst, send, recv, partner).start()


def swap_wait(src, dst, send, recv):
    remote(src, dst, send, recv, seq_partner()).wait()


class Links:
    def __init__(self, sems, zs):
        self.sems, self.used, self.zs = sems, 0, zs
        dp, self.x = lax.axis_index("dp"), lax.axis_index("seq")
        self.z, self.y, self.c = dp // 4, lax.rem(dp // 2, 2), lax.rem(dp, 2)
        self.core = (dp + 1 - 2 * self.c, self.x)
        self.across = (dp + 2 - 4 * self.y, self.x)
        self.facing = (dp, 1 - self.x)
        self.far = [lax.rem(self.z + k, zs) for k in range(1, zs)]

    def at_z(self, f):
        return (f * 4 + 2 * self.y + self.c, self.x)

    def take(self, count):
        self.used += count
        return self.used - count

    def local(self, src, dst):
        sem = self.take(1)
        return lambda: pltpu.make_async_copy(src(), dst(), self.sems.at[sem])

    def swap(self, src, dst, device):
        sem = self.take(2)
        return lambda: remote(src(), dst(), self.sems.at[sem], self.sems.at[sem + 1], device)

    def spread(self, src, dst):
        sem = self.take(2 * self.zs)

        def make(f, slot):
            return remote(
                src(f), dst(slot), self.sems.at[sem + f], self.sems.at[sem + self.zs + slot], self.at_z(f)
            )

        def start():
            for f in self.far:
                make(f, self.z).start()

        def wait():
            for f in self.far:
                make(f, self.z).wait_send()
                make(f, f).wait_recv()

        return start, wait

    def gather(self, src, dst, goal):
        sem = self.take(1 + self.zs)

        def make(slot):
            return remote(
                src(), dst(slot), self.sems.at[sem], self.sems.at[sem + 1 + slot], self.at_z(goal)
            )

        def start():
            pl.when(self.z != goal)(lambda: make(self.z).start())

        def wait():
            pl.when(self.z != goal)(lambda: make(self.z).wait_send())

            @pl.when(self.z == goal)
            def _():
                for f in self.far:
                    make(f).wait_recv()

        return start, wait


def add_to(dst, src, lead):
    for index in lead:
        dst[index] = dst[index] + src[index]


def grid_of(*sizes):
    return [()] if not sizes else [(i,) + r for i in range(sizes[0]) for r in grid_of(*sizes[1:])]


def round_up(value, unit):
    return -(-value // unit) * unit


def early_mod_rows(width):
    return round_up(4 * width // 128 + 1, 16)


def early_sum_rows(width, ff):
    return round_up((2 * width + ff) // 128, 8)


def put_rows(ref, start, row):
    for k in range(row.shape[1] // 128):
        ref[start + k : start + k + 1, :] = row[:, k * 128 : (k + 1) * 128].astype(ref.dtype)


def once(shape):
    zeros = (0,) * len(shape)
    return pl.BlockSpec(shape, lambda *_: zeros, pipeline_mode=pl.Buffered(1))


def project_kernel(own_ref, rem_ref, vec_ref, cos_ref, sin_ref, w_ref, act_ref, out_ref):
    step = pl.program_id(0)
    half, _ = own_ref.shape
    tile = 256

    @pl.when(step == 0)
    def _():
        scale = vec_ref[0:1, :]
        shift = vec_ref[1:2, :]
        for part, ref in enumerate((own_ref, rem_ref)):
            for t in range(half // tile):
                n, _ = norm_parts(ref[t * tile : (t + 1) * tile, :].astype(F32))
                act = (n * scale + shift).astype(BF)
                start = part * half + t * tile
                act_ref[:, start : start + tile] = act.T

    proj = mm(w_ref[...], act_ref[...])
    heads = proj.shape[0] // HD
    tokens = proj.shape[1]

    @pl.when(step < 4)
    def _():
        factor = jnp.where(step < 2, HD**-0.5, 1.0)
        cos = cos_ref[...] * factor
        sin = sin_ref[...] * factor
        for h in range(heads):
            a = proj[h * HD : h * HD + HD // 2]
            b = proj[h * HD + HD // 2 : (h + 1) * HD]
            out_ref[h * HD : h * HD + HD // 2, :] = (a * cos - b * sin).astype(BF)
            out_ref[h * HD + HD // 2 : (h + 1) * HD, :] = (b * cos + a * sin).astype(BF)

    @pl.when(step >= 4)
    def _():
        out_ref[...] = proj.astype(BF)


def project(own, rem, vec, cos_t, sin_t, w_qkv_t):
    half, width = own.shape
    tokens = 2 * half
    blk = width // 2
    return pl.pallas_call(
        project_kernel,
        grid=(6,),
        in_specs=[
            whole(own.shape),
            whole(rem.shape),
            whole(vec.shape),
            whole(cos_t.shape),
            whole(sin_t.shape),
            pl.BlockSpec((blk, width), lambda i: (i, 0)),
        ],
        out_specs=[
            whole((width, tokens)),
            pl.BlockSpec((blk, tokens), lambda i: (i, 0)),
        ],
        out_shape=[
            jax.ShapeDtypeStruct((width, tokens), BF),
            jax.ShapeDtypeStruct((3 * width, tokens), BF),
        ],
        compiler_params=params(),
        cost_estimate=pl.CostEstimate(
            flops=6 * tokens * width * width, bytes_accessed=14 << 20, transcendentals=0
        ),
        name="project",
    )(own, rem, vec, cos_t, sin_t, w_qkv_t)


def attend_kernel(
    q_ref, k_ref, v_ref, cot_ref, att_ref, e_ref, linv_ref, cot_rem, q_mask, v_ext, send, recv
):
    step = pl.program_id(0)
    cot_send = cot_ref.at[1 - lax.axis_index("seq")]

    @pl.when(step == 0)
    def _():
        swap_start(cot_send, cot_rem, send, recv)

    tokens = q_ref.shape[1]
    tile = 256
    zero = jnp.zeros((HD, tokens), BF)
    k_nat = k_ref[...].T
    q_mask[0, 0:HD, :] = q_ref[0:HD, :]
    q_mask[0, HD:, :] = zero
    q_mask[1, 0:HD, :] = zero
    q_mask[1, HD:, :] = q_ref[HD:, :]
    for h in range(2):
        v_ext[h, 0:HD, :] = v_ref[h * HD : (h + 1) * HD, :]
        v_ext[h, HD:, :] = jnp.ones((16, tokens), BF)
    def score(h, cols):
        return mm(k_nat, q_mask[h, :, cols])

    def soften(h, cols, s):
        e_ref[h, :, cols] = jnp.exp(s - jnp.max(s, axis=0, keepdims=True)).astype(BF)

    def mix(h, cols):
        mixed = mm(v_ext[h], e_ref[h, :, cols])
        linv = 1.0 / mixed[HD : HD + 1, :]
        linv_ref[0, h : h + 1, cols] = linv
        att_ref[h * HD : (h + 1) * HD, cols] = (mixed[0:HD, :] * linv).astype(BF)

    units = [(h, slice(t, t + tile)) for t in range(0, tokens, tile) for h in range(2)]
    coming = score(*units[0])
    for i, unit in enumerate(units):
        here = coming
        if i + 1 < len(units):
            coming = score(*units[i + 1])
        soften(*unit, here)
        if i > 0:
            mix(*units[i - 1])
    mix(*units[-1])

    @pl.when(step == pl.num_programs(0) - 1)
    def _():
        swap_wait(cot_send, cot_rem, send, recv)


def attend(qkv_t, cotangent):
    tokens = qkv_t.shape[1]
    width = HEADS * HD

    def part(k):
        return pl.BlockSpec((2 * HD, tokens), lambda i: (i + k * PAIRS, 0))

    return pl.pallas_call(
        attend_kernel,
        grid=(PAIRS,),
        in_specs=[part(0), part(1), part(2), ANY],
        out_specs=[
            part(0),
            pl.BlockSpec((2, tokens, tokens), lambda i: (i, 0, 0)),
            pl.BlockSpec((1, 8, tokens), lambda i: (i, 0, 0)),
            ANY,
        ],
        out_shape=[
            jax.ShapeDtypeStruct((width, tokens), BF),
            jax.ShapeDtypeStruct((HEADS, tokens, tokens), BF),
            jax.ShapeDtypeStruct((PAIRS, 8, tokens), F32),
            jax.ShapeDtypeStruct(cotangent.shape[1:], BF),
        ],
        scratch_shapes=[
            pltpu.VMEM((2, 2 * HD, tokens), BF),
            pltpu.VMEM((2, HD + 16, tokens), BF),
        ]
        + SEMS,
        compiler_params=params(collective_id=1),
        cost_estimate=pl.CostEstimate(
            flops=16 * tokens * tokens * width,
            bytes_accessed=30 << 20,
            transcendentals=HEADS * tokens * tokens,
        ),
        name="attend",
    )(qkv_t, qkv_t, qkv_t, cotangent)


def gelu_both(u):
    c = math.sqrt(2.0 / math.pi)
    u2 = u * u
    th = jnp.tanh(u * (c + (c * 0.044715) * u2))
    half = 0.5 * (1.0 + th)
    value = u * half
    slope = half + (0.5 * u) * (1.0 - th * th) * (c + (3.0 * c * 0.044715) * u2)
    return value, slope


def middle_kernel(
    att_ref,
    tok_own,
    tok_rem,
    cot_own,
    cot_rem,
    span_ref,
    vec_ref,
    b_up_ref,
    w_out_ref,
    w_up_ref,
    w_down_ref,
    out_own,
    out_rem,
    dx_ref,
    d_att_ref,
    g_out_ref,
    g_up_ref,
    g_down_ref,
    g_bup_ref,
    sums_ref,
    branch,
    x_one,
    act_two,
    d_down,
    down_acc,
    d_act,
    d_branch,
):
    step = pl.program_id(0)
    steps = pl.num_programs(0)
    tokens = att_ref.shape[1]
    half = tokens // 2
    tile = 256
    per_half = half // tile
    gate_one = vec_ref[0:1, :]
    mult_two = vec_ref[1:2, :]
    shift_two = vec_ref[2:3, :]
    gate_two = vec_ref[3:4, :]
    b_down = vec_ref[4:5, :]
    gain_two = vec_ref[5:6, :]
    scale_two = vec_ref[6:7, :]

    @pl.when(step == 0)
    def _():
        for part, (tok, cot) in enumerate(((tok_own, cot_own), (tok_rem, cot_rem))):
            for t in range(per_half):
                src = slice(t * tile, (t + 1) * tile)
                dst = slice(part * half + t * tile, part * half + (t + 1) * tile)
                br = mm(att_ref[:, dst], w_out_ref[...], TN)
                branch[dst, :] = br
                x = tok[src, :].astype(F32) + gate_one * br
                x_one[dst, :] = x
                n, _ = norm_parts(x)
                act_two[dst, :] = (n * mult_two + shift_two).astype(BF)
                grad_out = cot[src, :].astype(F32) * span_ref[dst, :]
                d_down[dst, :] = (gate_two * grad_out).astype(BF)

    up = mm(act_two[...], w_up_ref[...]) + b_up_ref[...]
    value, slope = gelu_both(up)
    hidden = value.astype(BF)
    d_hidden = mm(d_down[...], w_down_ref[...], NT)
    d_up_full = slope * d_hidden
    d_up = d_up_full.astype(BF)
    g_bup_ref[...] = col_sum(d_up.astype(F32))
    down_part = mm(hidden, w_down_ref[...])
    d_act_part = mm(d_up, w_up_ref[...], NT)
    g_down_ref[...] = mm(hidden, d_down[...], TN).astype(BF)
    g_up_ref[...] = mm(act_two[...], d_up, TN).astype(BF)

    @pl.when(step == 0)
    def _():
        down_acc[...] = down_part
        d_act[...] = d_act_part

    @pl.when(step > 0)
    def _():
        down_acc[...] += down_part
        d_act[...] += d_act_part

    @pl.when(step == steps - 1)
    def _():
        zero = jnp.zeros((1, gate_one.shape[1]), F32)
        s_gate_two, s_shift, s_pull, s_gate_one, s_bdown = zero, zero, zero, zero, zero
        for part, (cot, out) in enumerate(((cot_own, out_own), (cot_rem, out_rem))):
            for t in range(per_half):
                src = slice(t * tile, (t + 1) * tile)
                dst = slice(part * half + t * tile, part * half + (t + 1) * tile)
                x = x_one[dst, :]
                down = down_acc[dst, :] + b_down
                out[src, :] = (x + gate_two * down).astype(BF)
                grad_out = cot[src, :].astype(F32) * span_ref[dst, :]
                s_gate_two += col_sum(grad_out * down)
                s_bdown += col_sum(d_down[dst, :].astype(F32))
                n, rstd = norm_parts(x)
                da = d_act[dst, :]
                s_shift += col_sum(da)
                s_pull += col_sum(da * n)
                dx = grad_out + norm_pull(n, rstd, da * mult_two)
                dx_ref[dst, :] = dx
                s_gate_one += col_sum(dx * branch[dst, :])
                d_branch[dst, :] = (gate_one * dx).astype(BF)
        sums_ref[0:1, :] = s_gate_one
        sums_ref[1:2, :] = s_shift
        sums_ref[2:3, :] = s_pull * gain_two
        sums_ref[3:4, :] = s_gate_two
        sums_ref[4:5, :] = s_pull * (1.0 + scale_two)
        sums_ref[5:6, :] = s_bdown
        sums_ref[6:8, :] = jnp.zeros((2, gate_one.shape[1]), F32)
        g_out_ref[...] = mm(att_ref[...], d_branch[...]).astype(BF)
        d_att_ref[...] = mm(w_out_ref[...], d_branch[...], NT).astype(BF)


def middle(att_t, tok_own, tok_rem, cot_own, cot_rem, span, vec, b_up, w_out, w_up, w_down):
    width, tokens = att_t.shape
    half = tokens // 2
    ff = w_up.shape[1]
    tile = 512
    return pl.pallas_call(
        middle_kernel,
        grid=(ff // tile,),
        in_specs=[
            whole(att_t.shape),
            whole(tok_own.shape),
            whole(tok_rem.shape),
            whole(cot_own.shape),
            whole(cot_rem.shape),
            whole(span.shape),
            whole(vec.shape),
            pl.BlockSpec((1, tile), lambda i: (0, i)),
            whole(w_out.shape),
            pl.BlockSpec((width, tile), lambda i: (0, i)),
            pl.BlockSpec((tile, width), lambda i: (i, 0)),
        ],
        out_specs=[
            whole((half, width)),
            whole((half, width)),
            whole((tokens, width)),
            whole((width, tokens)),
            whole((width, width)),
            pl.BlockSpec((width, tile), lambda i: (0, i)),
            pl.BlockSpec((tile, width), lambda i: (i, 0)),
            pl.BlockSpec((1, tile), lambda i: (0, i)),
            whole((8, width)),
        ],
        out_shape=[
            jax.ShapeDtypeStruct((half, width), BF),
            jax.ShapeDtypeStruct((half, width), BF),
            jax.ShapeDtypeStruct((tokens, width), F32),
            jax.ShapeDtypeStruct((width, tokens), BF),
            jax.ShapeDtypeStruct((width, width), BF),
            jax.ShapeDtypeStruct((width, ff), BF),
            jax.ShapeDtypeStruct((ff, width), BF),
            jax.ShapeDtypeStruct((1, ff), F32),
            jax.ShapeDtypeStruct((8, width), F32),
        ],
        scratch_shapes=[
            pltpu.VMEM((tokens, width), F32),
            pltpu.VMEM((tokens, width), F32),
            pltpu.VMEM((tokens, width), BF),
            pltpu.VMEM((tokens, width), BF),
            pltpu.VMEM((tokens, width), F32),
            pltpu.VMEM((tokens, width), F32),
            pltpu.VMEM((tokens, width), BF),
        ],
        compiler_params=params(),
        cost_estimate=pl.CostEstimate(
            flops=12 * tokens * width * ff + 6 * tokens * width * width,
            bytes_accessed=40 << 20,
            transcendentals=tokens * ff,
        ),
        name="middle",
    )(att_t, tok_own, tok_rem, cot_own, cot_rem, span, vec, b_up, w_out, w_up, w_down)


def middle_links_kernel(
    zs,
    att_ref,
    tok_own,
    tok_rem,
    cot_own,
    cot_rem,
    span_ref,
    vec_ref,
    b_up_ref,
    w_out_ref,
    w_up_ref,
    w_down_ref,
    out_own,
    out_rem,
    dx_ref,
    d_att_ref,
    g_out_ref,
    g_up_ref,
    g_down_ref,
    up_last_ref,
    up_one_ref,
    up_two_ref,
    down_last_ref,
    down_one_ref,
    down_two_ref,
    mod_ref,
    sum_ref,
    branch,
    x_one,
    act_two,
    d_down,
    down_acc,
    d_act,
    d_branch,
    hidden,
    d_up,
    up_core,
    up_side,
    up_y,
    up_z,
    down_core,
    down_y,
    down_side,
    down_z,
    sems,
):
    step = pl.program_id(0)
    steps = zs
    tokens = att_ref.shape[1]
    width = att_ref.shape[0]
    half = tokens // 2
    cut = width // 2
    tile = 256
    per_half = half // tile
    gate_one = vec_ref[0:1, :]
    mult_two = vec_ref[1:2, :]
    shift_two = vec_ref[2:3, :]
    gate_two = vec_ref[3:4, :]
    b_down = vec_ref[4:5, :]
    gain_two = vec_ref[5:6, :]
    scale_two = vec_ref[6:7, :]

    links = Links(sems, zs)
    x, y, z, c = links.x, links.y, links.z, links.c
    tiles = range(steps - 1)

    def swaps(src, dst, device):
        return [links.swap(lambda j=j: src(j), lambda j=j: dst.at[j], device) for j in tiles]

    up_to_core = swaps(lambda j: g_up_ref.at[:, :, :, 1 - c], up_core, links.core)
    down_to_core = swaps(lambda j: g_down_ref.at[:, 1 - c], down_core, links.core)
    up_to_side = swaps(lambda j: up_core.at[j, 1 - x], up_side, links.facing)
    down_to_y = swaps(lambda j: down_core.at[j, 1 - y], down_y, links.across)
    up_to_y = swaps(lambda j: up_core.at[j, x, :, 1 - y], up_y, links.across)
    down_to_side = swaps(lambda j: down_core.at[j, y, 1 - x], down_side, links.facing)
    down_far = links.gather(lambda: down_core.at[0, y, x], lambda slot: down_z.at[slot], 0)
    up_far = links.spread(lambda f: up_core.at[0, x, f, y], lambda slot: up_z.at[slot])

    def core_stage(j):
        up_to_core[j]().start()
        down_to_core[j]().start()

    def first_stage(j):
        up_to_core[j]().wait()
        for h, a, b in grid_of(2, zs, 2):
            up_core[j, h, a, b] = up_core[j, h, a, b] + g_up_ref[h, a, b, c]
        up_to_side[j]().start()
        down_to_core[j]().wait()
        for b, h in grid_of(2, 2):
            down_core[j, b, h] = down_core[j, b, h] + g_down_ref[b, c, h]
        down_to_y[j]().start()

    def first_done(j):
        up_to_side[j]().wait()
        for a, b in grid_of(zs, 2):
            up_core[j, x, a, b] = up_core[j, x, a, b] + up_side[j, a, b]
        down_to_y[j]().wait()
        for h in range(2):
            down_core[j, y, h] = down_core[j, y, h] + down_y[j, h]

    def second_stage(j):
        first_done(j)
        up_to_y[j]().start()
        down_to_side[j]().start()

    def second_done(j):
        up_to_y[j]().wait()
        for a in range(zs):
            up_core[j, x, a, y] = up_core[j, x, a, y] + up_y[j, a]
        down_to_side[j]().wait()
        down_core[j, y, x] = down_core[j, y, x] + down_side[j]

    def third_stage():
        second_done(0)
        up_far[0]()
        down_far[0]()

    @pl.when(step == 0)
    def _():
        greet(links.core, links.across, links.facing, *[links.at_z(f) for f in links.far])
        for part, (tok, cot) in enumerate(((tok_own, cot_own), (tok_rem, cot_rem))):
            for t in range(per_half):
                src = slice(t * tile, (t + 1) * tile)
                dst = slice(part * half + t * tile, part * half + (t + 1) * tile)
                br = mm(att_ref[:, dst], w_out_ref[...], TN)
                branch[dst, :] = br
                xv = tok[src, :].astype(F32) + gate_one * br
                x_one[dst, :] = xv
                n, _ = norm_parts(xv)
                act_two[dst, :] = (n * mult_two + shift_two).astype(BF)
                grad_out = cot[src, :].astype(F32) * span_ref[dst, :]
                d_down[dst, :] = (gate_two * grad_out).astype(BF)
                down_acc[dst, :] = jnp.zeros((tile, width), F32)
                d_act[dst, :] = jnp.zeros((tile, width), F32)

    chunk = tokens // 4

    def one(k, bup):
        rows = rows_of(chunk, k)
        up = mm(act_two[rows, :], w_up_ref[...]) + b_up_ref[...]
        d_hidden = mm(d_down[rows, :], w_down_ref[...], NT)
        value, slope = gelu_both(up)
        low = value.astype(BF)
        hidden[rows, :] = low
        d_up_low = (slope * d_hidden).astype(BF)
        d_up[rows, :] = d_up_low
        down_acc[rows, :] += mm(low, w_down_ref[...])
        d_act[rows, :] += mm(d_up_low, w_up_ref[...], NT)
        return bup + col_sum(d_up_low.astype(F32))

    bup = lax.fori_loop(0, 4, one, jnp.zeros((1, w_up_ref.shape[1]), F32))
    for j in range(steps):
        pl.when(step == j)(lambda j=j: put_rows(sum_ref, 2 * width // 128 + j * bup.shape[1] // 128, bup))

    @pl.when(step == 1)
    def _():
        first_stage(0)

    @pl.when(step == 2)
    def _():
        second_stage(0)
        first_stage(1)

    @pl.when(step == 3)
    def _():
        second_stage(1)
        first_stage(2)

    chunk_out = width // 3
    g_down_flat = g_down_ref.reshape(width, width)
    g_up_flat = g_up_ref.reshape(2, width, cut)

    def grads(k, carry):
        outs = rows_of(chunk_out, k)
        g_down_flat[outs, :] = mm(hidden[:, outs], d_down[...], TN).astype(BF)
        g_up = mm(act_two[:, outs], d_up[...], TN).astype(BF)
        for h in range(2):
            g_up_flat[h, outs, :] = g_up[:, h * cut : (h + 1) * cut]
        return carry

    lax.fori_loop(0, 3, grads, 0)

    @pl.when(step == 0)
    def _():
        core_stage(0)

    @pl.when(step == 1)
    def _():
        core_stage(1)

    @pl.when(step == 2)
    def _():
        third_stage()
        core_stage(2)

    @pl.when(step == steps - 1)
    def _():
        zero = jnp.zeros((1, width), F32)
        s_gate_two, s_shift, s_pull, s_gate_one, s_bdown = zero, zero, zero, zero, zero
        for part, (cot, out) in enumerate(((cot_own, out_own), (cot_rem, out_rem))):
            for t in range(per_half):
                src = slice(t * tile, (t + 1) * tile)
                dst = slice(part * half + t * tile, part * half + (t + 1) * tile)
                xv = x_one[dst, :]
                down = down_acc[dst, :] + b_down
                out[src, :] = (xv + gate_two * down).astype(BF)
                grad_out = cot[src, :].astype(F32) * span_ref[dst, :]
                s_gate_two += col_sum(grad_out * down)
                s_bdown += col_sum(d_down[dst, :].astype(F32))
                n, rstd = norm_parts(xv)
                da = d_act[dst, :]
                s_shift += col_sum(da)
                s_pull += col_sum(da * n)
                dx = grad_out + norm_pull(n, rstd, da * mult_two)
                dx_ref[dst, :] = dx
                s_gate_one += col_sum(dx * branch[dst, :])
                d_branch[dst, :] = (gate_one * dx).astype(BF)
        lines = width // 128
        mod_ref[4 * lines :, :] = jnp.zeros((mod_ref.shape[0] - 4 * lines, 128), BF)
        for k, row in enumerate((s_gate_one, s_shift, s_pull * gain_two, s_gate_two)):
            put_rows(mod_ref, k * lines, row)
        put_rows(mod_ref, 4 * lines, vec_ref[7:8, 0:128])
        put_rows(sum_ref, 0, s_pull * (1.0 + scale_two))
        put_rows(sum_ref, lines, s_bdown)
        g_out = mm(att_ref[...], d_branch[...]).astype(BF)
        for h in range(2):
            g_out_ref[h] = g_out[:, h * cut : (h + 1) * cut].reshape(g_out_ref.shape[1:])
        d_att_ref[...] = mm(w_out_ref[...], d_branch[...], NT).astype(BF)
        up_far[1]()
        total = up_core[0, x, z, y].astype(F32)
        for f in links.far:
            total += up_z[f].astype(F32)
        up_last_ref[...] = total.astype(BF)
        down_far[1]()
        total = down_core[0, y, x].astype(F32)
        for f in links.far:
            total += down_z[f].astype(F32)
        down_last_ref[...] = total.astype(BF)
        second_done(1)
        for a in range(zs):
            up_one_ref[a] = up_core[1, x, a, y]
        down_one_ref[...] = down_core[1, y, x]
        first_done(2)
        up_two_ref[...] = up_core[2, x]
        down_two_ref[...] = down_core[2, y]


def middle_links(
    att_t, tok_own, tok_rem, cot_own, cot_rem, span, vec, b_up, w_out, w_up, w_down, zs
):
    width, tokens = att_t.shape
    half = tokens // 2
    cut = width // 2
    ff = w_up.shape[1]
    tile = ff // zs
    rows = width // (4 * zs)
    down_rows = tile // 4
    halves = (2, zs, 2, 2, rows, cut)
    down_half = (down_rows // 2, width)
    owned = (2, 2, 2) + down_half
    outs = [
        ((half, width), BF),
        ((half, width), BF),
        ((tokens, width), F32),
        ((width, tokens), BF),
        (halves, BF),
        (halves, BF),
        (owned, BF),
        ((rows, cut), BF),
        ((zs, rows, cut), BF),
        ((zs, 2, rows, cut), BF),
        (down_half, BF),
        (down_half, BF),
        ((2,) + down_half, BF),
        ((early_mod_rows(width), 128), BF),
        ((early_sum_rows(width, ff), 128), F32),
    ]
    return pl.pallas_call(
        functools.partial(middle_links_kernel, zs),
        grid=(zs,),
        in_specs=[
            once(att_t.shape),
            once(tok_own.shape),
            once(tok_rem.shape),
            once(cot_own.shape),
            once(cot_rem.shape),
            once(span.shape),
            once(vec.shape),
            pl.BlockSpec((1, tile), lambda i: (0, i)),
            once(w_out.shape),
            pl.BlockSpec((width, tile), lambda i: (0, i)),
            pl.BlockSpec((tile, width), lambda i: (i, 0)),
        ],
        out_specs=[once(shape) for shape, _ in outs],
        out_shape=[jax.ShapeDtypeStruct(*o) for o in outs],
        scratch_shapes=[
            pltpu.VMEM((tokens, width), F32),
            pltpu.VMEM((tokens, width), F32),
            pltpu.VMEM((tokens, width), BF),
            pltpu.VMEM((tokens, width), BF),
            pltpu.VMEM((tokens, width), F32),
            pltpu.VMEM((tokens, width), F32),
            pltpu.VMEM((tokens, width), BF),
            pltpu.VMEM((tokens, tile), BF),
            pltpu.VMEM((tokens, tile), BF),
            pltpu.VMEM((zs - 1, 2, zs, 2, rows, cut), BF),
            pltpu.VMEM((zs - 1, zs, 2, rows, cut), BF),
            pltpu.VMEM((zs - 1, zs, rows, cut), BF),
            pltpu.VMEM((zs, rows, cut), BF),
            pltpu.VMEM((zs - 1, 2, 2) + down_half, BF),
            pltpu.VMEM((zs - 1, 2) + down_half, BF),
            pltpu.VMEM((zs - 1,) + down_half, BF),
            pltpu.VMEM((zs,) + down_half, BF),
            pltpu.SemaphoreType.DMA((12 * (zs - 1) + 1 + 3 * zs,)),
        ],
        compiler_params=params(62, collective_id=4),
        cost_estimate=pl.CostEstimate(
            flops=12 * tokens * width * ff + 6 * tokens * width * width,
            bytes_accessed=40 << 20,
            transcendentals=tokens * ff,
        ),
        name="middle_links",
    )(att_t, tok_own, tok_rem, cot_own, cot_rem, span, vec, b_up, w_out, w_up, w_down)


def attend_back_kernel(
    q_ref,
    k_ref,
    v_ref,
    att_ref,
    d_att_ref,
    e_ref,
    linv_ref,
    cos_ref,
    sin_ref,
    give_ref,
    out_ref,
    take_ref,
    do_mask,
    send,
    recv,
):
    step = pl.program_id(0)

    @pl.when(step == 0)
    def _():
        swap_start(give_ref, take_ref, send, recv)

    tokens = q_ref.shape[1]
    tile = 256
    zero = jnp.zeros((HD, tokens), BF)
    v_nat = v_ref[...].T
    cos = cos_ref[...]
    sin = sin_ref[...]

    def unrotate(x):
        low = x.astype(BF).astype(F32)
        a, b = low[0 : HD // 2], low[HD // 2 :]
        return a * cos + b * sin, b * cos - a * sin

    for h in range(2):
        rows = slice(h * HD, (h + 1) * HD)
        linv = linv_ref[0, h : h + 1, :]
        d_o = d_att_ref[rows, :].astype(F32)
        d_os = (d_o * linv).astype(BF)
        do_mask[h, rows, :] = d_os
        do_mask[h, (1 - h) * HD : (2 - h) * HD, :] = zero
        inner = col_sum(d_o * att_ref[rows, :].astype(F32)) * linv
        d_values = mm(d_os, e_ref[h], NT)
        out_ref[2, rows, :] = d_values.astype(BF)
        d_keys = jnp.zeros((HD, tokens), F32)
        d_queries = []
        for t in range(tokens // tile):
            cols = slice(t * tile, (t + 1) * tile)
            d_probs = mm(v_nat, do_mask[h, :, cols])
            d_s = (e_ref[h, :, cols].astype(F32) * (d_probs - inner[:, cols])).astype(BF)
            d_queries.append(mm(k_ref[rows, :], d_s))
            d_keys += mm(q_ref[rows, cols], d_s, NT)
        dq = jnp.concatenate(d_queries, axis=1) * HD**-0.5
        lead, trail = unrotate(dq)
        out_ref[0, h * HD : h * HD + HD // 2, :] = lead.astype(BF)
        out_ref[0, h * HD + HD // 2 : (h + 1) * HD, :] = trail.astype(BF)
        lead, trail = unrotate(d_keys)
        out_ref[1, h * HD : h * HD + HD // 2, :] = lead.astype(BF)
        out_ref[1, h * HD + HD // 2 : (h + 1) * HD, :] = trail.astype(BF)

    @pl.when(step == pl.num_programs(0) - 1)
    def _():
        swap_wait(give_ref, take_ref, send, recv)


def attend_back(qkv_t, att_t, d_att_t, e, linv, cos_t, sin_t, give):
    tokens = qkv_t.shape[1]
    width = HEADS * HD

    def part(k):
        return pl.BlockSpec((2 * HD, tokens), lambda i: (i + k * PAIRS, 0))

    return pl.pallas_call(
        attend_back_kernel,
        grid=(PAIRS,),
        in_specs=[
            part(0),
            part(1),
            part(2),
            part(0),
            part(0),
            pl.BlockSpec((2, tokens, tokens), lambda i: (i, 0, 0)),
            pl.BlockSpec((1, 8, tokens), lambda i: (i, 0, 0)),
            whole(cos_t.shape),
            whole(sin_t.shape),
            ANY,
        ],
        out_specs=[pl.BlockSpec((3, 2 * HD, tokens), lambda i: (0, i, 0)), ANY],
        out_shape=[
            jax.ShapeDtypeStruct((3, width, tokens), BF),
            jax.ShapeDtypeStruct(give.shape, give.dtype),
        ],
        scratch_shapes=[pltpu.VMEM((2, 2 * HD, tokens), BF)] + SEMS,
        compiler_params=params(collective_id=2),
        cost_estimate=pl.CostEstimate(
            flops=32 * tokens * tokens * width, bytes_accessed=36 << 20, transcendentals=0
        ),
        name="attend_back",
    )(qkv_t, qkv_t, qkv_t, att_t, d_att_t, e, linv, cos_t, sin_t, give)


def tail_kernel(tok_own, tok_rem, d_proj_ref, w_ref, dx_ref, vec_ref, own_ref, rem_ref, sums_ref):
    step = pl.program_id(0)
    steps = pl.num_programs(0)
    mult_one = vec_ref[0:1, :]
    gain_one = vec_ref[2:3, :]
    scale_one = vec_ref[3:4, :]
    d_act = mm(d_proj_ref[...], w_ref[...], TN)

    def finish(tok, out):
        n, rstd = norm_parts(tok[...].astype(F32))
        grad = dx_ref[...] + norm_pull(n, rstd, d_act * mult_one)
        out[...] = grad.astype(out.dtype)
        return col_sum(d_act), col_sum(d_act * n)

    @pl.when(step == 0)
    def _():
        shift, pull = finish(tok_rem, rem_ref)
        sums_ref[0:1, :] = shift
        sums_ref[1:2, :] = pull
        sums_ref[2:, :] = jnp.zeros((6, shift.shape[1]), F32)

    @pl.when(step == steps - 1)
    def _():
        shift, pull = finish(tok_own, own_ref)
        shift = sums_ref[0:1, :] + shift
        pull = sums_ref[1:2, :] + pull
        sums_ref[0:1, :] = shift
        sums_ref[1:2, :] = pull * gain_one
        sums_ref[2:3, :] = pull * (1.0 + scale_one)


def tail(tok_own, tok_rem, d_proj_t, w_qkv_t, dx, vec):
    half, width = tok_own.shape
    return pl.pallas_call(
        tail_kernel,
        grid=(2,),
        in_specs=[
            whole(tok_own.shape),
            whole(tok_rem.shape),
            pl.BlockSpec((3 * width, half), lambda i: (0, 1 - i)),
            whole(w_qkv_t.shape),
            pl.BlockSpec((half, width), lambda i: (1 - i, 0)),
            whole(vec.shape),
        ],
        out_specs=[whole((half, width)), whole((half, width)), whole((8, width))],
        out_shape=[
            jax.ShapeDtypeStruct((half, width), F32),
            jax.ShapeDtypeStruct((half, width), BF),
            jax.ShapeDtypeStruct((8, width), F32),
        ],
        compiler_params=params(),
        cost_estimate=pl.CostEstimate(
            flops=12 * half * width * width, bytes_accessed=20 << 20, transcendentals=0
        ),
        name="tail",
    )(tok_own, tok_rem, d_proj_t, w_qkv_t, dx, vec)


def weight_grad_kernel(act_ref, d_proj_ref, out_ref):
    out_ref[...] = mm(act_ref[...], d_proj_ref[...], NT).astype(BF)


def weight_grad(act_t, d_proj_t):
    width, tokens = act_t.shape
    cols = d_proj_t.shape[0]
    tile = 768
    return pl.pallas_call(
        weight_grad_kernel,
        grid=(cols // tile,),
        in_specs=[whole(act_t.shape), pl.BlockSpec((tile, tokens), lambda i: (i, 0))],
        out_specs=pl.BlockSpec((width, tile), lambda i: (0, i)),
        out_shape=jax.ShapeDtypeStruct((width, cols), BF),
        compiler_params=params(),
        cost_estimate=pl.CostEstimate(
            flops=2 * cols * width * tokens, bytes_accessed=12 << 20, transcendentals=0
        ),
        name="weight_grad",
    )(act_t, d_proj_t)


def gather_stages(links, ref):
    z, y, c, x = links.z, links.y, links.c, links.x

    def pair(mine, theirs, device):
        sem = links.take(2)

        def make(slot):
            return remote(slot(), slot(), links.sems.at[sem], links.sems.at[sem + 1], device)

        def wait():
            make(mine).wait_send()
            make(theirs).wait_recv()

        return (lambda: make(mine).start()), wait

    sem = links.take(2 * links.zs)

    def make(f, slot):
        block = ref.at[slot, :, :, x]
        return remote(
            block, block, links.sems.at[sem + f], links.sems.at[sem + links.zs + slot], links.at_z(f)
        )

    def far_start():
        for f in links.far:
            make(f, z).start()

    def far_wait():
        for f in links.far:
            make(f, z).wait_send()
            make(f, f).wait_recv()

    return [
        pair(lambda: ref.at[z, y, c, x], lambda: ref.at[z, y, 1 - c, x], links.core),
        pair(lambda: ref.at[z, y, :, x], lambda: ref.at[z, 1 - y, :, x], links.across),
        (far_start, far_wait),
        pair(lambda: ref.at[:, :, :, x], lambda: ref.at[:, :, :, 1 - x], links.facing),
    ]


def sum_stages(links, ref, take, far):
    swaps = [
        links.swap(lambda: ref, lambda k=k: take.at[k], device)
        for k, device in enumerate((links.core, links.across, links.facing))
    ]
    far_start, far_wait = links.spread(lambda f: ref, lambda slot: far.at[slot])

    def finish(k):
        swaps[k]().wait()
        ref[...] += take[k]

    def far_finish():
        far_wait()
        far[links.z] = ref[...]
        total = far[0]
        for f in range(1, links.zs):
            total += far[f]
        ref[...] = total

    return [
        (lambda: swaps[0]().start(), lambda: finish(0)),
        (lambda: swaps[1]().start(), lambda: finish(1)),
        (far_start, far_finish),
        (lambda: swaps[2]().start(), lambda: finish(2)),
    ]


def back_kernel(zs, split, ins, outs, scratch):
    (
        q_ref,
        k_ref,
        v_ref,
        att_ref,
        d_att_ref,
        e_ref,
        linv_ref,
        cos_ref,
        sin_ref,
        own_ref,
        give_ref,
        up_last_ref,
        up_one_ref,
        up_two_ref,
        down_last_ref,
        down_one_ref,
        down_two_ref,
        raw_up,
        raw_out,
        raw_down,
        mod_ref,
        sum_ref,
        act_in,
        w_in,
        tok_own_in,
        tok_rem_in,
        dx_in,
        vec_ref,
    ) = ins
    result, grad_ref, s_qkv, s_out, s_up, s_down, *small_outs = outs
    (
        do_mask,
        d_proj,
        sems,
        u_own,
        u_y,
        u_z,
        u_last,
        u_facing,
        w_own,
        w_core,
        w_y,
        w_z,
        w_last,
        w_facing,
        d_own,
        d_core,
        d_y,
        d_side,
        d_sum,
        d_z,
        d_last,
        d_facing,
        q_raws,
        q_cores,
        q_ys,
        q_zs,
        q_lasts,
        q_facings,
        g_send,
        g_take,
        early_take,
        early_far,
        late_take,
        late_far,
        mod_early,
        mod_late,
        sum_early,
        sum_late,
        act_ref,
        w_ref,
        tok_own,
        tok_rem,
        dx_ref,
        g_own,
    ) = scratch
    step = pl.program_id(0)
    tokens = q_ref.shape[1]
    width = act_ref.shape[0]
    half = tokens // 2
    cut = width // 2
    links = Links(sems, zs)
    x, y, z, c = links.x, links.y, links.z, links.c

    fetch = [
        links.local(lambda p=p: p[0], lambda p=p: p[1])
        for p in (
            (act_in, act_ref),
            (w_in, w_ref),
            (tok_own_in, tok_own),
            (tok_rem_in, tok_rem),
            (dx_in, dx_ref),
        )
    ]
    u_load = [
        links.local(lambda: up_last_ref, lambda: u_last.at[0]),
        links.local(lambda: up_one_ref.at[z], lambda: u_own.at[0, z]),
        links.local(lambda: up_two_ref.at[:, y], lambda: u_own.at[1]),
    ]
    u_to_y = links.swap(lambda: up_two_ref.at[:, 1 - y], lambda: u_y, links.across)
    u_far = [
        links.spread(
            lambda f, j=j: up_one_ref.at[f] if j == 0 else u_own.at[1, f],
            lambda slot, j=j: u_z.at[j, slot],
        )
        for j in range(2)
    ]
    u_to_facing = [
        links.swap(lambda j=j: u_last.at[j], lambda j=j: u_facing.at[j], links.facing)
        for j in range(3)
    ]
    raws = (raw_up, raw_out)
    w_keep = [
        links.local(lambda r=r: r.at[:, :, :, c], lambda k=k: w_own.at[k]) for k, r in enumerate(raws)
    ]
    w_to_core = [
        links.swap(lambda r=r: r.at[:, :, :, 1 - c], lambda k=k: w_core.at[k], links.core)
        for k, r in enumerate(raws)
    ]
    w_to_y = [
        links.swap(lambda k=k: w_own.at[k, :, :, 1 - y], lambda k=k: w_y.at[k], links.across)
        for k in range(2)
    ]
    w_far = [
        links.spread(lambda f, k=k: w_own.at[k, :, f, y], lambda slot, k=k: w_z.at[k, slot])
        for k in range(2)
    ]
    w_to_facing = [
        links.swap(lambda k=k: w_last.at[k], lambda k=k: w_facing.at[k], links.facing)
        for k in range(2)
    ]
    d_keep = links.local(lambda: raw_down.at[:, c], lambda: d_own)
    d_to_core = links.swap(lambda: raw_down.at[:, 1 - c], lambda: d_core, links.core)
    d_to_y = links.swap(lambda: d_own.at[1 - y], lambda: d_y, links.across)
    d_to_side = [
        links.swap(lambda: down_two_ref.at[1 - x], lambda: d_side.at[0], links.facing),
        links.swap(lambda: d_own.at[y, 1 - x], lambda: d_side.at[1], links.facing),
    ]
    d_load = [
        links.local(lambda: down_last_ref, lambda: d_last),
        links.local(lambda: down_one_ref, lambda: d_sum.at[0]),
        links.local(lambda: down_two_ref.at[x], lambda: d_sum.at[1]),
    ]
    d_far = [
        links.gather(
            lambda j=j: down_one_ref if j == 1 else d_sum.at[j - 1], lambda slot: d_z.at[slot], j
        )
        for j in range(1, zs)
    ]
    d_to_facing = links.swap(lambda: d_last, lambda: d_facing, links.facing)
    groups = range(len(split))
    q_to_core = [
        links.swap(lambda g=g: q_raws[g].at[:, :, 1 - c], lambda g=g: q_cores[g], links.core)
        for g in groups
    ]
    q_to_y = [
        links.swap(lambda g=g: q_cores[g].at[:, 1 - y], lambda g=g: q_ys[g], links.across)
        for g in groups
    ]
    q_far = [
        links.spread(lambda f, g=g: q_cores[g].at[f, y], lambda slot, g=g: q_zs[g].at[slot])
        for g in groups
    ]
    q_to_facing = [
        links.swap(lambda g=g: q_lasts[g], lambda g=g: q_facings[g], links.facing) for g in groups
    ]
    keep_out = links.local(lambda: own_ref, lambda: result.at[x])
    out_sem = links.take(2)

    def cross_out(slot):
        return remote(give_ref, result.at[slot], sems.at[out_sem], sems.at[out_sem + 1], links.facing)

    give_grad = links.swap(lambda: g_send, lambda: g_take, links.facing)
    keep_grad = links.local(lambda: g_own, lambda: grad_ref.at[x])
    put_grad = links.local(lambda: g_own, lambda: grad_ref.at[1 - x])
    early = [
        gather_stages(links, mod_early),
        sum_stages(links, sum_early, early_take, early_far),
    ]
    late = [gather_stages(links, mod_late), sum_stages(links, sum_late, late_take, late_far)]

    def begin(arrays, stage):
        for stages in arrays:
            stages[stage][0]()

    def end(arrays, stage):
        for stages in arrays:
            stages[stage][1]()

    def sum_far(own, taken):
        total = own.astype(F32)
        for f in links.far:
            total += taken(f).astype(F32)
        return total.astype(BF)

    def u_z_done(j):
        u_far[j][1]()
        u_last[j + 1] = sum_far(u_own[j, z], lambda f: u_z[j, f])
        u_to_facing[j + 1]().start()

    def u_done(j):
        u_to_facing[j]().wait()
        mine, other = u_last[j].astype(F32), u_facing[j].astype(F32)
        start = j * width
        s_up[:, start : start + cut] = jnp.where(x == 0, mine, other)
        s_up[:, start + cut : start + width] = jnp.where(x == 0, other, mine)

    def w_core_done(k):
        w_keep[k]().wait()
        w_to_core[k]().wait()
        for h, a, b in grid_of(2, zs, 2):
            w_own[k, h, a, b] = w_own[k, h, a, b] + w_core[k, h, a, b]

    def w_y_done(k):
        w_to_y[k]().wait()
        for h, a in grid_of(2, zs):
            w_own[k, h, a, y] = w_own[k, h, a, y] + w_y[k, h, a]
        w_far[k][0]()

    def w_z_done(k):
        w_far[k][1]()
        for h in range(2):
            w_last[k, h] = sum_far(w_own[k, h, z, y], lambda f: w_z[k, f, h])
        w_to_facing[k]().start()

    def w_done(k):
        w_to_facing[k]().wait()
        out, start = (s_up, (zs - 1) * width) if k == 0 else (s_out, 0)
        for h in range(2):
            out[:, start + h * cut : start + (h + 1) * cut] = w_last[k, h].astype(F32) + w_facing[
                k, h
            ].astype(F32)

    def q_core_done(g):
        q_to_core[g]().wait()
        for a, b in grid_of(zs, 2):
            q_cores[g][a, b] = q_cores[g][a, b] + q_raws[g][a, b, c]
        q_to_y[g]().start()

    def q_y_done(g):
        q_to_y[g]().wait()
        for a in range(zs):
            q_cores[g][a, y] = q_cores[g][a, y] + q_ys[g][a]
        q_far[g][0]()

    def q_z_done(g):
        q_far[g][1]()
        q_lasts[g][...] = sum_far(q_cores[g][z, y], lambda f: q_zs[g][f])
        q_to_facing[g]().start()

    def q_done(g):
        q_to_facing[g]().wait()
        total = q_lasts[g][...].astype(F32) + q_facings[g][...].astype(F32)
        first, size = split[g][0] * HD, (split[g][1] - split[g][0]) * HD
        for p in range(3):
            s_qkv[:, p * width + first : p * width + first + size] = total[:, p * size : (p + 1) * size]

    def weight_grad_of(g):
        first, size = split[g][0] * HD, (split[g][1] - split[g][0]) * HD
        for p in range(3):
            rows = slice(p * width + first, p * width + first + size)
            part = mm(act_ref[...], d_proj[rows, :], NT).astype(BF)
            q_raws[g][:, :, :, :, p * size : (p + 1) * size] = part.reshape(
                q_raws[g].shape[:4] + (size,)
            )
        q_to_core[g]().start()


    def due_00():
        greet(links.core, links.across, links.facing, *[links.at_z(f) for f in links.far])
        d_to_core().start()
        d_keep().start()
        for k in range(2):
            w_to_core[k]().start()
            w_keep[k]().start()
        u_far[0][0]()
        d_far[0][0]()
        u_to_y().start()
        d_to_side[0]().start()
        for load in u_load + d_load:
            load().start()
        mod_early[z, y, c, x] = mod_ref[...]
        sum_early[...] = sum_ref[...]
        begin(early, 0)
        keep_out().start()
        cross_out(x).start()
        for load in fetch:
            load().start()

    def due_01():
        d_keep().wait()
        d_to_core().wait()
        for b, h in grid_of(2, 2):
            d_own[b, h] = d_own[b, h] + d_core[b, h]
        d_to_y().start()
        end(early, 0)
        begin(early, 1)

    def due_10():
        w_core_done(0)
        w_core_done(1)
        w_to_y[0]().start()
        u_load[0]().wait()
        u_to_facing[0]().start()

    def due_11():
        u_load[2]().wait()
        u_to_y().wait()
        for a in range(zs):
            u_own[1, a] = u_own[1, a] + u_y[a]
        u_far[1][0]()
        d_load[2]().wait()
        d_to_side[0]().wait()
        d_sum[1] = d_sum[1] + d_side[0]
        d_far[1][0]()
        end(early, 1)
        begin(early, 2)

    def due_20():
        fetch[0]().wait()
        weight_grad_of(0)
        d_to_y().wait()
        for h in range(2):
            d_own[y, h] = d_own[y, h] + d_y[h]
        d_to_side[1]().start()
        w_to_y[1]().start()

    def due_21():
        q_core_done(0)
        w_y_done(0)

    def due_30():
        u_load[1]().wait()
        u_z_done(0)
        d_to_side[1]().wait()
        d_sum[2] = d_own[y, x] + d_side[1]
        d_far[2][0]()
        end(early, 2)
        begin(early, 3)

    def due_31():
        w_y_done(1)
        q_y_done(0)

    def due_40():
        weight_grad_of(1)
        u_z_done(1)
        end(early, 3)

    def due_41():
        q_core_done(1)
        w_z_done(0)
        u_done(0)
        u_done(1)

    def due_50():
        for load in d_load[0:2]:
            load().wait()
        for j in range(zs - 1):
            d_far[j][1]()

        @pl.when(z > 0)
        def _():
            d_last[...] = sum_far(d_sum[jnp.maximum(z - 1, 0)], lambda f: d_z[f])

        d_to_facing().start()

    def due_51():
        q_y_done(1)
        w_z_done(1)
        u_done(2)

    due = (
        (due_00, due_01),
        (due_10, due_11),
        (due_20, due_21),
        (due_30, due_31),
        (due_40, due_41),
        (due_50, due_51),
    )

    def do_due(h):
        for k in range(PAIRS):
            pl.when(step == k)(due[k][h])


    @pl.when(step < PAIRS)
    def _():
        tile = 256
        zero = jnp.zeros((HD, tokens), BF)
        v_nat = v_ref[...].T
        cos = cos_ref[...]
        sin = sin_ref[...]

        def put(part, h, value):
            low = value.astype(BF).astype(F32)
            a, b = low[0 : HD // 2], low[HD // 2 :]
            start = part * width + step * 2 * HD + h * HD
            d_proj[pl.ds(pl.multiple_of(start, 32), 32), :] = (a * cos + b * sin).astype(BF)
            d_proj[pl.ds(pl.multiple_of(start + 32, 32), 32), :] = (b * cos - a * sin).astype(BF)

        do_due(0)
        inners, keys, values, queries = [], [], [], [[], []]
        for h in range(2):
            rows = slice(h * HD, (h + 1) * HD)
            linv = linv_ref[0, h : h + 1, :]
            d_o = d_att_ref[rows, :].astype(F32)
            do_mask[h, rows, :] = (d_o * linv).astype(BF)
            do_mask[h, (1 - h) * HD : (2 - h) * HD, :] = zero
            inners.append(col_sum(d_o * att_ref[rows, :].astype(F32)) * linv)

        def ahead(h, cols):
            return mm(v_nat, do_mask[h, :, cols])

        def centre(h, cols, d_probs):
            rows = slice(h * HD, (h + 1) * HD)
            e = e_ref[h, :, cols]
            part = mm(do_mask[h, rows, cols], e, NT)
            if cols.start == 0:
                values.append(part)
            else:
                values[h] += part
            return (e.astype(F32) * (d_probs - inners[h][:, cols])).astype(BF)

        def behind(h, cols, d_s):
            rows = slice(h * HD, (h + 1) * HD)
            queries[h].append(mm(k_ref[rows, :], d_s))
            part = mm(q_ref[rows, cols], d_s, NT)
            if cols.start == 0:
                keys.append(part)
            else:
                keys[h] += part
            if cols.stop == tokens:
                put(0, h, jnp.concatenate(queries[h], axis=1) * HD**-0.5)
                put(1, h, keys[h])
                start = 2 * width + step * 2 * HD + h * HD
                d_proj[pl.ds(pl.multiple_of(start, HD), HD), :] = values[h].astype(BF)

        units = [(h, slice(t, t + tile)) for h in range(2) for t in range(0, tokens, tile)]
        coming = ahead(*units[0])
        for i, unit in enumerate(units):
            if i == len(units) // 2:
                do_due(1)
            here = coming
            if i + 1 < len(units):
                coming = ahead(*units[i + 1])
            d_s = centre(*unit, here)
            if i > 0:
                behind(*units[i - 1], held)
            held = d_s
        behind(*units[-1], held)


    def finish(tok, cols):
        d_act = mm(d_proj[:, cols], w_ref[...], TN)
        n, rstd = norm_parts(tok[...].astype(F32))
        grad = dx_ref[cols, :] + norm_pull(n, rstd, d_act * vec_ref[0:1, :])
        return grad, col_sum(d_act), col_sum(d_act * n)

    @pl.when(step == PAIRS)
    def _():
        for load in fetch[1:]:
            load().wait()
        grad, shift, pull = finish(tok_rem, slice(half, 2 * half))
        g_send[...] = grad.astype(BF)
        give_grad().start()
        weight_grad_of(2)
        q_z_done(0)
        q_core_done(2)
        grad, shift_own, pull_own = finish(tok_own, slice(0, half))
        g_own[...] = grad
        keep_grad().start()
        shift += shift_own
        pull += pull_own
        lines = width // 128
        mine = mod_late.at[z, y, c, x]
        mine[2 * lines :, :] = jnp.zeros((mod_late.shape[4] - 2 * lines, 128), BF)
        put_rows(mine, 0, shift)
        put_rows(mine, lines, pull * vec_ref[2:3, :])
        sum_late[lines:, :] = jnp.zeros((sum_late.shape[0] - lines, 128), F32)
        put_rows(sum_late, 0, pull * (1.0 + vec_ref[3:4, :]))
        begin(late, 0)
        q_z_done(1)
        end(late, 0)
        begin(late, 1)
        q_y_done(2)
        end(late, 1)
        begin(late, 2)
        for k in range(2):
            w_done(k)
        d_to_facing().wait()
        mine, other = d_last[...].astype(F32), d_facing[...].astype(F32)
        rows_half = mine.shape[0]
        s_down[0:rows_half, :] = jnp.where(x == 0, mine, other)
        s_down[rows_half:, :] = jnp.where(x == 0, other, mine)
        end(late, 2)
        begin(late, 3)
        keep_out().wait()
        cross_out(x).wait_send()
        cross_out(1 - x).wait_recv()
        q_done(0)
        q_done(1)
        q_z_done(2)
        end(late, 3)
        give_grad().wait()
        keep_grad().wait()
        g_own[...] = g_take[...].astype(F32)
        put_grad().start()
        q_done(2)
        put_grad().wait()
        for out, value in zip(small_outs, (mod_early, mod_late, sum_early, sum_late)):
            out[...] = value[...]


def back(ins, zs, ff):
    q, att, d_att, e, linv, cos_t, sin_t = ins[:7]
    mod, sums, vec = ins[-8], ins[-7], ins[-1]
    width, tokens = att.shape
    half = tokens // 2
    cut = width // 2
    rows = width // (4 * zs)
    down_rows = ff // (4 * zs)
    down_half = (down_rows // 2, width)
    split = ((0, 4), (4, 8), (8, HEADS))
    sizes = [3 * (b - a) * HD for a, b in split]
    last = PAIRS - 1

    def part(k):
        return pl.BlockSpec((2 * HD, tokens), lambda i: (jnp.minimum(i, last) + k * PAIRS, 0))

    def vm(*shape, kind=BF):
        return pltpu.VMEM(shape, kind)

    lines = width // 128
    mod_early = (zs, 2, 2, 2) + mod.shape
    mod_late = (zs, 2, 2, 2, round_up(2 * lines, 16), 128)
    sum_late = (round_up(lines, 8), 128)
    outs = [
        ((half, width), F32),
        ((rows, 3 * width), F32),
        ((rows, width), F32),
        ((rows, ff), F32),
        ((down_rows, width), F32),
        (mod_early, BF),
        (mod_late, BF),
        (sums.shape, F32),
        (sum_late, F32),
    ]
    outs[0] = ((2, half, width), F32)
    fetched = ins[-6:-1]
    in_specs = (
        [part(0), part(1), part(2), part(0), part(0)]
        + [
            pl.BlockSpec((2, tokens, tokens), lambda i: (jnp.minimum(i, last), 0, 0)),
            pl.BlockSpec((1, 8, tokens), lambda i: (jnp.minimum(i, last), 0, 0)),
            once(cos_t.shape),
            once(sin_t.shape),
        ]
        + [ANY] * (len(ins) - 15)
        + [once(mod.shape), once(sums.shape)]
        + [ANY] * 5
        + [once(vec.shape)]
    )
    out_specs = [ANY, ANY] + [once(shape) for shape, _ in outs[1:]]
    out_shape = [jax.ShapeDtypeStruct((2, half, width), BF)] + [
        jax.ShapeDtypeStruct(*o) for o in outs
    ]
    scratch = [
        vm(2, 2 * HD, tokens),
        vm(3 * width, tokens),
        pltpu.SemaphoreType.DMA((250,)),
        vm(2, zs, rows, cut),
        vm(zs, rows, cut),
        vm(2, zs, rows, cut),
        vm(3, rows, cut),
        vm(3, rows, cut),
        vm(2, 2, zs, 2, rows, cut),
        vm(2, 2, zs, 2, rows, cut),
        vm(2, 2, zs, rows, cut),
        vm(2, zs, 2, rows, cut),
        vm(2, 2, rows, cut),
        vm(2, 2, rows, cut),
        vm(2, 2, *down_half),
        vm(2, 2, *down_half),
        vm(2, *down_half),
        vm(2, *down_half),
        vm(zs - 1, *down_half),
        vm(zs, *down_half),
        vm(*down_half),
        vm(*down_half),
        [vm(zs, 2, 2, rows, s) for s in sizes],
        [vm(zs, 2, rows, s) for s in sizes],
        [vm(zs, rows, s) for s in sizes],
        [vm(zs, rows, s) for s in sizes],
        [vm(rows, s) for s in sizes],
        [vm(rows, s) for s in sizes],
        vm(half, width),
        vm(half, width),
        vm(3, *sums.shape, kind=F32),
        vm(zs, *sums.shape, kind=F32),
        vm(3, *sum_late, kind=F32),
        vm(zs, *sum_late, kind=F32),
        vm(*mod_early),
        vm(*mod_late),
        vm(*sums.shape, kind=F32),
        vm(*sum_late, kind=F32),
    ]
    scratch += [vm(*a.shape, kind=a.dtype) for a in fetched]
    scratch += [vm(half, width, kind=F32)]
    flat, tree = jax.tree.flatten(scratch)
    n_in, n_out = len(in_specs), len(out_specs)

    def kernel(*refs):
        back_kernel(
            zs,
            split,
            refs[:n_in],
            refs[n_in : n_in + n_out],
            jax.tree.unflatten(tree, refs[n_in + n_out :]),
        )

    return pl.pallas_call(
        kernel,
        grid=(PAIRS + 1,),
        in_specs=in_specs,
        out_specs=out_specs,
        out_shape=out_shape,
        scratch_shapes=flat,
        compiler_params=params(62, collective_id=5),
        cost_estimate=pl.CostEstimate(
            flops=32 * tokens * tokens * width + 12 * tokens * width * width,
            bytes_accessed=60 << 20,
            transcendentals=0,
        ),
        name="back",
    )(q, q, q, att, d_att, e, linv, cos_t, sin_t, *ins[7:])


def time_features(time_steps, pair_count):
    frequency = jnp.exp(-math.log(10000.0) * jnp.arange(pair_count, dtype=F32) / pair_count)
    angles = time_steps.astype(F32)[:, None] * frequency[None, :]
    return jnp.concatenate([jnp.cos(angles), jnp.sin(angles)], axis=-1)


def per_device(
    tokens,
    cotangent,
    time_index,
    span_starts,
    span_lengths,
    w_ada,
    b_ada,
    gain_one,
    w_qkv,
    w_out,
    gain_two,
    w_up,
    b_up,
    w_down,
    b_down,
):
    seqs_dev, half, width = tokens.shape
    length = 2 * half
    rank = lax.axis_index("seq")
    swap = [(0, 1), (1, 0)]

    def pick(x, i):
        return lax.dynamic_index_in_dim(x, i, 0, keepdims=False)

    tok_own, tok_send = pick(tokens, rank), pick(tokens, 1 - rank)
    cot_own = pick(cotangent, rank)
    tok_rem = lax.ppermute(tok_send, "seq", swap)

    here = jnp.arange(half, dtype=jnp.int32)
    place = jnp.concatenate([rank * half + here, (1 - rank) * half + here])
    frequency = jnp.exp(-math.log(10000.0) * jnp.arange(HD // 2, dtype=F32) / (HD // 2))
    angles = frequency[:, None] * place.astype(F32)[None, :]
    cos_t, sin_t = jnp.cos(angles), jnp.sin(angles)
    start, extent = pick(span_starts, rank), pick(span_lengths, rank)
    span = jnp.where((place >= start) & (place < start + extent), 2.0, 0.5).astype(F32)[:, None]

    time_own = lax.dynamic_slice_in_dim(time_index, rank, 1)
    cond_act = jax.nn.silu(time_features(time_own, w_ada.shape[0] // 2))
    modulation = (
        jnp.dot(cond_act, w_ada.astype(F32), precision=lax.Precision.HIGHEST)[0] + b_ada
    )
    shift_one, scale_one, gate_one, shift_two, scale_two, gate_two = jnp.split(modulation, 6)
    zeros = jnp.zeros_like(shift_one)
    vec_one = jnp.stack(
        [gain_one * (1.0 + scale_one), shift_one, gain_one, scale_one, zeros, zeros, zeros, zeros]
    )
    vec_two = jnp.stack(
        [
            gate_one,
            gain_two * (1.0 + scale_two),
            shift_two,
            gate_two,
            b_down,
            gain_two,
            scale_two,
            jnp.pad(jnp.concatenate([time_own // 32, time_own % 32]).astype(F32), (0, width - 2)),
        ]
    )
    w_qkv_t = w_qkv.T

    dp, dps = lax.axis_index("dp"), lax.axis_size("dp")
    ff = w_up.shape[1]
    zs = dps // 4
    linked = zs == 4 and dps == 16 and width % (64 * zs) == 0 and ff == zs * width

    act_t, qkv_t = project(tok_own, tok_rem, vec_one, cos_t, sin_t, w_qkv_t)
    att_t, e, linv, cot_rem = attend(qkv_t, cotangent)
    if linked:
        out_own, out_rem, dx, d_att_t, raw_out, raw_up, raw_down, *partial, mod, sums = middle_links(
            att_t, tok_own, tok_rem, cot_own, cot_rem, span, vec_two, b_up[None], w_out, w_up, w_down, zs
        )
        ins = (qkv_t, att_t, d_att_t, e, linv, cos_t, sin_t, out_own, out_rem, *partial)
        ins += (raw_up, raw_out, raw_down, mod, sums, act_t, w_qkv_t, tok_own, tok_rem, dx, vec_one)
        output, grad_tokens, *shards, mod_early, mod_late, sum_early, sum_late = back(ins, zs, ff)
        mod_early = mod_early.reshape(2 * dps, -1).astype(F32)
        mod_late = mod_late.reshape(2 * dps, -1).astype(F32)
        d_mod_all = jnp.concatenate([mod_late[:, : 2 * width], mod_early[:, : 4 * width]], axis=1)
        time_all = 32.0 * mod_early[:, 4 * width] + mod_early[:, 4 * width + 1]
        small = jnp.concatenate(
            [sum_late.reshape(-1)[:width], sum_early.reshape(-1)[: 2 * width + ff]]
        )
    else:
        out_own, out_rem, dx, d_att_t, g_out, g_up, g_down, g_bup, sums_two = middle(
            att_t, tok_own, tok_rem, cot_own, cot_rem, span, vec_two, b_up[None], w_out, w_up, w_down
        )
        d_proj, out_back = attend_back(qkv_t, att_t, d_att_t, e, linv, cos_t, sin_t, out_rem)
        d_proj_t = d_proj.reshape(3 * width, length)
        g_own, g_rem, sums_one = tail(tok_own, tok_rem, d_proj_t, w_qkv_t, dx, vec_one)
        g_qkv = weight_grad(act_t, d_proj_t)

        def spread(own, other):
            first = jnp.where(rank == 0, own, other)
            second = jnp.where(rank == 0, other, own)
            return jnp.stack([first, second])

        output = spread(out_own, out_back)
        grad_tokens = spread(g_own, lax.ppermute(g_rem, "seq", swap).astype(F32))
        shards = [
            lax.psum(lax.psum_scatter(g, "dp", scatter_dimension=0, tiled=True), "seq").astype(F32)
            for g in (g_qkv, g_out, g_up, g_down)
        ]
        d_mod = jnp.concatenate([sums_one[:2].reshape(-1), sums_two[:4].reshape(-1)])
        small = jnp.concatenate([sums_one[2], sums_two[4], sums_two[5], g_bup[0]])
        d_mod_all = lax.all_gather(d_mod, ("dp", "seq"))
        time_all = lax.all_gather(time_own[0].astype(F32), ("dp", "seq"))
        small = lax.psum(small, ("dp", "seq"))

    def mine(x, axis=0):
        size = x.shape[axis] // dps
        return lax.dynamic_slice_in_dim(x, dp * size, size, axis)

    features = jax.nn.silu(time_features(time_all, w_ada.shape[0] // 2))
    s_w_ada = jnp.dot(mine(features, 1).T, d_mod_all, precision=lax.Precision.HIGHEST)
    s_b_ada = jnp.sum(mine(d_mod_all, 1), axis=0)
    s_gain_one = mine(small[:width])
    s_gain_two = mine(small[width : 2 * width])
    s_b_down = mine(small[2 * width : 3 * width])
    s_b_up = mine(small[3 * width :])
    s_qkv, s_out, s_up, s_down = shards

    return (
        output,
        grad_tokens,
        s_w_ada,
        s_b_ada,
        s_gain_one,
        s_qkv,
        s_out,
        s_gain_two,
        s_up,
        s_b_up,
        s_down,
        s_b_down,
    )


def solution(mesh):
    rows = P("dp", "seq", None)
    return jax.shard_map(
        per_device,
        mesh=mesh,
        in_specs=(rows, rows, P("dp"), P("dp"), P("dp")) + (P(),) * 10,
        out_specs=(
            rows,
            rows,
            P("dp", None),
            P("dp"),
            P("dp"),
            P("dp", None),
            P("dp", None),
            P("dp"),
            P("dp", None),
            P("dp"),
            P("dp", None),
            P("dp"),
        ),
        check_vma=False,
    )
```

```python
import functools
import math

import jax
import jax.numpy as jnp
import numpy as np
from jax import lax
from jax.experimental import pallas as pl
from jax.experimental.pallas import tpu as pltpu
from jax.sharding import PartitionSpec as P

HEADS = 12
HD = 64
PAIRS = HEADS // 2
NORM_EPS = 1e-05
LOG2E = math.log2(math.e)
BF = jnp.bfloat16
F32 = jnp.float32
MIB = 1 << 20

NN = (((1,), (0,)), ((), ()))
NT = (((1,), (1,)), ((), ()))
TN = (((0,), (0,)), ((), ()))


def mm(a, b, dims=NN):
    return lax.dot_general(a, b, dims, preferred_element_type=F32)


def norm_parts(x):
    centre = x - jnp.mean(x, axis=-1, keepdims=True)
    rstd = lax.rsqrt(jnp.mean(centre * centre, axis=-1, keepdims=True) + NORM_EPS)
    return centre * rstd, rstd


def norm_pull(n, rstd, dn):
    return rstd * (
        dn - jnp.mean(dn, axis=-1, keepdims=True) - n * jnp.mean(dn * n, axis=-1, keepdims=True)
    )


def col_sum(x):
    return jnp.sum(x, axis=0, keepdims=True)


def rows_of(size, index):
    return pl.ds(pl.multiple_of(index * size, size), size)


def params(mib=56, collective_id=None):
    if collective_id is None:
        return pltpu.CompilerParams(vmem_limit_bytes=mib * MIB)
    return pltpu.CompilerParams(
        vmem_limit_bytes=mib * MIB, collective_id=collective_id, has_side_effects=True
    )


def whole(shape):
    zeros = (0,) * len(shape)
    return pl.BlockSpec(shape, lambda *_: zeros)


MESH = pl.DeviceIdType.MESH
ANY = pl.BlockSpec(memory_space=pl.ANY)
SEMS = [pltpu.SemaphoreType.DMA, pltpu.SemaphoreType.DMA]


def greet(*partners):
    barrier = pltpu.get_barrier_semaphore()
    for partner in partners:
        pl.semaphore_signal(barrier, inc=1, device_id=partner, device_id_type=MESH)
    pl.semaphore_wait(barrier, len(partners))


def remote(src, dst, send, recv, device):
    return pltpu.make_async_remote_copy(
        src_ref=src, dst_ref=dst, send_sem=send, recv_sem=recv, device_id=device, device_id_type=MESH
    )


def seq_partner():
    return (lax.axis_index("dp"), 1 - lax.axis_index("seq"))


def swap_start(src, dst, send, recv):
    partner = seq_partner()
    greet(partner)
    remote(src, dst, send, recv, partner).start()


def swap_wait(src, dst, send, recv):
    remote(src, dst, send, recv, seq_partner()).wait()


class Links:
    def __init__(self, sems, zs):
        self.sems, self.used, self.zs = sems, 0, zs
        dp, self.x = lax.axis_index("dp"), lax.axis_index("seq")
        self.z, self.y, self.c = dp // 4, lax.rem(dp // 2, 2), lax.rem(dp, 2)
        self.core = (dp + 1 - 2 * self.c, self.x)
        self.across = (dp + 2 - 4 * self.y, self.x)
        self.facing = (dp, 1 - self.x)
        self.far = [lax.rem(self.z + k, zs) for k in range(1, zs)]

    def at_z(self, f):
        return (f * 4 + 2 * self.y + self.c, self.x)

    def take(self, count):
        self.used += count
        return self.used - count

    def local(self, src, dst):
        sem = self.take(1)
        return lambda: pltpu.make_async_copy(src(), dst(), self.sems.at[sem])

    def swap(self, src, dst, device):
        sem = self.take(2)
        return lambda: remote(src(), dst(), self.sems.at[sem], self.sems.at[sem + 1], device)

    def spread(self, src, dst):
        sem = self.take(2 * self.zs)

        def make(f, slot):
            return remote(
                src(f), dst(slot), self.sems.at[sem + f], self.sems.at[sem + self.zs + slot], self.at_z(f)
            )

        def start():
            for f in self.far:
                make(f, self.z).start()

        def wait():
            for f in self.far:
                make(f, self.z).wait_send()
                make(f, f).wait_recv()

        return start, wait

    def gather(self, src, dst, goal):
        sem = self.take(1 + self.zs)

        def make(slot):
            return remote(
                src(), dst(slot), self.sems.at[sem], self.sems.at[sem + 1 + slot], self.at_z(goal)
            )

        def start():
            pl.when(self.z != goal)(lambda: make(self.z).start())

        def wait():
            pl.when(self.z != goal)(lambda: make(self.z).wait_send())

            @pl.when(self.z == goal)
            def _():
                for f in self.far:
                    make(f).wait_recv()

        return start, wait


def add_to(dst, src, lead):
    for index in lead:
        dst[index] = dst[index] + src[index]


def grid_of(*sizes):
    return [()] if not sizes else [(i,) + r for i in range(sizes[0]) for r in grid_of(*sizes[1:])]


def round_up(value, unit):
    return -(-value // unit) * unit


def early_mod_rows(width):
    return round_up(4 * width // 128 + 1, 16)


def early_sum_rows(width, ff):
    return round_up((2 * width + ff) // 128, 8)


def put_rows(ref, start, row):
    for k in range(row.shape[1] // 128):
        ref[start + k : start + k + 1, :] = row[:, k * 128 : (k + 1) * 128].astype(ref.dtype)


def once(shape):
    zeros = (0,) * len(shape)
    return pl.BlockSpec(shape, lambda *_: zeros, pipeline_mode=pl.Buffered(1))


def split_three(x):
    parts = []
    for _ in range(3):
        low = x.astype(BF)
        parts.append(low)
        x = x - low.astype(F32)
    return parts


def features_of(angles, is_sin):
    raw = jnp.where(is_sin, jnp.sin(angles), jnp.cos(angles))
    return raw / (1.0 + jnp.exp(-raw))


def project_kernel(
    time_ref,
    start_ref,
    extent_ref,
    tokens_ref,
    cos_ref,
    sin_ref,
    w_ada_ref,
    b_ada_ref,
    gain_one_ref,
    gain_two_ref,
    b_down_ref,
    w_ref,
    act_ref,
    out_ref,
    w_t_ref,
    rem_ref,
    vec_one_ref,
    vec_two_ref,
    span_ref,
    cos_out,
    sin_out,
    own,
    rem,
    w_t,
    qkv,
    sems,
):
    step = pl.program_id(0)
    half, width = own.shape
    rows = w_t_ref.shape[0]
    tile = 128
    chunk = half // 2
    x = lax.axis_index("seq")
    keep = pltpu.make_async_copy(tokens_ref.at[x], own, sems.at[0])
    cross = [
        remote(
            tokens_ref.at[1 - x, k * chunk : (k + 1) * chunk],
            rem.at[k * chunk : (k + 1) * chunk],
            sems.at[1 + k],
            sems.at[3 + k],
            seq_partner(),
        )
        for k in range(2)
    ]
    spans = (slice(0, half), slice(half, half + chunk), slice(half + chunk, 2 * half))
    store = [
        pltpu.make_async_copy(qkv.at[:, span], out_ref.at[:, span], sems.at[5 + k])
        for k, span in enumerate(spans)
    ]

    def norm(src, first, size, start):
        scale, shift = vec_one_ref[0:1, :], vec_one_ref[1:2, :]
        for t in range(0, size, tile):
            n, _ = norm_parts(src[first + t : first + t + tile, :].astype(F32))
            act_ref[:, start + t : start + t + tile] = (n * scale + shift).astype(BF).T

    @pl.when(step == 0)
    def _():
        greet(seq_partner())
        for copy in cross:
            copy.start()
        keep.start()
        pairs = w_ada_ref.shape[0] // 2
        time = time_ref[x]
        lane = lax.broadcasted_iota(jnp.int32, (8, 2 * pairs), 1)
        place = jnp.where(lane < pairs, lane, lane - pairs).astype(F32)
        frequency = jnp.exp(-math.log(10000.0) * place / pairs)
        cond = features_of(time.astype(F32) * frequency, lane >= pairs)
        modulation = b_ada_ref[...].reshape(1, 6 * width)
        for part in split_three(cond):
            modulation = modulation + mm(part, w_ada_ref[...])[0:1, :]
        pieces = [modulation[:, k * width : (k + 1) * width] for k in range(6)]
        shift_one, scale_one, gate_one, shift_two, scale_two, gate_two = pieces
        gain_one, gain_two = (ref[...].reshape(1, width) for ref in (gain_one_ref, gain_two_ref))
        zeros = jnp.zeros((1, width), F32)
        first = (gain_one * (1.0 + scale_one), shift_one, gain_one, scale_one)
        for k, row in enumerate(first + (zeros,) * 4):
            vec_one_ref[k : k + 1, :] = row
        lanes = lax.broadcasted_iota(jnp.int32, (1, width), 1)
        stamp = jnp.where(lanes == 0, time // 32, jnp.where(lanes == 1, lax.rem(time, 32), 0))
        second = (
            gate_one,
            gain_two * (1.0 + scale_two),
            shift_two,
            gate_two,
            b_down_ref[...].reshape(1, width),
            gain_two,
            scale_two,
            stamp.astype(F32),
        )
        for k, row in enumerate(second):
            vec_two_ref[k : k + 1, :] = row
        begin, end = start_ref[x], start_ref[x] + extent_ref[x]
        index = lax.broadcasted_iota(jnp.int32, (half, 1), 0)
        for part, where in enumerate((x, 1 - x)):
            place = index + where * half
            inside = (place >= begin) & (place < end)
            span_ref[part * half : (part + 1) * half, :] = jnp.where(inside, 2.0, 0.5)
            cos_out[:, part * half : (part + 1) * half] = cos_ref[where]
            sin_out[:, part * half : (part + 1) * half] = sin_ref[where]
        keep.wait()
        norm(own, 0, half, 0)

    def rotated(proj, block, cols, factor):
        cos, sin = cos_out[:, cols] * factor, sin_out[:, cols] * factor
        parts = []
        for h in range(rows // HD):
            a = proj[h * HD : h * HD + HD // 2]
            b = proj[h * HD + HD // 2 : (h + 1) * HD]
            parts += [(a * cos - b * sin).astype(BF), (b * cos + a * sin).astype(BF)]
        qkv[block, cols] = jnp.concatenate(parts, axis=0)

    @pl.when(step < 6)
    def _():
        block = rows_of(rows, step)
        flipped = w_ref[...].T
        w_t[block, :] = flipped
        w_t_ref[...] = flipped
        proj = mm(flipped, act_ref[:, spans[0]])

        @pl.when(step < 4)
        def _():
            rotated(proj, block, spans[0], jnp.where(step < 2, HD**-0.5, 1.0))

        @pl.when(step >= 4)
        def _():
            qkv[block, spans[0]] = proj.astype(BF)

    for k in range(2):

        @pl.when(step == 6 + k)
        def _(k=k):
            store[k].start()
            cross[k].wait()
            got = slice(k * chunk, (k + 1) * chunk)
            rem_ref[got, :] = rem[got, :]
            norm(rem, k * chunk, chunk, half + k * chunk)
            cols = spans[1 + k]
            for turn in range(6):
                block = slice(turn * rows, (turn + 1) * rows)
                proj = mm(w_t[block, :], act_ref[:, cols])
                if turn < 4:
                    rotated(proj, block, cols, HD**-0.5 if turn < 2 else 1.0)
                else:
                    qkv[block, cols] = proj.astype(BF)
            if k == 1:
                store[2].start()
                for copy in store:
                    copy.wait()


def rotary_constants(length):
    angles = np.arange(length, dtype=np.float32)[None, :] * np.exp(
        -math.log(10000.0) * np.arange(HD // 2, dtype=np.float32) / np.float32(HD // 2)
    ).astype(np.float32)[:, None]
    angles = angles.reshape(HD // 2, 2, length // 2).transpose(1, 0, 2).astype(np.float64)
    return np.cos(angles).astype(np.float32), np.sin(angles).astype(np.float32)


def project(tokens, time_index, span_starts, span_lengths, w_ada, b_ada, gains, b_down, w_qkv):
    _, half, width = tokens.shape
    length = 2 * half
    blk = width // 2
    cos_all, sin_all = rotary_constants(length)
    smem = pl.BlockSpec(memory_space=pltpu.SMEM)
    outs = [
        ((width, length), BF),
        ((3 * width, length), BF),
        ((3 * width, width), BF),
        ((half, width), BF),
        ((8, width), F32),
        ((8, width), F32),
        ((length, 1), F32),
        ((HD // 2, length), F32),
        ((HD // 2, length), F32),
    ]
    out_specs = [once(shape) for shape, _ in outs]
    out_specs[1] = ANY
    out_specs[2] = pl.BlockSpec((blk, width), lambda i: (jnp.minimum(i, 5), 0))
    rows = [b_ada, *gains, b_down]
    return pl.pallas_call(
        project_kernel,
        grid=(8,),
        in_specs=[smem, smem, smem, ANY, once(cos_all.shape), once(sin_all.shape), once(w_ada.shape)]
        + [once(r.shape) for r in rows]
        + [pl.BlockSpec((width, blk), lambda i: (0, jnp.minimum(i, 5)))],
        out_specs=out_specs,
        out_shape=[jax.ShapeDtypeStruct(*o) for o in outs],
        scratch_shapes=[
            pltpu.VMEM((half, width), BF),
            pltpu.VMEM((half, width), BF),
            pltpu.VMEM((3 * width, width), BF),
            pltpu.VMEM((3 * width, length), BF),
            pltpu.SemaphoreType.DMA((8,)),
        ],
        compiler_params=params(collective_id=6),
        cost_estimate=pl.CostEstimate(
            flops=6 * length * width * width, bytes_accessed=20 << 20, transcendentals=0
        ),
        name="project",
    )(time_index, span_starts, span_lengths, tokens, cos_all, sin_all, w_ada, *rows, w_qkv)


def attend_kernel(
    q_ref, k_ref, v_ref, cot_ref, att_ref, e_ref, linv_ref, cot_rem, q_mask, v_ext, send, recv
):
    step = pl.program_id(0)
    cot_send = cot_ref.at[1 - lax.axis_index("seq")]

    @pl.when(step == 0)
    def _():
        swap_start(cot_send, cot_rem, send, recv)

    tokens = q_ref.shape[1]
    tile = 256
    zero = jnp.zeros((HD, tokens), BF)
    k_nat = k_ref[...].T
    q_mask[0, 0:HD, :] = q_ref[0:HD, :]
    q_mask[0, HD:, :] = zero
    q_mask[1, 0:HD, :] = zero
    q_mask[1, HD:, :] = q_ref[HD:, :]
    for h in range(2):
        v_ext[h, 0:HD, :] = v_ref[h * HD : (h + 1) * HD, :]
        v_ext[h, HD:, :] = jnp.ones((16, tokens), BF)
    def score(h, cols):
        return mm(k_nat, q_mask[h, :, cols])

    def soften(h, cols, s):
        e_ref[h, :, cols] = jnp.exp(s - jnp.max(s, axis=0, keepdims=True)).astype(BF)

    def mix(h, cols):
        mixed = mm(v_ext[h], e_ref[h, :, cols])
        linv = 1.0 / mixed[HD : HD + 1, :]
        linv_ref[0, h : h + 1, cols] = linv
        att_ref[h * HD : (h + 1) * HD, cols] = (mixed[0:HD, :] * linv).astype(BF)

    units = [(h, slice(t, t + tile)) for t in range(0, tokens, tile) for h in range(2)]
    coming = score(*units[0])
    for i, unit in enumerate(units):
        here = coming
        if i + 1 < len(units):
            coming = score(*units[i + 1])
        soften(*unit, here)
        if i > 0:
            mix(*units[i - 1])
    mix(*units[-1])

    @pl.when(step == pl.num_programs(0) - 1)
    def _():
        swap_wait(cot_send, cot_rem, send, recv)


def attend(qkv_t, cotangent):
    tokens = qkv_t.shape[1]
    width = HEADS * HD

    def part(k):
        return pl.BlockSpec((2 * HD, tokens), lambda i: (i + k * PAIRS, 0))

    return pl.pallas_call(
        attend_kernel,
        grid=(PAIRS,),
        in_specs=[part(0), part(1), part(2), ANY],
        out_specs=[
            part(0),
            pl.BlockSpec((2, tokens, tokens), lambda i: (i, 0, 0)),
            pl.BlockSpec((1, 8, tokens), lambda i: (i, 0, 0)),
            ANY,
        ],
        out_shape=[
            jax.ShapeDtypeStruct((width, tokens), BF),
            jax.ShapeDtypeStruct((HEADS, tokens, tokens), BF),
            jax.ShapeDtypeStruct((PAIRS, 8, tokens), F32),
            jax.ShapeDtypeStruct(cotangent.shape[1:], BF),
        ],
        scratch_shapes=[
            pltpu.VMEM((2, 2 * HD, tokens), BF),
            pltpu.VMEM((2, HD + 16, tokens), BF),
        ]
        + SEMS,
        compiler_params=params(collective_id=1),
        cost_estimate=pl.CostEstimate(
            flops=16 * tokens * tokens * width,
            bytes_accessed=30 << 20,
            transcendentals=HEADS * tokens * tokens,
        ),
        name="attend",
    )(qkv_t, qkv_t, qkv_t, cotangent)


def gelu_both(u):
    c = math.sqrt(2.0 / math.pi)
    u2 = u * u
    th = jnp.tanh(u * (c + (c * 0.044715) * u2))
    half = 0.5 * (1.0 + th)
    value = u * half
    slope = half + (0.5 * u) * (1.0 - th * th) * (c + (3.0 * c * 0.044715) * u2)
    return value, slope


def middle_kernel(
    att_ref,
    tok_own,
    tok_rem,
    cot_own,
    cot_rem,
    span_ref,
    vec_ref,
    b_up_ref,
    w_out_ref,
    w_up_ref,
    w_down_ref,
    out_own,
    out_rem,
    dx_ref,
    d_att_ref,
    g_out_ref,
    g_up_ref,
    g_down_ref,
    g_bup_ref,
    sums_ref,
    branch,
    x_one,
    act_two,
    d_down,
    down_acc,
    d_act,
    d_branch,
):
    step = pl.program_id(0)
    steps = pl.num_programs(0)
    tokens = att_ref.shape[1]
    half = tokens // 2
    tile = 256
    per_half = half // tile
    gate_one = vec_ref[0:1, :]
    mult_two = vec_ref[1:2, :]
    shift_two = vec_ref[2:3, :]
    gate_two = vec_ref[3:4, :]
    b_down = vec_ref[4:5, :]
    gain_two = vec_ref[5:6, :]
    scale_two = vec_ref[6:7, :]

    @pl.when(step == 0)
    def _():
        for part, (tok, cot) in enumerate(((tok_own, cot_own), (tok_rem, cot_rem))):
            for t in range(per_half):
                src = slice(t * tile, (t + 1) * tile)
                dst = slice(part * half + t * tile, part * half + (t + 1) * tile)
                br = mm(att_ref[:, dst], w_out_ref[...], TN)
                branch[dst, :] = br
                x = tok[src, :].astype(F32) + gate_one * br
                x_one[dst, :] = x
                n, _ = norm_parts(x)
                act_two[dst, :] = (n * mult_two + shift_two).astype(BF)
                grad_out = cot[src, :].astype(F32) * span_ref[dst, :]
                d_down[dst, :] = (gate_two * grad_out).astype(BF)

    up = mm(act_two[...], w_up_ref[...]) + b_up_ref[...]
    value, slope = gelu_both(up)
    hidden = value.astype(BF)
    d_hidden = mm(d_down[...], w_down_ref[...], NT)
    d_up_full = slope * d_hidden
    d_up = d_up_full.astype(BF)
    g_bup_ref[...] = col_sum(d_up.astype(F32))
    down_part = mm(hidden, w_down_ref[...])
    d_act_part = mm(d_up, w_up_ref[...], NT)
    g_down_ref[...] = mm(hidden, d_down[...], TN).astype(BF)
    g_up_ref[...] = mm(act_two[...], d_up, TN).astype(BF)

    @pl.when(step == 0)
    def _():
        down_acc[...] = down_part
        d_act[...] = d_act_part

    @pl.when(step > 0)
    def _():
        down_acc[...] += down_part
        d_act[...] += d_act_part

    @pl.when(step == steps - 1)
    def _():
        zero = jnp.zeros((1, gate_one.shape[1]), F32)
        s_gate_two, s_shift, s_pull, s_gate_one, s_bdown = zero, zero, zero, zero, zero
        for part, (cot, out) in enumerate(((cot_own, out_own), (cot_rem, out_rem))):
            for t in range(per_half):
                src = slice(t * tile, (t + 1) * tile)
                dst = slice(part * half + t * tile, part * half + (t + 1) * tile)
                x = x_one[dst, :]
                down = down_acc[dst, :] + b_down
                out[src, :] = (x + gate_two * down).astype(BF)
                grad_out = cot[src, :].astype(F32) * span_ref[dst, :]
                s_gate_two += col_sum(grad_out * down)
                s_bdown += col_sum(d_down[dst, :].astype(F32))
                n, rstd = norm_parts(x)
                da = d_act[dst, :]
                s_shift += col_sum(da)
                s_pull += col_sum(da * n)
                dx = grad_out + norm_pull(n, rstd, da * mult_two)
                dx_ref[dst, :] = dx
                s_gate_one += col_sum(dx * branch[dst, :])
                d_branch[dst, :] = (gate_one * dx).astype(BF)
        sums_ref[0:1, :] = s_gate_one
        sums_ref[1:2, :] = s_shift
        sums_ref[2:3, :] = s_pull * gain_two
        sums_ref[3:4, :] = s_gate_two
        sums_ref[4:5, :] = s_pull * (1.0 + scale_two)
        sums_ref[5:6, :] = s_bdown
        sums_ref[6:8, :] = jnp.zeros((2, gate_one.shape[1]), F32)
        g_out_ref[...] = mm(att_ref[...], d_branch[...]).astype(BF)
        d_att_ref[...] = mm(w_out_ref[...], d_branch[...], NT).astype(BF)


def middle(att_t, tok_own, tok_rem, cot_own, cot_rem, span, vec, b_up, w_out, w_up, w_down):
    width, tokens = att_t.shape
    half = tokens // 2
    ff = w_up.shape[1]
    tile = 512
    return pl.pallas_call(
        middle_kernel,
        grid=(ff // tile,),
        in_specs=[
            whole(att_t.shape),
            whole(tok_own.shape),
            whole(tok_rem.shape),
            whole(cot_own.shape),
            whole(cot_rem.shape),
            whole(span.shape),
            whole(vec.shape),
            pl.BlockSpec((1, tile), lambda i: (0, i)),
            whole(w_out.shape),
            pl.BlockSpec((width, tile), lambda i: (0, i)),
            pl.BlockSpec((tile, width), lambda i: (i, 0)),
        ],
        out_specs=[
            whole((half, width)),
            whole((half, width)),
            whole((tokens, width)),
            whole((width, tokens)),
            whole((width, width)),
            pl.BlockSpec((width, tile), lambda i: (0, i)),
            pl.BlockSpec((tile, width), lambda i: (i, 0)),
            pl.BlockSpec((1, tile), lambda i: (0, i)),
            whole((8, width)),
        ],
        out_shape=[
            jax.ShapeDtypeStruct((half, width), BF),
            jax.ShapeDtypeStruct((half, width), BF),
            jax.ShapeDtypeStruct((tokens, width), F32),
            jax.ShapeDtypeStruct((width, tokens), BF),
            jax.ShapeDtypeStruct((width, width), BF),
            jax.ShapeDtypeStruct((width, ff), BF),
            jax.ShapeDtypeStruct((ff, width), BF),
            jax.ShapeDtypeStruct((1, ff), F32),
            jax.ShapeDtypeStruct((8, width), F32),
        ],
        scratch_shapes=[
            pltpu.VMEM((tokens, width), F32),
            pltpu.VMEM((tokens, width), F32),
            pltpu.VMEM((tokens, width), BF),
            pltpu.VMEM((tokens, width), BF),
            pltpu.VMEM((tokens, width), F32),
            pltpu.VMEM((tokens, width), F32),
            pltpu.VMEM((tokens, width), BF),
        ],
        compiler_params=params(),
        cost_estimate=pl.CostEstimate(
            flops=12 * tokens * width * ff + 6 * tokens * width * width,
            bytes_accessed=40 << 20,
            transcendentals=tokens * ff,
        ),
        name="middle",
    )(att_t, tok_own, tok_rem, cot_own, cot_rem, span, vec, b_up, w_out, w_up, w_down)


def middle_links_kernel(
    zs,
    att_ref,
    tokens_ref,
    tok_rem,
    cot_ref,
    cot_rem,
    span_ref,
    vec_ref,
    b_up_ref,
    w_out_ref,
    w_up_ref,
    w_down_ref,
    out_own,
    out_rem,
    dx_ref,
    d_att_ref,
    g_out_ref,
    g_up_ref,
    g_down_ref,
    up_last_ref,
    up_one_ref,
    up_two_ref,
    down_last_ref,
    down_one_ref,
    down_two_ref,
    mod_ref,
    sum_ref,
    branch,
    x_one,
    act_two,
    d_down,
    down_acc,
    d_act,
    d_branch,
    hidden,
    d_up,
    up_core,
    up_side,
    up_y,
    up_z,
    down_core,
    down_y,
    down_side,
    down_z,
    sems,
):
    step = pl.program_id(0)
    steps = zs
    tokens = att_ref.shape[1]
    width = att_ref.shape[0]
    half = tokens // 2
    cut = width // 2
    tile = 256
    per_half = half // tile
    gate_one = vec_ref[0:1, :]
    mult_two = vec_ref[1:2, :]
    shift_two = vec_ref[2:3, :]
    gate_two = vec_ref[3:4, :]
    b_down = vec_ref[4:5, :]
    gain_two = vec_ref[5:6, :]
    scale_two = vec_ref[6:7, :]

    links = Links(sems, zs)
    x, y, z, c = links.x, links.y, links.z, links.c
    tok_own, cot_own = tokens_ref.at[x], cot_ref.at[x]
    tiles = range(steps - 1)

    def swaps(src, dst, device):
        return [links.swap(lambda j=j: src(j), lambda j=j: dst.at[j], device) for j in tiles]

    up_to_core = swaps(lambda j: g_up_ref.at[:, :, :, 1 - c], up_core, links.core)
    down_to_core = swaps(lambda j: g_down_ref.at[:, 1 - c], down_core, links.core)
    up_to_side = swaps(lambda j: up_core.at[j, 1 - x], up_side, links.facing)
    down_to_y = swaps(lambda j: down_core.at[j, 1 - y], down_y, links.across)
    up_to_y = swaps(lambda j: up_core.at[j, x, :, 1 - y], up_y, links.across)
    down_to_side = swaps(lambda j: down_core.at[j, y, 1 - x], down_side, links.facing)
    down_far = links.gather(lambda: down_core.at[0, y, x], lambda slot: down_z.at[slot], 0)
    up_far = links.spread(lambda f: up_core.at[0, x, f, y], lambda slot: up_z.at[slot])

    def core_stage(j):
        up_to_core[j]().start()
        down_to_core[j]().start()

    def first_stage(j):
        up_to_core[j]().wait()
        for h, a, b in grid_of(2, zs, 2):
            up_core[j, h, a, b] = up_core[j, h, a, b] + g_up_ref[h, a, b, c]
        up_to_side[j]().start()
        down_to_core[j]().wait()
        for b, h in grid_of(2, 2):
            down_core[j, b, h] = down_core[j, b, h] + g_down_ref[b, c, h]
        down_to_y[j]().start()

    def first_done(j):
        up_to_side[j]().wait()
        for a, b in grid_of(zs, 2):
            up_core[j, x, a, b] = up_core[j, x, a, b] + up_side[j, a, b]
        down_to_y[j]().wait()
        for h in range(2):
            down_core[j, y, h] = down_core[j, y, h] + down_y[j, h]

    def second_stage(j):
        first_done(j)
        up_to_y[j]().start()
        down_to_side[j]().start()

    def second_done(j):
        up_to_y[j]().wait()
        for a in range(zs):
            up_core[j, x, a, y] = up_core[j, x, a, y] + up_y[j, a]
        down_to_side[j]().wait()
        down_core[j, y, x] = down_core[j, y, x] + down_side[j]

    def third_stage():
        second_done(0)
        up_far[0]()
        down_far[0]()

    @pl.when(step == 0)
    def _():
        greet(links.core, links.across, links.facing, *[links.at_z(f) for f in links.far])
        for part, (tok, cot) in enumerate(((tok_own, cot_own), (tok_rem, cot_rem))):
            for t in range(per_half):
                src = slice(t * tile, (t + 1) * tile)
                dst = slice(part * half + t * tile, part * half + (t + 1) * tile)
                br = mm(att_ref[:, dst], w_out_ref[...], TN)
                branch[dst, :] = br
                xv = tok[src, :].astype(F32) + gate_one * br
                x_one[dst, :] = xv
                n, _ = norm_parts(xv)
                act_two[dst, :] = (n * mult_two + shift_two).astype(BF)
                grad_out = cot[src, :].astype(F32) * span_ref[dst, :]
                d_down[dst, :] = (gate_two * grad_out).astype(BF)
                down_acc[dst, :] = jnp.zeros((tile, width), F32)
                d_act[dst, :] = jnp.zeros((tile, width), F32)

    chunk = tokens // 4

    def one(k, bup):
        rows = rows_of(chunk, k)
        up = mm(act_two[rows, :], w_up_ref[...]) + b_up_ref[...]
        d_hidden = mm(d_down[rows, :], w_down_ref[...], NT)
        value, slope = gelu_both(up)
        low = value.astype(BF)
        hidden[rows, :] = low
        d_up_low = (slope * d_hidden).astype(BF)
        d_up[rows, :] = d_up_low
        down_acc[rows, :] += mm(low, w_down_ref[...])
        d_act[rows, :] += mm(d_up_low, w_up_ref[...], NT)
        return bup + col_sum(d_up_low.astype(F32))

    bup = lax.fori_loop(0, 4, one, jnp.zeros((1, w_up_ref.shape[1]), F32))
    for j in range(steps):
        pl.when(step == j)(lambda j=j: put_rows(sum_ref, 2 * width // 128 + j * bup.shape[1] // 128, bup))

    @pl.when(step == 1)
    def _():
        first_stage(0)

    @pl.when(step == 2)
    def _():
        second_stage(0)
        first_stage(1)

    @pl.when(step == 3)
    def _():
        second_stage(1)
        first_stage(2)

    chunk_out = width // 3
    g_down_flat = g_down_ref.reshape(width, width)
    g_up_flat = g_up_ref.reshape(2, width, cut)

    def grads(k, carry):
        outs = rows_of(chunk_out, k)
        g_down_flat[outs, :] = mm(hidden[:, outs], d_down[...], TN).astype(BF)
        g_up = mm(act_two[:, outs], d_up[...], TN).astype(BF)
        for h in range(2):
            g_up_flat[h, outs, :] = g_up[:, h * cut : (h + 1) * cut]
        return carry

    lax.fori_loop(0, 3, grads, 0)

    @pl.when(step == 0)
    def _():
        core_stage(0)

    @pl.when(step == 1)
    def _():
        core_stage(1)

    @pl.when(step == 2)
    def _():
        third_stage()
        core_stage(2)

    @pl.when(step == steps - 1)
    def _():
        zero = jnp.zeros((1, width), F32)
        s_gate_two, s_shift, s_pull, s_gate_one, s_bdown = zero, zero, zero, zero, zero
        for part, (cot, out) in enumerate(((cot_own, out_own), (cot_rem, out_rem))):
            for t in range(per_half):
                src = slice(t * tile, (t + 1) * tile)
                dst = slice(part * half + t * tile, part * half + (t + 1) * tile)
                xv = x_one[dst, :]
                down = down_acc[dst, :] + b_down
                out[src, :] = (xv + gate_two * down).astype(BF)
                grad_out = cot[src, :].astype(F32) * span_ref[dst, :]
                s_gate_two += col_sum(grad_out * down)
                s_bdown += col_sum(d_down[dst, :].astype(F32))
                n, rstd = norm_parts(xv)
                da = d_act[dst, :]
                s_shift += col_sum(da)
                s_pull += col_sum(da * n)
                dx = grad_out + norm_pull(n, rstd, da * mult_two)
                dx_ref[dst, :] = dx
                s_gate_one += col_sum(dx * branch[dst, :])
                d_branch[dst, :] = (gate_one * dx).astype(BF)
        lines = width // 128
        mod_ref[4 * lines :, :] = jnp.zeros((mod_ref.shape[0] - 4 * lines, 128), BF)
        for k, row in enumerate((s_gate_one, s_shift, s_pull * gain_two, s_gate_two)):
            put_rows(mod_ref, k * lines, row)
        put_rows(mod_ref, 4 * lines, vec_ref[7:8, 0:128])
        put_rows(sum_ref, 0, s_pull * (1.0 + scale_two))
        put_rows(sum_ref, lines, s_bdown)
        g_out = mm(att_ref[...], d_branch[...]).astype(BF)
        for h in range(2):
            g_out_ref[h] = g_out[:, h * cut : (h + 1) * cut].reshape(g_out_ref.shape[1:])
        d_att_ref[...] = mm(w_out_ref[...], d_branch[...], NT).astype(BF)
        up_far[1]()
        total = up_core[0, x, z, y].astype(F32)
        for f in links.far:
            total += up_z[f].astype(F32)
        up_last_ref[...] = total.astype(BF)
        down_far[1]()
        total = down_core[0, y, x].astype(F32)
        for f in links.far:
            total += down_z[f].astype(F32)
        down_last_ref[...] = total.astype(BF)
        second_done(1)
        for a in range(zs):
            up_one_ref[a] = up_core[1, x, a, y]
        down_one_ref[...] = down_core[1, y, x]
        first_done(2)
        up_two_ref[...] = up_core[2, x]
        down_two_ref[...] = down_core[2, y]


def middle_links(
    att_t, tok_all, tok_rem, cot_all, cot_rem, span, vec, b_up, w_out, w_up, w_down, zs
):
    width, tokens = att_t.shape
    half = tokens // 2
    cut = width // 2
    ff = w_up.shape[1]
    tile = ff // zs
    rows = width // (4 * zs)
    down_rows = tile // 4
    halves = (2, zs, 2, 2, rows, cut)
    down_half = (down_rows // 2, width)
    owned = (2, 2, 2) + down_half
    outs = [
        ((half, width), BF),
        ((half, width), BF),
        ((tokens, width), F32),
        ((width, tokens), BF),
        (halves, BF),
        (halves, BF),
        (owned, BF),
        ((rows, cut), BF),
        ((zs, rows, cut), BF),
        ((zs, 2, rows, cut), BF),
        (down_half, BF),
        (down_half, BF),
        ((2,) + down_half, BF),
        ((early_mod_rows(width), 128), BF),
        ((early_sum_rows(width, ff), 128), F32),
    ]
    return pl.pallas_call(
        functools.partial(middle_links_kernel, zs),
        grid=(zs,),
        in_specs=[
            once(att_t.shape),
            once(tok_all.shape),
            once(tok_rem.shape),
            once(cot_all.shape),
            once(cot_rem.shape),
            once(span.shape),
            once(vec.shape),
            pl.BlockSpec((1, tile), lambda i: (0, i)),
            once(w_out.shape),
            pl.BlockSpec((width, tile), lambda i: (0, i)),
            pl.BlockSpec((tile, width), lambda i: (i, 0)),
        ],
        out_specs=[once(shape) for shape, _ in outs],
        out_shape=[jax.ShapeDtypeStruct(*o) for o in outs],
        scratch_shapes=[
            pltpu.VMEM((tokens, width), F32),
            pltpu.VMEM((tokens, width), F32),
            pltpu.VMEM((tokens, width), BF),
            pltpu.VMEM((tokens, width), BF),
            pltpu.VMEM((tokens, width), F32),
            pltpu.VMEM((tokens, width), F32),
            pltpu.VMEM((tokens, width), BF),
            pltpu.VMEM((tokens, tile), BF),
            pltpu.VMEM((tokens, tile), BF),
            pltpu.VMEM((zs - 1, 2, zs, 2, rows, cut), BF),
            pltpu.VMEM((zs - 1, zs, 2, rows, cut), BF),
            pltpu.VMEM((zs - 1, zs, rows, cut), BF),
            pltpu.VMEM((zs, rows, cut), BF),
            pltpu.VMEM((zs - 1, 2, 2) + down_half, BF),
            pltpu.VMEM((zs - 1, 2) + down_half, BF),
            pltpu.VMEM((zs - 1,) + down_half, BF),
            pltpu.VMEM((zs,) + down_half, BF),
            pltpu.SemaphoreType.DMA((12 * (zs - 1) + 1 + 3 * zs,)),
        ],
        compiler_params=params(62, collective_id=4),
        cost_estimate=pl.CostEstimate(
            flops=12 * tokens * width * ff + 6 * tokens * width * width,
            bytes_accessed=40 << 20,
            transcendentals=tokens * ff,
        ),
        name="middle_links",
    )(att_t, tok_all, tok_rem, cot_all, cot_rem, span, vec, b_up, w_out, w_up, w_down)


def attend_back_kernel(
    q_ref,
    k_ref,
    v_ref,
    att_ref,
    d_att_ref,
    e_ref,
    linv_ref,
    cos_ref,
    sin_ref,
    give_ref,
    out_ref,
    take_ref,
    do_mask,
    send,
    recv,
):
    step = pl.program_id(0)

    @pl.when(step == 0)
    def _():
        swap_start(give_ref, take_ref, send, recv)

    tokens = q_ref.shape[1]
    tile = 256
    zero = jnp.zeros((HD, tokens), BF)
    v_nat = v_ref[...].T
    cos = cos_ref[...]
    sin = sin_ref[...]

    def unrotate(x):
        low = x.astype(BF).astype(F32)
        a, b = low[0 : HD // 2], low[HD // 2 :]
        return a * cos + b * sin, b * cos - a * sin

    for h in range(2):
        rows = slice(h * HD, (h + 1) * HD)
        linv = linv_ref[0, h : h + 1, :]
        d_o = d_att_ref[rows, :].astype(F32)
        d_os = (d_o * linv).astype(BF)
        do_mask[h, rows, :] = d_os
        do_mask[h, (1 - h) * HD : (2 - h) * HD, :] = zero
        inner = col_sum(d_o * att_ref[rows, :].astype(F32)) * linv
        d_values = mm(d_os, e_ref[h], NT)
        out_ref[2, rows, :] = d_values.astype(BF)
        d_keys = jnp.zeros((HD, tokens), F32)
        d_queries = []
        for t in range(tokens // tile):
            cols = slice(t * tile, (t + 1) * tile)
            d_probs = mm(v_nat, do_mask[h, :, cols])
            d_s = (e_ref[h, :, cols].astype(F32) * (d_probs - inner[:, cols])).astype(BF)
            d_queries.append(mm(k_ref[rows, :], d_s))
            d_keys += mm(q_ref[rows, cols], d_s, NT)
        dq = jnp.concatenate(d_queries, axis=1) * HD**-0.5
        lead, trail = unrotate(dq)
        out_ref[0, h * HD : h * HD + HD // 2, :] = lead.astype(BF)
        out_ref[0, h * HD + HD // 2 : (h + 1) * HD, :] = trail.astype(BF)
        lead, trail = unrotate(d_keys)
        out_ref[1, h * HD : h * HD + HD // 2, :] = lead.astype(BF)
        out_ref[1, h * HD + HD // 2 : (h + 1) * HD, :] = trail.astype(BF)

    @pl.when(step == pl.num_programs(0) - 1)
    def _():
        swap_wait(give_ref, take_ref, send, recv)


def attend_back(qkv_t, att_t, d_att_t, e, linv, cos_t, sin_t, give):
    tokens = qkv_t.shape[1]
    width = HEADS * HD

    def part(k):
        return pl.BlockSpec((2 * HD, tokens), lambda i: (i + k * PAIRS, 0))

    return pl.pallas_call(
        attend_back_kernel,
        grid=(PAIRS,),
        in_specs=[
            part(0),
            part(1),
            part(2),
            part(0),
            part(0),
            pl.BlockSpec((2, tokens, tokens), lambda i: (i, 0, 0)),
            pl.BlockSpec((1, 8, tokens), lambda i: (i, 0, 0)),
            whole(cos_t.shape),
            whole(sin_t.shape),
            ANY,
        ],
        out_specs=[pl.BlockSpec((3, 2 * HD, tokens), lambda i: (0, i, 0)), ANY],
        out_shape=[
            jax.ShapeDtypeStruct((3, width, tokens), BF),
            jax.ShapeDtypeStruct(give.shape, give.dtype),
        ],
        scratch_shapes=[pltpu.VMEM((2, 2 * HD, tokens), BF)] + SEMS,
        compiler_params=params(collective_id=2),
        cost_estimate=pl.CostEstimate(
            flops=32 * tokens * tokens * width, bytes_accessed=36 << 20, transcendentals=0
        ),
        name="attend_back",
    )(qkv_t, qkv_t, qkv_t, att_t, d_att_t, e, linv, cos_t, sin_t, give)


def tail_kernel(tok_own, tok_rem, d_proj_ref, w_ref, dx_ref, vec_ref, own_ref, rem_ref, sums_ref):
    step = pl.program_id(0)
    steps = pl.num_programs(0)
    mult_one = vec_ref[0:1, :]
    gain_one = vec_ref[2:3, :]
    scale_one = vec_ref[3:4, :]
    d_act = mm(d_proj_ref[...], w_ref[...], TN)

    def finish(tok, out):
        n, rstd = norm_parts(tok[...].astype(F32))
        grad = dx_ref[...] + norm_pull(n, rstd, d_act * mult_one)
        out[...] = grad.astype(out.dtype)
        return col_sum(d_act), col_sum(d_act * n)

    @pl.when(step == 0)
    def _():
        shift, pull = finish(tok_rem, rem_ref)
        sums_ref[0:1, :] = shift
        sums_ref[1:2, :] = pull
        sums_ref[2:, :] = jnp.zeros((6, shift.shape[1]), F32)

    @pl.when(step == steps - 1)
    def _():
        shift, pull = finish(tok_own, own_ref)
        shift = sums_ref[0:1, :] + shift
        pull = sums_ref[1:2, :] + pull
        sums_ref[0:1, :] = shift
        sums_ref[1:2, :] = pull * gain_one
        sums_ref[2:3, :] = pull * (1.0 + scale_one)


def tail(tok_own, tok_rem, d_proj_t, w_qkv_t, dx, vec):
    half, width = tok_own.shape
    return pl.pallas_call(
        tail_kernel,
        grid=(2,),
        in_specs=[
            whole(tok_own.shape),
            whole(tok_rem.shape),
            pl.BlockSpec((3 * width, half), lambda i: (0, 1 - i)),
            whole(w_qkv_t.shape),
            pl.BlockSpec((half, width), lambda i: (1 - i, 0)),
            whole(vec.shape),
        ],
        out_specs=[whole((half, width)), whole((half, width)), whole((8, width))],
        out_shape=[
            jax.ShapeDtypeStruct((half, width), F32),
            jax.ShapeDtypeStruct((half, width), BF),
            jax.ShapeDtypeStruct((8, width), F32),
        ],
        compiler_params=params(),
        cost_estimate=pl.CostEstimate(
            flops=12 * half * width * width, bytes_accessed=20 << 20, transcendentals=0
        ),
        name="tail",
    )(tok_own, tok_rem, d_proj_t, w_qkv_t, dx, vec)


def weight_grad_kernel(act_ref, d_proj_ref, out_ref):
    out_ref[...] = mm(act_ref[...], d_proj_ref[...], NT).astype(BF)


def weight_grad(act_t, d_proj_t):
    width, tokens = act_t.shape
    cols = d_proj_t.shape[0]
    tile = 768
    return pl.pallas_call(
        weight_grad_kernel,
        grid=(cols // tile,),
        in_specs=[whole(act_t.shape), pl.BlockSpec((tile, tokens), lambda i: (i, 0))],
        out_specs=pl.BlockSpec((width, tile), lambda i: (0, i)),
        out_shape=jax.ShapeDtypeStruct((width, cols), BF),
        compiler_params=params(),
        cost_estimate=pl.CostEstimate(
            flops=2 * cols * width * tokens, bytes_accessed=12 << 20, transcendentals=0
        ),
        name="weight_grad",
    )(act_t, d_proj_t)


def gather_stages(links, ref):
    z, y, c, x = links.z, links.y, links.c, links.x

    def pair(mine, theirs, device):
        sem = links.take(2)

        def make(slot):
            return remote(slot(), slot(), links.sems.at[sem], links.sems.at[sem + 1], device)

        def wait():
            make(mine).wait_send()
            make(theirs).wait_recv()

        return (lambda: make(mine).start()), wait

    sem = links.take(2 * links.zs)

    def make(f, slot):
        block = ref.at[slot, :, :, x]
        return remote(
            block, block, links.sems.at[sem + f], links.sems.at[sem + links.zs + slot], links.at_z(f)
        )

    def far_start():
        for f in links.far:
            make(f, z).start()

    def far_wait():
        for f in links.far:
            make(f, z).wait_send()
            make(f, f).wait_recv()

    return [
        pair(lambda: ref.at[z, y, c, x], lambda: ref.at[z, y, 1 - c, x], links.core),
        pair(lambda: ref.at[z, y, :, x], lambda: ref.at[z, 1 - y, :, x], links.across),
        (far_start, far_wait),
        pair(lambda: ref.at[:, :, :, x], lambda: ref.at[:, :, :, 1 - x], links.facing),
    ]


def sum_stages(links, ref, take, far):
    swaps = [
        links.swap(lambda: ref, lambda k=k: take.at[k], device)
        for k, device in enumerate((links.core, links.across, links.facing))
    ]
    far_start, far_wait = links.spread(lambda f: ref, lambda slot: far.at[slot])

    def finish(k):
        swaps[k]().wait()
        ref[...] += take[k]

    def far_finish():
        far_wait()
        far[links.z] = ref[...]
        total = far[0]
        for f in range(1, links.zs):
            total += far[f]
        ref[...] = total

    return [
        (lambda: swaps[0]().start(), lambda: finish(0)),
        (lambda: swaps[1]().start(), lambda: finish(1)),
        (far_start, far_finish),
        (lambda: swaps[2]().start(), lambda: finish(2)),
    ]


def back_kernel(zs, split, ins, outs, scratch):
    (
        q_ref,
        k_ref,
        v_ref,
        att_ref,
        d_att_ref,
        e_ref,
        linv_ref,
        cos_ref,
        sin_ref,
        own_ref,
        give_ref,
        up_last_ref,
        up_one_ref,
        up_two_ref,
        down_last_ref,
        down_one_ref,
        down_two_ref,
        raw_up,
        raw_out,
        raw_down,
        mod_ref,
        sum_ref,
        act_in,
        w_in,
        tok_own_in,
        tok_rem_in,
        dx_in,
        vec_ref,
    ) = ins
    result, grad_ref, s_qkv, s_out, s_up, s_down, *small_outs = outs
    (
        do_mask,
        d_proj,
        sems,
        u_own,
        u_y,
        u_z,
        u_last,
        u_facing,
        w_own,
        w_core,
        w_y,
        w_z,
        w_last,
        w_facing,
        d_own,
        d_core,
        d_y,
        d_side,
        d_sum,
        d_z,
        d_last,
        d_facing,
        q_raws,
        q_cores,
        q_ys,
        q_zs,
        q_lasts,
        q_facings,
        g_send,
        g_take,
        early_take,
        early_far,
        late_take,
        late_far,
        mod_early,
        mod_late,
        sum_early,
        sum_late,
        act_ref,
        w_ref,
        tok_own,
        tok_rem,
        dx_ref,
        g_own,
    ) = scratch
    step = pl.program_id(0)
    tokens = q_ref.shape[1]
    width = act_ref.shape[0]
    half = tokens // 2
    cut = width // 2
    links = Links(sems, zs)
    x, y, z, c = links.x, links.y, links.z, links.c

    fetch = [
        links.local(lambda p=p: p[0], lambda p=p: p[1])
        for p in (
            (act_in, act_ref),
            (w_in, w_ref),
            (tok_own_in.at[x], tok_own),
            (tok_rem_in, tok_rem),
            (dx_in, dx_ref),
        )
    ]
    u_load = [
        links.local(lambda: up_last_ref, lambda: u_last.at[0]),
        links.local(lambda: up_one_ref.at[z], lambda: u_own.at[0, z]),
        links.local(lambda: up_two_ref.at[:, y], lambda: u_own.at[1]),
    ]
    u_to_y = links.swap(lambda: up_two_ref.at[:, 1 - y], lambda: u_y, links.across)
    u_far = [
        links.spread(
            lambda f, j=j: up_one_ref.at[f] if j == 0 else u_own.at[1, f],
            lambda slot, j=j: u_z.at[j, slot],
        )
        for j in range(2)
    ]
    u_to_facing = [
        links.swap(lambda j=j: u_last.at[j], lambda j=j: u_facing.at[j], links.facing)
        for j in range(3)
    ]
    raws = (raw_up, raw_out)
    w_keep = [
        links.local(lambda r=r: r.at[:, :, :, c], lambda k=k: w_own.at[k]) for k, r in enumerate(raws)
    ]
    w_to_core = [
        links.swap(lambda r=r: r.at[:, :, :, 1 - c], lambda k=k: w_core.at[k], links.core)
        for k, r in enumerate(raws)
    ]
    w_to_y = [
        links.swap(lambda k=k: w_own.at[k, :, :, 1 - y], lambda k=k: w_y.at[k], links.across)
        for k in range(2)
    ]
    w_far = [
        links.spread(lambda f, k=k: w_own.at[k, :, f, y], lambda slot, k=k: w_z.at[k, slot])
        for k in range(2)
    ]
    w_to_facing = [
        links.swap(lambda k=k: w_last.at[k], lambda k=k: w_facing.at[k], links.facing)
        for k in range(2)
    ]
    d_keep = links.local(lambda: raw_down.at[:, c], lambda: d_own)
    d_to_core = links.swap(lambda: raw_down.at[:, 1 - c], lambda: d_core, links.core)
    d_to_y = links.swap(lambda: d_own.at[1 - y], lambda: d_y, links.across)
    d_to_side = [
        links.swap(lambda: down_two_ref.at[1 - x], lambda: d_side.at[0], links.facing),
        links.swap(lambda: d_own.at[y, 1 - x], lambda: d_side.at[1], links.facing),
    ]
    d_load = [
        links.local(lambda: down_last_ref, lambda: d_last),
        links.local(lambda: down_one_ref, lambda: d_sum.at[0]),
        links.local(lambda: down_two_ref.at[x], lambda: d_sum.at[1]),
    ]
    d_far = [
        links.gather(
            lambda j=j: down_one_ref if j == 1 else d_sum.at[j - 1], lambda slot: d_z.at[slot], j
        )
        for j in range(1, zs)
    ]
    d_to_facing = links.swap(lambda: d_last, lambda: d_facing, links.facing)
    groups = range(len(split))
    q_to_core = [
        links.swap(lambda g=g: q_raws[g].at[:, :, 1 - c], lambda g=g: q_cores[g], links.core)
        for g in groups
    ]
    q_to_y = [
        links.swap(lambda g=g: q_cores[g].at[:, 1 - y], lambda g=g: q_ys[g], links.across)
        for g in groups
    ]
    q_far = [
        links.spread(lambda f, g=g: q_cores[g].at[f, y], lambda slot, g=g: q_zs[g].at[slot])
        for g in groups
    ]
    q_to_facing = [
        links.swap(lambda g=g: q_lasts[g], lambda g=g: q_facings[g], links.facing) for g in groups
    ]
    keep_out = links.local(lambda: own_ref, lambda: result.at[x])
    out_sem = links.take(2)

    def cross_out(slot):
        return remote(give_ref, result.at[slot], sems.at[out_sem], sems.at[out_sem + 1], links.facing)

    give_grad = links.swap(lambda: g_send, lambda: g_take, links.facing)
    keep_grad = links.local(lambda: g_own, lambda: grad_ref.at[x])
    put_grad = links.local(lambda: g_own, lambda: grad_ref.at[1 - x])
    early = [
        gather_stages(links, mod_early),
        sum_stages(links, sum_early, early_take, early_far),
    ]
    late = [gather_stages(links, mod_late), sum_stages(links, sum_late, late_take, late_far)]

    def begin(arrays, stage):
        for stages in arrays:
            stages[stage][0]()

    def end(arrays, stage):
        for stages in arrays:
            stages[stage][1]()

    def sum_far(own, taken):
        total = own.astype(F32)
        for f in links.far:
            total += taken(f).astype(F32)
        return total.astype(BF)

    def u_z_done(j):
        u_far[j][1]()
        u_last[j + 1] = sum_far(u_own[j, z], lambda f: u_z[j, f])
        u_to_facing[j + 1]().start()

    def u_done(j):
        u_to_facing[j]().wait()
        mine, other = u_last[j].astype(F32), u_facing[j].astype(F32)
        start = j * width
        s_up[:, start : start + cut] = jnp.where(x == 0, mine, other)
        s_up[:, start + cut : start + width] = jnp.where(x == 0, other, mine)

    def w_core_done(k):
        w_keep[k]().wait()
        w_to_core[k]().wait()
        for h, a, b in grid_of(2, zs, 2):
            w_own[k, h, a, b] = w_own[k, h, a, b] + w_core[k, h, a, b]

    def w_y_done(k):
        w_to_y[k]().wait()
        for h, a in grid_of(2, zs):
            w_own[k, h, a, y] = w_own[k, h, a, y] + w_y[k, h, a]
        w_far[k][0]()

    def w_z_done(k):
        w_far[k][1]()
        for h in range(2):
            w_last[k, h] = sum_far(w_own[k, h, z, y], lambda f: w_z[k, f, h])
        w_to_facing[k]().start()

    def w_done(k):
        w_to_facing[k]().wait()
        out, start = (s_up, (zs - 1) * width) if k == 0 else (s_out, 0)
        for h in range(2):
            out[:, start + h * cut : start + (h + 1) * cut] = w_last[k, h].astype(F32) + w_facing[
                k, h
            ].astype(F32)

    def q_core_done(g):
        q_to_core[g]().wait()
        for a, b in grid_of(zs, 2):
            q_cores[g][a, b] = q_cores[g][a, b] + q_raws[g][a, b, c]
        q_to_y[g]().start()

    def q_y_done(g):
        q_to_y[g]().wait()
        for a in range(zs):
            q_cores[g][a, y] = q_cores[g][a, y] + q_ys[g][a]
        q_far[g][0]()

    def q_z_done(g):
        q_far[g][1]()
        q_lasts[g][...] = sum_far(q_cores[g][z, y], lambda f: q_zs[g][f])
        q_to_facing[g]().start()

    def q_done(g):
        q_to_facing[g]().wait()
        total = q_lasts[g][...].astype(F32) + q_facings[g][...].astype(F32)
        first, size = split[g][0] * HD, (split[g][1] - split[g][0]) * HD
        for p in range(3):
            s_qkv[:, p * width + first : p * width + first + size] = total[:, p * size : (p + 1) * size]

    def weight_grad_of(g):
        first, size = split[g][0] * HD, (split[g][1] - split[g][0]) * HD
        for p in range(3):
            rows = slice(p * width + first, p * width + first + size)
            part = mm(act_ref[...], d_proj[rows, :], NT).astype(BF)
            q_raws[g][:, :, :, :, p * size : (p + 1) * size] = part.reshape(
                q_raws[g].shape[:4] + (size,)
            )
        q_to_core[g]().start()


    def due_00():
        greet(links.core, links.across, links.facing, *[links.at_z(f) for f in links.far])
        d_to_core().start()
        d_keep().start()
        for k in range(2):
            w_to_core[k]().start()
            w_keep[k]().start()
        u_far[0][0]()
        d_far[0][0]()
        u_to_y().start()
        d_to_side[0]().start()
        for load in u_load + d_load:
            load().start()
        mod_early[z, y, c, x] = mod_ref[...]
        sum_early[...] = sum_ref[...]
        begin(early, 0)
        keep_out().start()
        cross_out(x).start()
        for load in fetch:
            load().start()

    def due_01():
        d_keep().wait()
        d_to_core().wait()
        for b, h in grid_of(2, 2):
            d_own[b, h] = d_own[b, h] + d_core[b, h]
        d_to_y().start()
        end(early, 0)
        begin(early, 1)

    def due_10():
        w_core_done(0)
        w_core_done(1)
        w_to_y[0]().start()
        u_load[0]().wait()
        u_to_facing[0]().start()

    def due_11():
        u_load[2]().wait()
        u_to_y().wait()
        for a in range(zs):
            u_own[1, a] = u_own[1, a] + u_y[a]
        u_far[1][0]()
        d_load[2]().wait()
        d_to_side[0]().wait()
        d_sum[1] = d_sum[1] + d_side[0]
        d_far[1][0]()
        end(early, 1)
        begin(early, 2)

    def due_20():
        fetch[0]().wait()
        weight_grad_of(0)
        d_to_y().wait()
        for h in range(2):
            d_own[y, h] = d_own[y, h] + d_y[h]
        d_to_side[1]().start()
        w_to_y[1]().start()

    def due_21():
        q_core_done(0)
        w_y_done(0)

    def due_30():
        u_load[1]().wait()
        u_z_done(0)
        d_to_side[1]().wait()
        d_sum[2] = d_own[y, x] + d_side[1]
        d_far[2][0]()
        end(early, 2)
        begin(early, 3)

    def due_31():
        w_y_done(1)
        q_y_done(0)

    def due_40():
        weight_grad_of(1)
        u_z_done(1)
        end(early, 3)

    def due_41():
        q_core_done(1)
        w_z_done(0)
        u_done(0)
        u_done(1)

    def due_50():
        for load in d_load[0:2]:
            load().wait()
        for j in range(zs - 1):
            d_far[j][1]()

        @pl.when(z > 0)
        def _():
            d_last[...] = sum_far(d_sum[jnp.maximum(z - 1, 0)], lambda f: d_z[f])

        d_to_facing().start()

    def due_51():
        q_y_done(1)
        w_z_done(1)
        u_done(2)

    due = (
        (due_00, due_01),
        (due_10, due_11),
        (due_20, due_21),
        (due_30, due_31),
        (due_40, due_41),
        (due_50, due_51),
    )

    def do_due(h):
        for k in range(PAIRS):
            pl.when(step == k)(due[k][h])


    @pl.when(step < PAIRS)
    def _():
        tile = 256
        zero = jnp.zeros((HD, tokens), BF)
        v_nat = v_ref[...].T
        cos = cos_ref[...]
        sin = sin_ref[...]

        def put(part, h, value):
            low = value.astype(BF).astype(F32)
            a, b = low[0 : HD // 2], low[HD // 2 :]
            start = part * width + step * 2 * HD + h * HD
            d_proj[pl.ds(pl.multiple_of(start, 32), 32), :] = (a * cos + b * sin).astype(BF)
            d_proj[pl.ds(pl.multiple_of(start + 32, 32), 32), :] = (b * cos - a * sin).astype(BF)

        do_due(0)
        inners, keys, values, queries = [], [], [], [[], []]
        for h in range(2):
            rows = slice(h * HD, (h + 1) * HD)
            linv = linv_ref[0, h : h + 1, :]
            d_o = d_att_ref[rows, :].astype(F32)
            do_mask[h, rows, :] = (d_o * linv).astype(BF)
            do_mask[h, (1 - h) * HD : (2 - h) * HD, :] = zero
            inners.append(col_sum(d_o * att_ref[rows, :].astype(F32)) * linv)

        def ahead(h, cols):
            return mm(v_nat, do_mask[h, :, cols])

        def centre(h, cols, d_probs):
            rows = slice(h * HD, (h + 1) * HD)
            e = e_ref[h, :, cols]
            part = mm(do_mask[h, rows, cols], e, NT)
            if cols.start == 0:
                values.append(part)
            else:
                values[h] += part
            return (e.astype(F32) * (d_probs - inners[h][:, cols])).astype(BF)

        def behind(h, cols, d_s):
            rows = slice(h * HD, (h + 1) * HD)
            queries[h].append(mm(k_ref[rows, :], d_s))
            part = mm(q_ref[rows, cols], d_s, NT)
            if cols.start == 0:
                keys.append(part)
            else:
                keys[h] += part
            if cols.stop == tokens:
                put(0, h, jnp.concatenate(queries[h], axis=1) * HD**-0.5)
                put(1, h, keys[h])
                start = 2 * width + step * 2 * HD + h * HD
                d_proj[pl.ds(pl.multiple_of(start, HD), HD), :] = values[h].astype(BF)

        units = [(h, slice(t, t + tile)) for h in range(2) for t in range(0, tokens, tile)]
        coming = ahead(*units[0])
        for i, unit in enumerate(units):
            if i == len(units) // 2:
                do_due(1)
            here = coming
            if i + 1 < len(units):
                coming = ahead(*units[i + 1])
            d_s = centre(*unit, here)
            if i > 0:
                behind(*units[i - 1], held)
            held = d_s
        behind(*units[-1], held)


    def finish(tok, cols):
        d_act = mm(d_proj[:, cols], w_ref[...], TN)
        n, rstd = norm_parts(tok[...].astype(F32))
        grad = dx_ref[cols, :] + norm_pull(n, rstd, d_act * vec_ref[0:1, :])
        return grad, col_sum(d_act), col_sum(d_act * n)

    @pl.when(step == PAIRS)
    def _():
        for load in fetch[1:]:
            load().wait()
        grad, shift, pull = finish(tok_rem, slice(half, 2 * half))
        g_send[...] = grad.astype(BF)
        give_grad().start()
        weight_grad_of(2)
        q_z_done(0)
        q_core_done(2)
        grad, shift_own, pull_own = finish(tok_own, slice(0, half))
        g_own[...] = grad
        keep_grad().start()
        shift += shift_own
        pull += pull_own
        lines = width // 128
        mine = mod_late.at[z, y, c, x]
        mine[2 * lines :, :] = jnp.zeros((mod_late.shape[4] - 2 * lines, 128), BF)
        put_rows(mine, 0, shift)
        put_rows(mine, lines, pull * vec_ref[2:3, :])
        sum_late[lines:, :] = jnp.zeros((sum_late.shape[0] - lines, 128), F32)
        put_rows(sum_late, 0, pull * (1.0 + vec_ref[3:4, :]))
        begin(late, 0)
        q_z_done(1)
        end(late, 0)
        begin(late, 1)
        q_y_done(2)
        end(late, 1)
        begin(late, 2)
        for k in range(2):
            w_done(k)
        d_to_facing().wait()
        mine, other = d_last[...].astype(F32), d_facing[...].astype(F32)
        rows_half = mine.shape[0]
        s_down[0:rows_half, :] = jnp.where(x == 0, mine, other)
        s_down[rows_half:, :] = jnp.where(x == 0, other, mine)
        end(late, 2)
        begin(late, 3)
        keep_out().wait()
        cross_out(x).wait_send()
        cross_out(1 - x).wait_recv()
        q_done(0)
        q_done(1)
        q_z_done(2)
        end(late, 3)
        give_grad().wait()
        keep_grad().wait()
        g_own[...] = g_take[...].astype(F32)
        put_grad().start()
        q_done(2)
        put_grad().wait()
        for out, value in zip(small_outs, (mod_early, mod_late, sum_early, sum_late)):
            out[...] = value[...]


def back(ins, zs, ff):
    q, att, d_att, e, linv, cos_t, sin_t = ins[:7]
    mod, sums, vec = ins[-8], ins[-7], ins[-1]
    width, tokens = att.shape
    half = tokens // 2
    cut = width // 2
    rows = width // (4 * zs)
    down_rows = ff // (4 * zs)
    down_half = (down_rows // 2, width)
    split = ((0, 4), (4, 8), (8, HEADS))
    sizes = [3 * (b - a) * HD for a, b in split]
    last = PAIRS - 1

    def part(k):
        return pl.BlockSpec((2 * HD, tokens), lambda i: (jnp.minimum(i, last) + k * PAIRS, 0))

    def vm(*shape, kind=BF):
        return pltpu.VMEM(shape, kind)

    lines = width // 128
    mod_early = (zs, 2, 2, 2) + mod.shape
    mod_late = (zs, 2, 2, 2, round_up(2 * lines, 16), 128)
    sum_late = (round_up(lines, 8), 128)
    outs = [
        ((half, width), F32),
        ((rows, 3 * width), F32),
        ((rows, width), F32),
        ((rows, ff), F32),
        ((down_rows, width), F32),
        (mod_early, BF),
        (mod_late, BF),
        (sums.shape, F32),
        (sum_late, F32),
    ]
    outs[0] = ((2, half, width), F32)
    fetched = ins[-6:-1]
    in_specs = (
        [part(0), part(1), part(2), part(0), part(0)]
        + [
            pl.BlockSpec((2, tokens, tokens), lambda i: (jnp.minimum(i, last), 0, 0)),
            pl.BlockSpec((1, 8, tokens), lambda i: (jnp.minimum(i, last), 0, 0)),
            once(cos_t.shape),
            once(sin_t.shape),
        ]
        + [ANY] * (len(ins) - 15)
        + [once(mod.shape), once(sums.shape)]
        + [ANY] * 5
        + [once(vec.shape)]
    )
    out_specs = [ANY, ANY] + [once(shape) for shape, _ in outs[1:]]
    out_shape = [jax.ShapeDtypeStruct((2, half, width), BF)] + [
        jax.ShapeDtypeStruct(*o) for o in outs
    ]
    scratch = [
        vm(2, 2 * HD, tokens),
        vm(3 * width, tokens),
        pltpu.SemaphoreType.DMA((250,)),
        vm(2, zs, rows, cut),
        vm(zs, rows, cut),
        vm(2, zs, rows, cut),
        vm(3, rows, cut),
        vm(3, rows, cut),
        vm(2, 2, zs, 2, rows, cut),
        vm(2, 2, zs, 2, rows, cut),
        vm(2, 2, zs, rows, cut),
        vm(2, zs, 2, rows, cut),
        vm(2, 2, rows, cut),
        vm(2, 2, rows, cut),
        vm(2, 2, *down_half),
        vm(2, 2, *down_half),
        vm(2, *down_half),
        vm(2, *down_half),
        vm(zs - 1, *down_half),
        vm(zs, *down_half),
        vm(*down_half),
        vm(*down_half),
        [vm(zs, 2, 2, rows, s) for s in sizes],
        [vm(zs, 2, rows, s) for s in sizes],
        [vm(zs, rows, s) for s in sizes],
        [vm(zs, rows, s) for s in sizes],
        [vm(rows, s) for s in sizes],
        [vm(rows, s) for s in sizes],
        vm(half, width),
        vm(half, width),
        vm(3, *sums.shape, kind=F32),
        vm(zs, *sums.shape, kind=F32),
        vm(3, *sum_late, kind=F32),
        vm(zs, *sum_late, kind=F32),
        vm(*mod_early),
        vm(*mod_late),
        vm(*sums.shape, kind=F32),
        vm(*sum_late, kind=F32),
    ]
    scratch += [vm(*a.shape[-2:], kind=a.dtype) for a in fetched]
    scratch += [vm(half, width, kind=F32)]
    flat, tree = jax.tree.flatten(scratch)
    n_in, n_out = len(in_specs), len(out_specs)

    def kernel(*refs):
        back_kernel(
            zs,
            split,
            refs[:n_in],
            refs[n_in : n_in + n_out],
            jax.tree.unflatten(tree, refs[n_in + n_out :]),
        )

    return pl.pallas_call(
        kernel,
        grid=(PAIRS + 1,),
        in_specs=in_specs,
        out_specs=out_specs,
        out_shape=out_shape,
        scratch_shapes=flat,
        compiler_params=params(62, collective_id=5),
        cost_estimate=pl.CostEstimate(
            flops=32 * tokens * tokens * width + 12 * tokens * width * width,
            bytes_accessed=60 << 20,
            transcendentals=0,
        ),
        name="back",
    )(q, q, q, att, d_att, e, linv, cos_t, sin_t, *ins[7:])


def time_features(time_steps, pair_count):
    frequency = jnp.exp(-math.log(10000.0) * jnp.arange(pair_count, dtype=F32) / pair_count)
    angles = time_steps.astype(F32)[:, None] * frequency[None, :]
    return jnp.concatenate([jnp.cos(angles), jnp.sin(angles)], axis=-1)


def per_device(
    tokens,
    cotangent,
    time_index,
    span_starts,
    span_lengths,
    w_ada,
    b_ada,
    gain_one,
    w_qkv,
    w_out,
    gain_two,
    w_up,
    b_up,
    w_down,
    b_down,
):
    seqs_dev, half, width = tokens.shape
    length = 2 * half
    rank = lax.axis_index("seq")
    swap = [(0, 1), (1, 0)]

    def pick(x, i):
        return lax.dynamic_index_in_dim(x, i, 0, keepdims=False)

    time_own = lax.dynamic_slice_in_dim(time_index, rank, 1)
    dp, dps = lax.axis_index("dp"), lax.axis_size("dp")
    ff = w_up.shape[1]
    zs = dps // 4
    linked = zs == 4 and dps == 16 and width % (64 * zs) == 0 and ff == zs * width

    act_t, qkv_t, w_qkv_t, tok_rem, vec_one, vec_two, span, cos_t, sin_t = project(
        tokens, time_index, span_starts, span_lengths, w_ada, b_ada, (gain_one, gain_two), b_down, w_qkv
    )
    att_t, e, linv, cot_rem = attend(qkv_t, cotangent)
    if linked:
        out_own, out_rem, dx, d_att_t, raw_out, raw_up, raw_down, *partial, mod, sums = middle_links(
            att_t, tokens, tok_rem, cotangent, cot_rem, span, vec_two, b_up[None], w_out, w_up, w_down, zs
        )
        ins = (qkv_t, att_t, d_att_t, e, linv, cos_t, sin_t, out_own, out_rem, *partial)
        ins += (raw_up, raw_out, raw_down, mod, sums, act_t, w_qkv_t, tokens, tok_rem, dx, vec_one)
        output, grad_tokens, *shards, mod_early, mod_late, sum_early, sum_late = back(ins, zs, ff)
        mod_early = mod_early.reshape(2 * dps, -1).astype(F32)
        mod_late = mod_late.reshape(2 * dps, -1).astype(F32)
        d_mod_all = jnp.concatenate([mod_late[:, : 2 * width], mod_early[:, : 4 * width]], axis=1)
        time_all = 32.0 * mod_early[:, 4 * width] + mod_early[:, 4 * width + 1]
        small = jnp.concatenate(
            [sum_late.reshape(-1)[:width], sum_early.reshape(-1)[: 2 * width + ff]]
        )
    else:
        tok_own, cot_own = pick(tokens, rank), pick(cotangent, rank)
        out_own, out_rem, dx, d_att_t, g_out, g_up, g_down, g_bup, sums_two = middle(
            att_t, tok_own, tok_rem, cot_own, cot_rem, span, vec_two, b_up[None], w_out, w_up, w_down
        )
        d_proj, out_back = attend_back(qkv_t, att_t, d_att_t, e, linv, cos_t, sin_t, out_rem)
        d_proj_t = d_proj.reshape(3 * width, length)
        g_own, g_rem, sums_one = tail(tok_own, tok_rem, d_proj_t, w_qkv_t, dx, vec_one)
        g_qkv = weight_grad(act_t, d_proj_t)

        def spread(own, other):
            first = jnp.where(rank == 0, own, other)
            second = jnp.where(rank == 0, other, own)
            return jnp.stack([first, second])

        output = spread(out_own, out_back)
        grad_tokens = spread(g_own, lax.ppermute(g_rem, "seq", swap).astype(F32))
        shards = [
            lax.psum(lax.psum_scatter(g, "dp", scatter_dimension=0, tiled=True), "seq").astype(F32)
            for g in (g_qkv, g_out, g_up, g_down)
        ]
        d_mod = jnp.concatenate([sums_one[:2].reshape(-1), sums_two[:4].reshape(-1)])
        small = jnp.concatenate([sums_one[2], sums_two[4], sums_two[5], g_bup[0]])
        d_mod_all = lax.all_gather(d_mod, ("dp", "seq"))
        time_all = lax.all_gather(time_own[0].astype(F32), ("dp", "seq"))
        small = lax.psum(small, ("dp", "seq"))

    def mine(x, axis=0):
        size = x.shape[axis] // dps
        return lax.dynamic_slice_in_dim(x, dp * size, size, axis)

    features = jax.nn.silu(time_features(time_all, w_ada.shape[0] // 2))
    s_w_ada = jnp.dot(mine(features, 1).T, d_mod_all, precision=lax.Precision.HIGHEST)
    s_b_ada = jnp.sum(mine(d_mod_all, 1), axis=0)
    s_gain_one = mine(small[:width])
    s_gain_two = mine(small[width : 2 * width])
    s_b_down = mine(small[2 * width : 3 * width])
    s_b_up = mine(small[3 * width :])
    s_qkv, s_out, s_up, s_down = shards

    return (
        output,
        grad_tokens,
        s_w_ada,
        s_b_ada,
        s_gain_one,
        s_qkv,
        s_out,
        s_gain_two,
        s_up,
        s_b_up,
        s_down,
        s_b_down,
    )


def solution(mesh):
    rows = P("dp", "seq", None)
    return jax.shard_map(
        per_device,
        mesh=mesh,
        in_specs=(rows, rows, P("dp"), P("dp"), P("dp")) + (P(),) * 10,
        out_specs=(
            rows,
            rows,
            P("dp", None),
            P("dp"),
            P("dp"),
            P("dp", None),
            P("dp", None),
            P("dp"),
            P("dp", None),
            P("dp"),
            P("dp", None),
            P("dp"),
        ),
        check_vma=False,
    )
```

```python
import functools
import math

import jax
import jax.numpy as jnp
import numpy as np
from jax import lax
from jax.experimental import pallas as pl
from jax.experimental.pallas import tpu as pltpu
from jax.sharding import PartitionSpec as P

HEADS = 12
HD = 64
PAIRS = HEADS // 2
NORM_EPS = 1e-05
LOG2E = math.log2(math.e)
BF = jnp.bfloat16
F32 = jnp.float32
MIB = 1 << 20

NN = (((1,), (0,)), ((), ()))
NT = (((1,), (1,)), ((), ()))
TN = (((0,), (0,)), ((), ()))


def mm(a, b, dims=NN):
    return lax.dot_general(a, b, dims, preferred_element_type=F32)


def norm_parts(x):
    centre = x - jnp.mean(x, axis=-1, keepdims=True)
    rstd = lax.rsqrt(jnp.mean(centre * centre, axis=-1, keepdims=True) + NORM_EPS)
    return centre * rstd, rstd


def norm_pull(n, rstd, dn):
    return rstd * (
        dn - jnp.mean(dn, axis=-1, keepdims=True) - n * jnp.mean(dn * n, axis=-1, keepdims=True)
    )


def col_sum(x):
    return jnp.sum(x, axis=0, keepdims=True)


def rows_of(size, index):
    return pl.ds(pl.multiple_of(index * size, size), size)


def params(mib=56, collective_id=None):
    if collective_id is None:
        return pltpu.CompilerParams(vmem_limit_bytes=mib * MIB)
    return pltpu.CompilerParams(
        vmem_limit_bytes=mib * MIB, collective_id=collective_id, has_side_effects=True
    )


def whole(shape):
    zeros = (0,) * len(shape)
    return pl.BlockSpec(shape, lambda *_: zeros)


MESH = pl.DeviceIdType.MESH
ANY = pl.BlockSpec(memory_space=pl.ANY)
SEMS = [pltpu.SemaphoreType.DMA, pltpu.SemaphoreType.DMA]


def greet(*partners):
    barrier = pltpu.get_barrier_semaphore()
    for partner in partners:
        pl.semaphore_signal(barrier, inc=1, device_id=partner, device_id_type=MESH)
    pl.semaphore_wait(barrier, len(partners))


def remote(src, dst, send, recv, device):
    return pltpu.make_async_remote_copy(
        src_ref=src, dst_ref=dst, send_sem=send, recv_sem=recv, device_id=device, device_id_type=MESH
    )


def seq_partner():
    return (lax.axis_index("dp"), 1 - lax.axis_index("seq"))


def swap_start(src, dst, send, recv):
    partner = seq_partner()
    greet(partner)
    remote(src, dst, send, recv, partner).start()


def swap_wait(src, dst, send, recv):
    remote(src, dst, send, recv, seq_partner()).wait()


class Links:
    def __init__(self, sems, zs):
        self.sems, self.used, self.zs = sems, 0, zs
        dp, self.x = lax.axis_index("dp"), lax.axis_index("seq")
        self.z, self.y, self.c = dp // 4, lax.rem(dp // 2, 2), lax.rem(dp, 2)
        self.core = (dp + 1 - 2 * self.c, self.x)
        self.across = (dp + 2 - 4 * self.y, self.x)
        self.facing = (dp, 1 - self.x)
        self.far = [lax.rem(self.z + k, zs) for k in range(1, zs)]
        self.upper, self.lower = self.z // 2, lax.rem(self.z, 2)
        self.near = self.at_z(2 * self.upper + 1 - self.lower)
        self.beyond = self.at_z(2 * (1 - self.upper) + self.lower)

    def at_z(self, f):
        return (f * 4 + 2 * self.y + self.c, self.x)

    def take(self, count):
        self.used += count
        return self.used - count

    def local(self, src, dst):
        sem = self.take(1)
        return lambda: pltpu.make_async_copy(src(), dst(), self.sems.at[sem])

    def swap(self, src, dst, device):
        sem = self.take(2)
        return lambda: remote(src(), dst(), self.sems.at[sem], self.sems.at[sem + 1], device)

    def spread(self, src, dst):
        sem = self.take(2 * self.zs)

        def make(f, slot):
            return remote(
                src(f), dst(slot), self.sems.at[sem + f], self.sems.at[sem + self.zs + slot], self.at_z(f)
            )

        def start():
            for f in self.far:
                make(f, self.z).start()

        def wait():
            for f in self.far:
                make(f, self.z).wait_send()
                make(f, f).wait_recv()

        return start, wait

    def to_goal(self, src, dst, goal):
        upper, lower = goal // 2, goal % 2
        near = self.swap(src, lambda: dst().at[0], self.near)
        beyond = self.swap(src, lambda: dst().at[1], self.beyond)
        on_side = self.lower == lower

        def start():
            pl.when(self.lower != lower)(lambda: near().start())

        def middle():
            pl.when(self.lower != lower)(lambda: near().wait_send())

            @pl.when(on_side)
            def _():
                near().wait_recv()
                src()[...] = src()[...] + dst()[0]
                pl.when(self.upper != upper)(lambda: beyond().start())

        def finish():
            pl.when(on_side & (self.upper != upper))(lambda: beyond().wait_send())

            @pl.when(on_side & (self.upper == upper))
            def _():
                beyond().wait_recv()
                src()[...] = src()[...] + dst()[1]

        return start, middle, finish


def grid_of(*sizes):
    return [()] if not sizes else [(i,) + r for i in range(sizes[0]) for r in grid_of(*sizes[1:])]


def round_up(value, unit):
    return -(-value // unit) * unit


def early_mod_rows(width):
    return round_up(4 * width // 128 + 1, 16)


def early_sum_rows(width, ff):
    return round_up((2 * width + ff) // 128, 8)


def put_rows(ref, start, row):
    for k in range(row.shape[1] // 128):
        ref[start + k : start + k + 1, :] = row[:, k * 128 : (k + 1) * 128].astype(ref.dtype)


def once(shape):
    zeros = (0,) * len(shape)
    return pl.BlockSpec(shape, lambda *_: zeros, pipeline_mode=pl.Buffered(1))


def split_three(x):
    parts = []
    for _ in range(3):
        low = x.astype(BF)
        parts.append(low)
        x = x - low.astype(F32)
    return parts


def features_of(angles, is_sin):
    raw = jnp.where(is_sin, jnp.sin(angles), jnp.cos(angles))
    return raw / (1.0 + jnp.exp(-raw))


def project_kernel(
    time_ref,
    start_ref,
    extent_ref,
    tokens_ref,
    cos_ref,
    sin_ref,
    w_ada_ref,
    b_ada_ref,
    gain_one_ref,
    gain_two_ref,
    b_down_ref,
    w_ref,
    act_ref,
    out_ref,
    w_t_ref,
    rem_ref,
    vec_one_ref,
    vec_two_ref,
    span_ref,
    cos_out,
    sin_out,
    own,
    rem,
    w_t,
    qkv,
    sems,
):
    step = pl.program_id(0)
    half, width = own.shape
    rows = w_t_ref.shape[0]
    tile = 128
    chunk = half // 2
    x = lax.axis_index("seq")
    keep = pltpu.make_async_copy(tokens_ref.at[x], own, sems.at[0])
    cross = [
        remote(
            tokens_ref.at[1 - x, k * chunk : (k + 1) * chunk],
            rem.at[k * chunk : (k + 1) * chunk],
            sems.at[1 + k],
            sems.at[3 + k],
            seq_partner(),
        )
        for k in range(2)
    ]
    spans = (slice(0, half), slice(half, half + chunk), slice(half + chunk, 2 * half))
    store = [
        pltpu.make_async_copy(qkv.at[:, span], out_ref.at[:, span], sems.at[5 + k])
        for k, span in enumerate(spans)
    ]

    def norm(src, first, size, start):
        scale, shift = vec_one_ref[0:1, :], vec_one_ref[1:2, :]
        for t in range(0, size, tile):
            n, _ = norm_parts(src[first + t : first + t + tile, :].astype(F32))
            act_ref[:, start + t : start + t + tile] = (n * scale + shift).astype(BF).T

    @pl.when(step == 0)
    def _():
        greet(seq_partner())
        for copy in cross:
            copy.start()
        keep.start()
        pairs = w_ada_ref.shape[0] // 2
        time = time_ref[x]
        lane = lax.broadcasted_iota(jnp.int32, (8, 2 * pairs), 1)
        place = jnp.where(lane < pairs, lane, lane - pairs).astype(F32)
        frequency = jnp.exp(-math.log(10000.0) * place / pairs)
        cond = features_of(time.astype(F32) * frequency, lane >= pairs)
        modulation = b_ada_ref[...].reshape(1, 6 * width)
        for part in split_three(cond):
            modulation = modulation + mm(part, w_ada_ref[...])[0:1, :]
        pieces = [modulation[:, k * width : (k + 1) * width] for k in range(6)]
        shift_one, scale_one, gate_one, shift_two, scale_two, gate_two = pieces
        gain_one, gain_two = (ref[...].reshape(1, width) for ref in (gain_one_ref, gain_two_ref))
        zeros = jnp.zeros((1, width), F32)
        first = (gain_one * (1.0 + scale_one), shift_one, gain_one, scale_one)
        for k, row in enumerate(first + (zeros,) * 4):
            vec_one_ref[k : k + 1, :] = row
        lanes = lax.broadcasted_iota(jnp.int32, (1, width), 1)
        stamp = jnp.where(lanes == 0, time // 32, jnp.where(lanes == 1, lax.rem(time, 32), 0))
        second = (
            gate_one,
            gain_two * (1.0 + scale_two),
            shift_two,
            gate_two,
            b_down_ref[...].reshape(1, width),
            gain_two,
            scale_two,
            stamp.astype(F32),
        )
        for k, row in enumerate(second):
            vec_two_ref[k : k + 1, :] = row
        begin, end = start_ref[x], start_ref[x] + extent_ref[x]
        index = lax.broadcasted_iota(jnp.int32, (half, 1), 0)
        for part, where in enumerate((x, 1 - x)):
            place = index + where * half
            inside = (place >= begin) & (place < end)
            span_ref[part * half : (part + 1) * half, :] = jnp.where(inside, 2.0, 0.5)
            cos_out[:, part * half : (part + 1) * half] = cos_ref[where]
            sin_out[:, part * half : (part + 1) * half] = sin_ref[where]
        keep.wait()
        norm(own, 0, half, 0)

    def rotated(proj, block, cols, factor):
        cos, sin = cos_out[:, cols] * factor, sin_out[:, cols] * factor
        parts = []
        for h in range(rows // HD):
            a = proj[h * HD : h * HD + HD // 2]
            b = proj[h * HD + HD // 2 : (h + 1) * HD]
            parts += [(a * cos - b * sin).astype(BF), (b * cos + a * sin).astype(BF)]
        qkv[block, cols] = jnp.concatenate(parts, axis=0)

    @pl.when(step < 6)
    def _():
        block = rows_of(rows, step)
        flipped = w_ref[...].T
        w_t[block, :] = flipped
        w_t_ref[...] = flipped
        proj = mm(flipped, act_ref[:, spans[0]])

        @pl.when(step < 4)
        def _():
            rotated(proj, block, spans[0], jnp.where(step < 2, HD**-0.5, 1.0))

        @pl.when(step >= 4)
        def _():
            qkv[block, spans[0]] = proj.astype(BF)

    for k in range(2):

        @pl.when(step == 6 + k)
        def _(k=k):
            store[k].start()
            cross[k].wait()
            got = slice(k * chunk, (k + 1) * chunk)
            rem_ref[got, :] = rem[got, :]
            norm(rem, k * chunk, chunk, half + k * chunk)
            cols = spans[1 + k]
            for turn in range(6):
                block = slice(turn * rows, (turn + 1) * rows)
                proj = mm(w_t[block, :], act_ref[:, cols])
                if turn < 4:
                    rotated(proj, block, cols, HD**-0.5 if turn < 2 else 1.0)
                else:
                    qkv[block, cols] = proj.astype(BF)
            if k == 1:
                store[2].start()
                for copy in store:
                    copy.wait()


def rotary_constants(length):
    angles = np.arange(length, dtype=np.float32)[None, :] * np.exp(
        -math.log(10000.0) * np.arange(HD // 2, dtype=np.float32) / np.float32(HD // 2)
    ).astype(np.float32)[:, None]
    angles = angles.reshape(HD // 2, 2, length // 2).transpose(1, 0, 2).astype(np.float64)
    return np.cos(angles).astype(np.float32), np.sin(angles).astype(np.float32)


def project(tokens, time_index, span_starts, span_lengths, w_ada, b_ada, gains, b_down, w_qkv):
    _, half, width = tokens.shape
    length = 2 * half
    blk = width // 2
    cos_all, sin_all = rotary_constants(length)
    smem = pl.BlockSpec(memory_space=pltpu.SMEM)
    outs = [
        ((width, length), BF),
        ((3 * width, length), BF),
        ((3 * width, width), BF),
        ((half, width), BF),
        ((8, width), F32),
        ((8, width), F32),
        ((length, 1), F32),
        ((HD // 2, length), F32),
        ((HD // 2, length), F32),
    ]
    out_specs = [once(shape) for shape, _ in outs]
    out_specs[1] = ANY
    out_specs[2] = pl.BlockSpec((blk, width), lambda i: (jnp.minimum(i, 5), 0))
    rows = [b_ada, *gains, b_down]
    return pl.pallas_call(
        project_kernel,
        grid=(8,),
        in_specs=[smem, smem, smem, ANY, once(cos_all.shape), once(sin_all.shape), once(w_ada.shape)]
        + [once(r.shape) for r in rows]
        + [pl.BlockSpec((width, blk), lambda i: (0, jnp.minimum(i, 5)))],
        out_specs=out_specs,
        out_shape=[jax.ShapeDtypeStruct(*o) for o in outs],
        scratch_shapes=[
            pltpu.VMEM((half, width), BF),
            pltpu.VMEM((half, width), BF),
            pltpu.VMEM((3 * width, width), BF),
            pltpu.VMEM((3 * width, length), BF),
            pltpu.SemaphoreType.DMA((8,)),
        ],
        compiler_params=params(collective_id=6),
        cost_estimate=pl.CostEstimate(
            flops=6 * length * width * width, bytes_accessed=20 << 20, transcendentals=0
        ),
        name="project",
    )(time_index, span_starts, span_lengths, tokens, cos_all, sin_all, w_ada, *rows, w_qkv)


def attend_kernel(
    q_ref, k_ref, v_ref, cot_ref, att_ref, e_ref, linv_ref, cot_rem, q_mask, v_ext, send, recv
):
    step = pl.program_id(0)
    cot_send = cot_ref.at[1 - lax.axis_index("seq")]

    @pl.when(step == 0)
    def _():
        swap_start(cot_send, cot_rem, send, recv)

    tokens = q_ref.shape[1]
    tile = 256
    zero = jnp.zeros((HD, tokens), BF)
    k_nat = k_ref[...].T
    q_mask[0, 0:HD, :] = q_ref[0:HD, :]
    q_mask[0, HD:, :] = zero
    q_mask[1, 0:HD, :] = zero
    q_mask[1, HD:, :] = q_ref[HD:, :]
    for h in range(2):
        v_ext[h, 0:HD, :] = v_ref[h * HD : (h + 1) * HD, :]
        v_ext[h, HD:, :] = jnp.ones((16, tokens), BF)
    def score(h, cols):
        return mm(k_nat, q_mask[h, :, cols])

    def soften(h, cols, s):
        e_ref[h, :, cols] = jnp.exp(s - jnp.max(s, axis=0, keepdims=True)).astype(BF)

    def mix(h, cols):
        mixed = mm(v_ext[h], e_ref[h, :, cols])
        linv = 1.0 / mixed[HD : HD + 1, :]
        linv_ref[0, h : h + 1, cols] = linv
        att_ref[h * HD : (h + 1) * HD, cols] = (mixed[0:HD, :] * linv).astype(BF)

    units = [(h, slice(t, t + tile)) for t in range(0, tokens, tile) for h in range(2)]
    coming = score(*units[0])
    for i, unit in enumerate(units):
        here = coming
        if i + 1 < len(units):
            coming = score(*units[i + 1])
        soften(*unit, here)
        if i > 0:
            mix(*units[i - 1])
    mix(*units[-1])

    @pl.when(step == pl.num_programs(0) - 1)
    def _():
        swap_wait(cot_send, cot_rem, send, recv)


def attend(qkv_t, cotangent):
    tokens = qkv_t.shape[1]
    width = HEADS * HD

    def part(k):
        return pl.BlockSpec((2 * HD, tokens), lambda i: (i + k * PAIRS, 0))

    return pl.pallas_call(
        attend_kernel,
        grid=(PAIRS,),
        in_specs=[part(0), part(1), part(2), ANY],
        out_specs=[
            part(0),
            pl.BlockSpec((2, tokens, tokens), lambda i: (i, 0, 0)),
            pl.BlockSpec((1, 8, tokens), lambda i: (i, 0, 0)),
            ANY,
        ],
        out_shape=[
            jax.ShapeDtypeStruct((width, tokens), BF),
            jax.ShapeDtypeStruct((HEADS, tokens, tokens), BF),
            jax.ShapeDtypeStruct((PAIRS, 8, tokens), F32),
            jax.ShapeDtypeStruct(cotangent.shape[1:], BF),
        ],
        scratch_shapes=[
            pltpu.VMEM((2, 2 * HD, tokens), BF),
            pltpu.VMEM((2, HD + 16, tokens), BF),
        ]
        + SEMS,
        compiler_params=params(collective_id=1),
        cost_estimate=pl.CostEstimate(
            flops=16 * tokens * tokens * width,
            bytes_accessed=30 << 20,
            transcendentals=HEADS * tokens * tokens,
        ),
        name="attend",
    )(qkv_t, qkv_t, qkv_t, cotangent)


def gelu_both(u):
    c = math.sqrt(2.0 / math.pi)
    u2 = u * u
    th = jnp.tanh(u * (c + (c * 0.044715) * u2))
    half = 0.5 * (1.0 + th)
    value = u * half
    slope = half + (0.5 * u) * (1.0 - th * th) * (c + (3.0 * c * 0.044715) * u2)
    return value, slope


def middle_kernel(
    att_ref,
    tok_own,
    tok_rem,
    cot_own,
    cot_rem,
    span_ref,
    vec_ref,
    b_up_ref,
    w_out_ref,
    w_up_ref,
    w_down_ref,
    out_own,
    out_rem,
    dx_ref,
    d_att_ref,
    g_out_ref,
    g_up_ref,
    g_down_ref,
    g_bup_ref,
    sums_ref,
    branch,
    x_one,
    act_two,
    d_down,
    down_acc,
    d_act,
    d_branch,
):
    step = pl.program_id(0)
    steps = pl.num_programs(0)
    tokens = att_ref.shape[1]
    half = tokens // 2
    tile = 256
    per_half = half // tile
    gate_one = vec_ref[0:1, :]
    mult_two = vec_ref[1:2, :]
    shift_two = vec_ref[2:3, :]
    gate_two = vec_ref[3:4, :]
    b_down = vec_ref[4:5, :]
    gain_two = vec_ref[5:6, :]
    scale_two = vec_ref[6:7, :]

    @pl.when(step == 0)
    def _():
        for part, (tok, cot) in enumerate(((tok_own, cot_own), (tok_rem, cot_rem))):
            for t in range(per_half):
                src = slice(t * tile, (t + 1) * tile)
                dst = slice(part * half + t * tile, part * half + (t + 1) * tile)
                br = mm(att_ref[:, dst], w_out_ref[...], TN)
                branch[dst, :] = br
                x = tok[src, :].astype(F32) + gate_one * br
                x_one[dst, :] = x
                n, _ = norm_parts(x)
                act_two[dst, :] = (n * mult_two + shift_two).astype(BF)
                grad_out = cot[src, :].astype(F32) * span_ref[dst, :]
                d_down[dst, :] = (gate_two * grad_out).astype(BF)

    up = mm(act_two[...], w_up_ref[...]) + b_up_ref[...]
    value, slope = gelu_both(up)
    hidden = value.astype(BF)
    d_hidden = mm(d_down[...], w_down_ref[...], NT)
    d_up_full = slope * d_hidden
    d_up = d_up_full.astype(BF)
    g_bup_ref[...] = col_sum(d_up.astype(F32))
    down_part = mm(hidden, w_down_ref[...])
    d_act_part = mm(d_up, w_up_ref[...], NT)
    g_down_ref[...] = mm(hidden, d_down[...], TN).astype(BF)
    g_up_ref[...] = mm(act_two[...], d_up, TN).astype(BF)

    @pl.when(step == 0)
    def _():
        down_acc[...] = down_part
        d_act[...] = d_act_part

    @pl.when(step > 0)
    def _():
        down_acc[...] += down_part
        d_act[...] += d_act_part

    @pl.when(step == steps - 1)
    def _():
        zero = jnp.zeros((1, gate_one.shape[1]), F32)
        s_gate_two, s_shift, s_pull, s_gate_one, s_bdown = zero, zero, zero, zero, zero
        for part, (cot, out) in enumerate(((cot_own, out_own), (cot_rem, out_rem))):
            for t in range(per_half):
                src = slice(t * tile, (t + 1) * tile)
                dst = slice(part * half + t * tile, part * half + (t + 1) * tile)
                x = x_one[dst, :]
                down = down_acc[dst, :] + b_down
                out[src, :] = (x + gate_two * down).astype(BF)
                grad_out = cot[src, :].astype(F32) * span_ref[dst, :]
                s_gate_two += col_sum(grad_out * down)
                s_bdown += col_sum(d_down[dst, :].astype(F32))
                n, rstd = norm_parts(x)
                da = d_act[dst, :]
                s_shift += col_sum(da)
                s_pull += col_sum(da * n)
                dx = grad_out + norm_pull(n, rstd, da * mult_two)
                dx_ref[dst, :] = dx
                s_gate_one += col_sum(dx * branch[dst, :])
                d_branch[dst, :] = (gate_one * dx).astype(BF)
        sums_ref[0:1, :] = s_gate_one
        sums_ref[1:2, :] = s_shift
        sums_ref[2:3, :] = s_pull * gain_two
        sums_ref[3:4, :] = s_gate_two
        sums_ref[4:5, :] = s_pull * (1.0 + scale_two)
        sums_ref[5:6, :] = s_bdown
        sums_ref[6:8, :] = jnp.zeros((2, gate_one.shape[1]), F32)
        g_out_ref[...] = mm(att_ref[...], d_branch[...]).astype(BF)
        d_att_ref[...] = mm(w_out_ref[...], d_branch[...], NT).astype(BF)


def middle(att_t, tok_own, tok_rem, cot_own, cot_rem, span, vec, b_up, w_out, w_up, w_down):
    width, tokens = att_t.shape
    half = tokens // 2
    ff = w_up.shape[1]
    tile = 512
    return pl.pallas_call(
        middle_kernel,
        grid=(ff // tile,),
        in_specs=[
            whole(att_t.shape),
            whole(tok_own.shape),
            whole(tok_rem.shape),
            whole(cot_own.shape),
            whole(cot_rem.shape),
            whole(span.shape),
            whole(vec.shape),
            pl.BlockSpec((1, tile), lambda i: (0, i)),
            whole(w_out.shape),
            pl.BlockSpec((width, tile), lambda i: (0, i)),
            pl.BlockSpec((tile, width), lambda i: (i, 0)),
        ],
        out_specs=[
            whole((half, width)),
            whole((half, width)),
            whole((tokens, width)),
            whole((width, tokens)),
            whole((width, width)),
            pl.BlockSpec((width, tile), lambda i: (0, i)),
            pl.BlockSpec((tile, width), lambda i: (i, 0)),
            pl.BlockSpec((1, tile), lambda i: (0, i)),
            whole((8, width)),
        ],
        out_shape=[
            jax.ShapeDtypeStruct((half, width), BF),
            jax.ShapeDtypeStruct((half, width), BF),
            jax.ShapeDtypeStruct((tokens, width), F32),
            jax.ShapeDtypeStruct((width, tokens), BF),
            jax.ShapeDtypeStruct((width, width), BF),
            jax.ShapeDtypeStruct((width, ff), BF),
            jax.ShapeDtypeStruct((ff, width), BF),
            jax.ShapeDtypeStruct((1, ff), F32),
            jax.ShapeDtypeStruct((8, width), F32),
        ],
        scratch_shapes=[
            pltpu.VMEM((tokens, width), F32),
            pltpu.VMEM((tokens, width), F32),
            pltpu.VMEM((tokens, width), BF),
            pltpu.VMEM((tokens, width), BF),
            pltpu.VMEM((tokens, width), F32),
            pltpu.VMEM((tokens, width), F32),
            pltpu.VMEM((tokens, width), BF),
        ],
        compiler_params=params(),
        cost_estimate=pl.CostEstimate(
            flops=12 * tokens * width * ff + 6 * tokens * width * width,
            bytes_accessed=40 << 20,
            transcendentals=tokens * ff,
        ),
        name="middle",
    )(att_t, tok_own, tok_rem, cot_own, cot_rem, span, vec, b_up, w_out, w_up, w_down)


def middle_links_kernel(
    zs,
    att_ref,
    tokens_ref,
    tok_rem,
    cot_ref,
    cot_rem,
    span_ref,
    vec_ref,
    b_up_ref,
    w_out_ref,
    w_up_ref,
    w_down_ref,
    out_own,
    out_rem,
    dx_ref,
    d_att_ref,
    g_out_ref,
    g_up_ref,
    g_down_ref,
    up_last_ref,
    up_one_ref,
    up_two_ref,
    down_last_ref,
    down_one_ref,
    down_two_ref,
    mod_ref,
    sum_ref,
    branch,
    x_one,
    act_two,
    d_down,
    down_acc,
    d_act,
    d_branch,
    hidden,
    d_up,
    up_core,
    up_side,
    up_y,
    up_z,
    down_core,
    down_y,
    down_side,
    down_z,
    sems,
):
    step = pl.program_id(0)
    steps = zs
    tokens = att_ref.shape[1]
    width = att_ref.shape[0]
    half = tokens // 2
    cut = width // 2
    tile = 256
    per_half = half // tile
    gate_one = vec_ref[0:1, :]
    mult_two = vec_ref[1:2, :]
    shift_two = vec_ref[2:3, :]
    gate_two = vec_ref[3:4, :]
    b_down = vec_ref[4:5, :]
    gain_two = vec_ref[5:6, :]
    scale_two = vec_ref[6:7, :]

    links = Links(sems, zs)
    x, y, z, c = links.x, links.y, links.z, links.c
    tok_own, cot_own = tokens_ref.at[x], cot_ref.at[x]
    tiles = range(steps - 1)

    def swaps(src, dst, device):
        return [links.swap(lambda j=j: src(j), lambda j=j: dst.at[j], device) for j in tiles]

    up_to_core = swaps(lambda j: g_up_ref.at[:, :, :, :, 1 - c], up_core, links.core)
    down_to_core = swaps(lambda j: g_down_ref.at[:, 1 - c], down_core, links.core)
    up_to_side = swaps(lambda j: up_core.at[j, 1 - x], up_side, links.facing)
    down_to_y = swaps(lambda j: down_core.at[j, 1 - y], down_y, links.across)
    up_to_y = swaps(lambda j: up_core.at[j, x, :, :, 1 - y], up_y, links.across)
    down_to_side = swaps(lambda j: down_core.at[j, y, 1 - x], down_side, links.facing)
    h, b = links.upper, links.lower
    down_goal = links.to_goal(lambda: down_core.at[0, y, x], lambda: down_z, 0)
    up_near = links.swap(lambda: up_core.at[0, x, :, 1 - b, y], lambda: up_z.at[0:2], links.near)
    up_beyond = links.swap(lambda: up_core.at[0, x, 1 - h, b, y], lambda: up_z.at[2], links.beyond)

    def core_stage(j):
        up_to_core[j]().start()
        down_to_core[j]().start()

    def first_stage(j):
        up_to_core[j]().wait()
        for i in grid_of(2, 2, 2, 2):
            up_core[(j, *i)] = up_core[(j, *i)] + g_up_ref[(*i, c)]
        up_to_side[j]().start()
        down_to_core[j]().wait()
        for i, k in grid_of(2, 2):
            down_core[j, i, k] = down_core[j, i, k] + g_down_ref[i, c, k]
        down_to_y[j]().start()

    def first_done(j):
        up_to_side[j]().wait()
        for i in grid_of(2, 2, 2):
            up_core[(j, x, *i)] = up_core[(j, x, *i)] + up_side[(j, *i)]
        down_to_y[j]().wait()
        for k in range(2):
            down_core[j, y, k] = down_core[j, y, k] + down_y[j, k]

    def second_stage(j):
        first_done(j)
        up_to_y[j]().start()
        down_to_side[j]().start()

    def second_done(j):
        up_to_y[j]().wait()
        for i in grid_of(2, 2):
            up_core[(j, x, *i, y)] = up_core[(j, x, *i, y)] + up_y[(j, *i)]
        down_to_side[j]().wait()
        down_core[j, y, x] = down_core[j, y, x] + down_side[j]

    def third_stage():
        second_done(0)
        up_near().start()
        down_goal[0]()

    def fourth_stage():
        up_near().wait()
        for k in range(2):
            up_core[0, x, k, b, y] = up_core[0, x, k, b, y] + up_z[k]
        up_beyond().start()
        down_goal[1]()

    @pl.when(step == 0)
    def _():
        greet(links.core, links.across, links.facing, *[links.at_z(f) for f in links.far])
        for part, (tok, cot) in enumerate(((tok_own, cot_own), (tok_rem, cot_rem))):
            for t in range(per_half):
                src = slice(t * tile, (t + 1) * tile)
                dst = slice(part * half + t * tile, part * half + (t + 1) * tile)
                br = mm(att_ref[:, dst], w_out_ref[...], TN)
                branch[dst, :] = br
                xv = tok[src, :].astype(F32) + gate_one * br
                x_one[dst, :] = xv
                n, _ = norm_parts(xv)
                act_two[dst, :] = (n * mult_two + shift_two).astype(BF)
                grad_out = cot[src, :].astype(F32) * span_ref[dst, :]
                d_down[dst, :] = (gate_two * grad_out).astype(BF)
                down_acc[dst, :] = jnp.zeros((tile, width), F32)
                d_act[dst, :] = jnp.zeros((tile, width), F32)

    chunk = tokens // 4

    def one(k, bup):
        rows = rows_of(chunk, k)
        up = mm(act_two[rows, :], w_up_ref[...]) + b_up_ref[...]
        d_hidden = mm(d_down[rows, :], w_down_ref[...], NT)
        value, slope = gelu_both(up)
        low = value.astype(BF)
        hidden[rows, :] = low
        d_up_low = (slope * d_hidden).astype(BF)
        d_up[rows, :] = d_up_low
        down_acc[rows, :] += mm(low, w_down_ref[...])
        d_act[rows, :] += mm(d_up_low, w_up_ref[...], NT)
        return bup + col_sum(d_up_low.astype(F32))

    bup = lax.fori_loop(0, 4, one, jnp.zeros((1, w_up_ref.shape[1]), F32))
    for j in range(steps):
        pl.when(step == j)(lambda j=j: put_rows(sum_ref, 2 * width // 128 + j * bup.shape[1] // 128, bup))

    @pl.when(step == 1)
    def _():
        first_stage(0)

    @pl.when(step == 2)
    def _():
        second_stage(0)
        first_stage(1)

    @pl.when(step == 3)
    def _():
        second_stage(1)
        first_stage(2)

    chunk_out = width // 3
    g_down_flat = g_down_ref.reshape(width, width)
    g_up_flat = g_up_ref.reshape(2, width, cut)

    def grads(turn, carry):
        outs = rows_of(chunk_out, turn)
        g_down_flat[outs, :] = mm(hidden[:, outs], d_down[...], TN).astype(BF)
        g_up = mm(act_two[:, outs], d_up[...], TN).astype(BF)
        for k in range(2):
            g_up_flat[k, outs, :] = g_up[:, k * cut : (k + 1) * cut]
        return carry

    lax.fori_loop(0, 3, grads, 0)

    @pl.when(step == 0)
    def _():
        core_stage(0)

    @pl.when(step == 1)
    def _():
        core_stage(1)

    @pl.when(step == 2)
    def _():
        third_stage()
        core_stage(2)

    @pl.when(step == steps - 1)
    def _():
        fourth_stage()
        zero = jnp.zeros((1, width), F32)
        s_gate_two, s_shift, s_pull, s_gate_one, s_bdown = zero, zero, zero, zero, zero
        for part, (cot, out) in enumerate(((cot_own, out_own), (cot_rem, out_rem))):
            for t in range(per_half):
                src = slice(t * tile, (t + 1) * tile)
                dst = slice(part * half + t * tile, part * half + (t + 1) * tile)
                xv = x_one[dst, :]
                down = down_acc[dst, :] + b_down
                out[src, :] = (xv + gate_two * down).astype(BF)
                grad_out = cot[src, :].astype(F32) * span_ref[dst, :]
                s_gate_two += col_sum(grad_out * down)
                s_bdown += col_sum(d_down[dst, :].astype(F32))
                n, rstd = norm_parts(xv)
                da = d_act[dst, :]
                s_shift += col_sum(da)
                s_pull += col_sum(da * n)
                dx = grad_out + norm_pull(n, rstd, da * mult_two)
                dx_ref[dst, :] = dx
                s_gate_one += col_sum(dx * branch[dst, :])
                d_branch[dst, :] = (gate_one * dx).astype(BF)
        lines = width // 128
        mod_ref[4 * lines :, :] = jnp.zeros((mod_ref.shape[0] - 4 * lines, 128), BF)
        for k, row in enumerate((s_gate_one, s_shift, s_pull * gain_two, s_gate_two)):
            put_rows(mod_ref, k * lines, row)
        put_rows(mod_ref, 4 * lines, vec_ref[7:8, 0:128])
        put_rows(sum_ref, 0, s_pull * (1.0 + scale_two))
        put_rows(sum_ref, lines, s_bdown)
        g_out = mm(att_ref[...], d_branch[...]).astype(BF)
        for k in range(2):
            g_out_ref[k] = g_out[:, k * cut : (k + 1) * cut].reshape(g_out_ref.shape[1:])
        d_att_ref[...] = mm(w_out_ref[...], d_branch[...], NT).astype(BF)
        up_beyond().wait()
        up_last_ref[...] = up_core[0, x, h, b, y] + up_z[2]
        down_goal[2]()
        down_last_ref[...] = down_core[0, y, x]
        second_done(1)
        for i, k in grid_of(2, 2):
            up_one_ref[i, k] = up_core[1, x, i, k, y]
        down_one_ref[...] = down_core[1, y, x]
        first_done(2)
        up_two_ref[...] = up_core[2, x]
        down_two_ref[...] = down_core[2, y]


def middle_links(
    att_t, tok_all, tok_rem, cot_all, cot_rem, span, vec, b_up, w_out, w_up, w_down, zs
):
    width, tokens = att_t.shape
    half = tokens // 2
    cut = width // 2
    ff = w_up.shape[1]
    tile = ff // zs
    rows = width // (4 * zs)
    down_rows = tile // 4
    halves = (2, 2, 2, 2, 2, rows, cut)
    down_half = (down_rows // 2, width)
    owned = (2, 2, 2) + down_half
    outs = [
        ((half, width), BF),
        ((half, width), BF),
        ((tokens, width), F32),
        ((width, tokens), BF),
        (halves, BF),
        (halves, BF),
        (owned, BF),
        ((rows, cut), BF),
        ((2, 2, rows, cut), BF),
        ((2, 2, 2, rows, cut), BF),
        (down_half, BF),
        (down_half, BF),
        ((2,) + down_half, BF),
        ((early_mod_rows(width), 128), BF),
        ((early_sum_rows(width, ff), 128), F32),
    ]
    return pl.pallas_call(
        functools.partial(middle_links_kernel, zs),
        grid=(zs,),
        in_specs=[
            once(att_t.shape),
            once(tok_all.shape),
            once(tok_rem.shape),
            once(cot_all.shape),
            once(cot_rem.shape),
            once(span.shape),
            once(vec.shape),
            pl.BlockSpec((1, tile), lambda i: (0, i)),
            once(w_out.shape),
            pl.BlockSpec((width, tile), lambda i: (0, i)),
            pl.BlockSpec((tile, width), lambda i: (i, 0)),
        ],
        out_specs=[once(shape) for shape, _ in outs],
        out_shape=[jax.ShapeDtypeStruct(*o) for o in outs],
        scratch_shapes=[
            pltpu.VMEM((tokens, width), F32),
            pltpu.VMEM((tokens, width), F32),
            pltpu.VMEM((tokens, width), BF),
            pltpu.VMEM((tokens, width), BF),
            pltpu.VMEM((tokens, width), F32),
            pltpu.VMEM((tokens, width), F32),
            pltpu.VMEM((tokens, width), BF),
            pltpu.VMEM((tokens, tile), BF),
            pltpu.VMEM((tokens, tile), BF),
            pltpu.VMEM((zs - 1, 2, 2, 2, 2, rows, cut), BF),
            pltpu.VMEM((zs - 1, 2, 2, 2, rows, cut), BF),
            pltpu.VMEM((zs - 1, 2, 2, rows, cut), BF),
            pltpu.VMEM((3, rows, cut), BF),
            pltpu.VMEM((zs - 1, 2, 2) + down_half, BF),
            pltpu.VMEM((zs - 1, 2) + down_half, BF),
            pltpu.VMEM((zs - 1,) + down_half, BF),
            pltpu.VMEM((2,) + down_half, BF),
            pltpu.SemaphoreType.DMA((12 * (zs - 1) + 8,)),
        ],
        compiler_params=params(62, collective_id=4),
        cost_estimate=pl.CostEstimate(
            flops=12 * tokens * width * ff + 6 * tokens * width * width,
            bytes_accessed=40 << 20,
            transcendentals=tokens * ff,
        ),
        name="middle_links",
    )(att_t, tok_all, tok_rem, cot_all, cot_rem, span, vec, b_up, w_out, w_up, w_down)


def attend_back_kernel(
    q_ref,
    k_ref,
    v_ref,
    att_ref,
    d_att_ref,
    e_ref,
    linv_ref,
    cos_ref,
    sin_ref,
    give_ref,
    out_ref,
    take_ref,
    do_mask,
    send,
    recv,
):
    step = pl.program_id(0)

    @pl.when(step == 0)
    def _():
        swap_start(give_ref, take_ref, send, recv)

    tokens = q_ref.shape[1]
    tile = 256
    zero = jnp.zeros((HD, tokens), BF)
    v_nat = v_ref[...].T
    cos = cos_ref[...]
    sin = sin_ref[...]

    def unrotate(x):
        low = x.astype(BF).astype(F32)
        a, b = low[0 : HD // 2], low[HD // 2 :]
        return a * cos + b * sin, b * cos - a * sin

    for h in range(2):
        rows = slice(h * HD, (h + 1) * HD)
        linv = linv_ref[0, h : h + 1, :]
        d_o = d_att_ref[rows, :].astype(F32)
        d_os = (d_o * linv).astype(BF)
        do_mask[h, rows, :] = d_os
        do_mask[h, (1 - h) * HD : (2 - h) * HD, :] = zero
        inner = col_sum(d_o * att_ref[rows, :].astype(F32)) * linv
        d_values = mm(d_os, e_ref[h], NT)
        out_ref[2, rows, :] = d_values.astype(BF)
        d_keys = jnp.zeros((HD, tokens), F32)
        d_queries = []
        for t in range(tokens // tile):
            cols = slice(t * tile, (t + 1) * tile)
            d_probs = mm(v_nat, do_mask[h, :, cols])
            d_s = (e_ref[h, :, cols].astype(F32) * (d_probs - inner[:, cols])).astype(BF)
            d_queries.append(mm(k_ref[rows, :], d_s))
            d_keys += mm(q_ref[rows, cols], d_s, NT)
        dq = jnp.concatenate(d_queries, axis=1) * HD**-0.5
        lead, trail = unrotate(dq)
        out_ref[0, h * HD : h * HD + HD // 2, :] = lead.astype(BF)
        out_ref[0, h * HD + HD // 2 : (h + 1) * HD, :] = trail.astype(BF)
        lead, trail = unrotate(d_keys)
        out_ref[1, h * HD : h * HD + HD // 2, :] = lead.astype(BF)
        out_ref[1, h * HD + HD // 2 : (h + 1) * HD, :] = trail.astype(BF)

    @pl.when(step == pl.num_programs(0) - 1)
    def _():
        swap_wait(give_ref, take_ref, send, recv)


def attend_back(qkv_t, att_t, d_att_t, e, linv, cos_t, sin_t, give):
    tokens = qkv_t.shape[1]
    width = HEADS * HD

    def part(k):
        return pl.BlockSpec((2 * HD, tokens), lambda i: (i + k * PAIRS, 0))

    return pl.pallas_call(
        attend_back_kernel,
        grid=(PAIRS,),
        in_specs=[
            part(0),
            part(1),
            part(2),
            part(0),
            part(0),
            pl.BlockSpec((2, tokens, tokens), lambda i: (i, 0, 0)),
            pl.BlockSpec((1, 8, tokens), lambda i: (i, 0, 0)),
            whole(cos_t.shape),
            whole(sin_t.shape),
            ANY,
        ],
        out_specs=[pl.BlockSpec((3, 2 * HD, tokens), lambda i: (0, i, 0)), ANY],
        out_shape=[
            jax.ShapeDtypeStruct((3, width, tokens), BF),
            jax.ShapeDtypeStruct(give.shape, give.dtype),
        ],
        scratch_shapes=[pltpu.VMEM((2, 2 * HD, tokens), BF)] + SEMS,
        compiler_params=params(collective_id=2),
        cost_estimate=pl.CostEstimate(
            flops=32 * tokens * tokens * width, bytes_accessed=36 << 20, transcendentals=0
        ),
        name="attend_back",
    )(qkv_t, qkv_t, qkv_t, att_t, d_att_t, e, linv, cos_t, sin_t, give)


def tail_kernel(tok_own, tok_rem, d_proj_ref, w_ref, dx_ref, vec_ref, own_ref, rem_ref, sums_ref):
    step = pl.program_id(0)
    steps = pl.num_programs(0)
    mult_one = vec_ref[0:1, :]
    gain_one = vec_ref[2:3, :]
    scale_one = vec_ref[3:4, :]
    d_act = mm(d_proj_ref[...], w_ref[...], TN)

    def finish(tok, out):
        n, rstd = norm_parts(tok[...].astype(F32))
        grad = dx_ref[...] + norm_pull(n, rstd, d_act * mult_one)
        out[...] = grad.astype(out.dtype)
        return col_sum(d_act), col_sum(d_act * n)

    @pl.when(step == 0)
    def _():
        shift, pull = finish(tok_rem, rem_ref)
        sums_ref[0:1, :] = shift
        sums_ref[1:2, :] = pull
        sums_ref[2:, :] = jnp.zeros((6, shift.shape[1]), F32)

    @pl.when(step == steps - 1)
    def _():
        shift, pull = finish(tok_own, own_ref)
        shift = sums_ref[0:1, :] + shift
        pull = sums_ref[1:2, :] + pull
        sums_ref[0:1, :] = shift
        sums_ref[1:2, :] = pull * gain_one
        sums_ref[2:3, :] = pull * (1.0 + scale_one)


def tail(tok_own, tok_rem, d_proj_t, w_qkv_t, dx, vec):
    half, width = tok_own.shape
    return pl.pallas_call(
        tail_kernel,
        grid=(2,),
        in_specs=[
            whole(tok_own.shape),
            whole(tok_rem.shape),
            pl.BlockSpec((3 * width, half), lambda i: (0, 1 - i)),
            whole(w_qkv_t.shape),
            pl.BlockSpec((half, width), lambda i: (1 - i, 0)),
            whole(vec.shape),
        ],
        out_specs=[whole((half, width)), whole((half, width)), whole((8, width))],
        out_shape=[
            jax.ShapeDtypeStruct((half, width), F32),
            jax.ShapeDtypeStruct((half, width), BF),
            jax.ShapeDtypeStruct((8, width), F32),
        ],
        compiler_params=params(),
        cost_estimate=pl.CostEstimate(
            flops=12 * half * width * width, bytes_accessed=20 << 20, transcendentals=0
        ),
        name="tail",
    )(tok_own, tok_rem, d_proj_t, w_qkv_t, dx, vec)


def weight_grad_kernel(act_ref, d_proj_ref, out_ref):
    out_ref[...] = mm(act_ref[...], d_proj_ref[...], NT).astype(BF)


def weight_grad(act_t, d_proj_t):
    width, tokens = act_t.shape
    cols = d_proj_t.shape[0]
    tile = 768
    return pl.pallas_call(
        weight_grad_kernel,
        grid=(cols // tile,),
        in_specs=[whole(act_t.shape), pl.BlockSpec((tile, tokens), lambda i: (i, 0))],
        out_specs=pl.BlockSpec((width, tile), lambda i: (0, i)),
        out_shape=jax.ShapeDtypeStruct((width, cols), BF),
        compiler_params=params(),
        cost_estimate=pl.CostEstimate(
            flops=2 * cols * width * tokens, bytes_accessed=12 << 20, transcendentals=0
        ),
        name="weight_grad",
    )(act_t, d_proj_t)


def gather_stages(links, ref):
    z, y, c, x = links.z, links.y, links.c, links.x

    def pair(mine, theirs, device):
        sem = links.take(2)

        def make(slot):
            return remote(slot(), slot(), links.sems.at[sem], links.sems.at[sem + 1], device)

        def wait():
            make(mine).wait_send()
            make(theirs).wait_recv()

        return (lambda: make(mine).start()), wait

    sem = links.take(2 * links.zs)

    def make(f, slot):
        block = ref.at[slot, :, :, x]
        return remote(
            block, block, links.sems.at[sem + f], links.sems.at[sem + links.zs + slot], links.at_z(f)
        )

    def far_start():
        for f in links.far:
            make(f, z).start()

    def far_wait():
        for f in links.far:
            make(f, z).wait_send()
            make(f, f).wait_recv()

    return [
        pair(lambda: ref.at[z, y, c, x], lambda: ref.at[z, y, 1 - c, x], links.core),
        pair(lambda: ref.at[z, y, :, x], lambda: ref.at[z, 1 - y, :, x], links.across),
        (far_start, far_wait),
        pair(lambda: ref.at[:, :, :, x], lambda: ref.at[:, :, :, 1 - x], links.facing),
    ]


def sum_stages(links, ref, take, far):
    swaps = [
        links.swap(lambda: ref, lambda k=k: take.at[k], device)
        for k, device in enumerate((links.core, links.across, links.facing))
    ]
    far_start, far_wait = links.spread(lambda f: ref, lambda slot: far.at[slot])

    def finish(k):
        swaps[k]().wait()
        ref[...] += take[k]

    def far_finish():
        far_wait()
        far[links.z] = ref[...]
        total = far[0]
        for f in range(1, links.zs):
            total += far[f]
        ref[...] = total

    return [
        (lambda: swaps[0]().start(), lambda: finish(0)),
        (lambda: swaps[1]().start(), lambda: finish(1)),
        (far_start, far_finish),
        (lambda: swaps[2]().start(), lambda: finish(2)),
    ]


def back_kernel(zs, split, ins, outs, scratch):
    (
        q_ref,
        k_ref,
        v_ref,
        att_ref,
        d_att_ref,
        e_ref,
        linv_ref,
        cos_ref,
        sin_ref,
        give_ref,
        up_last_ref,
        up_one_ref,
        up_two_ref,
        down_last_ref,
        down_one_ref,
        down_two_ref,
        raw_up,
        raw_out,
        raw_down,
        mod_ref,
        sum_ref,
        act_in,
        w_in,
        tok_own_in,
        tok_rem_in,
        dx_in,
        vec_ref,
    ) = ins
    result, grad_ref, grad_take, s_qkv, s_out, s_up, s_down, *small_outs = outs
    (
        do_mask,
        d_proj,
        sems,
        u_own,
        u_y,
        u_z,
        u_last,
        u_facing,
        w_own,
        w_core,
        w_y,
        w_z,
        w_far,
        w_last,
        w_facing,
        d_own,
        d_core,
        d_y,
        d_side,
        d_sum,
        d_z,
        d_last,
        d_facing,
        q_raws,
        q_cores,
        q_ys,
        q_zs,
        q_lasts,
        q_facings,
        g_send,
        g_take,
        early_take,
        early_far,
        late_take,
        late_far,
        mod_early,
        mod_late,
        sum_early,
        sum_late,
        act_ref,
        w_ref,
        tok_own,
        tok_rem,
        dx_ref,
        g_own,
    ) = scratch
    step = pl.program_id(0)
    tokens = q_ref.shape[1]
    width = act_ref.shape[0]
    half = tokens // 2
    cut = width // 2
    links = Links(sems, zs)
    x, y, z, c = links.x, links.y, links.z, links.c
    h, b = links.upper, links.lower

    fetch = [
        links.local(lambda p=p: p[0], lambda p=p: p[1])
        for p in (
            (act_in, act_ref),
            (w_in, w_ref),
            (tok_own_in.at[x], tok_own),
            (tok_rem_in, tok_rem),
            (dx_in, dx_ref),
        )
    ]
    u_load = [
        links.local(lambda: up_last_ref, lambda: u_last.at[0]),
        links.local(lambda: up_one_ref.at[:, b], lambda: u_own.at[0, :, b]),
        links.local(lambda: up_two_ref.at[:, :, y], lambda: u_own.at[1]),
    ]
    u_to_y = links.swap(lambda: up_two_ref.at[:, :, 1 - y], lambda: u_y, links.across)
    u_near = [
        links.swap(
            lambda j=j: up_one_ref.at[:, 1 - b] if j == 0 else u_own.at[1, :, 1 - b],
            lambda j=j: u_z.at[j, 0:2],
            links.near,
        )
        for j in range(2)
    ]
    u_beyond = [
        links.swap(lambda j=j: u_own.at[j, 1 - h, b], lambda j=j: u_z.at[j, 2], links.beyond)
        for j in range(2)
    ]
    u_to_facing = [
        links.swap(lambda j=j: u_last.at[j], lambda j=j: u_facing.at[j], links.facing)
        for j in range(3)
    ]
    raws = (raw_up, raw_out)
    w_keep = [
        links.local(lambda r=r: r.at[:, :, :, :, c], lambda k=k: w_own.at[k]) for k, r in enumerate(raws)
    ]
    w_to_core = [
        links.swap(lambda r=r: r.at[:, :, :, :, 1 - c], lambda k=k: w_core.at[k], links.core)
        for k, r in enumerate(raws)
    ]
    w_to_y = [
        links.swap(lambda k=k: w_own.at[k, :, :, :, 1 - y], lambda k=k: w_y.at[k], links.across)
        for k in range(2)
    ]
    w_near = [
        links.swap(
            lambda k=k: w_own.at[k, :, :, 1 - b, y], lambda k=k: w_z.at[k], links.near
        )
        for k in range(2)
    ]
    w_beyond = [
        links.swap(
            lambda k=k: w_own.at[k, :, 1 - h, b, y], lambda k=k: w_far.at[k], links.beyond
        )
        for k in range(2)
    ]
    w_to_facing = [
        links.swap(lambda k=k: w_last.at[k], lambda k=k: w_facing.at[k], links.facing)
        for k in range(2)
    ]
    d_keep = links.local(lambda: raw_down.at[:, c], lambda: d_own)
    d_to_core = links.swap(lambda: raw_down.at[:, 1 - c], lambda: d_core, links.core)
    d_to_y = links.swap(lambda: d_own.at[1 - y], lambda: d_y, links.across)
    d_to_side = [
        links.swap(lambda: down_two_ref.at[1 - x], lambda: d_side.at[0], links.facing),
        links.swap(lambda: d_own.at[y, 1 - x], lambda: d_side.at[1], links.facing),
    ]
    d_load = [
        links.local(lambda: down_last_ref, lambda: d_last),
        links.local(lambda: down_one_ref, lambda: d_sum.at[0]),
        links.local(lambda: down_two_ref.at[x], lambda: d_sum.at[1]),
    ]
    d_goal = [
        links.to_goal(lambda j=j: d_sum.at[j - 1], lambda j=j: d_z.at[j - 1], j) for j in range(1, zs)
    ]
    d_to_facing = links.swap(lambda: d_last, lambda: d_facing, links.facing)
    groups = range(len(split))
    q_to_core = [
        links.swap(lambda g=g: q_raws[g].at[:, :, :, 1 - c], lambda g=g: q_cores[g], links.core)
        for g in groups
    ]
    q_to_y = [
        links.swap(lambda g=g: q_cores[g].at[:, :, 1 - y], lambda g=g: q_ys[g], links.across)
        for g in groups
    ]
    q_near = [
        links.swap(lambda g=g: q_cores[g].at[:, 1 - b, y], lambda g=g: q_zs[g].at[0:2], links.near)
        for g in groups
    ]
    q_beyond = [
        links.swap(lambda g=g: q_cores[g].at[1 - h, b, y], lambda g=g: q_zs[g].at[2], links.beyond)
        for g in groups
    ]
    q_to_facing = [
        links.swap(lambda g=g: q_lasts[g], lambda g=g: q_facings[g], links.facing) for g in groups
    ]
    cross_out = links.swap(lambda: give_ref, lambda: result, links.facing)

    give_grad = links.swap(lambda: g_send, lambda: g_take, links.facing)
    keep_grad = links.local(lambda: g_own, lambda: grad_ref)
    put_grad = links.local(lambda: g_take, lambda: grad_take)
    early = [
        gather_stages(links, mod_early),
        sum_stages(links, sum_early, early_take, early_far),
    ]
    late = [gather_stages(links, mod_late), sum_stages(links, sum_late, late_take, late_far)]

    def begin(arrays, stage):
        for stages in arrays:
            stages[stage][0]()

    def end(arrays, stage):
        for stages in arrays:
            stages[stage][1]()

    def u_near_done(j):
        u_near[j]().wait()
        for k in range(2):
            u_own[j, k, b] = u_own[j, k, b] + u_z[j, k]
        u_beyond[j]().start()

    def u_beyond_done(j):
        u_beyond[j]().wait()
        u_last[j + 1] = u_own[j, h, b] + u_z[j, 2]
        u_to_facing[j + 1]().start()

    def u_done(j):
        u_to_facing[j]().wait()
        mine, other = u_last[j].astype(F32), u_facing[j].astype(F32)
        start = j * width
        s_up[:, start : start + cut] = jnp.where(x == 0, mine, other)
        s_up[:, start + cut : start + width] = jnp.where(x == 0, other, mine)

    def w_core_done(k):
        w_keep[k]().wait()
        w_to_core[k]().wait()
        for i in grid_of(2, 2, 2, 2):
            w_own[(k, *i)] = w_own[(k, *i)] + w_core[(k, *i)]

    def w_y_done(k):
        w_to_y[k]().wait()
        for i in grid_of(2, 2, 2):
            w_own[(k, *i, y)] = w_own[(k, *i, y)] + w_y[(k, *i)]
        w_near[k]().start()

    def w_near_done(k):
        w_near[k]().wait()
        for i, j in grid_of(2, 2):
            w_own[k, i, j, b, y] = w_own[k, i, j, b, y] + w_z[k, i, j]
        w_beyond[k]().start()

    def w_beyond_done(k):
        w_beyond[k]().wait()
        for i in range(2):
            w_last[k, i] = w_own[k, i, h, b, y] + w_far[k, i]
        w_to_facing[k]().start()

    def w_done(k):
        w_to_facing[k]().wait()
        out, start = (s_up, (zs - 1) * width) if k == 0 else (s_out, 0)
        for i in range(2):
            out[:, start + i * cut : start + (i + 1) * cut] = w_last[k, i].astype(F32) + w_facing[
                k, i
            ].astype(F32)

    def q_core_done(g):
        q_to_core[g]().wait()
        for i in grid_of(2, 2, 2):
            q_cores[g][i] = q_cores[g][i] + q_raws[g][(*i, c)]

    def q_y_done(g):
        q_to_y[g]().wait()
        for i in grid_of(2, 2):
            q_cores[g][(*i, y)] = q_cores[g][(*i, y)] + q_ys[g][i]
        q_near[g]().start()

    def q_near_done(g):
        q_near[g]().wait()
        for k in range(2):
            q_cores[g][k, b, y] = q_cores[g][k, b, y] + q_zs[g][k]
        q_beyond[g]().start()

    def q_beyond_done(g):
        q_beyond[g]().wait()
        q_lasts[g][...] = q_cores[g][h, b, y] + q_zs[g][2]
        q_to_facing[g]().start()

    def q_done(g):
        q_to_facing[g]().wait()
        total = q_lasts[g][...].astype(F32) + q_facings[g][...].astype(F32)
        first, size = split[g][0] * HD, (split[g][1] - split[g][0]) * HD
        for p in range(3):
            s_qkv[:, p * width + first : p * width + first + size] = total[:, p * size : (p + 1) * size]

    def weight_grad_of(g):
        first, size = split[g][0] * HD, (split[g][1] - split[g][0]) * HD
        for p in range(3):
            rows = slice(p * width + first, p * width + first + size)
            part = mm(act_ref[...], d_proj[rows, :], NT).astype(BF)
            q_raws[g][:, :, :, :, :, p * size : (p + 1) * size] = part.reshape(
                q_raws[g].shape[:5] + (size,)
            )
        q_to_core[g]().start()


    def due_00():
        greet(links.core, links.across, links.facing, *[links.at_z(f) for f in links.far])
        d_to_core().start()
        d_keep().start()
        for k in range(2):
            w_to_core[k]().start()
            w_keep[k]().start()
        u_near[0]().start()
        u_to_y().start()
        d_to_side[0]().start()
        for load in u_load + d_load:
            load().start()
        mod_early[z, y, c, x] = mod_ref[...]
        sum_early[...] = sum_ref[...]
        begin(early, 0)
        cross_out().start()
        for load in fetch:
            load().start()

    def due_01():
        d_load[1]().wait()
        d_goal[0][0]()
        d_keep().wait()
        d_to_core().wait()
        for i, k in grid_of(2, 2):
            d_own[i, k] = d_own[i, k] + d_core[i, k]
        d_to_y().start()
        end(early, 0)
        begin(early, 1)

    def due_10():
        w_core_done(0)
        w_core_done(1)
        u_load[0]().wait()
        u_to_facing[0]().start()

    def due_11():
        u_load[2]().wait()
        u_to_y().wait()
        for i in grid_of(2, 2):
            u_own[(1, *i)] = u_own[(1, *i)] + u_y[i]
        u_near[1]().start()
        u_load[1]().wait()
        u_near_done(0)
        d_goal[0][1]()
        end(early, 1)
        begin(early, 2)

    def due_20():
        fetch[0]().wait()
        weight_grad_of(0)
        d_load[2]().wait()
        d_to_side[0]().wait()
        d_sum[1] = d_sum[1] + d_side[0]
        d_goal[1][0]()

    def due_21():
        d_to_y().wait()
        for k in range(2):
            d_own[y, k] = d_own[y, k] + d_y[k]
        d_to_side[1]().start()
        w_to_y[0]().start()
        q_core_done(0)
        u_near_done(1)
        u_beyond_done(0)
        end(early, 2)
        begin(early, 3)

    def due_30():
        d_goal[1][1]()

    def due_31():
        w_y_done(0)
        q_to_y[0]().start()

    def due_40():
        weight_grad_of(1)
        d_to_side[1]().wait()
        d_sum[2] = d_own[y, x] + d_side[1]
        d_goal[2][0]()
        u_beyond_done(1)
        end(early, 3)

    def due_41():
        q_core_done(1)
        w_near_done(0)
        u_done(0)

    def due_50():
        q_y_done(0)
        q_to_y[1]().start()
        d_goal[2][1]()

    def due_51():
        w_beyond_done(0)
        u_done(1)

    due = (
        (due_00, due_01),
        (due_10, due_11),
        (due_20, due_21),
        (due_30, due_31),
        (due_40, due_41),
        (due_50, due_51),
    )

    def do_due(h):
        for k in range(PAIRS):
            pl.when(step == k)(due[k][h])


    @pl.when(step < PAIRS)
    def _():
        tile = 256
        zero = jnp.zeros((HD, tokens), BF)
        v_nat = v_ref[...].T
        cos = cos_ref[...]
        sin = sin_ref[...]

        def put(part, h, value):
            low = value.astype(BF).astype(F32)
            a, b = low[0 : HD // 2], low[HD // 2 :]
            start = part * width + step * 2 * HD + h * HD
            d_proj[pl.ds(pl.multiple_of(start, 32), 32), :] = (a * cos + b * sin).astype(BF)
            d_proj[pl.ds(pl.multiple_of(start + 32, 32), 32), :] = (b * cos - a * sin).astype(BF)

        do_due(0)
        inners, keys, values, queries = [], [], [], [[], []]
        for h in range(2):
            rows = slice(h * HD, (h + 1) * HD)
            linv = linv_ref[0, h : h + 1, :]
            d_o = d_att_ref[rows, :].astype(F32)
            do_mask[h, rows, :] = (d_o * linv).astype(BF)
            do_mask[h, (1 - h) * HD : (2 - h) * HD, :] = zero
            inners.append(col_sum(d_o * att_ref[rows, :].astype(F32)) * linv)

        def ahead(h, cols):
            return mm(v_nat, do_mask[h, :, cols])

        def centre(h, cols, d_probs):
            rows = slice(h * HD, (h + 1) * HD)
            e = e_ref[h, :, cols]
            part = mm(do_mask[h, rows, cols], e, NT)
            if cols.start == 0:
                values.append(part)
            else:
                values[h] += part
            return (e.astype(F32) * (d_probs - inners[h][:, cols])).astype(BF)

        def behind(h, cols, d_s):
            rows = slice(h * HD, (h + 1) * HD)
            queries[h].append(mm(k_ref[rows, :], d_s))
            part = mm(q_ref[rows, cols], d_s, NT)
            if cols.start == 0:
                keys.append(part)
            else:
                keys[h] += part
            if cols.stop == tokens:
                put(0, h, jnp.concatenate(queries[h], axis=1) * HD**-0.5)
                put(1, h, keys[h])
                start = 2 * width + step * 2 * HD + h * HD
                d_proj[pl.ds(pl.multiple_of(start, HD), HD), :] = values[h].astype(BF)

        units = [(h, slice(t, t + tile)) for h in range(2) for t in range(0, tokens, tile)]
        coming = ahead(*units[0])
        for i, unit in enumerate(units):
            if i == len(units) // 2:
                do_due(1)
            here = coming
            if i + 1 < len(units):
                coming = ahead(*units[i + 1])
            d_s = centre(*unit, here)
            if i > 0:
                behind(*units[i - 1], held)
            held = d_s
        behind(*units[-1], held)


    def finish(tok, cols):
        d_act = mm(d_proj[:, cols], w_ref[...], TN)
        n, rstd = norm_parts(tok[...].astype(F32))
        grad = dx_ref[cols, :] + norm_pull(n, rstd, d_act * vec_ref[0:1, :])
        return grad, col_sum(d_act), col_sum(d_act * n)

    @pl.when(step == PAIRS)
    def _():
        for load in fetch[1:]:
            load().wait()
        weight_grad_of(2)
        grad, shift, pull = finish(tok_rem, slice(half, 2 * half))
        g_send[...] = grad.astype(BF)
        give_grad().start()
        q_y_done(1)
        q_core_done(2)
        q_to_y[2]().start()
        q_near_done(0)
        w_to_y[1]().start()
        grad, shift_own, pull_own = finish(tok_own, slice(0, half))
        g_own[...] = grad
        keep_grad().start()
        shift += shift_own
        pull += pull_own
        lines = width // 128
        mine = mod_late.at[z, y, c, x]
        mine[2 * lines :, :] = jnp.zeros((mod_late.shape[4] - 2 * lines, 128), BF)
        put_rows(mine, 0, shift)
        put_rows(mine, lines, pull * vec_ref[2:3, :])
        sum_late[lines:, :] = jnp.zeros((sum_late.shape[0] - lines, 128), F32)
        put_rows(sum_late, 0, pull * (1.0 + vec_ref[3:4, :]))
        begin(late, 0)
        q_near_done(1)
        q_beyond_done(0)
        end(late, 0)
        begin(late, 1)
        d_load[0]().wait()
        for j in range(zs - 1):
            d_goal[j][2]()

        @pl.when(z > 0)
        def _():
            d_last[...] = d_sum[jnp.maximum(z - 1, 0)]

        d_to_facing().start()
        q_y_done(2)
        end(late, 1)
        begin(late, 2)
        q_beyond_done(1)
        w_y_done(1)
        q_near_done(2)
        u_done(2)
        end(late, 2)
        begin(late, 3)
        w_near_done(1)
        w_done(0)
        q_beyond_done(2)
        w_beyond_done(1)
        d_to_facing().wait()
        mine, other = d_last[...].astype(F32), d_facing[...].astype(F32)
        rows_half = mine.shape[0]
        s_down[0:rows_half, :] = jnp.where(x == 0, mine, other)
        s_down[rows_half:, :] = jnp.where(x == 0, other, mine)
        cross_out().wait()
        q_done(0)
        q_done(1)
        end(late, 3)
        give_grad().wait()
        put_grad().start()
        keep_grad().wait()
        q_done(2)
        w_done(1)
        put_grad().wait()
        for out, value in zip(small_outs, (mod_early, mod_late, sum_early, sum_late)):
            out[...] = value[...]


def back(ins, zs, ff):
    q, att, d_att, e, linv, cos_t, sin_t = ins[:7]
    mod, sums, vec = ins[-8], ins[-7], ins[-1]
    width, tokens = att.shape
    half = tokens // 2
    cut = width // 2
    rows = width // (4 * zs)
    down_rows = ff // (4 * zs)
    down_half = (down_rows // 2, width)
    split = ((0, 4), (4, 8), (8, HEADS))
    sizes = [3 * (b - a) * HD for a, b in split]
    last = PAIRS - 1

    def part(k):
        return pl.BlockSpec((2 * HD, tokens), lambda i: (jnp.minimum(i, last) + k * PAIRS, 0))

    def vm(*shape, kind=BF):
        return pltpu.VMEM(shape, kind)

    lines = width // 128
    mod_early = (zs, 2, 2, 2) + mod.shape
    mod_late = (zs, 2, 2, 2, round_up(2 * lines, 16), 128)
    sum_late = (round_up(lines, 8), 128)
    outs = [
        ((half, width), F32),
        ((rows, 3 * width), F32),
        ((rows, width), F32),
        ((rows, ff), F32),
        ((down_rows, width), F32),
        (mod_early, BF),
        (mod_late, BF),
        (sums.shape, F32),
        (sum_late, F32),
    ]
    outs = [((half, width), F32), ((half, width), BF)] + outs[1:]
    fetched = ins[-6:-1]
    in_specs = (
        [part(0), part(1), part(2), part(0), part(0)]
        + [
            pl.BlockSpec((2, tokens, tokens), lambda i: (jnp.minimum(i, last), 0, 0)),
            pl.BlockSpec((1, 8, tokens), lambda i: (jnp.minimum(i, last), 0, 0)),
            once(cos_t.shape),
            once(sin_t.shape),
        ]
        + [ANY] * (len(ins) - 15)
        + [once(mod.shape), once(sums.shape)]
        + [ANY] * 5
        + [once(vec.shape)]
    )
    out_specs = [ANY, ANY, ANY] + [once(shape) for shape, _ in outs[2:]]
    out_shape = [jax.ShapeDtypeStruct((half, width), BF)] + [
        jax.ShapeDtypeStruct(*o) for o in outs
    ]
    scratch = [
        vm(2, 2 * HD, tokens),
        vm(3 * width, tokens),
        pltpu.SemaphoreType.DMA((250,)),
        vm(2, 2, 2, rows, cut),
        vm(2, 2, rows, cut),
        vm(2, 3, rows, cut),
        vm(3, rows, cut),
        vm(3, rows, cut),
        vm(2, 2, 2, 2, 2, rows, cut),
        vm(2, 2, 2, 2, 2, rows, cut),
        vm(2, 2, 2, 2, rows, cut),
        vm(2, 2, 2, rows, cut),
        vm(2, 2, rows, cut),
        vm(2, 2, rows, cut),
        vm(2, 2, rows, cut),
        vm(2, 2, *down_half),
        vm(2, 2, *down_half),
        vm(2, *down_half),
        vm(2, *down_half),
        vm(zs - 1, *down_half),
        vm(zs - 1, 2, *down_half),
        vm(*down_half),
        vm(*down_half),
        [vm(2, 2, 2, 2, rows, s) for s in sizes],
        [vm(2, 2, 2, rows, s) for s in sizes],
        [vm(2, 2, rows, s) for s in sizes],
        [vm(3, rows, s) for s in sizes],
        [vm(rows, s) for s in sizes],
        [vm(rows, s) for s in sizes],
        vm(half, width),
        vm(half, width),
        vm(3, *sums.shape, kind=F32),
        vm(zs, *sums.shape, kind=F32),
        vm(3, *sum_late, kind=F32),
        vm(zs, *sum_late, kind=F32),
        vm(*mod_early),
        vm(*mod_late),
        vm(*sums.shape, kind=F32),
        vm(*sum_late, kind=F32),
    ]
    scratch += [vm(*a.shape[-2:], kind=a.dtype) for a in fetched]
    scratch += [vm(half, width, kind=F32)]
    flat, tree = jax.tree.flatten(scratch)
    n_in, n_out = len(in_specs), len(out_specs)

    def kernel(*refs):
        back_kernel(
            zs,
            split,
            refs[:n_in],
            refs[n_in : n_in + n_out],
            jax.tree.unflatten(tree, refs[n_in + n_out :]),
        )

    return pl.pallas_call(
        kernel,
        grid=(PAIRS + 1,),
        in_specs=in_specs,
        out_specs=out_specs,
        out_shape=out_shape,
        scratch_shapes=flat,
        compiler_params=params(62, collective_id=5),
        cost_estimate=pl.CostEstimate(
            flops=32 * tokens * tokens * width + 12 * tokens * width * width,
            bytes_accessed=60 << 20,
            transcendentals=0,
        ),
        name="back",
    )(q, q, q, att, d_att, e, linv, cos_t, sin_t, *ins[7:])


def iota2(shape, axis):
    return lax.broadcasted_iota(jnp.int32, shape, axis)


def finish_kernel(pairs, early_ref, late_ref, sum_early_ref, sum_late_ref, *refs):
    sources, refs = refs[:8], refs[8:]
    output, grad, *shards, w_ada, b_ada, gain_one, gain_two, b_down, b_up = refs[:12]
    held, (wide, sems) = refs[12:20], refs[20:]
    x = lax.axis_index("seq")
    goals = [output.at[x], output.at[1 - x], grad.at[x], grad.at[1 - x], *shards]
    loads = [
        pltpu.make_async_copy(src, dst, sems.at[0, k])
        for k, (src, dst) in enumerate(zip(sources, held))
    ]
    stores = [
        pltpu.make_async_copy(wide if k == 3 else src, dst, sems.at[1, k])
        for k, (src, dst) in enumerate(zip(held, goals))
    ]
    for copy in loads:
        copy.start()
    for k in range(8):
        loads[k].wait()
        if k == 3:
            wide[...] = held[3][...].astype(F32)
        stores[k].start()
    dp = lax.axis_index("dp")
    rows, lines = w_ada.shape[0], early_ref.shape[1]
    width = gain_one.shape[0] * lax.axis_size("dp")
    per_line = width // 128
    stamp_line = 4 * per_line
    blocks = []
    for ref, first, count in ((late_ref, 0, 2 * per_line), (early_ref, 2 * per_line, 4 * per_line)):
        seqs, period = ref.shape[0], ref.shape[1]
        flat = ref[...].reshape(seqs * period, 128)
        stamps = early_ref[...].reshape(seqs * lines, 128)
        shape = (seqs * lines, seqs * period)
        line, col = iota2(shape, 0), iota2(shape, 1)
        pick = (line // lines == col // period) & (lax.rem(line, lines) == stamp_line)
        time = mm(stamps, jnp.where(pick, 1.0, 0.0).astype(BF), TN)
        time = 32.0 * time[0:1, :] + time[1:2, :]
        shape = (rows, seqs * period)
        index = dp * rows + iota2(shape, 0)
        place = jnp.where(index < pairs, index, index - pairs).astype(F32)
        angles = time * jnp.exp(-math.log(10000.0) * place / pairs)
        cond = features_of(angles, index >= pairs)
        shape = (period * rows, seqs * period)
        same = iota2(shape, 0) // rows == lax.rem(iota2(shape, 1), period)
        total = jnp.zeros((period * rows, 128), F32)
        for part in split_three(cond):
            spread = jnp.concatenate([part.astype(F32)] * period, axis=0)
            total += mm(jnp.where(same, spread, 0.0).astype(BF), flat)
        for k in range(count):
            start = (first + k) * 128
            w_ada[:, start : start + 128] = total[k * rows : (k + 1) * rows]
        shape = (period, seqs * period)
        same = iota2(shape, 0) == lax.rem(iota2(shape, 1), period)
        sums = mm(jnp.where(same, 1.0, 0.0).astype(BF), flat)
        blocks += [sums[k : k + 1] for k in range(count)]

    def mine(parts, out):
        row = jnp.concatenate(parts, axis=1)
        size, full = out.shape[0], row.shape[1]
        row = pltpu.roll(row, lax.rem(full - dp * size, full), 1)
        out[...] = row[0, 0:size]

    def lines_of(ref, first, count):
        return [ref[first + k : first + k + 1, :] for k in range(count)]

    mine(blocks, b_ada)
    mine(lines_of(sum_late_ref, 0, per_line), gain_one)
    mine(lines_of(sum_early_ref, 0, per_line), gain_two)
    mine(lines_of(sum_early_ref, per_line, per_line), b_down)
    mine(lines_of(sum_early_ref, 2 * per_line, b_up.shape[0] * lax.axis_size("dp") // 128), b_up)
    for copy in stores:
        copy.wait()


def finish_all(big, mod_early, mod_late, sum_early, sum_late, cond_width, width, ff, dps):
    seqs = 2 * dps
    mod_early = mod_early.reshape(seqs, *mod_early.shape[-2:])
    mod_late = mod_late.reshape(seqs, *mod_late.shape[-2:])
    smalls = (mod_early, mod_late, sum_early, sum_late)
    vmem = pl.BlockSpec(memory_space=pltpu.VMEM)
    half = big[0].shape[0]
    out_shape = [jax.ShapeDtypeStruct((2, half, width), kind) for kind in (BF, F32)]
    out_shape += [jax.ShapeDtypeStruct(a.shape, a.dtype) for a in big[4:]]
    out_shape += [jax.ShapeDtypeStruct((cond_width // dps, 6 * width), F32)]
    out_shape += [
        jax.ShapeDtypeStruct((n // dps,), F32) for n in (6 * width, width, width, width, ff)
    ]
    return pl.pallas_call(
        functools.partial(finish_kernel, cond_width // 2),
        in_specs=[vmem] * 4 + [ANY] * len(big),
        out_specs=[ANY] * 6 + [vmem] * 6,
        out_shape=out_shape,
        scratch_shapes=[pltpu.VMEM(a.shape, a.dtype) for a in big]
        + [pltpu.VMEM((half, width), F32), pltpu.SemaphoreType.DMA((2, len(big)))],
        compiler_params=params(),
        name="finish_all",
    )(*smalls, *big)


def time_features(time_steps, pair_count):
    frequency = jnp.exp(-math.log(10000.0) * jnp.arange(pair_count, dtype=F32) / pair_count)
    angles = time_steps.astype(F32)[:, None] * frequency[None, :]
    return jnp.concatenate([jnp.cos(angles), jnp.sin(angles)], axis=-1)


def per_device(
    tokens,
    cotangent,
    time_index,
    span_starts,
    span_lengths,
    w_ada,
    b_ada,
    gain_one,
    w_qkv,
    w_out,
    gain_two,
    w_up,
    b_up,
    w_down,
    b_down,
):
    seqs_dev, half, width = tokens.shape
    length = 2 * half
    rank = lax.axis_index("seq")
    swap = [(0, 1), (1, 0)]

    def pick(x, i):
        return lax.dynamic_index_in_dim(x, i, 0, keepdims=False)

    time_own = lax.dynamic_slice_in_dim(time_index, rank, 1)
    dp, dps = lax.axis_index("dp"), lax.axis_size("dp")
    ff = w_up.shape[1]
    zs = dps // 4
    linked = zs == 4 and dps == 16 and width % (64 * zs) == 0 and ff == zs * width

    act_t, qkv_t, w_qkv_t, tok_rem, vec_one, vec_two, span, cos_t, sin_t = project(
        tokens, time_index, span_starts, span_lengths, w_ada, b_ada, (gain_one, gain_two), b_down, w_qkv
    )
    att_t, e, linv, cot_rem = attend(qkv_t, cotangent)
    if linked:
        out_own, out_rem, dx, d_att_t, raw_out, raw_up, raw_down, *partial, mod, sums = middle_links(
            att_t, tokens, tok_rem, cotangent, cot_rem, span, vec_two, b_up[None], w_out, w_up, w_down, zs
        )
        ins = (qkv_t, att_t, d_att_t, e, linv, cos_t, sin_t, out_rem, *partial)
        ins += (raw_up, raw_out, raw_down, mod, sums, act_t, w_qkv_t, tokens, tok_rem, dx, vec_one)
        taken, g_own, g_take, *shards, mod_early, mod_late, sum_early, sum_late = back(ins, zs, ff)
        output, grad_tokens, *shards, s_w_ada, s_b_ada, s_gain_one, s_gain_two, s_b_down, s_b_up = (
            finish_all(
                (out_own, taken, g_own, g_take, *shards),
                mod_early,
                mod_late,
                sum_early,
                sum_late,
                w_ada.shape[0],
                width,
                ff,
                dps,
            )
        )
    else:
        tok_own, cot_own = pick(tokens, rank), pick(cotangent, rank)
        out_own, out_rem, dx, d_att_t, g_out, g_up, g_down, g_bup, sums_two = middle(
            att_t, tok_own, tok_rem, cot_own, cot_rem, span, vec_two, b_up[None], w_out, w_up, w_down
        )
        d_proj, out_back = attend_back(qkv_t, att_t, d_att_t, e, linv, cos_t, sin_t, out_rem)
        d_proj_t = d_proj.reshape(3 * width, length)
        g_own, g_rem, sums_one = tail(tok_own, tok_rem, d_proj_t, w_qkv_t, dx, vec_one)
        g_qkv = weight_grad(act_t, d_proj_t)

        def spread(own, other):
            first = jnp.where(rank == 0, own, other)
            second = jnp.where(rank == 0, other, own)
            return jnp.stack([first, second])

        output = spread(out_own, out_back)
        grad_tokens = spread(g_own, lax.ppermute(g_rem, "seq", swap).astype(F32))
        shards = [
            lax.psum(lax.psum_scatter(g, "dp", scatter_dimension=0, tiled=True), "seq").astype(F32)
            for g in (g_qkv, g_out, g_up, g_down)
        ]
        d_mod = jnp.concatenate([sums_one[:2].reshape(-1), sums_two[:4].reshape(-1)])
        small = jnp.concatenate([sums_one[2], sums_two[4], sums_two[5], g_bup[0]])
        d_mod_all = lax.all_gather(d_mod, ("dp", "seq"))
        time_all = lax.all_gather(time_own[0].astype(F32), ("dp", "seq"))
        small = lax.psum(small, ("dp", "seq"))

        def mine(x, axis=0):
            size = x.shape[axis] // dps
            return lax.dynamic_slice_in_dim(x, dp * size, size, axis)

        features = jax.nn.silu(time_features(time_all, w_ada.shape[0] // 2))
        s_w_ada = jnp.dot(mine(features, 1).T, d_mod_all, precision=lax.Precision.HIGHEST)
        s_b_ada = jnp.sum(mine(d_mod_all, 1), axis=0)
        s_gain_one = mine(small[:width])
        s_gain_two = mine(small[width : 2 * width])
        s_b_down = mine(small[2 * width : 3 * width])
        s_b_up = mine(small[3 * width :])

    s_qkv, s_out, s_up, s_down = shards

    return (
        output,
        grad_tokens,
        s_w_ada,
        s_b_ada,
        s_gain_one,
        s_qkv,
        s_out,
        s_gain_two,
        s_up,
        s_b_up,
        s_down,
        s_b_down,
    )


def solution(mesh):
    rows = P("dp", "seq", None)
    return jax.shard_map(
        per_device,
        mesh=mesh,
        in_specs=(rows, rows, P("dp"), P("dp"), P("dp")) + (P(),) * 10,
        out_specs=(
            rows,
            rows,
            P("dp", None),
            P("dp"),
            P("dp"),
            P("dp", None),
            P("dp", None),
            P("dp"),
            P("dp", None),
            P("dp"),
            P("dp", None),
            P("dp"),
        ),
        check_vma=False,
    )
```

```python
import functools
import math

import jax
import jax.numpy as jnp
import numpy as np
from jax import lax
from jax.experimental import pallas as pl
from jax.experimental.pallas import tpu as pltpu
from jax.sharding import PartitionSpec as P

HEADS = 12
HD = 64
PAIRS = HEADS // 2
NORM_EPS = 1e-05
LOG2E = math.log2(math.e)
BF = jnp.bfloat16
F32 = jnp.float32
MIB = 1 << 20

NN = (((1,), (0,)), ((), ()))
NT = (((1,), (1,)), ((), ()))
TN = (((0,), (0,)), ((), ()))


def mm(a, b, dims=NN):
    return lax.dot_general(a, b, dims, preferred_element_type=F32)


def norm_parts(x):
    centre = x - jnp.mean(x, axis=-1, keepdims=True)
    rstd = lax.rsqrt(jnp.mean(centre * centre, axis=-1, keepdims=True) + NORM_EPS)
    return centre * rstd, rstd


def norm_pull(n, rstd, dn):
    return rstd * (
        dn - jnp.mean(dn, axis=-1, keepdims=True) - n * jnp.mean(dn * n, axis=-1, keepdims=True)
    )


def col_sum(x):
    return jnp.sum(x, axis=0, keepdims=True)


def rows_of(size, index):
    return pl.ds(pl.multiple_of(index * size, size), size)


def params(mib=56, collective_id=None):
    if collective_id is None:
        return pltpu.CompilerParams(vmem_limit_bytes=mib * MIB)
    return pltpu.CompilerParams(
        vmem_limit_bytes=mib * MIB, collective_id=collective_id, has_side_effects=True
    )


def whole(shape):
    zeros = (0,) * len(shape)
    return pl.BlockSpec(shape, lambda *_: zeros)


MESH = pl.DeviceIdType.MESH
ANY = pl.BlockSpec(memory_space=pl.ANY)
SEMS = [pltpu.SemaphoreType.DMA, pltpu.SemaphoreType.DMA]


def greet(*partners):
    barrier = pltpu.get_barrier_semaphore()
    for partner in partners:
        pl.semaphore_signal(barrier, inc=1, device_id=partner, device_id_type=MESH)
    pl.semaphore_wait(barrier, len(partners))


def remote(src, dst, send, recv, device):
    return pltpu.make_async_remote_copy(
        src_ref=src, dst_ref=dst, send_sem=send, recv_sem=recv, device_id=device, device_id_type=MESH
    )


def seq_partner():
    return (lax.axis_index("dp"), 1 - lax.axis_index("seq"))


def swap_start(src, dst, send, recv):
    partner = seq_partner()
    greet(partner)
    remote(src, dst, send, recv, partner).start()


def swap_wait(src, dst, send, recv):
    remote(src, dst, send, recv, seq_partner()).wait()


class Links:
    def __init__(self, sems, zs):
        self.sems, self.used, self.zs = sems, 0, zs
        dp, self.x = lax.axis_index("dp"), lax.axis_index("seq")
        self.z, self.y, self.c = dp // 4, lax.rem(dp // 2, 2), lax.rem(dp, 2)
        self.core = (dp + 1 - 2 * self.c, self.x)
        self.across = (dp + 2 - 4 * self.y, self.x)
        self.facing = (dp, 1 - self.x)
        self.far = [lax.rem(self.z + k, zs) for k in range(1, zs)]
        self.upper, self.lower = self.z // 2, lax.rem(self.z, 2)
        self.near = self.at_z(2 * self.upper + 1 - self.lower)
        self.beyond = self.at_z(2 * (1 - self.upper) + self.lower)

    def at_z(self, f):
        return (f * 4 + 2 * self.y + self.c, self.x)

    def take(self, count):
        self.used += count
        return self.used - count

    def local(self, src, dst):
        sem = self.take(1)
        return lambda: pltpu.make_async_copy(src(), dst(), self.sems.at[sem])

    def swap(self, src, dst, device):
        sem = self.take(2)
        return lambda: remote(src(), dst(), self.sems.at[sem], self.sems.at[sem + 1], device)

    def spread(self, src, dst):
        sem = self.take(2 * self.zs)

        def make(f, slot):
            return remote(
                src(f), dst(slot), self.sems.at[sem + f], self.sems.at[sem + self.zs + slot], self.at_z(f)
            )

        def start():
            for f in self.far:
                make(f, self.z).start()

        def wait():
            for f in self.far:
                make(f, self.z).wait_send()
                make(f, f).wait_recv()

        return start, wait

    def to_goal(self, src, dst, goal):
        upper, lower = goal // 2, goal % 2
        near = self.swap(src, lambda: dst().at[0], self.near)
        beyond = self.swap(src, lambda: dst().at[1], self.beyond)
        on_side = self.lower == lower

        def start():
            pl.when(self.lower != lower)(lambda: near().start())

        def middle():
            pl.when(self.lower != lower)(lambda: near().wait_send())

            @pl.when(on_side)
            def _():
                near().wait_recv()
                src()[...] = src()[...] + dst()[0]
                pl.when(self.upper != upper)(lambda: beyond().start())

        def finish():
            pl.when(on_side & (self.upper != upper))(lambda: beyond().wait_send())

            @pl.when(on_side & (self.upper == upper))
            def _():
                beyond().wait_recv()
                src()[...] = src()[...] + dst()[1]

        return start, middle, finish


def grid_of(*sizes):
    return [()] if not sizes else [(i,) + r for i in range(sizes[0]) for r in grid_of(*sizes[1:])]


def round_up(value, unit):
    return -(-value // unit) * unit


def early_mod_rows(width):
    return round_up(4 * width // 128 + 1, 16)


def early_sum_rows(width, ff):
    return round_up((2 * width + ff) // 128, 8)


def put_rows(ref, start, row):
    for k in range(row.shape[1] // 128):
        ref[start + k : start + k + 1, :] = row[:, k * 128 : (k + 1) * 128].astype(ref.dtype)


def once(shape):
    zeros = (0,) * len(shape)
    return pl.BlockSpec(shape, lambda *_: zeros, pipeline_mode=pl.Buffered(1))


def split_three(x):
    parts = []
    for _ in range(3):
        low = x.astype(BF)
        parts.append(low)
        x = x - low.astype(F32)
    return parts


def features_of(angles, is_sin):
    raw = jnp.where(is_sin, jnp.sin(angles), jnp.cos(angles))
    return raw / (1.0 + jnp.exp(-raw))


def project_kernel(
    time_ref,
    start_ref,
    extent_ref,
    tokens_ref,
    cos_ref,
    sin_ref,
    w_ada_ref,
    b_ada_ref,
    gain_one_ref,
    gain_two_ref,
    b_down_ref,
    w_ref,
    act_ref,
    out_ref,
    w_t_ref,
    rem_ref,
    vec_one_ref,
    vec_two_ref,
    span_ref,
    cos_out,
    sin_out,
    own,
    rem,
    w_t,
    qkv,
    sems,
):
    step = pl.program_id(0)
    half, width = own.shape
    rows = w_t_ref.shape[0]
    tile = 128
    chunk = half // 2
    x = lax.axis_index("seq")
    keep = pltpu.make_async_copy(tokens_ref.at[x], own, sems.at[0])
    cross = [
        remote(
            tokens_ref.at[1 - x, k * chunk : (k + 1) * chunk],
            rem.at[k * chunk : (k + 1) * chunk],
            sems.at[1 + k],
            sems.at[3 + k],
            seq_partner(),
        )
        for k in range(2)
    ]
    spans = (slice(0, half), slice(half, half + chunk), slice(half + chunk, 2 * half))
    store = [
        pltpu.make_async_copy(qkv.at[:, span], out_ref.at[:, span], sems.at[5 + k])
        for k, span in enumerate(spans)
    ]

    def norm(src, first, size, start):
        scale, shift = vec_one_ref[0:1, :], vec_one_ref[1:2, :]
        for t in range(0, size, tile):
            n, _ = norm_parts(src[first + t : first + t + tile, :].astype(F32))
            act_ref[:, start + t : start + t + tile] = (n * scale + shift).astype(BF).T

    @pl.when(step == 0)
    def _():
        greet(seq_partner())
        for copy in cross:
            copy.start()
        keep.start()
        pairs = w_ada_ref.shape[0] // 2
        time = time_ref[x]
        lane = lax.broadcasted_iota(jnp.int32, (8, 2 * pairs), 1)
        place = jnp.where(lane < pairs, lane, lane - pairs).astype(F32)
        frequency = jnp.exp(-math.log(10000.0) * place / pairs)
        cond = features_of(time.astype(F32) * frequency, lane >= pairs)
        modulation = b_ada_ref[...].reshape(1, 6 * width)
        for part in split_three(cond):
            modulation = modulation + mm(part, w_ada_ref[...])[0:1, :]
        pieces = [modulation[:, k * width : (k + 1) * width] for k in range(6)]
        shift_one, scale_one, gate_one, shift_two, scale_two, gate_two = pieces
        gain_one, gain_two = (ref[...].reshape(1, width) for ref in (gain_one_ref, gain_two_ref))
        zeros = jnp.zeros((1, width), F32)
        first = (gain_one * (1.0 + scale_one), shift_one, gain_one, scale_one)
        for k, row in enumerate(first + (zeros,) * 4):
            vec_one_ref[k : k + 1, :] = row
        lanes = lax.broadcasted_iota(jnp.int32, (1, width), 1)
        stamp = jnp.where(lanes == 0, time // 32, jnp.where(lanes == 1, lax.rem(time, 32), 0))
        second = (
            gate_one,
            gain_two * (1.0 + scale_two),
            shift_two,
            gate_two,
            b_down_ref[...].reshape(1, width),
            gain_two,
            scale_two,
            stamp.astype(F32),
        )
        for k, row in enumerate(second):
            vec_two_ref[k : k + 1, :] = row
        begin, end = start_ref[x], start_ref[x] + extent_ref[x]
        index = lax.broadcasted_iota(jnp.int32, (half, 1), 0)
        for part, where in enumerate((x, 1 - x)):
            place = index + where * half
            inside = (place >= begin) & (place < end)
            span_ref[part * half : (part + 1) * half, :] = jnp.where(inside, 2.0, 0.5)
            cos_out[:, part * half : (part + 1) * half] = cos_ref[where]
            sin_out[:, part * half : (part + 1) * half] = sin_ref[where]
        keep.wait()
        norm(own, 0, half, 0)

    def rotated(proj, block, cols, factor):
        cos, sin = cos_out[:, cols] * factor, sin_out[:, cols] * factor
        parts = []
        for h in range(rows // HD):
            a = proj[h * HD : h * HD + HD // 2]
            b = proj[h * HD + HD // 2 : (h + 1) * HD]
            parts += [(a * cos - b * sin).astype(BF), (b * cos + a * sin).astype(BF)]
        qkv[block, cols] = jnp.concatenate(parts, axis=0)

    @pl.when(step < 6)
    def _():
        block = rows_of(rows, step)
        flipped = w_ref[...].T
        w_t[block, :] = flipped
        w_t_ref[...] = flipped
        proj = mm(flipped, act_ref[:, spans[0]])

        @pl.when(step < 4)
        def _():
            rotated(proj, block, spans[0], jnp.where(step < 2, HD**-0.5, 1.0))

        @pl.when(step >= 4)
        def _():
            qkv[block, spans[0]] = proj.astype(BF)

    for k in range(2):

        @pl.when(step == 6 + k)
        def _(k=k):
            store[k].start()
            cross[k].wait()
            got = slice(k * chunk, (k + 1) * chunk)
            rem_ref[got, :] = rem[got, :]
            norm(rem, k * chunk, chunk, half + k * chunk)
            cols = spans[1 + k]
            for turn in range(6):
                block = slice(turn * rows, (turn + 1) * rows)
                proj = mm(w_t[block, :], act_ref[:, cols])
                if turn < 4:
                    rotated(proj, block, cols, HD**-0.5 if turn < 2 else 1.0)
                else:
                    qkv[block, cols] = proj.astype(BF)
            if k == 1:
                store[2].start()
                for copy in store:
                    copy.wait()


def rotary_constants(length):
    angles = np.arange(length, dtype=np.float32)[None, :] * np.exp(
        -math.log(10000.0) * np.arange(HD // 2, dtype=np.float32) / np.float32(HD // 2)
    ).astype(np.float32)[:, None]
    angles = angles.reshape(HD // 2, 2, length // 2).transpose(1, 0, 2).astype(np.float64)
    return np.cos(angles).astype(np.float32), np.sin(angles).astype(np.float32)


def project(tokens, time_index, span_starts, span_lengths, w_ada, b_ada, gains, b_down, w_qkv):
    _, half, width = tokens.shape
    length = 2 * half
    blk = width // 2
    cos_all, sin_all = rotary_constants(length)
    smem = pl.BlockSpec(memory_space=pltpu.SMEM)
    outs = [
        ((width, length), BF),
        ((3 * width, length), BF),
        ((3 * width, width), BF),
        ((half, width), BF),
        ((8, width), F32),
        ((8, width), F32),
        ((length, 1), F32),
        ((HD // 2, length), F32),
        ((HD // 2, length), F32),
    ]
    out_specs = [once(shape) for shape, _ in outs]
    out_specs[1] = ANY
    out_specs[2] = pl.BlockSpec((blk, width), lambda i: (jnp.minimum(i, 5), 0))
    rows = [b_ada, *gains, b_down]
    return pl.pallas_call(
        project_kernel,
        grid=(8,),
        in_specs=[smem, smem, smem, ANY, once(cos_all.shape), once(sin_all.shape), once(w_ada.shape)]
        + [once(r.shape) for r in rows]
        + [pl.BlockSpec((width, blk), lambda i: (0, jnp.minimum(i, 5)))],
        out_specs=out_specs,
        out_shape=[jax.ShapeDtypeStruct(*o) for o in outs],
        scratch_shapes=[
            pltpu.VMEM((half, width), BF),
            pltpu.VMEM((half, width), BF),
            pltpu.VMEM((3 * width, width), BF),
            pltpu.VMEM((3 * width, length), BF),
            pltpu.SemaphoreType.DMA((8,)),
        ],
        compiler_params=params(collective_id=6),
        cost_estimate=pl.CostEstimate(
            flops=6 * length * width * width, bytes_accessed=20 << 20, transcendentals=0
        ),
        name="project",
    )(time_index, span_starts, span_lengths, tokens, cos_all, sin_all, w_ada, *rows, w_qkv)


def attend_kernel(
    q_ref, k_ref, v_ref, cot_ref, att_ref, e_ref, linv_ref, cot_rem, q_mask, v_ext, send, recv
):
    step = pl.program_id(0)
    cot_send = cot_ref.at[1 - lax.axis_index("seq")]

    @pl.when(step == 0)
    def _():
        swap_start(cot_send, cot_rem, send, recv)

    tokens = q_ref.shape[1]
    tile = 256
    zero = jnp.zeros((HD, tokens), BF)
    k_nat = k_ref[...].T
    q_mask[0, 0:HD, :] = q_ref[0:HD, :]
    q_mask[0, HD:, :] = zero
    q_mask[1, 0:HD, :] = zero
    q_mask[1, HD:, :] = q_ref[HD:, :]
    for h in range(2):
        v_ext[h, 0:HD, :] = v_ref[h * HD : (h + 1) * HD, :]
        v_ext[h, HD:, :] = jnp.ones((16, tokens), BF)
    def score(h, cols):
        return mm(k_nat, q_mask[h, :, cols])

    def soften(h, cols, s):
        e_ref[h, :, cols] = jnp.exp(s - jnp.max(s, axis=0, keepdims=True)).astype(BF)

    def mix(h, cols):
        mixed = mm(v_ext[h], e_ref[h, :, cols])
        linv = 1.0 / mixed[HD : HD + 1, :]
        linv_ref[0, h : h + 1, cols] = linv
        att_ref[h * HD : (h + 1) * HD, cols] = (mixed[0:HD, :] * linv).astype(BF)

    units = [(h, slice(t, t + tile)) for t in range(0, tokens, tile) for h in range(2)]
    coming = score(*units[0])
    for i, unit in enumerate(units):
        here = coming
        if i + 1 < len(units):
            coming = score(*units[i + 1])
        soften(*unit, here)
        if i > 0:
            mix(*units[i - 1])
    mix(*units[-1])

    @pl.when(step == pl.num_programs(0) - 1)
    def _():
        swap_wait(cot_send, cot_rem, send, recv)


def attend(qkv_t, cotangent):
    tokens = qkv_t.shape[1]
    width = HEADS * HD

    def part(k):
        return pl.BlockSpec((2 * HD, tokens), lambda i: (i + k * PAIRS, 0))

    return pl.pallas_call(
        attend_kernel,
        grid=(PAIRS,),
        in_specs=[part(0), part(1), part(2), ANY],
        out_specs=[
            part(0),
            pl.BlockSpec((2, tokens, tokens), lambda i: (i, 0, 0)),
            pl.BlockSpec((1, 8, tokens), lambda i: (i, 0, 0)),
            ANY,
        ],
        out_shape=[
            jax.ShapeDtypeStruct((width, tokens), BF),
            jax.ShapeDtypeStruct((HEADS, tokens, tokens), BF),
            jax.ShapeDtypeStruct((PAIRS, 8, tokens), F32),
            jax.ShapeDtypeStruct(cotangent.shape[1:], BF),
        ],
        scratch_shapes=[
            pltpu.VMEM((2, 2 * HD, tokens), BF),
            pltpu.VMEM((2, HD + 16, tokens), BF),
        ]
        + SEMS,
        compiler_params=params(collective_id=1),
        cost_estimate=pl.CostEstimate(
            flops=16 * tokens * tokens * width,
            bytes_accessed=30 << 20,
            transcendentals=HEADS * tokens * tokens,
        ),
        name="attend",
    )(qkv_t, qkv_t, qkv_t, cotangent)


def gelu_both(u):
    c = math.sqrt(2.0 / math.pi)
    u2 = u * u
    th = jnp.tanh(u * (c + (c * 0.044715) * u2))
    half = 0.5 * (1.0 + th)
    value = u * half
    slope = half + (0.5 * u) * (1.0 - th * th) * (c + (3.0 * c * 0.044715) * u2)
    return value, slope


def middle_kernel(
    att_ref,
    tok_own,
    tok_rem,
    cot_own,
    cot_rem,
    span_ref,
    vec_ref,
    b_up_ref,
    w_out_ref,
    w_up_ref,
    w_down_ref,
    out_own,
    out_rem,
    dx_ref,
    d_att_ref,
    g_out_ref,
    g_up_ref,
    g_down_ref,
    g_bup_ref,
    sums_ref,
    branch,
    x_one,
    act_two,
    d_down,
    down_acc,
    d_act,
    d_branch,
):
    step = pl.program_id(0)
    steps = pl.num_programs(0)
    tokens = att_ref.shape[1]
    half = tokens // 2
    tile = 256
    per_half = half // tile
    gate_one = vec_ref[0:1, :]
    mult_two = vec_ref[1:2, :]
    shift_two = vec_ref[2:3, :]
    gate_two = vec_ref[3:4, :]
    b_down = vec_ref[4:5, :]
    gain_two = vec_ref[5:6, :]
    scale_two = vec_ref[6:7, :]

    @pl.when(step == 0)
    def _():
        for part, (tok, cot) in enumerate(((tok_own, cot_own), (tok_rem, cot_rem))):
            for t in range(per_half):
                src = slice(t * tile, (t + 1) * tile)
                dst = slice(part * half + t * tile, part * half + (t + 1) * tile)
                br = mm(att_ref[:, dst], w_out_ref[...], TN)
                branch[dst, :] = br
                x = tok[src, :].astype(F32) + gate_one * br
                x_one[dst, :] = x
                n, _ = norm_parts(x)
                act_two[dst, :] = (n * mult_two + shift_two).astype(BF)
                grad_out = cot[src, :].astype(F32) * span_ref[dst, :]
                d_down[dst, :] = (gate_two * grad_out).astype(BF)

    up = mm(act_two[...], w_up_ref[...]) + b_up_ref[...]
    value, slope = gelu_both(up)
    hidden = value.astype(BF)
    d_hidden = mm(d_down[...], w_down_ref[...], NT)
    d_up_full = slope * d_hidden
    d_up = d_up_full.astype(BF)
    g_bup_ref[...] = col_sum(d_up.astype(F32))
    down_part = mm(hidden, w_down_ref[...])
    d_act_part = mm(d_up, w_up_ref[...], NT)
    g_down_ref[...] = mm(hidden, d_down[...], TN).astype(BF)
    g_up_ref[...] = mm(act_two[...], d_up, TN).astype(BF)

    @pl.when(step == 0)
    def _():
        down_acc[...] = down_part
        d_act[...] = d_act_part

    @pl.when(step > 0)
    def _():
        down_acc[...] += down_part
        d_act[...] += d_act_part

    @pl.when(step == steps - 1)
    def _():
        zero = jnp.zeros((1, gate_one.shape[1]), F32)
        s_gate_two, s_shift, s_pull, s_gate_one, s_bdown = zero, zero, zero, zero, zero
        for part, (cot, out) in enumerate(((cot_own, out_own), (cot_rem, out_rem))):
            for t in range(per_half):
                src = slice(t * tile, (t + 1) * tile)
                dst = slice(part * half + t * tile, part * half + (t + 1) * tile)
                x = x_one[dst, :]
                down = down_acc[dst, :] + b_down
                out[src, :] = (x + gate_two * down).astype(BF)
                grad_out = cot[src, :].astype(F32) * span_ref[dst, :]
                s_gate_two += col_sum(grad_out * down)
                s_bdown += col_sum(d_down[dst, :].astype(F32))
                n, rstd = norm_parts(x)
                da = d_act[dst, :]
                s_shift += col_sum(da)
                s_pull += col_sum(da * n)
                dx = grad_out + norm_pull(n, rstd, da * mult_two)
                dx_ref[dst, :] = dx
                s_gate_one += col_sum(dx * branch[dst, :])
                d_branch[dst, :] = (gate_one * dx).astype(BF)
        sums_ref[0:1, :] = s_gate_one
        sums_ref[1:2, :] = s_shift
        sums_ref[2:3, :] = s_pull * gain_two
        sums_ref[3:4, :] = s_gate_two
        sums_ref[4:5, :] = s_pull * (1.0 + scale_two)
        sums_ref[5:6, :] = s_bdown
        sums_ref[6:8, :] = jnp.zeros((2, gate_one.shape[1]), F32)
        g_out_ref[...] = mm(att_ref[...], d_branch[...]).astype(BF)
        d_att_ref[...] = mm(w_out_ref[...], d_branch[...], NT).astype(BF)


def middle(att_t, tok_own, tok_rem, cot_own, cot_rem, span, vec, b_up, w_out, w_up, w_down):
    width, tokens = att_t.shape
    half = tokens // 2
    ff = w_up.shape[1]
    tile = 512
    return pl.pallas_call(
        middle_kernel,
        grid=(ff // tile,),
        in_specs=[
            whole(att_t.shape),
            whole(tok_own.shape),
            whole(tok_rem.shape),
            whole(cot_own.shape),
            whole(cot_rem.shape),
            whole(span.shape),
            whole(vec.shape),
            pl.BlockSpec((1, tile), lambda i: (0, i)),
            whole(w_out.shape),
            pl.BlockSpec((width, tile), lambda i: (0, i)),
            pl.BlockSpec((tile, width), lambda i: (i, 0)),
        ],
        out_specs=[
            whole((half, width)),
            whole((half, width)),
            whole((tokens, width)),
            whole((width, tokens)),
            whole((width, width)),
            pl.BlockSpec((width, tile), lambda i: (0, i)),
            pl.BlockSpec((tile, width), lambda i: (i, 0)),
            pl.BlockSpec((1, tile), lambda i: (0, i)),
            whole((8, width)),
        ],
        out_shape=[
            jax.ShapeDtypeStruct((half, width), BF),
            jax.ShapeDtypeStruct((half, width), BF),
            jax.ShapeDtypeStruct((tokens, width), F32),
            jax.ShapeDtypeStruct((width, tokens), BF),
            jax.ShapeDtypeStruct((width, width), BF),
            jax.ShapeDtypeStruct((width, ff), BF),
            jax.ShapeDtypeStruct((ff, width), BF),
            jax.ShapeDtypeStruct((1, ff), F32),
            jax.ShapeDtypeStruct((8, width), F32),
        ],
        scratch_shapes=[
            pltpu.VMEM((tokens, width), F32),
            pltpu.VMEM((tokens, width), F32),
            pltpu.VMEM((tokens, width), BF),
            pltpu.VMEM((tokens, width), BF),
            pltpu.VMEM((tokens, width), F32),
            pltpu.VMEM((tokens, width), F32),
            pltpu.VMEM((tokens, width), BF),
        ],
        compiler_params=params(),
        cost_estimate=pl.CostEstimate(
            flops=12 * tokens * width * ff + 6 * tokens * width * width,
            bytes_accessed=40 << 20,
            transcendentals=tokens * ff,
        ),
        name="middle",
    )(att_t, tok_own, tok_rem, cot_own, cot_rem, span, vec, b_up, w_out, w_up, w_down)


def middle_links_kernel(
    zs,
    att_ref,
    tokens_ref,
    tok_rem,
    cot_ref,
    cot_rem,
    span_ref,
    vec_ref,
    b_up_ref,
    w_out_ref,
    w_up_ref,
    w_down_ref,
    out_own,
    out_rem,
    dx_ref,
    d_att_ref,
    g_out_ref,
    g_up_ref,
    g_down_ref,
    up_last_ref,
    up_one_ref,
    up_two_ref,
    down_last_ref,
    down_one_ref,
    down_two_ref,
    mod_ref,
    sum_ref,
    branch,
    x_one,
    act_two,
    d_down,
    down_acc,
    d_act,
    d_branch,
    hidden,
    d_up,
    up_core,
    up_side,
    up_y,
    up_z,
    down_core,
    down_y,
    down_side,
    down_z,
    sems,
):
    step = pl.program_id(0)
    steps = zs
    tokens = att_ref.shape[1]
    width = att_ref.shape[0]
    half = tokens // 2
    cut = width // 2
    tile = 256
    per_half = half // tile
    gate_one = vec_ref[0:1, :]
    mult_two = vec_ref[1:2, :]
    shift_two = vec_ref[2:3, :]
    gate_two = vec_ref[3:4, :]
    b_down = vec_ref[4:5, :]
    gain_two = vec_ref[5:6, :]
    scale_two = vec_ref[6:7, :]

    links = Links(sems, zs)
    x, y, z, c = links.x, links.y, links.z, links.c
    tok_own, cot_own = tokens_ref.at[x], cot_ref.at[x]
    tiles = range(steps - 1)

    def swaps(src, dst, device):
        return [links.swap(lambda j=j: src(j), lambda j=j: dst.at[j], device) for j in tiles]

    up_to_core = swaps(lambda j: g_up_ref.at[:, :, :, :, 1 - c], up_core, links.core)
    down_to_core = swaps(lambda j: g_down_ref.at[:, 1 - c], down_core, links.core)
    up_to_side = swaps(lambda j: up_core.at[j, 1 - x], up_side, links.facing)
    down_to_y = swaps(lambda j: down_core.at[j, 1 - y], down_y, links.across)
    up_to_y = swaps(lambda j: up_core.at[j, x, :, :, 1 - y], up_y, links.across)
    down_to_side = swaps(lambda j: down_core.at[j, y, 1 - x], down_side, links.facing)
    h, b = links.upper, links.lower
    down_goal = links.to_goal(lambda: down_core.at[0, y, x], lambda: down_z, 0)
    up_near = links.swap(lambda: up_core.at[0, x, :, 1 - b, y], lambda: up_z.at[0:2], links.near)
    up_beyond = links.swap(lambda: up_core.at[0, x, 1 - h, b, y], lambda: up_z.at[2], links.beyond)

    def core_stage(j):
        up_to_core[j]().start()
        down_to_core[j]().start()

    def first_stage(j):
        up_to_core[j]().wait()
        for i in grid_of(2, 2, 2, 2):
            up_core[(j, *i)] = up_core[(j, *i)] + g_up_ref[(*i, c)]
        up_to_side[j]().start()
        down_to_core[j]().wait()
        for i, k in grid_of(2, 2):
            down_core[j, i, k] = down_core[j, i, k] + g_down_ref[i, c, k]
        down_to_y[j]().start()

    def first_done(j):
        up_to_side[j]().wait()
        for i in grid_of(2, 2, 2):
            up_core[(j, x, *i)] = up_core[(j, x, *i)] + up_side[(j, *i)]
        down_to_y[j]().wait()
        for k in range(2):
            down_core[j, y, k] = down_core[j, y, k] + down_y[j, k]

    def second_stage(j):
        first_done(j)
        up_to_y[j]().start()
        down_to_side[j]().start()

    def second_done(j):
        up_to_y[j]().wait()
        for i in grid_of(2, 2):
            up_core[(j, x, *i, y)] = up_core[(j, x, *i, y)] + up_y[(j, *i)]
        down_to_side[j]().wait()
        down_core[j, y, x] = down_core[j, y, x] + down_side[j]

    def third_stage():
        second_done(0)
        up_near().start()
        down_goal[0]()

    def fourth_stage():
        up_near().wait()
        for k in range(2):
            up_core[0, x, k, b, y] = up_core[0, x, k, b, y] + up_z[k]
        up_beyond().start()
        down_goal[1]()

    @pl.when(step == 0)
    def _():
        greet(links.core, links.across, links.facing, *[links.at_z(f) for f in links.far])
        for part, (tok, cot) in enumerate(((tok_own, cot_own), (tok_rem, cot_rem))):
            for t in range(per_half):
                src = slice(t * tile, (t + 1) * tile)
                dst = slice(part * half + t * tile, part * half + (t + 1) * tile)
                br = mm(att_ref[:, dst], w_out_ref[...], TN)
                branch[dst, :] = br
                xv = tok[src, :].astype(F32) + gate_one * br
                x_one[dst, :] = xv
                n, _ = norm_parts(xv)
                act_two[dst, :] = (n * mult_two + shift_two).astype(BF)
                grad_out = cot[src, :].astype(F32) * span_ref[dst, :]
                d_down[dst, :] = (gate_two * grad_out).astype(BF)
                down_acc[dst, :] = jnp.zeros((tile, width), F32)
                d_act[dst, :] = jnp.zeros((tile, width), F32)

    chunk = tokens // 2

    def one(k, bup):
        rows = rows_of(chunk, k)
        up = mm(act_two[rows, :], w_up_ref[...]) + b_up_ref[...]
        d_hidden = mm(d_down[rows, :], w_down_ref[...], NT)
        value, slope = gelu_both(up)
        low = value.astype(BF)
        hidden[rows, :] = low
        d_up_low = (slope * d_hidden).astype(BF)
        d_up[rows, :] = d_up_low
        down_acc[rows, :] += mm(low, w_down_ref[...])
        d_act[rows, :] += mm(d_up_low, w_up_ref[...], NT)
        return bup + col_sum(d_up_low.astype(F32))

    bup = lax.fori_loop(0, 2, one, jnp.zeros((1, w_up_ref.shape[1]), F32))
    for j in range(steps):
        pl.when(step == j)(lambda j=j: put_rows(sum_ref, 2 * width // 128 + j * bup.shape[1] // 128, bup))

    @pl.when(step == 1)
    def _():
        first_stage(0)

    @pl.when(step == 2)
    def _():
        second_stage(0)
        first_stage(1)

    @pl.when(step == 3)
    def _():
        third_stage()
        second_stage(1)
        first_stage(2)

    chunk_out = width // 3
    g_down_flat = g_down_ref.reshape(width, width)
    g_up_flat = g_up_ref.reshape(2, width, cut)

    def grads(turn, carry):
        outs = rows_of(chunk_out, turn)
        g_down_flat[outs, :] = mm(hidden[:, outs], d_down[...], TN).astype(BF)
        g_up = mm(act_two[:, outs], d_up[...], TN).astype(BF)
        for k in range(2):
            g_up_flat[k, outs, :] = g_up[:, k * cut : (k + 1) * cut]
        return carry

    lax.fori_loop(0, 3, grads, 0)

    @pl.when(step == 0)
    def _():
        core_stage(0)

    @pl.when(step == 1)
    def _():
        core_stage(1)

    @pl.when(step == 2)
    def _():
        core_stage(2)

    @pl.when(step == steps - 1)
    def _():
        fourth_stage()
        zero = jnp.zeros((1, width), F32)
        s_gate_two, s_shift, s_pull, s_gate_one, s_bdown = zero, zero, zero, zero, zero
        for part, (cot, out) in enumerate(((cot_own, out_own), (cot_rem, out_rem))):
            for t in range(per_half):
                src = slice(t * tile, (t + 1) * tile)
                dst = slice(part * half + t * tile, part * half + (t + 1) * tile)
                xv = x_one[dst, :]
                down = down_acc[dst, :] + b_down
                out[src, :] = (xv + gate_two * down).astype(BF)
                grad_out = cot[src, :].astype(F32) * span_ref[dst, :]
                s_gate_two += col_sum(grad_out * down)
                s_bdown += col_sum(d_down[dst, :].astype(F32))
                n, rstd = norm_parts(xv)
                da = d_act[dst, :]
                s_shift += col_sum(da)
                s_pull += col_sum(da * n)
                dx = grad_out + norm_pull(n, rstd, da * mult_two)
                dx_ref[dst, :] = dx
                s_gate_one += col_sum(dx * branch[dst, :])
                d_branch[dst, :] = (gate_one * dx).astype(BF)
        lines = width // 128
        mod_ref[4 * lines :, :] = jnp.zeros((mod_ref.shape[0] - 4 * lines, 128), BF)
        for k, row in enumerate((s_gate_one, s_shift, s_pull * gain_two, s_gate_two)):
            put_rows(mod_ref, k * lines, row)
        put_rows(mod_ref, 4 * lines, vec_ref[7:8, 0:128])
        put_rows(sum_ref, 0, s_pull * (1.0 + scale_two))
        put_rows(sum_ref, lines, s_bdown)
        g_out = mm(att_ref[...], d_branch[...]).astype(BF)
        for k in range(2):
            g_out_ref[k] = g_out[:, k * cut : (k + 1) * cut].reshape(g_out_ref.shape[1:])
        d_att_ref[...] = mm(w_out_ref[...], d_branch[...], NT).astype(BF)
        up_beyond().wait()
        up_last_ref[...] = up_core[0, x, h, b, y] + up_z[2]
        down_goal[2]()
        down_last_ref[...] = down_core[0, y, x]
        second_done(1)
        for i, k in grid_of(2, 2):
            up_one_ref[i, k] = up_core[1, x, i, k, y]
        down_one_ref[...] = down_core[1, y, x]
        first_done(2)
        up_two_ref[...] = up_core[2, x]
        down_two_ref[...] = down_core[2, y]


def middle_links(
    att_t, tok_all, tok_rem, cot_all, cot_rem, span, vec, b_up, w_out, w_up, w_down, zs
):
    width, tokens = att_t.shape
    half = tokens // 2
    cut = width // 2
    ff = w_up.shape[1]
    tile = ff // zs
    rows = width // (4 * zs)
    down_rows = tile // 4
    halves = (2, 2, 2, 2, 2, rows, cut)
    down_half = (down_rows // 2, width)
    owned = (2, 2, 2) + down_half
    outs = [
        ((half, width), BF),
        ((half, width), BF),
        ((tokens, width), F32),
        ((width, tokens), BF),
        (halves, BF),
        (halves, BF),
        (owned, BF),
        ((rows, cut), BF),
        ((2, 2, rows, cut), BF),
        ((2, 2, 2, rows, cut), BF),
        (down_half, BF),
        (down_half, BF),
        ((2,) + down_half, BF),
        ((early_mod_rows(width), 128), BF),
        ((early_sum_rows(width, ff), 128), F32),
    ]
    return pl.pallas_call(
        functools.partial(middle_links_kernel, zs),
        grid=(zs,),
        in_specs=[
            once(att_t.shape),
            once(tok_all.shape),
            once(tok_rem.shape),
            once(cot_all.shape),
            once(cot_rem.shape),
            once(span.shape),
            once(vec.shape),
            pl.BlockSpec((1, tile), lambda i: (0, i)),
            once(w_out.shape),
            pl.BlockSpec((width, tile), lambda i: (0, i)),
            pl.BlockSpec((tile, width), lambda i: (i, 0)),
        ],
        out_specs=[once(shape) for shape, _ in outs],
        out_shape=[jax.ShapeDtypeStruct(*o) for o in outs],
        scratch_shapes=[
            pltpu.VMEM((tokens, width), F32),
            pltpu.VMEM((tokens, width), F32),
            pltpu.VMEM((tokens, width), BF),
            pltpu.VMEM((tokens, width), BF),
            pltpu.VMEM((tokens, width), F32),
            pltpu.VMEM((tokens, width), F32),
            pltpu.VMEM((tokens, width), BF),
            pltpu.VMEM((tokens, tile), BF),
            pltpu.VMEM((tokens, tile), BF),
            pltpu.VMEM((zs - 1, 2, 2, 2, 2, rows, cut), BF),
            pltpu.VMEM((zs - 1, 2, 2, 2, rows, cut), BF),
            pltpu.VMEM((zs - 1, 2, 2, rows, cut), BF),
            pltpu.VMEM((3, rows, cut), BF),
            pltpu.VMEM((zs - 1, 2, 2) + down_half, BF),
            pltpu.VMEM((zs - 1, 2) + down_half, BF),
            pltpu.VMEM((zs - 1,) + down_half, BF),
            pltpu.VMEM((2,) + down_half, BF),
            pltpu.SemaphoreType.DMA((12 * (zs - 1) + 8,)),
        ],
        compiler_params=params(62, collective_id=4),
        cost_estimate=pl.CostEstimate(
            flops=12 * tokens * width * ff + 6 * tokens * width * width,
            bytes_accessed=40 << 20,
            transcendentals=tokens * ff,
        ),
        name="middle_links",
    )(att_t, tok_all, tok_rem, cot_all, cot_rem, span, vec, b_up, w_out, w_up, w_down)


def attend_back_kernel(
    q_ref,
    k_ref,
    v_ref,
    att_ref,
    d_att_ref,
    e_ref,
    linv_ref,
    cos_ref,
    sin_ref,
    give_ref,
    out_ref,
    take_ref,
    do_mask,
    send,
    recv,
):
    step = pl.program_id(0)

    @pl.when(step == 0)
    def _():
        swap_start(give_ref, take_ref, send, recv)

    tokens = q_ref.shape[1]
    tile = 256
    zero = jnp.zeros((HD, tokens), BF)
    v_nat = v_ref[...].T
    cos = cos_ref[...]
    sin = sin_ref[...]

    def unrotate(x):
        low = x.astype(BF).astype(F32)
        a, b = low[0 : HD // 2], low[HD // 2 :]
        return a * cos + b * sin, b * cos - a * sin

    for h in range(2):
        rows = slice(h * HD, (h + 1) * HD)
        linv = linv_ref[0, h : h + 1, :]
        d_o = d_att_ref[rows, :].astype(F32)
        d_os = (d_o * linv).astype(BF)
        do_mask[h, rows, :] = d_os
        do_mask[h, (1 - h) * HD : (2 - h) * HD, :] = zero
        inner = col_sum(d_o * att_ref[rows, :].astype(F32)) * linv
        d_values = mm(d_os, e_ref[h], NT)
        out_ref[2, rows, :] = d_values.astype(BF)
        d_keys = jnp.zeros((HD, tokens), F32)
        d_queries = []
        for t in range(tokens // tile):
            cols = slice(t * tile, (t + 1) * tile)
            d_probs = mm(v_nat, do_mask[h, :, cols])
            d_s = (e_ref[h, :, cols].astype(F32) * (d_probs - inner[:, cols])).astype(BF)
            d_queries.append(mm(k_ref[rows, :], d_s))
            d_keys += mm(q_ref[rows, cols], d_s, NT)
        dq = jnp.concatenate(d_queries, axis=1) * HD**-0.5
        lead, trail = unrotate(dq)
        out_ref[0, h * HD : h * HD + HD // 2, :] = lead.astype(BF)
        out_ref[0, h * HD + HD // 2 : (h + 1) * HD, :] = trail.astype(BF)
        lead, trail = unrotate(d_keys)
        out_ref[1, h * HD : h * HD + HD // 2, :] = lead.astype(BF)
        out_ref[1, h * HD + HD // 2 : (h + 1) * HD, :] = trail.astype(BF)

    @pl.when(step == pl.num_programs(0) - 1)
    def _():
        swap_wait(give_ref, take_ref, send, recv)


def attend_back(qkv_t, att_t, d_att_t, e, linv, cos_t, sin_t, give):
    tokens = qkv_t.shape[1]
    width = HEADS * HD

    def part(k):
        return pl.BlockSpec((2 * HD, tokens), lambda i: (i + k * PAIRS, 0))

    return pl.pallas_call(
        attend_back_kernel,
        grid=(PAIRS,),
        in_specs=[
            part(0),
            part(1),
            part(2),
            part(0),
            part(0),
            pl.BlockSpec((2, tokens, tokens), lambda i: (i, 0, 0)),
            pl.BlockSpec((1, 8, tokens), lambda i: (i, 0, 0)),
            whole(cos_t.shape),
            whole(sin_t.shape),
            ANY,
        ],
        out_specs=[pl.BlockSpec((3, 2 * HD, tokens), lambda i: (0, i, 0)), ANY],
        out_shape=[
            jax.ShapeDtypeStruct((3, width, tokens), BF),
            jax.ShapeDtypeStruct(give.shape, give.dtype),
        ],
        scratch_shapes=[pltpu.VMEM((2, 2 * HD, tokens), BF)] + SEMS,
        compiler_params=params(collective_id=2),
        cost_estimate=pl.CostEstimate(
            flops=32 * tokens * tokens * width, bytes_accessed=36 << 20, transcendentals=0
        ),
        name="attend_back",
    )(qkv_t, qkv_t, qkv_t, att_t, d_att_t, e, linv, cos_t, sin_t, give)


def tail_kernel(tok_own, tok_rem, d_proj_ref, w_ref, dx_ref, vec_ref, own_ref, rem_ref, sums_ref):
    step = pl.program_id(0)
    steps = pl.num_programs(0)
    mult_one = vec_ref[0:1, :]
    gain_one = vec_ref[2:3, :]
    scale_one = vec_ref[3:4, :]
    d_act = mm(d_proj_ref[...], w_ref[...], TN)

    def finish(tok, out):
        n, rstd = norm_parts(tok[...].astype(F32))
        grad = dx_ref[...] + norm_pull(n, rstd, d_act * mult_one)
        out[...] = grad.astype(out.dtype)
        return col_sum(d_act), col_sum(d_act * n)

    @pl.when(step == 0)
    def _():
        shift, pull = finish(tok_rem, rem_ref)
        sums_ref[0:1, :] = shift
        sums_ref[1:2, :] = pull
        sums_ref[2:, :] = jnp.zeros((6, shift.shape[1]), F32)

    @pl.when(step == steps - 1)
    def _():
        shift, pull = finish(tok_own, own_ref)
        shift = sums_ref[0:1, :] + shift
        pull = sums_ref[1:2, :] + pull
        sums_ref[0:1, :] = shift
        sums_ref[1:2, :] = pull * gain_one
        sums_ref[2:3, :] = pull * (1.0 + scale_one)


def tail(tok_own, tok_rem, d_proj_t, w_qkv_t, dx, vec):
    half, width = tok_own.shape
    return pl.pallas_call(
        tail_kernel,
        grid=(2,),
        in_specs=[
            whole(tok_own.shape),
            whole(tok_rem.shape),
            pl.BlockSpec((3 * width, half), lambda i: (0, 1 - i)),
            whole(w_qkv_t.shape),
            pl.BlockSpec((half, width), lambda i: (1 - i, 0)),
            whole(vec.shape),
        ],
        out_specs=[whole((half, width)), whole((half, width)), whole((8, width))],
        out_shape=[
            jax.ShapeDtypeStruct((half, width), F32),
            jax.ShapeDtypeStruct((half, width), BF),
            jax.ShapeDtypeStruct((8, width), F32),
        ],
        compiler_params=params(),
        cost_estimate=pl.CostEstimate(
            flops=12 * half * width * width, bytes_accessed=20 << 20, transcendentals=0
        ),
        name="tail",
    )(tok_own, tok_rem, d_proj_t, w_qkv_t, dx, vec)


def weight_grad_kernel(act_ref, d_proj_ref, out_ref):
    out_ref[...] = mm(act_ref[...], d_proj_ref[...], NT).astype(BF)


def weight_grad(act_t, d_proj_t):
    width, tokens = act_t.shape
    cols = d_proj_t.shape[0]
    tile = 768
    return pl.pallas_call(
        weight_grad_kernel,
        grid=(cols // tile,),
        in_specs=[whole(act_t.shape), pl.BlockSpec((tile, tokens), lambda i: (i, 0))],
        out_specs=pl.BlockSpec((width, tile), lambda i: (0, i)),
        out_shape=jax.ShapeDtypeStruct((width, cols), BF),
        compiler_params=params(),
        cost_estimate=pl.CostEstimate(
            flops=2 * cols * width * tokens, bytes_accessed=12 << 20, transcendentals=0
        ),
        name="weight_grad",
    )(act_t, d_proj_t)


def gather_stages(links, ref):
    z, y, c, x = links.z, links.y, links.c, links.x

    def pair(mine, theirs, device):
        sem = links.take(2)

        def make(slot):
            return remote(slot(), slot(), links.sems.at[sem], links.sems.at[sem + 1], device)

        def wait():
            make(mine).wait_send()
            make(theirs).wait_recv()

        return (lambda: make(mine).start()), wait

    sem = links.take(2 * links.zs)

    def make(f, slot):
        block = ref.at[slot, :, :, x]
        return remote(
            block, block, links.sems.at[sem + f], links.sems.at[sem + links.zs + slot], links.at_z(f)
        )

    def far_start():
        for f in links.far:
            make(f, z).start()

    def far_wait():
        for f in links.far:
            make(f, z).wait_send()
            make(f, f).wait_recv()

    return [
        pair(lambda: ref.at[z, y, c, x], lambda: ref.at[z, y, 1 - c, x], links.core),
        pair(lambda: ref.at[z, y, :, x], lambda: ref.at[z, 1 - y, :, x], links.across),
        (far_start, far_wait),
        pair(lambda: ref.at[:, :, :, x], lambda: ref.at[:, :, :, 1 - x], links.facing),
    ]


def sum_stages(links, ref, take, far):
    swaps = [
        links.swap(lambda: ref, lambda k=k: take.at[k], device)
        for k, device in enumerate((links.core, links.across, links.facing))
    ]
    far_start, far_wait = links.spread(lambda f: ref, lambda slot: far.at[slot])

    def finish(k):
        swaps[k]().wait()
        ref[...] += take[k]

    def far_finish():
        far_wait()
        far[links.z] = ref[...]
        total = far[0]
        for f in range(1, links.zs):
            total += far[f]
        ref[...] = total

    return [
        (lambda: swaps[0]().start(), lambda: finish(0)),
        (lambda: swaps[1]().start(), lambda: finish(1)),
        (far_start, far_finish),
        (lambda: swaps[2]().start(), lambda: finish(2)),
    ]


def back_kernel(zs, split, ins, outs, scratch):
    (
        q_ref,
        k_ref,
        v_ref,
        att_ref,
        d_att_ref,
        e_ref,
        linv_ref,
        cos_ref,
        sin_ref,
        give_ref,
        up_last_ref,
        up_one_ref,
        up_two_ref,
        down_last_ref,
        down_one_ref,
        down_two_ref,
        raw_up,
        raw_out,
        raw_down,
        mod_ref,
        sum_ref,
        act_in,
        w_in,
        tok_own_in,
        tok_rem_in,
        dx_in,
        vec_ref,
    ) = ins
    result, grad_ref, grad_take, s_qkv, s_out, s_up, s_down, *small_outs = outs
    (
        do_mask,
        d_proj,
        sems,
        u_own,
        u_y,
        u_z,
        u_last,
        u_facing,
        w_own,
        w_core,
        w_y,
        w_z,
        w_far,
        w_last,
        w_facing,
        d_own,
        d_core,
        d_y,
        d_side,
        d_sum,
        d_z,
        d_last,
        d_facing,
        q_raws,
        q_cores,
        q_ys,
        q_zs,
        q_lasts,
        q_facings,
        g_send,
        g_take,
        early_take,
        early_far,
        late_take,
        late_far,
        mod_early,
        mod_late,
        sum_early,
        sum_late,
        act_ref,
        w_ref,
        tok_own,
        tok_rem,
        dx_ref,
        g_own,
    ) = scratch
    step = pl.program_id(0)
    tokens = q_ref.shape[1]
    width = act_ref.shape[0]
    half = tokens // 2
    cut = width // 2
    links = Links(sems, zs)
    x, y, z, c = links.x, links.y, links.z, links.c
    h, b = links.upper, links.lower

    fetch = [
        links.local(lambda p=p: p[0], lambda p=p: p[1])
        for p in (
            (act_in, act_ref),
            (w_in, w_ref),
            (tok_own_in.at[x], tok_own),
            (tok_rem_in, tok_rem),
            (dx_in, dx_ref),
        )
    ]
    u_load = [
        links.local(lambda: up_last_ref, lambda: u_last.at[0]),
        links.local(lambda: up_one_ref.at[:, b], lambda: u_own.at[0, :, b]),
        links.local(lambda: up_two_ref.at[:, :, y], lambda: u_own.at[1]),
    ]
    u_to_y = links.swap(lambda: up_two_ref.at[:, :, 1 - y], lambda: u_y, links.across)
    u_near = [
        links.swap(
            lambda j=j: up_one_ref.at[:, 1 - b] if j == 0 else u_own.at[1, :, 1 - b],
            lambda j=j: u_z.at[j, 0:2],
            links.near,
        )
        for j in range(2)
    ]
    u_beyond = [
        links.swap(lambda j=j: u_own.at[j, 1 - h, b], lambda j=j: u_z.at[j, 2], links.beyond)
        for j in range(2)
    ]
    u_to_facing = [
        links.swap(lambda j=j: u_last.at[j], lambda j=j: u_facing.at[j], links.facing)
        for j in range(3)
    ]
    raws = (raw_up, raw_out)
    w_keep = [
        links.local(lambda r=r: r.at[:, :, :, :, c], lambda k=k: w_own.at[k]) for k, r in enumerate(raws)
    ]
    w_to_core = [
        links.swap(lambda r=r: r.at[:, :, :, :, 1 - c], lambda k=k: w_core.at[k], links.core)
        for k, r in enumerate(raws)
    ]
    w_to_y = [
        links.swap(lambda k=k: w_own.at[k, :, :, :, 1 - y], lambda k=k: w_y.at[k], links.across)
        for k in range(2)
    ]
    w_near = [
        links.swap(
            lambda k=k: w_own.at[k, :, :, 1 - b, y], lambda k=k: w_z.at[k], links.near
        )
        for k in range(2)
    ]
    w_beyond = [
        links.swap(
            lambda k=k: w_own.at[k, :, 1 - h, b, y], lambda k=k: w_far.at[k], links.beyond
        )
        for k in range(2)
    ]
    w_to_facing = [
        links.swap(lambda k=k: w_last.at[k], lambda k=k: w_facing.at[k], links.facing)
        for k in range(2)
    ]
    d_keep = links.local(lambda: raw_down.at[:, c], lambda: d_own)
    d_to_core = links.swap(lambda: raw_down.at[:, 1 - c], lambda: d_core, links.core)
    d_to_y = links.swap(lambda: d_own.at[1 - y], lambda: d_y, links.across)
    d_to_side = [
        links.swap(lambda: down_two_ref.at[1 - x], lambda: d_side.at[0], links.facing),
        links.swap(lambda: d_own.at[y, 1 - x], lambda: d_side.at[1], links.facing),
    ]
    d_load = [
        links.local(lambda: down_last_ref, lambda: d_last),
        links.local(lambda: down_one_ref, lambda: d_sum.at[0]),
        links.local(lambda: down_two_ref.at[x], lambda: d_sum.at[1]),
    ]
    d_goal = [
        links.to_goal(lambda j=j: d_sum.at[j - 1], lambda j=j: d_z.at[j - 1], j) for j in range(1, zs)
    ]
    d_to_facing = links.swap(lambda: d_last, lambda: d_facing, links.facing)
    groups = range(len(split))
    q_to_core = [
        links.swap(lambda g=g: q_raws[g].at[:, :, :, 1 - c], lambda g=g: q_cores[g], links.core)
        for g in groups
    ]
    q_to_y = [
        links.swap(lambda g=g: q_cores[g].at[:, :, 1 - y], lambda g=g: q_ys[g], links.across)
        for g in groups
    ]
    q_near = [
        links.swap(lambda g=g: q_cores[g].at[:, 1 - b, y], lambda g=g: q_zs[g].at[0:2], links.near)
        for g in groups
    ]
    q_beyond = [
        links.swap(lambda g=g: q_cores[g].at[1 - h, b, y], lambda g=g: q_zs[g].at[2], links.beyond)
        for g in groups
    ]
    q_to_facing = [
        links.swap(lambda g=g: q_lasts[g], lambda g=g: q_facings[g], links.facing) for g in groups
    ]
    cross_out = links.swap(lambda: give_ref, lambda: result, links.facing)

    give_grad = links.swap(lambda: g_send, lambda: g_take, links.facing)
    keep_grad = links.local(lambda: g_own, lambda: grad_ref)
    put_grad = links.local(lambda: g_take, lambda: grad_take)
    early = [
        gather_stages(links, mod_early),
        sum_stages(links, sum_early, early_take, early_far),
    ]
    late = [gather_stages(links, mod_late), sum_stages(links, sum_late, late_take, late_far)]

    def begin(arrays, stage):
        for stages in arrays:
            stages[stage][0]()

    def end(arrays, stage):
        for stages in arrays:
            stages[stage][1]()

    def u_near_done(j):
        u_near[j]().wait()
        for k in range(2):
            u_own[j, k, b] = u_own[j, k, b] + u_z[j, k]
        u_beyond[j]().start()

    def u_beyond_done(j):
        u_beyond[j]().wait()
        u_last[j + 1] = u_own[j, h, b] + u_z[j, 2]
        u_to_facing[j + 1]().start()

    def u_done(j):
        u_to_facing[j]().wait()
        mine, other = u_last[j].astype(F32), u_facing[j].astype(F32)
        start = j * width
        s_up[:, start : start + cut] = jnp.where(x == 0, mine, other)
        s_up[:, start + cut : start + width] = jnp.where(x == 0, other, mine)

    def w_core_done(k):
        w_keep[k]().wait()
        w_to_core[k]().wait()
        for i in grid_of(2, 2, 2, 2):
            w_own[(k, *i)] = w_own[(k, *i)] + w_core[(k, *i)]

    def w_y_done(k):
        w_to_y[k]().wait()
        for i in grid_of(2, 2, 2):
            w_own[(k, *i, y)] = w_own[(k, *i, y)] + w_y[(k, *i)]
        w_near[k]().start()

    def w_near_done(k):
        w_near[k]().wait()
        for i, j in grid_of(2, 2):
            w_own[k, i, j, b, y] = w_own[k, i, j, b, y] + w_z[k, i, j]
        w_beyond[k]().start()

    def w_beyond_done(k):
        w_beyond[k]().wait()
        for i in range(2):
            w_last[k, i] = w_own[k, i, h, b, y] + w_far[k, i]
        w_to_facing[k]().start()

    def w_done(k):
        w_to_facing[k]().wait()
        out, start = (s_up, (zs - 1) * width) if k == 0 else (s_out, 0)
        for i in range(2):
            out[:, start + i * cut : start + (i + 1) * cut] = w_last[k, i].astype(F32) + w_facing[
                k, i
            ].astype(F32)

    def q_core_done(g):
        q_to_core[g]().wait()
        for i in grid_of(2, 2, 2):
            q_cores[g][i] = q_cores[g][i] + q_raws[g][(*i, c)]

    def q_y_done(g):
        q_to_y[g]().wait()
        for i in grid_of(2, 2):
            q_cores[g][(*i, y)] = q_cores[g][(*i, y)] + q_ys[g][i]
        q_near[g]().start()

    def q_near_done(g):
        q_near[g]().wait()
        for k in range(2):
            q_cores[g][k, b, y] = q_cores[g][k, b, y] + q_zs[g][k]
        q_beyond[g]().start()

    def q_beyond_done(g):
        q_beyond[g]().wait()
        q_lasts[g][...] = q_cores[g][h, b, y] + q_zs[g][2]
        q_to_facing[g]().start()

    def q_done(g):
        q_to_facing[g]().wait()
        total = q_lasts[g][...].astype(F32) + q_facings[g][...].astype(F32)
        first, size = split[g][0] * HD, (split[g][1] - split[g][0]) * HD
        for p in range(3):
            s_qkv[:, p * width + first : p * width + first + size] = total[:, p * size : (p + 1) * size]

    def weight_grad_of(g):
        first, size = split[g][0] * HD, (split[g][1] - split[g][0]) * HD
        for p in range(3):
            rows = slice(p * width + first, p * width + first + size)
            part = mm(act_ref[...], d_proj[rows, :], NT).astype(BF)
            q_raws[g][:, :, :, :, :, p * size : (p + 1) * size] = part.reshape(
                q_raws[g].shape[:5] + (size,)
            )
        q_to_core[g]().start()


    def due_00():
        greet(links.core, links.across, links.facing, *[links.at_z(f) for f in links.far])
        d_to_core().start()
        d_keep().start()
        for k in range(2):
            w_to_core[k]().start()
            w_keep[k]().start()
        u_near[0]().start()
        u_to_y().start()
        d_to_side[0]().start()
        for load in u_load + d_load:
            load().start()
        mod_early[z, y, c, x] = mod_ref[...]
        sum_early[...] = sum_ref[...]
        begin(early, 0)
        cross_out().start()
        for load in fetch:
            load().start()

    def due_01():
        d_load[1]().wait()
        d_goal[0][0]()
        d_keep().wait()
        d_to_core().wait()
        for i, k in grid_of(2, 2):
            d_own[i, k] = d_own[i, k] + d_core[i, k]
        d_to_y().start()
        end(early, 0)
        begin(early, 1)

    def due_10():
        w_core_done(0)
        w_core_done(1)
        u_load[0]().wait()
        u_to_facing[0]().start()

    def due_11():
        u_load[2]().wait()
        u_to_y().wait()
        for i in grid_of(2, 2):
            u_own[(1, *i)] = u_own[(1, *i)] + u_y[i]
        u_near[1]().start()
        w_to_y[0]().start()
        u_load[1]().wait()
        u_near_done(0)
        d_goal[0][1]()
        end(early, 1)
        begin(early, 2)

    def due_20():
        fetch[0]().wait()
        weight_grad_of(0)
        d_load[2]().wait()
        d_to_side[0]().wait()
        d_sum[1] = d_sum[1] + d_side[0]
        d_goal[1][0]()

    def due_21():
        d_to_y().wait()
        for k in range(2):
            d_own[y, k] = d_own[y, k] + d_y[k]
        d_to_side[1]().start()
        q_core_done(0)
        q_to_y[0]().start()
        u_near_done(1)
        u_beyond_done(0)
        end(early, 2)
        begin(early, 3)

    def due_30():
        w_y_done(0)
        w_to_y[1]().start()
        d_goal[1][1]()

    def due_31():
        d_to_side[1]().wait()
        d_sum[2] = d_own[y, x] + d_side[1]
        d_goal[2][0]()

    def due_40():
        weight_grad_of(1)
        w_near_done(0)
        q_y_done(0)
        u_beyond_done(1)
        end(early, 3)

    def due_41():
        q_core_done(1)
        q_to_y[1]().start()
        d_goal[2][1]()
        u_done(0)

    def due_50():
        w_beyond_done(0)
        w_y_done(1)
        q_near_done(0)
        u_done(1)

    def due_51():
        d_load[0]().wait()
        for j in range(zs - 1):
            d_goal[j][2]()

        @pl.when(z > 0)
        def _():
            d_last[...] = d_sum[jnp.maximum(z - 1, 0)]

        d_to_facing().start()
        q_beyond_done(0)

    due = (
        (due_00, due_01),
        (due_10, due_11),
        (due_20, due_21),
        (due_30, due_31),
        (due_40, due_41),
        (due_50, due_51),
    )

    def do_due(h):
        for k in range(PAIRS):
            pl.when(step == k)(due[k][h])


    @pl.when(step < PAIRS)
    def _():
        tile = 256
        zero = jnp.zeros((HD, tokens), BF)
        v_nat = v_ref[...].T
        cos = cos_ref[...]
        sin = sin_ref[...]

        def put(part, h, value):
            low = value.astype(BF).astype(F32)
            a, b = low[0 : HD // 2], low[HD // 2 :]
            start = part * width + step * 2 * HD + h * HD
            d_proj[pl.ds(pl.multiple_of(start, 32), 32), :] = (a * cos + b * sin).astype(BF)
            d_proj[pl.ds(pl.multiple_of(start + 32, 32), 32), :] = (b * cos - a * sin).astype(BF)

        do_due(0)
        inners, keys, values, queries = [], [], [], [[], []]
        for h in range(2):
            rows = slice(h * HD, (h + 1) * HD)
            linv = linv_ref[0, h : h + 1, :]
            d_o = d_att_ref[rows, :].astype(F32)
            do_mask[h, rows, :] = (d_o * linv).astype(BF)
            do_mask[h, (1 - h) * HD : (2 - h) * HD, :] = zero
            inners.append(col_sum(d_o * att_ref[rows, :].astype(F32)) * linv)

        def ahead(h, cols):
            return mm(v_nat, do_mask[h, :, cols])

        def centre(h, cols, d_probs):
            rows = slice(h * HD, (h + 1) * HD)
            e = e_ref[h, :, cols]
            part = mm(do_mask[h, rows, cols], e, NT)
            if cols.start == 0:
                values.append(part)
            else:
                values[h] += part
            return (e.astype(F32) * (d_probs - inners[h][:, cols])).astype(BF)

        def behind(h, cols, d_s):
            rows = slice(h * HD, (h + 1) * HD)
            queries[h].append(mm(k_ref[rows, :], d_s))
            part = mm(q_ref[rows, cols], d_s, NT)
            if cols.start == 0:
                keys.append(part)
            else:
                keys[h] += part
            if cols.stop == tokens:
                put(0, h, jnp.concatenate(queries[h], axis=1) * HD**-0.5)
                put(1, h, keys[h])
                start = 2 * width + step * 2 * HD + h * HD
                d_proj[pl.ds(pl.multiple_of(start, HD), HD), :] = values[h].astype(BF)

        units = [(h, slice(t, t + tile)) for h in range(2) for t in range(0, tokens, tile)]
        coming = ahead(*units[0])
        for i, unit in enumerate(units):
            if i == len(units) // 2:
                do_due(1)
            here = coming
            if i + 1 < len(units):
                coming = ahead(*units[i + 1])
            d_s = centre(*unit, here)
            if i > 0:
                behind(*units[i - 1], held)
            held = d_s
        behind(*units[-1], held)


    def finish(tok, cols):
        d_act = mm(d_proj[:, cols], w_ref[...], TN)
        n, rstd = norm_parts(tok[...].astype(F32))
        grad = dx_ref[cols, :] + norm_pull(n, rstd, d_act * vec_ref[0:1, :])
        return grad, col_sum(d_act), col_sum(d_act * n)

    @pl.when(step == PAIRS)
    def _():
        for load in fetch[1:]:
            load().wait()
        weight_grad_of(2)
        grad, shift, pull = finish(tok_rem, slice(half, 2 * half))
        g_send[...] = grad.astype(BF)
        give_grad().start()
        q_core_done(2)
        q_to_y[2]().start()
        q_y_done(1)
        w_near_done(1)
        grad, shift_own, pull_own = finish(tok_own, slice(0, half))
        g_own[...] = grad
        keep_grad().start()
        shift += shift_own
        pull += pull_own
        lines = width // 128
        mine = mod_late.at[z, y, c, x]
        mine[2 * lines :, :] = jnp.zeros((mod_late.shape[4] - 2 * lines, 128), BF)
        put_rows(mine, 0, shift)
        put_rows(mine, lines, pull * vec_ref[2:3, :])
        sum_late[lines:, :] = jnp.zeros((sum_late.shape[0] - lines, 128), F32)
        put_rows(sum_late, 0, pull * (1.0 + vec_ref[3:4, :]))
        begin(late, 0)
        q_near_done(1)
        w_beyond_done(1)
        q_y_done(2)
        end(late, 0)
        begin(late, 1)
        u_done(2)
        w_done(0)
        q_done(0)
        end(late, 1)
        begin(late, 2)
        q_beyond_done(1)
        q_near_done(2)
        end(late, 2)
        begin(late, 3)
        d_to_facing().wait()
        mine, other = d_last[...].astype(F32), d_facing[...].astype(F32)
        rows_half = mine.shape[0]
        s_down[0:rows_half, :] = jnp.where(x == 0, mine, other)
        s_down[rows_half:, :] = jnp.where(x == 0, other, mine)
        q_beyond_done(2)
        cross_out().wait()
        w_done(1)
        q_done(1)
        end(late, 3)
        give_grad().wait()
        put_grad().start()
        keep_grad().wait()
        q_done(2)
        put_grad().wait()
        for out, value in zip(small_outs, (mod_early, mod_late, sum_early, sum_late)):
            out[...] = value[...]


def back(ins, zs, ff):
    q, att, d_att, e, linv, cos_t, sin_t = ins[:7]
    mod, sums, vec = ins[-8], ins[-7], ins[-1]
    width, tokens = att.shape
    half = tokens // 2
    cut = width // 2
    rows = width // (4 * zs)
    down_rows = ff // (4 * zs)
    down_half = (down_rows // 2, width)
    split = ((0, 4), (4, 8), (8, HEADS))
    sizes = [3 * (b - a) * HD for a, b in split]
    last = PAIRS - 1

    def part(k):
        return pl.BlockSpec((2 * HD, tokens), lambda i: (jnp.minimum(i, last) + k * PAIRS, 0))

    def vm(*shape, kind=BF):
        return pltpu.VMEM(shape, kind)

    lines = width // 128
    mod_early = (zs, 2, 2, 2) + mod.shape
    mod_late = (zs, 2, 2, 2, round_up(2 * lines, 16), 128)
    sum_late = (round_up(lines, 8), 128)
    outs = [
        ((half, width), F32),
        ((rows, 3 * width), F32),
        ((rows, width), F32),
        ((rows, ff), F32),
        ((down_rows, width), F32),
        (mod_early, BF),
        (mod_late, BF),
        (sums.shape, F32),
        (sum_late, F32),
    ]
    outs = [((half, width), F32), ((half, width), BF)] + outs[1:]
    fetched = ins[-6:-1]
    in_specs = (
        [part(0), part(1), part(2), part(0), part(0)]
        + [
            pl.BlockSpec((2, tokens, tokens), lambda i: (jnp.minimum(i, last), 0, 0)),
            pl.BlockSpec((1, 8, tokens), lambda i: (jnp.minimum(i, last), 0, 0)),
            once(cos_t.shape),
            once(sin_t.shape),
        ]
        + [ANY] * (len(ins) - 15)
        + [once(mod.shape), once(sums.shape)]
        + [ANY] * 5
        + [once(vec.shape)]
    )
    out_specs = [ANY, ANY, ANY] + [once(shape) for shape, _ in outs[2:]]
    out_shape = [jax.ShapeDtypeStruct((half, width), BF)] + [
        jax.ShapeDtypeStruct(*o) for o in outs
    ]
    scratch = [
        vm(2, 2 * HD, tokens),
        vm(3 * width, tokens),
        pltpu.SemaphoreType.DMA((250,)),
        vm(2, 2, 2, rows, cut),
        vm(2, 2, rows, cut),
        vm(2, 3, rows, cut),
        vm(3, rows, cut),
        vm(3, rows, cut),
        vm(2, 2, 2, 2, 2, rows, cut),
        vm(2, 2, 2, 2, 2, rows, cut),
        vm(2, 2, 2, 2, rows, cut),
        vm(2, 2, 2, rows, cut),
        vm(2, 2, rows, cut),
        vm(2, 2, rows, cut),
        vm(2, 2, rows, cut),
        vm(2, 2, *down_half),
        vm(2, 2, *down_half),
        vm(2, *down_half),
        vm(2, *down_half),
        vm(zs - 1, *down_half),
        vm(zs - 1, 2, *down_half),
        vm(*down_half),
        vm(*down_half),
        [vm(2, 2, 2, 2, rows, s) for s in sizes],
        [vm(2, 2, 2, rows, s) for s in sizes],
        [vm(2, 2, rows, s) for s in sizes],
        [vm(3, rows, s) for s in sizes],
        [vm(rows, s) for s in sizes],
        [vm(rows, s) for s in sizes],
        vm(half, width),
        vm(half, width),
        vm(3, *sums.shape, kind=F32),
        vm(zs, *sums.shape, kind=F32),
        vm(3, *sum_late, kind=F32),
        vm(zs, *sum_late, kind=F32),
        vm(*mod_early),
        vm(*mod_late),
        vm(*sums.shape, kind=F32),
        vm(*sum_late, kind=F32),
    ]
    scratch += [vm(*a.shape[-2:], kind=a.dtype) for a in fetched]
    scratch += [vm(half, width, kind=F32)]
    flat, tree = jax.tree.flatten(scratch)
    n_in, n_out = len(in_specs), len(out_specs)

    def kernel(*refs):
        back_kernel(
            zs,
            split,
            refs[:n_in],
            refs[n_in : n_in + n_out],
            jax.tree.unflatten(tree, refs[n_in + n_out :]),
        )

    return pl.pallas_call(
        kernel,
        grid=(PAIRS + 1,),
        in_specs=in_specs,
        out_specs=out_specs,
        out_shape=out_shape,
        scratch_shapes=flat,
        compiler_params=params(62, collective_id=5),
        cost_estimate=pl.CostEstimate(
            flops=32 * tokens * tokens * width + 12 * tokens * width * width,
            bytes_accessed=60 << 20,
            transcendentals=0,
        ),
        name="back",
    )(q, q, q, att, d_att, e, linv, cos_t, sin_t, *ins[7:])


def iota2(shape, axis):
    return lax.broadcasted_iota(jnp.int32, shape, axis)


def finish_kernel(pairs, early_ref, late_ref, sum_early_ref, sum_late_ref, *refs):
    sources, refs = refs[:8], refs[8:]
    output, grad, *shards, w_ada, b_ada, gain_one, gain_two, b_down, b_up = refs[:12]
    held, (wide, sems) = refs[12:20], refs[20:]
    x = lax.axis_index("seq")
    goals = [output.at[x], output.at[1 - x], grad.at[x], grad.at[1 - x], *shards]
    loads = [
        pltpu.make_async_copy(src, dst, sems.at[0, k])
        for k, (src, dst) in enumerate(zip(sources, held))
    ]
    stores = [
        pltpu.make_async_copy(wide if k == 3 else src, dst, sems.at[1, k])
        for k, (src, dst) in enumerate(zip(held, goals))
    ]
    for copy in loads:
        copy.start()
    for k in range(8):
        loads[k].wait()
        if k == 3:
            wide[...] = held[3][...].astype(F32)
        stores[k].start()
    dp = lax.axis_index("dp")
    rows, lines = w_ada.shape[0], early_ref.shape[1]
    width = gain_one.shape[0] * lax.axis_size("dp")
    per_line = width // 128
    stamp_line = 4 * per_line
    blocks = []
    for ref, first, count in ((late_ref, 0, 2 * per_line), (early_ref, 2 * per_line, 4 * per_line)):
        seqs, period = ref.shape[0], ref.shape[1]
        flat = ref[...].reshape(seqs * period, 128)
        stamps = early_ref[...].reshape(seqs * lines, 128)
        shape = (seqs * lines, seqs * period)
        line, col = iota2(shape, 0), iota2(shape, 1)
        pick = (line // lines == col // period) & (lax.rem(line, lines) == stamp_line)
        time = mm(stamps, jnp.where(pick, 1.0, 0.0).astype(BF), TN)
        time = 32.0 * time[0:1, :] + time[1:2, :]
        shape = (rows, seqs * period)
        index = dp * rows + iota2(shape, 0)
        place = jnp.where(index < pairs, index, index - pairs).astype(F32)
        angles = time * jnp.exp(-math.log(10000.0) * place / pairs)
        cond = features_of(angles, index >= pairs)
        shape = (period * rows, seqs * period)
        same = iota2(shape, 0) // rows == lax.rem(iota2(shape, 1), period)
        total = jnp.zeros((period * rows, 128), F32)
        for part in split_three(cond):
            spread = jnp.concatenate([part.astype(F32)] * period, axis=0)
            total += mm(jnp.where(same, spread, 0.0).astype(BF), flat)
        for k in range(count):
            start = (first + k) * 128
            w_ada[:, start : start + 128] = total[k * rows : (k + 1) * rows]
        shape = (period, seqs * period)
        same = iota2(shape, 0) == lax.rem(iota2(shape, 1), period)
        sums = mm(jnp.where(same, 1.0, 0.0).astype(BF), flat)
        blocks += [sums[k : k + 1] for k in range(count)]

    def mine(parts, out):
        row = jnp.concatenate(parts, axis=1)
        size, full = out.shape[0], row.shape[1]
        row = pltpu.roll(row, lax.rem(full - dp * size, full), 1)
        out[...] = row[0, 0:size]

    def lines_of(ref, first, count):
        return [ref[first + k : first + k + 1, :] for k in range(count)]

    mine(blocks, b_ada)
    mine(lines_of(sum_late_ref, 0, per_line), gain_one)
    mine(lines_of(sum_early_ref, 0, per_line), gain_two)
    mine(lines_of(sum_early_ref, per_line, per_line), b_down)
    mine(lines_of(sum_early_ref, 2 * per_line, b_up.shape[0] * lax.axis_size("dp") // 128), b_up)
    for copy in stores:
        copy.wait()


def finish_all(big, mod_early, mod_late, sum_early, sum_late, cond_width, width, ff, dps):
    seqs = 2 * dps
    mod_early = mod_early.reshape(seqs, *mod_early.shape[-2:])
    mod_late = mod_late.reshape(seqs, *mod_late.shape[-2:])
    smalls = (mod_early, mod_late, sum_early, sum_late)
    vmem = pl.BlockSpec(memory_space=pltpu.VMEM)
    half = big[0].shape[0]
    out_shape = [jax.ShapeDtypeStruct((2, half, width), kind) for kind in (BF, F32)]
    out_shape += [jax.ShapeDtypeStruct(a.shape, a.dtype) for a in big[4:]]
    out_shape += [jax.ShapeDtypeStruct((cond_width // dps, 6 * width), F32)]
    out_shape += [
        jax.ShapeDtypeStruct((n // dps,), F32) for n in (6 * width, width, width, width, ff)
    ]
    return pl.pallas_call(
        functools.partial(finish_kernel, cond_width // 2),
        in_specs=[vmem] * 4 + [ANY] * len(big),
        out_specs=[ANY] * 6 + [vmem] * 6,
        out_shape=out_shape,
        scratch_shapes=[pltpu.VMEM(a.shape, a.dtype) for a in big]
        + [pltpu.VMEM((half, width), F32), pltpu.SemaphoreType.DMA((2, len(big)))],
        compiler_params=params(),
        name="finish_all",
    )(*smalls, *big)


def time_features(time_steps, pair_count):
    frequency = jnp.exp(-math.log(10000.0) * jnp.arange(pair_count, dtype=F32) / pair_count)
    angles = time_steps.astype(F32)[:, None] * frequency[None, :]
    return jnp.concatenate([jnp.cos(angles), jnp.sin(angles)], axis=-1)


def per_device(
    tokens,
    cotangent,
    time_index,
    span_starts,
    span_lengths,
    w_ada,
    b_ada,
    gain_one,
    w_qkv,
    w_out,
    gain_two,
    w_up,
    b_up,
    w_down,
    b_down,
):
    seqs_dev, half, width = tokens.shape
    length = 2 * half
    rank = lax.axis_index("seq")
    swap = [(0, 1), (1, 0)]

    def pick(x, i):
        return lax.dynamic_index_in_dim(x, i, 0, keepdims=False)

    time_own = lax.dynamic_slice_in_dim(time_index, rank, 1)
    dp, dps = lax.axis_index("dp"), lax.axis_size("dp")
    ff = w_up.shape[1]
    zs = dps // 4
    linked = zs == 4 and dps == 16 and width % (64 * zs) == 0 and ff == zs * width

    act_t, qkv_t, w_qkv_t, tok_rem, vec_one, vec_two, span, cos_t, sin_t = project(
        tokens, time_index, span_starts, span_lengths, w_ada, b_ada, (gain_one, gain_two), b_down, w_qkv
    )
    att_t, e, linv, cot_rem = attend(qkv_t, cotangent)
    if linked:
        out_own, out_rem, dx, d_att_t, raw_out, raw_up, raw_down, *partial, mod, sums = middle_links(
            att_t, tokens, tok_rem, cotangent, cot_rem, span, vec_two, b_up[None], w_out, w_up, w_down, zs
        )
        ins = (qkv_t, att_t, d_att_t, e, linv, cos_t, sin_t, out_rem, *partial)
        ins += (raw_up, raw_out, raw_down, mod, sums, act_t, w_qkv_t, tokens, tok_rem, dx, vec_one)
        taken, g_own, g_take, *shards, mod_early, mod_late, sum_early, sum_late = back(ins, zs, ff)
        output, grad_tokens, *shards, s_w_ada, s_b_ada, s_gain_one, s_gain_two, s_b_down, s_b_up = (
            finish_all(
                (out_own, taken, g_own, g_take, *shards),
                mod_early,
                mod_late,
                sum_early,
                sum_late,
                w_ada.shape[0],
                width,
                ff,
                dps,
            )
        )
    else:
        tok_own, cot_own = pick(tokens, rank), pick(cotangent, rank)
        out_own, out_rem, dx, d_att_t, g_out, g_up, g_down, g_bup, sums_two = middle(
            att_t, tok_own, tok_rem, cot_own, cot_rem, span, vec_two, b_up[None], w_out, w_up, w_down
        )
        d_proj, out_back = attend_back(qkv_t, att_t, d_att_t, e, linv, cos_t, sin_t, out_rem)
        d_proj_t = d_proj.reshape(3 * width, length)
        g_own, g_rem, sums_one = tail(tok_own, tok_rem, d_proj_t, w_qkv_t, dx, vec_one)
        g_qkv = weight_grad(act_t, d_proj_t)

        def spread(own, other):
            first = jnp.where(rank == 0, own, other)
            second = jnp.where(rank == 0, other, own)
            return jnp.stack([first, second])

        output = spread(out_own, out_back)
        grad_tokens = spread(g_own, lax.ppermute(g_rem, "seq", swap).astype(F32))
        shards = [
            lax.psum(lax.psum_scatter(g, "dp", scatter_dimension=0, tiled=True), "seq").astype(F32)
            for g in (g_qkv, g_out, g_up, g_down)
        ]
        d_mod = jnp.concatenate([sums_one[:2].reshape(-1), sums_two[:4].reshape(-1)])
        small = jnp.concatenate([sums_one[2], sums_two[4], sums_two[5], g_bup[0]])
        d_mod_all = lax.all_gather(d_mod, ("dp", "seq"))
        time_all = lax.all_gather(time_own[0].astype(F32), ("dp", "seq"))
        small = lax.psum(small, ("dp", "seq"))

        def mine(x, axis=0):
            size = x.shape[axis] // dps
            return lax.dynamic_slice_in_dim(x, dp * size, size, axis)

        features = jax.nn.silu(time_features(time_all, w_ada.shape[0] // 2))
        s_w_ada = jnp.dot(mine(features, 1).T, d_mod_all, precision=lax.Precision.HIGHEST)
        s_b_ada = jnp.sum(mine(d_mod_all, 1), axis=0)
        s_gain_one = mine(small[:width])
        s_gain_two = mine(small[width : 2 * width])
        s_b_down = mine(small[2 * width : 3 * width])
        s_b_up = mine(small[3 * width :])

    s_qkv, s_out, s_up, s_down = shards

    return (
        output,
        grad_tokens,
        s_w_ada,
        s_b_ada,
        s_gain_one,
        s_qkv,
        s_out,
        s_gain_two,
        s_up,
        s_b_up,
        s_down,
        s_b_down,
    )


def solution(mesh):
    rows = P("dp", "seq", None)
    return jax.shard_map(
        per_device,
        mesh=mesh,
        in_specs=(rows, rows, P("dp"), P("dp"), P("dp")) + (P(),) * 10,
        out_specs=(
            rows,
            rows,
            P("dp", None),
            P("dp"),
            P("dp"),
            P("dp", None),
            P("dp", None),
            P("dp"),
            P("dp", None),
            P("dp"),
            P("dp", None),
            P("dp"),
        ),
        check_vma=False,
    )
```

```python
import functools
import math

import jax
import jax.numpy as jnp
import numpy as np
from jax import lax
from jax.experimental import pallas as pl
from jax.experimental.pallas import tpu as pltpu
from jax.sharding import PartitionSpec as P

HEADS = 12
HD = 64
PAIRS = HEADS // 2
NORM_EPS = 1e-05
LOG2E = math.log2(math.e)
BF = jnp.bfloat16
F32 = jnp.float32
MIB = 1 << 20

NN = (((1,), (0,)), ((), ()))
NT = (((1,), (1,)), ((), ()))
TN = (((0,), (0,)), ((), ()))


def mm(a, b, dims=NN):
    return lax.dot_general(a, b, dims, preferred_element_type=F32)


def norm_parts(x):
    centre = x - jnp.mean(x, axis=-1, keepdims=True)
    rstd = lax.rsqrt(jnp.mean(centre * centre, axis=-1, keepdims=True) + NORM_EPS)
    return centre * rstd, rstd


def norm_pull(n, rstd, dn):
    return rstd * (
        dn - jnp.mean(dn, axis=-1, keepdims=True) - n * jnp.mean(dn * n, axis=-1, keepdims=True)
    )


def col_sum(x):
    return jnp.sum(x, axis=0, keepdims=True)


def rows_of(size, index):
    return pl.ds(pl.multiple_of(index * size, size), size)


def params(mib=56, collective_id=None):
    if collective_id is None:
        return pltpu.CompilerParams(vmem_limit_bytes=mib * MIB)
    return pltpu.CompilerParams(
        vmem_limit_bytes=mib * MIB, collective_id=collective_id, has_side_effects=True
    )


def whole(shape):
    zeros = (0,) * len(shape)
    return pl.BlockSpec(shape, lambda *_: zeros)


MESH = pl.DeviceIdType.MESH
ANY = pl.BlockSpec(memory_space=pl.ANY)
SEMS = [pltpu.SemaphoreType.DMA, pltpu.SemaphoreType.DMA]


def greet(*partners):
    barrier = pltpu.get_barrier_semaphore()
    for partner in partners:
        pl.semaphore_signal(barrier, inc=1, device_id=partner, device_id_type=MESH)
    pl.semaphore_wait(barrier, len(partners))


def remote(src, dst, send, recv, device):
    return pltpu.make_async_remote_copy(
        src_ref=src, dst_ref=dst, send_sem=send, recv_sem=recv, device_id=device, device_id_type=MESH
    )


def seq_partner():
    return (lax.axis_index("dp"), 1 - lax.axis_index("seq"))


def swap_start(src, dst, send, recv):
    partner = seq_partner()
    greet(partner)
    remote(src, dst, send, recv, partner).start()


def swap_wait(src, dst, send, recv):
    remote(src, dst, send, recv, seq_partner()).wait()


class Links:
    def __init__(self, sems, zs):
        self.sems, self.used, self.zs = sems, 0, zs
        dp, self.x = lax.axis_index("dp"), lax.axis_index("seq")
        self.z, self.y, self.c = dp // 4, lax.rem(dp // 2, 2), lax.rem(dp, 2)
        self.core = (dp + 1 - 2 * self.c, self.x)
        self.across = (dp + 2 - 4 * self.y, self.x)
        self.facing = (dp, 1 - self.x)
        self.far = [lax.rem(self.z + k, zs) for k in range(1, zs)]
        self.upper, self.lower = self.z // 2, lax.rem(self.z, 2)
        self.near = self.at_z(2 * self.upper + 1 - self.lower)
        self.beyond = self.at_z(2 * (1 - self.upper) + self.lower)

    def at_z(self, f):
        return (f * 4 + 2 * self.y + self.c, self.x)

    def take(self, count):
        self.used += count
        return self.used - count

    def local(self, src, dst):
        sem = self.take(1)
        return lambda: pltpu.make_async_copy(src(), dst(), self.sems.at[sem])

    def swap(self, src, dst, device):
        sem = self.take(2)
        return lambda: remote(src(), dst(), self.sems.at[sem], self.sems.at[sem + 1], device)

    def spread(self, src, dst):
        sem = self.take(2 * self.zs)

        def make(f, slot):
            return remote(
                src(f), dst(slot), self.sems.at[sem + f], self.sems.at[sem + self.zs + slot], self.at_z(f)
            )

        def start():
            for f in self.far:
                make(f, self.z).start()

        def wait():
            for f in self.far:
                make(f, self.z).wait_send()
                make(f, f).wait_recv()

        return start, wait

    def to_goal(self, src, dst, goal):
        upper, lower = goal // 2, goal % 2
        near = self.swap(src, lambda: dst().at[0], self.near)
        beyond = self.swap(src, lambda: dst().at[1], self.beyond)
        on_side = self.lower == lower

        def start():
            pl.when(self.lower != lower)(lambda: near().start())

        def middle():
            pl.when(self.lower != lower)(lambda: near().wait_send())

            @pl.when(on_side)
            def _():
                near().wait_recv()
                src()[...] = src()[...] + dst()[0]
                pl.when(self.upper != upper)(lambda: beyond().start())

        def finish():
            pl.when(on_side & (self.upper != upper))(lambda: beyond().wait_send())

            @pl.when(on_side & (self.upper == upper))
            def _():
                beyond().wait_recv()
                src()[...] = src()[...] + dst()[1]

        return start, middle, finish


def grid_of(*sizes):
    return [()] if not sizes else [(i,) + r for i in range(sizes[0]) for r in grid_of(*sizes[1:])]


def round_up(value, unit):
    return -(-value // unit) * unit


def early_mod_rows(width):
    return round_up(4 * width // 128 + 1, 16)


def early_sum_rows(width, ff):
    return round_up((2 * width + ff) // 128, 8)


def put_rows(ref, start, row):
    for k in range(row.shape[1] // 128):
        ref[start + k : start + k + 1, :] = row[:, k * 128 : (k + 1) * 128].astype(ref.dtype)


def once(shape):
    zeros = (0,) * len(shape)
    return pl.BlockSpec(shape, lambda *_: zeros, pipeline_mode=pl.Buffered(1))


def split_three(x):
    parts = []
    for _ in range(3):
        low = x.astype(BF)
        parts.append(low)
        x = x - low.astype(F32)
    return parts


def features_of(angles, is_sin):
    raw = jnp.where(is_sin, jnp.sin(angles), jnp.cos(angles))
    return raw / (1.0 + jnp.exp(-raw))


def project_kernel(
    time_ref,
    start_ref,
    extent_ref,
    tokens_ref,
    cos_ref,
    sin_ref,
    w_ada_ref,
    b_ada_ref,
    gain_one_ref,
    gain_two_ref,
    b_down_ref,
    w_ref,
    act_ref,
    out_ref,
    w_t_ref,
    rem_ref,
    vec_one_ref,
    vec_two_ref,
    span_ref,
    cos_out,
    sin_out,
    own,
    rem,
    w_t,
    qkv,
    sems,
):
    step = pl.program_id(0)
    half, width = own.shape
    rows = w_t_ref.shape[0]
    tile = 128
    chunk = half // 2
    x = lax.axis_index("seq")
    keep = pltpu.make_async_copy(tokens_ref.at[x], own, sems.at[0])
    cross = [
        remote(
            tokens_ref.at[1 - x, k * chunk : (k + 1) * chunk],
            rem.at[k * chunk : (k + 1) * chunk],
            sems.at[1 + k],
            sems.at[3 + k],
            seq_partner(),
        )
        for k in range(2)
    ]
    spans = (slice(0, half), slice(half, half + chunk), slice(half + chunk, 2 * half))
    store = [
        pltpu.make_async_copy(qkv.at[:, span], out_ref.at[:, span], sems.at[5 + k])
        for k, span in enumerate(spans)
    ]

    def norm(src, first, size, start):
        scale, shift = vec_one_ref[0:1, :], vec_one_ref[1:2, :]
        for t in range(0, size, tile):
            n, _ = norm_parts(src[first + t : first + t + tile, :].astype(F32))
            act_ref[:, start + t : start + t + tile] = (n * scale + shift).astype(BF).T

    @pl.when(step == 0)
    def _():
        greet(seq_partner())
        for copy in cross:
            copy.start()
        keep.start()
        pairs = w_ada_ref.shape[0] // 2
        time = time_ref[x]
        lane = lax.broadcasted_iota(jnp.int32, (8, 2 * pairs), 1)
        place = jnp.where(lane < pairs, lane, lane - pairs).astype(F32)
        frequency = jnp.exp(-math.log(10000.0) * place / pairs)
        cond = features_of(time.astype(F32) * frequency, lane >= pairs)
        modulation = b_ada_ref[...].reshape(1, 6 * width)
        for part in split_three(cond):
            modulation = modulation + mm(part, w_ada_ref[...])[0:1, :]
        pieces = [modulation[:, k * width : (k + 1) * width] for k in range(6)]
        shift_one, scale_one, gate_one, shift_two, scale_two, gate_two = pieces
        gain_one, gain_two = (ref[...].reshape(1, width) for ref in (gain_one_ref, gain_two_ref))
        zeros = jnp.zeros((1, width), F32)
        first = (gain_one * (1.0 + scale_one), shift_one, gain_one, scale_one)
        for k, row in enumerate(first + (zeros,) * 4):
            vec_one_ref[k : k + 1, :] = row
        lanes = lax.broadcasted_iota(jnp.int32, (1, width), 1)
        stamp = jnp.where(lanes == 0, time // 32, jnp.where(lanes == 1, lax.rem(time, 32), 0))
        second = (
            gate_one,
            gain_two * (1.0 + scale_two),
            shift_two,
            gate_two,
            b_down_ref[...].reshape(1, width),
            gain_two,
            scale_two,
            stamp.astype(F32),
        )
        for k, row in enumerate(second):
            vec_two_ref[k : k + 1, :] = row
        begin, end = start_ref[x], start_ref[x] + extent_ref[x]
        index = lax.broadcasted_iota(jnp.int32, (half, 1), 0)
        for part, where in enumerate((x, 1 - x)):
            place = index + where * half
            inside = (place >= begin) & (place < end)
            span_ref[part * half : (part + 1) * half, :] = jnp.where(inside, 2.0, 0.5)
            cos_out[:, part * half : (part + 1) * half] = cos_ref[where]
            sin_out[:, part * half : (part + 1) * half] = sin_ref[where]
        keep.wait()
        norm(own, 0, half, 0)

    def rotated(proj, block, cols, factor):
        cos, sin = cos_out[:, cols] * factor, sin_out[:, cols] * factor
        parts = []
        for h in range(rows // HD):
            a = proj[h * HD : h * HD + HD // 2]
            b = proj[h * HD + HD // 2 : (h + 1) * HD]
            parts += [(a * cos - b * sin).astype(BF), (b * cos + a * sin).astype(BF)]
        qkv[block, cols] = jnp.concatenate(parts, axis=0)

    @pl.when(step < 6)
    def _():
        block = rows_of(rows, step)
        flipped = w_ref[...].T
        w_t[block, :] = flipped
        w_t_ref[...] = flipped
        proj = mm(flipped, act_ref[:, spans[0]])

        @pl.when(step < 4)
        def _():
            rotated(proj, block, spans[0], jnp.where(step < 2, HD**-0.5, 1.0))

        @pl.when(step >= 4)
        def _():
            qkv[block, spans[0]] = proj.astype(BF)

    for k in range(2):

        @pl.when(step == 6 + k)
        def _(k=k):
            store[k].start()
            cross[k].wait()
            got = slice(k * chunk, (k + 1) * chunk)
            rem_ref[got, :] = rem[got, :]
            norm(rem, k * chunk, chunk, half + k * chunk)
            cols = spans[1 + k]
            for turn in range(6):
                block = slice(turn * rows, (turn + 1) * rows)
                proj = mm(w_t[block, :], act_ref[:, cols])
                if turn < 4:
                    rotated(proj, block, cols, HD**-0.5 if turn < 2 else 1.0)
                else:
                    qkv[block, cols] = proj.astype(BF)
            if k == 1:
                store[2].start()
                for copy in store:
                    copy.wait()


def rotary_constants(length):
    angles = np.arange(length, dtype=np.float32)[None, :] * np.exp(
        -math.log(10000.0) * np.arange(HD // 2, dtype=np.float32) / np.float32(HD // 2)
    ).astype(np.float32)[:, None]
    angles = angles.reshape(HD // 2, 2, length // 2).transpose(1, 0, 2).astype(np.float64)
    return np.cos(angles).astype(np.float32), np.sin(angles).astype(np.float32)


def project(tokens, time_index, span_starts, span_lengths, w_ada, b_ada, gains, b_down, w_qkv):
    _, half, width = tokens.shape
    length = 2 * half
    blk = width // 2
    cos_all, sin_all = rotary_constants(length)
    smem = pl.BlockSpec(memory_space=pltpu.SMEM)
    outs = [
        ((width, length), BF),
        ((3 * width, length), BF),
        ((3 * width, width), BF),
        ((half, width), BF),
        ((8, width), F32),
        ((8, width), F32),
        ((length, 1), F32),
        ((HD // 2, length), F32),
        ((HD // 2, length), F32),
    ]
    out_specs = [once(shape) for shape, _ in outs]
    out_specs[1] = ANY
    out_specs[2] = pl.BlockSpec((blk, width), lambda i: (jnp.minimum(i, 5), 0))
    rows = [b_ada, *gains, b_down]
    return pl.pallas_call(
        project_kernel,
        grid=(8,),
        in_specs=[smem, smem, smem, ANY, once(cos_all.shape), once(sin_all.shape), once(w_ada.shape)]
        + [once(r.shape) for r in rows]
        + [pl.BlockSpec((width, blk), lambda i: (0, jnp.minimum(i, 5)))],
        out_specs=out_specs,
        out_shape=[jax.ShapeDtypeStruct(*o) for o in outs],
        scratch_shapes=[
            pltpu.VMEM((half, width), BF),
            pltpu.VMEM((half, width), BF),
            pltpu.VMEM((3 * width, width), BF),
            pltpu.VMEM((3 * width, length), BF),
            pltpu.SemaphoreType.DMA((8,)),
        ],
        compiler_params=params(collective_id=6),
        cost_estimate=pl.CostEstimate(
            flops=6 * length * width * width, bytes_accessed=20 << 20, transcendentals=0
        ),
        name="project",
    )(time_index, span_starts, span_lengths, tokens, cos_all, sin_all, w_ada, *rows, w_qkv)


def attend_kernel(
    q_ref, k_ref, v_ref, cot_ref, att_ref, e_ref, linv_ref, cot_rem, q_mask, v_ext, send, recv
):
    step = pl.program_id(0)
    cot_send = cot_ref.at[1 - lax.axis_index("seq")]

    @pl.when(step == 0)
    def _():
        swap_start(cot_send, cot_rem, send, recv)

    tokens = q_ref.shape[1]
    tile = 256
    zero = jnp.zeros((HD, tokens), BF)
    k_nat = k_ref[...].T
    q_mask[0, 0:HD, :] = q_ref[0:HD, :]
    q_mask[0, HD:, :] = zero
    q_mask[1, 0:HD, :] = zero
    q_mask[1, HD:, :] = q_ref[HD:, :]
    for h in range(2):
        v_ext[h, 0:HD, :] = v_ref[h * HD : (h + 1) * HD, :]
        v_ext[h, HD:, :] = jnp.ones((16, tokens), BF)
    def score(h, cols):
        return mm(k_nat, q_mask[h, :, cols])

    def soften(h, cols, s):
        e_ref[h, :, cols] = jnp.exp(s - jnp.max(s, axis=0, keepdims=True)).astype(BF)

    def mix(h, cols):
        mixed = mm(v_ext[h], e_ref[h, :, cols])
        linv = 1.0 / mixed[HD : HD + 1, :]
        linv_ref[0, h : h + 1, cols] = linv
        att_ref[h * HD : (h + 1) * HD, cols] = (mixed[0:HD, :] * linv).astype(BF)

    units = [(h, slice(t, t + tile)) for t in range(0, tokens, tile) for h in range(2)]
    coming = score(*units[0])
    for i, unit in enumerate(units):
        here = coming
        if i + 1 < len(units):
            coming = score(*units[i + 1])
        soften(*unit, here)
        if i > 0:
            mix(*units[i - 1])
    mix(*units[-1])

    @pl.when(step == pl.num_programs(0) - 1)
    def _():
        swap_wait(cot_send, cot_rem, send, recv)


def attend(qkv_t, cotangent):
    tokens = qkv_t.shape[1]
    width = HEADS * HD

    def part(k):
        return pl.BlockSpec((2 * HD, tokens), lambda i: (i + k * PAIRS, 0))

    return pl.pallas_call(
        attend_kernel,
        grid=(PAIRS,),
        in_specs=[part(0), part(1), part(2), ANY],
        out_specs=[
            part(0),
            pl.BlockSpec((2, tokens, tokens), lambda i: (i, 0, 0)),
            pl.BlockSpec((1, 8, tokens), lambda i: (i, 0, 0)),
            ANY,
        ],
        out_shape=[
            jax.ShapeDtypeStruct((width, tokens), BF),
            jax.ShapeDtypeStruct((HEADS, tokens, tokens), BF),
            jax.ShapeDtypeStruct((PAIRS, 8, tokens), F32),
            jax.ShapeDtypeStruct(cotangent.shape[1:], BF),
        ],
        scratch_shapes=[
            pltpu.VMEM((2, 2 * HD, tokens), BF),
            pltpu.VMEM((2, HD + 16, tokens), BF),
        ]
        + SEMS,
        compiler_params=params(collective_id=1),
        cost_estimate=pl.CostEstimate(
            flops=16 * tokens * tokens * width,
            bytes_accessed=30 << 20,
            transcendentals=HEADS * tokens * tokens,
        ),
        name="attend",
    )(qkv_t, qkv_t, qkv_t, cotangent)


def gelu_both(u):
    c = math.sqrt(2.0 / math.pi)
    u2 = u * u
    th = jnp.tanh(u * (c + (c * 0.044715) * u2))
    half = 0.5 * (1.0 + th)
    value = u * half
    slope = half + (0.5 * u) * (1.0 - th * th) * (c + (3.0 * c * 0.044715) * u2)
    return value, slope


def middle_kernel(
    att_ref,
    tok_own,
    tok_rem,
    cot_own,
    cot_rem,
    span_ref,
    vec_ref,
    b_up_ref,
    w_out_ref,
    w_up_ref,
    w_down_ref,
    out_own,
    out_rem,
    dx_ref,
    d_att_ref,
    g_out_ref,
    g_up_ref,
    g_down_ref,
    g_bup_ref,
    sums_ref,
    branch,
    x_one,
    act_two,
    d_down,
    down_acc,
    d_act,
    d_branch,
):
    step = pl.program_id(0)
    steps = pl.num_programs(0)
    tokens = att_ref.shape[1]
    half = tokens // 2
    tile = 256
    per_half = half // tile
    gate_one = vec_ref[0:1, :]
    mult_two = vec_ref[1:2, :]
    shift_two = vec_ref[2:3, :]
    gate_two = vec_ref[3:4, :]
    b_down = vec_ref[4:5, :]
    gain_two = vec_ref[5:6, :]
    scale_two = vec_ref[6:7, :]

    @pl.when(step == 0)
    def _():
        for part, (tok, cot) in enumerate(((tok_own, cot_own), (tok_rem, cot_rem))):
            for t in range(per_half):
                src = slice(t * tile, (t + 1) * tile)
                dst = slice(part * half + t * tile, part * half + (t + 1) * tile)
                br = mm(att_ref[:, dst], w_out_ref[...], TN)
                branch[dst, :] = br
                x = tok[src, :].astype(F32) + gate_one * br
                x_one[dst, :] = x
                n, _ = norm_parts(x)
                act_two[dst, :] = (n * mult_two + shift_two).astype(BF)
                grad_out = cot[src, :].astype(F32) * span_ref[dst, :]
                d_down[dst, :] = (gate_two * grad_out).astype(BF)

    up = mm(act_two[...], w_up_ref[...]) + b_up_ref[...]
    value, slope = gelu_both(up)
    hidden = value.astype(BF)
    d_hidden = mm(d_down[...], w_down_ref[...], NT)
    d_up_full = slope * d_hidden
    d_up = d_up_full.astype(BF)
    g_bup_ref[...] = col_sum(d_up.astype(F32))
    down_part = mm(hidden, w_down_ref[...])
    d_act_part = mm(d_up, w_up_ref[...], NT)
    g_down_ref[...] = mm(hidden, d_down[...], TN).astype(BF)
    g_up_ref[...] = mm(act_two[...], d_up, TN).astype(BF)

    @pl.when(step == 0)
    def _():
        down_acc[...] = down_part
        d_act[...] = d_act_part

    @pl.when(step > 0)
    def _():
        down_acc[...] += down_part
        d_act[...] += d_act_part

    @pl.when(step == steps - 1)
    def _():
        zero = jnp.zeros((1, gate_one.shape[1]), F32)
        s_gate_two, s_shift, s_pull, s_gate_one, s_bdown = zero, zero, zero, zero, zero
        for part, (cot, out) in enumerate(((cot_own, out_own), (cot_rem, out_rem))):
            for t in range(per_half):
                src = slice(t * tile, (t + 1) * tile)
                dst = slice(part * half + t * tile, part * half + (t + 1) * tile)
                x = x_one[dst, :]
                down = down_acc[dst, :] + b_down
                out[src, :] = (x + gate_two * down).astype(BF)
                grad_out = cot[src, :].astype(F32) * span_ref[dst, :]
                s_gate_two += col_sum(grad_out * down)
                s_bdown += col_sum(d_down[dst, :].astype(F32))
                n, rstd = norm_parts(x)
                da = d_act[dst, :]
                s_shift += col_sum(da)
                s_pull += col_sum(da * n)
                dx = grad_out + norm_pull(n, rstd, da * mult_two)
                dx_ref[dst, :] = dx
                s_gate_one += col_sum(dx * branch[dst, :])
                d_branch[dst, :] = (gate_one * dx).astype(BF)
        sums_ref[0:1, :] = s_gate_one
        sums_ref[1:2, :] = s_shift
        sums_ref[2:3, :] = s_pull * gain_two
        sums_ref[3:4, :] = s_gate_two
        sums_ref[4:5, :] = s_pull * (1.0 + scale_two)
        sums_ref[5:6, :] = s_bdown
        sums_ref[6:8, :] = jnp.zeros((2, gate_one.shape[1]), F32)
        g_out_ref[...] = mm(att_ref[...], d_branch[...]).astype(BF)
        d_att_ref[...] = mm(w_out_ref[...], d_branch[...], NT).astype(BF)


def middle(att_t, tok_own, tok_rem, cot_own, cot_rem, span, vec, b_up, w_out, w_up, w_down):
    width, tokens = att_t.shape
    half = tokens // 2
    ff = w_up.shape[1]
    tile = 512
    return pl.pallas_call(
        middle_kernel,
        grid=(ff // tile,),
        in_specs=[
            whole(att_t.shape),
            whole(tok_own.shape),
            whole(tok_rem.shape),
            whole(cot_own.shape),
            whole(cot_rem.shape),
            whole(span.shape),
            whole(vec.shape),
            pl.BlockSpec((1, tile), lambda i: (0, i)),
            whole(w_out.shape),
            pl.BlockSpec((width, tile), lambda i: (0, i)),
            pl.BlockSpec((tile, width), lambda i: (i, 0)),
        ],
        out_specs=[
            whole((half, width)),
            whole((half, width)),
            whole((tokens, width)),
            whole((width, tokens)),
            whole((width, width)),
            pl.BlockSpec((width, tile), lambda i: (0, i)),
            pl.BlockSpec((tile, width), lambda i: (i, 0)),
            pl.BlockSpec((1, tile), lambda i: (0, i)),
            whole((8, width)),
        ],
        out_shape=[
            jax.ShapeDtypeStruct((half, width), BF),
            jax.ShapeDtypeStruct((half, width), BF),
            jax.ShapeDtypeStruct((tokens, width), F32),
            jax.ShapeDtypeStruct((width, tokens), BF),
            jax.ShapeDtypeStruct((width, width), BF),
            jax.ShapeDtypeStruct((width, ff), BF),
            jax.ShapeDtypeStruct((ff, width), BF),
            jax.ShapeDtypeStruct((1, ff), F32),
            jax.ShapeDtypeStruct((8, width), F32),
        ],
        scratch_shapes=[
            pltpu.VMEM((tokens, width), F32),
            pltpu.VMEM((tokens, width), F32),
            pltpu.VMEM((tokens, width), BF),
            pltpu.VMEM((tokens, width), BF),
            pltpu.VMEM((tokens, width), F32),
            pltpu.VMEM((tokens, width), F32),
            pltpu.VMEM((tokens, width), BF),
        ],
        compiler_params=params(),
        cost_estimate=pl.CostEstimate(
            flops=12 * tokens * width * ff + 6 * tokens * width * width,
            bytes_accessed=40 << 20,
            transcendentals=tokens * ff,
        ),
        name="middle",
    )(att_t, tok_own, tok_rem, cot_own, cot_rem, span, vec, b_up, w_out, w_up, w_down)


def middle_links_kernel(
    zs,
    att_ref,
    tokens_ref,
    tok_rem,
    cot_ref,
    cot_rem,
    span_ref,
    vec_ref,
    b_up_ref,
    w_out_ref,
    w_up_ref,
    w_down_ref,
    out_own,
    out_rem,
    dx_ref,
    d_att_ref,
    g_out_ref,
    g_up_ref,
    g_down_ref,
    up_last_ref,
    up_one_ref,
    up_two_ref,
    down_last_ref,
    down_one_ref,
    down_two_ref,
    mod_ref,
    sum_ref,
    branch,
    x_one,
    act_two,
    d_down,
    down_acc,
    d_act,
    d_branch,
    hidden,
    d_up,
    up_core,
    up_side,
    up_y,
    up_z,
    down_core,
    down_y,
    down_side,
    down_z,
    sems,
):
    step = pl.program_id(0)
    steps = zs
    tokens = att_ref.shape[1]
    width = att_ref.shape[0]
    half = tokens // 2
    cut = width // 2
    tile = 256
    per_half = half // tile
    gate_one = vec_ref[0:1, :]
    mult_two = vec_ref[1:2, :]
    shift_two = vec_ref[2:3, :]
    gate_two = vec_ref[3:4, :]
    b_down = vec_ref[4:5, :]
    gain_two = vec_ref[5:6, :]
    scale_two = vec_ref[6:7, :]

    links = Links(sems, zs)
    x, y, z, c = links.x, links.y, links.z, links.c
    tok_own, cot_own = tokens_ref.at[x], cot_ref.at[x]
    tiles = range(steps - 1)

    def swaps(src, dst, device):
        return [links.swap(lambda j=j: src(j), lambda j=j: dst.at[j], device) for j in tiles]

    up_to_core = swaps(lambda j: g_up_ref.at[:, :, :, :, 1 - c], up_core, links.core)
    down_to_core = swaps(lambda j: g_down_ref.at[:, 1 - c], down_core, links.core)
    up_to_side = swaps(lambda j: up_core.at[j, 1 - x], up_side, links.facing)
    down_to_y = swaps(lambda j: down_core.at[j, 1 - y], down_y, links.across)
    up_to_y = swaps(lambda j: up_core.at[j, x, :, :, 1 - y], up_y, links.across)
    down_to_side = swaps(lambda j: down_core.at[j, y, 1 - x], down_side, links.facing)
    h, b = links.upper, links.lower
    down_goal = links.to_goal(lambda: down_core.at[0, y, x], lambda: down_z, 0)
    up_near = links.swap(lambda: up_core.at[0, x, :, 1 - b, y], lambda: up_z.at[0:2], links.near)
    up_beyond = links.swap(lambda: up_core.at[0, x, 1 - h, b, y], lambda: up_z.at[2], links.beyond)

    def core_stage(j):
        up_to_core[j]().start()
        down_to_core[j]().start()

    def first_stage(j):
        up_to_core[j]().wait()
        for i in grid_of(2, 2, 2, 2):
            up_core[(j, *i)] = up_core[(j, *i)] + g_up_ref[(*i, c)]
        up_to_side[j]().start()
        down_to_core[j]().wait()
        for i, k in grid_of(2, 2):
            down_core[j, i, k] = down_core[j, i, k] + g_down_ref[i, c, k]
        down_to_y[j]().start()

    def first_done(j):
        up_to_side[j]().wait()
        for i in grid_of(2, 2, 2):
            up_core[(j, x, *i)] = up_core[(j, x, *i)] + up_side[(j, *i)]
        down_to_y[j]().wait()
        for k in range(2):
            down_core[j, y, k] = down_core[j, y, k] + down_y[j, k]

    def second_stage(j):
        first_done(j)
        up_to_y[j]().start()
        down_to_side[j]().start()

    def second_done(j):
        up_to_y[j]().wait()
        for i in grid_of(2, 2):
            up_core[(j, x, *i, y)] = up_core[(j, x, *i, y)] + up_y[(j, *i)]
        down_to_side[j]().wait()
        down_core[j, y, x] = down_core[j, y, x] + down_side[j]

    def third_stage():
        second_done(0)
        up_near().start()
        down_goal[0]()

    def fourth_stage():
        up_near().wait()
        for k in range(2):
            up_core[0, x, k, b, y] = up_core[0, x, k, b, y] + up_z[k]
        up_beyond().start()
        down_goal[1]()

    @pl.when(step == 0)
    def _():
        greet(links.core, links.across, links.facing, *[links.at_z(f) for f in links.far])
        for part, (tok, cot) in enumerate(((tok_own, cot_own), (tok_rem, cot_rem))):
            for t in range(per_half):
                src = slice(t * tile, (t + 1) * tile)
                dst = slice(part * half + t * tile, part * half + (t + 1) * tile)
                br = mm(att_ref[:, dst], w_out_ref[...], TN)
                branch[dst, :] = br
                xv = tok[src, :].astype(F32) + gate_one * br
                x_one[dst, :] = xv
                n, _ = norm_parts(xv)
                act_two[dst, :] = (n * mult_two + shift_two).astype(BF)
                grad_out = cot[src, :].astype(F32) * span_ref[dst, :]
                d_down[dst, :] = (gate_two * grad_out).astype(BF)
                down_acc[dst, :] = jnp.zeros((tile, width), F32)
                d_act[dst, :] = jnp.zeros((tile, width), F32)

    chunk = tokens // 2

    def one(k, bup):
        rows = rows_of(chunk, k)
        up = mm(act_two[rows, :], w_up_ref[...]) + b_up_ref[...]
        d_hidden = mm(d_down[rows, :], w_down_ref[...], NT)
        value, slope = gelu_both(up)
        low = value.astype(BF)
        hidden[rows, :] = low
        d_up_low = (slope * d_hidden).astype(BF)
        d_up[rows, :] = d_up_low
        down_acc[rows, :] += mm(low, w_down_ref[...])
        d_act[rows, :] += mm(d_up_low, w_up_ref[...], NT)
        return bup + col_sum(d_up_low.astype(F32))

    bup = lax.fori_loop(0, 2, one, jnp.zeros((1, w_up_ref.shape[1]), F32))
    for j in range(steps):
        pl.when(step == j)(lambda j=j: put_rows(sum_ref, 2 * width // 128 + j * bup.shape[1] // 128, bup))

    @pl.when(step == 1)
    def _():
        first_stage(0)

    @pl.when(step == 2)
    def _():
        second_stage(0)
        first_stage(1)

    @pl.when(step == 3)
    def _():
        third_stage()
        second_stage(1)
        first_stage(2)

    chunk_out = width // 3
    g_down_flat = g_down_ref.reshape(width, width)
    g_up_flat = g_up_ref.reshape(2, width, cut)

    def grads(turn, carry):
        outs = rows_of(chunk_out, turn)
        g_down_flat[outs, :] = mm(hidden[:, outs], d_down[...], TN).astype(BF)
        g_up = mm(act_two[:, outs], d_up[...], TN).astype(BF)
        for k in range(2):
            g_up_flat[k, outs, :] = g_up[:, k * cut : (k + 1) * cut]
        return carry

    lax.fori_loop(0, 3, grads, 0)

    @pl.when(step == 0)
    def _():
        core_stage(0)

    @pl.when(step == 1)
    def _():
        core_stage(1)

    @pl.when(step == 2)
    def _():
        core_stage(2)

    @pl.when(step == steps - 1)
    def _():
        fourth_stage()
        zero = jnp.zeros((1, width), F32)
        s_gate_two, s_shift, s_pull, s_gate_one, s_bdown = zero, zero, zero, zero, zero
        for part, (cot, out) in enumerate(((cot_own, out_own), (cot_rem, out_rem))):
            for t in range(per_half):
                src = slice(t * tile, (t + 1) * tile)
                dst = slice(part * half + t * tile, part * half + (t + 1) * tile)
                xv = x_one[dst, :]
                down = down_acc[dst, :] + b_down
                out[src, :] = (xv + gate_two * down).astype(BF)
                grad_out = cot[src, :].astype(F32) * span_ref[dst, :]
                s_gate_two += col_sum(grad_out * down)
                s_bdown += col_sum(d_down[dst, :].astype(F32))
                n, rstd = norm_parts(xv)
                da = d_act[dst, :]
                s_shift += col_sum(da)
                s_pull += col_sum(da * n)
                dx = grad_out + norm_pull(n, rstd, da * mult_two)
                dx_ref[dst, :] = dx
                s_gate_one += col_sum(dx * branch[dst, :])
                d_branch[dst, :] = (gate_one * dx).astype(BF)
        lines = width // 128
        mod_ref[4 * lines :, :] = jnp.zeros((mod_ref.shape[0] - 4 * lines, 128), BF)
        for k, row in enumerate((s_gate_one, s_shift, s_pull * gain_two, s_gate_two)):
            put_rows(mod_ref, k * lines, row)
        put_rows(mod_ref, 4 * lines, vec_ref[7:8, 0:128])
        put_rows(sum_ref, 0, s_pull * (1.0 + scale_two))
        put_rows(sum_ref, lines, s_bdown)
        g_out = mm(att_ref[...], d_branch[...]).astype(BF)
        for k in range(2):
            g_out_ref[k] = g_out[:, k * cut : (k + 1) * cut].reshape(g_out_ref.shape[1:])
        d_att_ref[...] = mm(w_out_ref[...], d_branch[...], NT).astype(BF)
        up_beyond().wait()
        up_last_ref[...] = up_core[0, x, h, b, y] + up_z[2]
        down_goal[2]()
        down_last_ref[...] = down_core[0, y, x]
        second_done(1)
        for i, k in grid_of(2, 2):
            up_one_ref[i, k] = up_core[1, x, i, k, y]
        down_one_ref[...] = down_core[1, y, x]
        first_done(2)
        up_two_ref[...] = up_core[2, x]
        down_two_ref[...] = down_core[2, y]


def middle_links(
    att_t, tok_all, tok_rem, cot_all, cot_rem, span, vec, b_up, w_out, w_up, w_down, zs
):
    width, tokens = att_t.shape
    half = tokens // 2
    cut = width // 2
    ff = w_up.shape[1]
    tile = ff // zs
    rows = width // (4 * zs)
    down_rows = tile // 4
    halves = (2, 2, 2, 2, 2, rows, cut)
    down_half = (down_rows // 2, width)
    owned = (2, 2, 2) + down_half
    outs = [
        ((half, width), BF),
        ((half, width), BF),
        ((tokens, width), F32),
        ((width, tokens), BF),
        (halves, BF),
        (halves, BF),
        (owned, BF),
        ((rows, cut), BF),
        ((2, 2, rows, cut), BF),
        ((2, 2, 2, rows, cut), BF),
        (down_half, BF),
        (down_half, BF),
        ((2,) + down_half, BF),
        ((early_mod_rows(width), 128), BF),
        ((early_sum_rows(width, ff), 128), F32),
    ]
    return pl.pallas_call(
        functools.partial(middle_links_kernel, zs),
        grid=(zs,),
        in_specs=[
            once(att_t.shape),
            once(tok_all.shape),
            once(tok_rem.shape),
            once(cot_all.shape),
            once(cot_rem.shape),
            once(span.shape),
            once(vec.shape),
            pl.BlockSpec((1, tile), lambda i: (0, i)),
            once(w_out.shape),
            pl.BlockSpec((width, tile), lambda i: (0, i)),
            pl.BlockSpec((tile, width), lambda i: (i, 0)),
        ],
        out_specs=[once(shape) for shape, _ in outs],
        out_shape=[jax.ShapeDtypeStruct(*o) for o in outs],
        scratch_shapes=[
            pltpu.VMEM((tokens, width), F32),
            pltpu.VMEM((tokens, width), F32),
            pltpu.VMEM((tokens, width), BF),
            pltpu.VMEM((tokens, width), BF),
            pltpu.VMEM((tokens, width), F32),
            pltpu.VMEM((tokens, width), F32),
            pltpu.VMEM((tokens, width), BF),
            pltpu.VMEM((tokens, tile), BF),
            pltpu.VMEM((tokens, tile), BF),
            pltpu.VMEM((zs - 1, 2, 2, 2, 2, rows, cut), BF),
            pltpu.VMEM((zs - 1, 2, 2, 2, rows, cut), BF),
            pltpu.VMEM((zs - 1, 2, 2, rows, cut), BF),
            pltpu.VMEM((3, rows, cut), BF),
            pltpu.VMEM((zs - 1, 2, 2) + down_half, BF),
            pltpu.VMEM((zs - 1, 2) + down_half, BF),
            pltpu.VMEM((zs - 1,) + down_half, BF),
            pltpu.VMEM((2,) + down_half, BF),
            pltpu.SemaphoreType.DMA((12 * (zs - 1) + 8,)),
        ],
        compiler_params=params(62, collective_id=4),
        cost_estimate=pl.CostEstimate(
            flops=12 * tokens * width * ff + 6 * tokens * width * width,
            bytes_accessed=40 << 20,
            transcendentals=tokens * ff,
        ),
        name="middle_links",
    )(att_t, tok_all, tok_rem, cot_all, cot_rem, span, vec, b_up, w_out, w_up, w_down)


def attend_back_kernel(
    q_ref,
    k_ref,
    v_ref,
    att_ref,
    d_att_ref,
    e_ref,
    linv_ref,
    cos_ref,
    sin_ref,
    give_ref,
    out_ref,
    take_ref,
    do_mask,
    send,
    recv,
):
    step = pl.program_id(0)

    @pl.when(step == 0)
    def _():
        swap_start(give_ref, take_ref, send, recv)

    tokens = q_ref.shape[1]
    tile = 256
    zero = jnp.zeros((HD, tokens), BF)
    v_nat = v_ref[...].T
    cos = cos_ref[...]
    sin = sin_ref[...]

    def unrotate(x):
        low = x.astype(BF).astype(F32)
        a, b = low[0 : HD // 2], low[HD // 2 :]
        return a * cos + b * sin, b * cos - a * sin

    for h in range(2):
        rows = slice(h * HD, (h + 1) * HD)
        linv = linv_ref[0, h : h + 1, :]
        d_o = d_att_ref[rows, :].astype(F32)
        d_os = (d_o * linv).astype(BF)
        do_mask[h, rows, :] = d_os
        do_mask[h, (1 - h) * HD : (2 - h) * HD, :] = zero
        inner = col_sum(d_o * att_ref[rows, :].astype(F32)) * linv
        d_values = mm(d_os, e_ref[h], NT)
        out_ref[2, rows, :] = d_values.astype(BF)
        d_keys = jnp.zeros((HD, tokens), F32)
        d_queries = []
        for t in range(tokens // tile):
            cols = slice(t * tile, (t + 1) * tile)
            d_probs = mm(v_nat, do_mask[h, :, cols])
            d_s = (e_ref[h, :, cols].astype(F32) * (d_probs - inner[:, cols])).astype(BF)
            d_queries.append(mm(k_ref[rows, :], d_s))
            d_keys += mm(q_ref[rows, cols], d_s, NT)
        dq = jnp.concatenate(d_queries, axis=1) * HD**-0.5
        lead, trail = unrotate(dq)
        out_ref[0, h * HD : h * HD + HD // 2, :] = lead.astype(BF)
        out_ref[0, h * HD + HD // 2 : (h + 1) * HD, :] = trail.astype(BF)
        lead, trail = unrotate(d_keys)
        out_ref[1, h * HD : h * HD + HD // 2, :] = lead.astype(BF)
        out_ref[1, h * HD + HD // 2 : (h + 1) * HD, :] = trail.astype(BF)

    @pl.when(step == pl.num_programs(0) - 1)
    def _():
        swap_wait(give_ref, take_ref, send, recv)


def attend_back(qkv_t, att_t, d_att_t, e, linv, cos_t, sin_t, give):
    tokens = qkv_t.shape[1]
    width = HEADS * HD

    def part(k):
        return pl.BlockSpec((2 * HD, tokens), lambda i: (i + k * PAIRS, 0))

    return pl.pallas_call(
        attend_back_kernel,
        grid=(PAIRS,),
        in_specs=[
            part(0),
            part(1),
            part(2),
            part(0),
            part(0),
            pl.BlockSpec((2, tokens, tokens), lambda i: (i, 0, 0)),
            pl.BlockSpec((1, 8, tokens), lambda i: (i, 0, 0)),
            whole(cos_t.shape),
            whole(sin_t.shape),
            ANY,
        ],
        out_specs=[pl.BlockSpec((3, 2 * HD, tokens), lambda i: (0, i, 0)), ANY],
        out_shape=[
            jax.ShapeDtypeStruct((3, width, tokens), BF),
            jax.ShapeDtypeStruct(give.shape, give.dtype),
        ],
        scratch_shapes=[pltpu.VMEM((2, 2 * HD, tokens), BF)] + SEMS,
        compiler_params=params(collective_id=2),
        cost_estimate=pl.CostEstimate(
            flops=32 * tokens * tokens * width, bytes_accessed=36 << 20, transcendentals=0
        ),
        name="attend_back",
    )(qkv_t, qkv_t, qkv_t, att_t, d_att_t, e, linv, cos_t, sin_t, give)


def tail_kernel(tok_own, tok_rem, d_proj_ref, w_ref, dx_ref, vec_ref, own_ref, rem_ref, sums_ref):
    step = pl.program_id(0)
    steps = pl.num_programs(0)
    mult_one = vec_ref[0:1, :]
    gain_one = vec_ref[2:3, :]
    scale_one = vec_ref[3:4, :]
    d_act = mm(d_proj_ref[...], w_ref[...], TN)

    def finish(tok, out):
        n, rstd = norm_parts(tok[...].astype(F32))
        grad = dx_ref[...] + norm_pull(n, rstd, d_act * mult_one)
        out[...] = grad.astype(out.dtype)
        return col_sum(d_act), col_sum(d_act * n)

    @pl.when(step == 0)
    def _():
        shift, pull = finish(tok_rem, rem_ref)
        sums_ref[0:1, :] = shift
        sums_ref[1:2, :] = pull
        sums_ref[2:, :] = jnp.zeros((6, shift.shape[1]), F32)

    @pl.when(step == steps - 1)
    def _():
        shift, pull = finish(tok_own, own_ref)
        shift = sums_ref[0:1, :] + shift
        pull = sums_ref[1:2, :] + pull
        sums_ref[0:1, :] = shift
        sums_ref[1:2, :] = pull * gain_one
        sums_ref[2:3, :] = pull * (1.0 + scale_one)


def tail(tok_own, tok_rem, d_proj_t, w_qkv_t, dx, vec):
    half, width = tok_own.shape
    return pl.pallas_call(
        tail_kernel,
        grid=(2,),
        in_specs=[
            whole(tok_own.shape),
            whole(tok_rem.shape),
            pl.BlockSpec((3 * width, half), lambda i: (0, 1 - i)),
            whole(w_qkv_t.shape),
            pl.BlockSpec((half, width), lambda i: (1 - i, 0)),
            whole(vec.shape),
        ],
        out_specs=[whole((half, width)), whole((half, width)), whole((8, width))],
        out_shape=[
            jax.ShapeDtypeStruct((half, width), F32),
            jax.ShapeDtypeStruct((half, width), BF),
            jax.ShapeDtypeStruct((8, width), F32),
        ],
        compiler_params=params(),
        cost_estimate=pl.CostEstimate(
            flops=12 * half * width * width, bytes_accessed=20 << 20, transcendentals=0
        ),
        name="tail",
    )(tok_own, tok_rem, d_proj_t, w_qkv_t, dx, vec)


def weight_grad_kernel(act_ref, d_proj_ref, out_ref):
    out_ref[...] = mm(act_ref[...], d_proj_ref[...], NT).astype(BF)


def weight_grad(act_t, d_proj_t):
    width, tokens = act_t.shape
    cols = d_proj_t.shape[0]
    tile = 768
    return pl.pallas_call(
        weight_grad_kernel,
        grid=(cols // tile,),
        in_specs=[whole(act_t.shape), pl.BlockSpec((tile, tokens), lambda i: (i, 0))],
        out_specs=pl.BlockSpec((width, tile), lambda i: (0, i)),
        out_shape=jax.ShapeDtypeStruct((width, cols), BF),
        compiler_params=params(),
        cost_estimate=pl.CostEstimate(
            flops=2 * cols * width * tokens, bytes_accessed=12 << 20, transcendentals=0
        ),
        name="weight_grad",
    )(act_t, d_proj_t)


def gather_stages(links, ref):
    z, y, c, x = links.z, links.y, links.c, links.x

    def pair(mine, theirs, device):
        sem = links.take(2)

        def make(slot):
            return remote(slot(), slot(), links.sems.at[sem], links.sems.at[sem + 1], device)

        def wait():
            make(mine).wait_send()
            make(theirs).wait_recv()

        return (lambda: make(mine).start()), wait

    sem = links.take(2 * links.zs)

    def make(f, slot):
        block = ref.at[slot, :, :, x]
        return remote(
            block, block, links.sems.at[sem + f], links.sems.at[sem + links.zs + slot], links.at_z(f)
        )

    def far_start():
        for f in links.far:
            make(f, z).start()

    def far_wait():
        for f in links.far:
            make(f, z).wait_send()
            make(f, f).wait_recv()

    return [
        pair(lambda: ref.at[z, y, c, x], lambda: ref.at[z, y, 1 - c, x], links.core),
        pair(lambda: ref.at[z, y, :, x], lambda: ref.at[z, 1 - y, :, x], links.across),
        (far_start, far_wait),
        pair(lambda: ref.at[:, :, :, x], lambda: ref.at[:, :, :, 1 - x], links.facing),
    ]


def sum_stages(links, ref, take, far):
    swaps = [
        links.swap(lambda: ref, lambda k=k: take.at[k], device)
        for k, device in enumerate((links.core, links.across, links.facing))
    ]
    far_start, far_wait = links.spread(lambda f: ref, lambda slot: far.at[slot])

    def finish(k):
        swaps[k]().wait()
        ref[...] += take[k]

    def far_finish():
        far_wait()
        far[links.z] = ref[...]
        total = far[0]
        for f in range(1, links.zs):
            total += far[f]
        ref[...] = total

    return [
        (lambda: swaps[0]().start(), lambda: finish(0)),
        (lambda: swaps[1]().start(), lambda: finish(1)),
        (far_start, far_finish),
        (lambda: swaps[2]().start(), lambda: finish(2)),
    ]


def back_kernel(zs, split, ins, outs, scratch):
    (
        q_ref,
        k_ref,
        v_ref,
        att_ref,
        d_att_ref,
        e_ref,
        linv_ref,
        cos_ref,
        sin_ref,
        give_ref,
        up_last_ref,
        up_one_ref,
        up_two_ref,
        down_last_ref,
        down_one_ref,
        down_two_ref,
        raw_up,
        raw_out,
        raw_down,
        mod_ref,
        sum_ref,
        act_in,
        w_in,
        tok_own_in,
        tok_rem_in,
        dx_in,
        vec_ref,
    ) = ins
    result, grad_ref, grad_take, s_qkv, s_out, s_up, s_down, *small_outs = outs
    (
        do_mask,
        d_proj,
        sems,
        u_own,
        u_y,
        u_z,
        u_last,
        u_facing,
        w_own,
        w_core,
        w_y,
        w_z,
        w_far,
        w_last,
        w_facing,
        d_own,
        d_core,
        d_y,
        d_side,
        d_sum,
        d_z,
        d_last,
        d_facing,
        q_raws,
        q_cores,
        q_ys,
        q_zs,
        q_lasts,
        q_facings,
        g_send,
        g_take,
        early_take,
        early_far,
        late_take,
        late_far,
        mod_early,
        mod_late,
        sum_early,
        sum_late,
        act_ref,
        w_ref,
        tok_own,
        tok_rem,
        dx_ref,
        g_own,
    ) = scratch
    step = pl.program_id(0)
    tokens = q_ref.shape[1]
    width = act_ref.shape[0]
    half = tokens // 2
    cut = width // 2
    links = Links(sems, zs)
    x, y, z, c = links.x, links.y, links.z, links.c
    h, b = links.upper, links.lower

    fetch = [
        links.local(lambda p=p: p[0], lambda p=p: p[1])
        for p in (
            (act_in, act_ref),
            (w_in, w_ref),
            (tok_own_in.at[x], tok_own),
            (tok_rem_in, tok_rem),
            (dx_in, dx_ref),
        )
    ]
    u_load = [
        links.local(lambda: up_last_ref, lambda: u_last.at[0]),
        links.local(lambda: up_one_ref.at[:, b], lambda: u_own.at[0, :, b]),
        links.local(lambda: up_two_ref.at[:, :, y], lambda: u_own.at[1]),
    ]
    u_to_y = links.swap(lambda: up_two_ref.at[:, :, 1 - y], lambda: u_y, links.across)
    u_near = [
        links.swap(
            lambda j=j: up_one_ref.at[:, 1 - b] if j == 0 else u_own.at[1, :, 1 - b],
            lambda j=j: u_z.at[j, 0:2],
            links.near,
        )
        for j in range(2)
    ]
    u_beyond = [
        links.swap(lambda j=j: u_own.at[j, 1 - h, b], lambda j=j: u_z.at[j, 2], links.beyond)
        for j in range(2)
    ]
    u_to_facing = [
        links.swap(lambda j=j: u_last.at[j], lambda j=j: u_facing.at[j], links.facing)
        for j in range(3)
    ]
    raws = (raw_up, raw_out)
    w_keep = [
        links.local(lambda r=r: r.at[:, :, :, :, c], lambda k=k: w_own.at[k]) for k, r in enumerate(raws)
    ]
    w_to_core = [
        links.swap(lambda r=r: r.at[:, :, :, :, 1 - c], lambda k=k: w_core.at[k], links.core)
        for k, r in enumerate(raws)
    ]
    w_to_y = [
        links.swap(lambda k=k: w_own.at[k, :, :, :, 1 - y], lambda k=k: w_y.at[k], links.across)
        for k in range(2)
    ]
    w_near = [
        links.swap(
            lambda k=k: w_own.at[k, :, :, 1 - b, y], lambda k=k: w_z.at[k], links.near
        )
        for k in range(2)
    ]
    w_beyond = [
        links.swap(
            lambda k=k: w_own.at[k, :, 1 - h, b, y], lambda k=k: w_far.at[k], links.beyond
        )
        for k in range(2)
    ]
    w_to_facing = [
        links.swap(lambda k=k: w_last.at[k], lambda k=k: w_facing.at[k], links.facing)
        for k in range(2)
    ]
    d_keep = links.local(lambda: raw_down.at[:, c], lambda: d_own)
    d_to_core = links.swap(lambda: raw_down.at[:, 1 - c], lambda: d_core, links.core)
    d_to_y = links.swap(lambda: d_own.at[1 - y], lambda: d_y, links.across)
    d_to_side = [
        links.swap(lambda: down_two_ref.at[1 - x], lambda: d_side.at[0], links.facing),
        links.swap(lambda: d_own.at[y, 1 - x], lambda: d_side.at[1], links.facing),
    ]
    d_load = [
        links.local(lambda: down_last_ref, lambda: d_last),
        links.local(lambda: down_one_ref, lambda: d_sum.at[0]),
        links.local(lambda: down_two_ref.at[x], lambda: d_sum.at[1]),
    ]
    d_goal = [
        links.to_goal(lambda j=j: d_sum.at[j - 1], lambda j=j: d_z.at[j - 1], j) for j in range(1, zs)
    ]
    d_to_facing = links.swap(lambda: d_last, lambda: d_facing, links.facing)
    groups = range(len(split))
    q_to_core = [
        links.swap(lambda g=g: q_raws[g].at[:, :, :, 1 - c], lambda g=g: q_cores[g], links.core)
        for g in groups
    ]
    q_to_y = [
        links.swap(lambda g=g: q_cores[g].at[:, :, 1 - y], lambda g=g: q_ys[g], links.across)
        for g in groups
    ]
    q_near = [
        links.swap(lambda g=g: q_cores[g].at[:, 1 - b, y], lambda g=g: q_zs[g].at[0:2], links.near)
        for g in groups
    ]
    q_beyond = [
        links.swap(lambda g=g: q_cores[g].at[1 - h, b, y], lambda g=g: q_zs[g].at[2], links.beyond)
        for g in groups
    ]
    q_to_facing = [
        links.swap(lambda g=g: q_lasts[g], lambda g=g: q_facings[g], links.facing) for g in groups
    ]
    cross_out = links.swap(lambda: give_ref, lambda: result, links.facing)

    give_grad = links.swap(lambda: g_send, lambda: g_take, links.facing)
    keep_grad = links.local(lambda: g_own, lambda: grad_ref)
    put_grad = links.local(lambda: g_take, lambda: grad_take)
    early = [
        gather_stages(links, mod_early),
        sum_stages(links, sum_early, early_take, early_far),
    ]
    late = [gather_stages(links, mod_late), sum_stages(links, sum_late, late_take, late_far)]

    def begin(arrays, stage):
        for stages in arrays:
            stages[stage][0]()

    def end(arrays, stage):
        for stages in arrays:
            stages[stage][1]()

    def u_near_done(j):
        u_near[j]().wait()
        for k in range(2):
            u_own[j, k, b] = u_own[j, k, b] + u_z[j, k]
        u_beyond[j]().start()

    def u_beyond_done(j):
        u_beyond[j]().wait()
        u_last[j + 1] = u_own[j, h, b] + u_z[j, 2]
        u_to_facing[j + 1]().start()

    def u_done(j):
        u_to_facing[j]().wait()
        mine, other = u_last[j].astype(F32), u_facing[j].astype(F32)
        start = j * width
        s_up[:, start : start + cut] = jnp.where(x == 0, mine, other)
        s_up[:, start + cut : start + width] = jnp.where(x == 0, other, mine)

    def w_core_done(k):
        w_keep[k]().wait()
        w_to_core[k]().wait()
        for i in grid_of(2, 2, 2, 2):
            w_own[(k, *i)] = w_own[(k, *i)] + w_core[(k, *i)]

    def w_y_done(k):
        w_to_y[k]().wait()
        for i in grid_of(2, 2, 2):
            w_own[(k, *i, y)] = w_own[(k, *i, y)] + w_y[(k, *i)]
        w_near[k]().start()

    def w_near_done(k):
        w_near[k]().wait()
        for i, j in grid_of(2, 2):
            w_own[k, i, j, b, y] = w_own[k, i, j, b, y] + w_z[k, i, j]
        w_beyond[k]().start()

    def w_beyond_done(k):
        w_beyond[k]().wait()
        for i in range(2):
            w_last[k, i] = w_own[k, i, h, b, y] + w_far[k, i]
        w_to_facing[k]().start()

    def w_done(k):
        w_to_facing[k]().wait()
        out, start = (s_up, (zs - 1) * width) if k == 0 else (s_out, 0)
        for i in range(2):
            out[:, start + i * cut : start + (i + 1) * cut] = w_last[k, i].astype(F32) + w_facing[
                k, i
            ].astype(F32)

    def q_core_done(g):
        q_to_core[g]().wait()
        for i in grid_of(2, 2, 2):
            q_cores[g][i] = q_cores[g][i] + q_raws[g][(*i, c)]

    def q_y_done(g):
        q_to_y[g]().wait()
        for i in grid_of(2, 2):
            q_cores[g][(*i, y)] = q_cores[g][(*i, y)] + q_ys[g][i]
        q_near[g]().start()

    def q_near_done(g):
        q_near[g]().wait()
        for k in range(2):
            q_cores[g][k, b, y] = q_cores[g][k, b, y] + q_zs[g][k]
        q_beyond[g]().start()

    def q_beyond_done(g):
        q_beyond[g]().wait()
        q_lasts[g][...] = q_cores[g][h, b, y] + q_zs[g][2]
        q_to_facing[g]().start()

    def q_done(g):
        q_to_facing[g]().wait()
        total = q_lasts[g][...].astype(F32) + q_facings[g][...].astype(F32)
        first, size = split[g][0] * HD, (split[g][1] - split[g][0]) * HD
        for p in range(3):
            s_qkv[:, p * width + first : p * width + first + size] = total[:, p * size : (p + 1) * size]

    def weight_grad_of(g):
        first, size = split[g][0] * HD, (split[g][1] - split[g][0]) * HD
        for p in range(3):
            rows = slice(p * width + first, p * width + first + size)
            part = mm(act_ref[...], d_proj[rows, :], NT).astype(BF)
            q_raws[g][:, :, :, :, :, p * size : (p + 1) * size] = part.reshape(
                q_raws[g].shape[:5] + (size,)
            )
        q_to_core[g]().start()


    def due_00():
        greet(links.core, links.across, links.facing, *[links.at_z(f) for f in links.far])
        d_to_core().start()
        d_keep().start()
        for k in range(2):
            w_to_core[k]().start()
            w_keep[k]().start()
        u_near[0]().start()
        u_to_y().start()
        d_to_side[0]().start()
        for load in u_load + d_load:
            load().start()
        mod_early[z, y, c, x] = mod_ref[...]
        sum_early[...] = sum_ref[...]
        begin(early, 0)
        for load in fetch:
            load().start()

    def due_01():
        d_load[1]().wait()
        d_goal[0][0]()
        d_keep().wait()
        d_to_core().wait()
        for i, k in grid_of(2, 2):
            d_own[i, k] = d_own[i, k] + d_core[i, k]
        d_to_y().start()
        end(early, 0)
        begin(early, 1)

    def due_10():
        w_core_done(0)
        w_core_done(1)
        u_load[0]().wait()
        u_to_facing[0]().start()

    def due_11():
        u_load[2]().wait()
        u_to_y().wait()
        for i in grid_of(2, 2):
            u_own[(1, *i)] = u_own[(1, *i)] + u_y[i]
        u_near[1]().start()
        w_to_y[0]().start()
        u_load[1]().wait()
        u_near_done(0)
        d_goal[0][1]()
        end(early, 1)
        begin(early, 2)
        cross_out().start()

    def due_20():
        fetch[0]().wait()
        weight_grad_of(0)
        d_load[2]().wait()
        d_to_side[0]().wait()
        d_sum[1] = d_sum[1] + d_side[0]
        d_goal[1][0]()

    def due_21():
        d_to_y().wait()
        for k in range(2):
            d_own[y, k] = d_own[y, k] + d_y[k]
        d_to_side[1]().start()
        q_core_done(0)
        q_to_y[0]().start()
        u_near_done(1)
        u_beyond_done(0)
        end(early, 2)
        begin(early, 3)

    def due_30():
        w_y_done(0)
        w_to_y[1]().start()
        d_goal[1][1]()

    def due_31():
        d_to_side[1]().wait()
        d_sum[2] = d_own[y, x] + d_side[1]
        d_goal[2][0]()

    def due_40():
        weight_grad_of(1)
        w_near_done(0)
        q_y_done(0)
        u_beyond_done(1)
        end(early, 3)

    def due_41():
        q_core_done(1)
        q_to_y[1]().start()
        d_goal[2][1]()
        u_done(0)

    def due_50():
        w_beyond_done(0)
        w_y_done(1)
        q_near_done(0)
        u_done(1)

    def due_51():
        d_load[0]().wait()
        for j in range(zs - 1):
            d_goal[j][2]()

        @pl.when(z > 0)
        def _():
            d_last[...] = d_sum[jnp.maximum(z - 1, 0)]

        d_to_facing().start()
        q_beyond_done(0)

    due = (
        (due_00, due_01),
        (due_10, due_11),
        (due_20, due_21),
        (due_30, due_31),
        (due_40, due_41),
        (due_50, due_51),
    )

    def do_due(h):
        for k in range(PAIRS):
            pl.when(step == k)(due[k][h])


    @pl.when(step < PAIRS)
    def _():
        tile = 256
        zero = jnp.zeros((HD, tokens), BF)
        v_nat = v_ref[...].T
        cos = cos_ref[...]
        sin = sin_ref[...]

        def put(part, h, value):
            low = value.astype(BF).astype(F32)
            a, b = low[0 : HD // 2], low[HD // 2 :]
            start = part * width + step * 2 * HD + h * HD
            d_proj[pl.ds(pl.multiple_of(start, 32), 32), :] = (a * cos + b * sin).astype(BF)
            d_proj[pl.ds(pl.multiple_of(start + 32, 32), 32), :] = (b * cos - a * sin).astype(BF)

        do_due(0)
        inners, keys, values, queries = [], [], [], [[], []]
        for h in range(2):
            rows = slice(h * HD, (h + 1) * HD)
            linv = linv_ref[0, h : h + 1, :]
            d_o = d_att_ref[rows, :].astype(F32)
            do_mask[h, rows, :] = (d_o * linv).astype(BF)
            do_mask[h, (1 - h) * HD : (2 - h) * HD, :] = zero
            inners.append(col_sum(d_o * att_ref[rows, :].astype(F32)) * linv)

        def ahead(h, cols):
            return mm(v_nat, do_mask[h, :, cols])

        def centre(h, cols, d_probs):
            rows = slice(h * HD, (h + 1) * HD)
            e = e_ref[h, :, cols]
            part = mm(do_mask[h, rows, cols], e, NT)
            if cols.start == 0:
                values.append(part)
            else:
                values[h] += part
            return (e.astype(F32) * (d_probs - inners[h][:, cols])).astype(BF)

        def behind(h, cols, d_s):
            rows = slice(h * HD, (h + 1) * HD)
            queries[h].append(mm(k_ref[rows, :], d_s))
            part = mm(q_ref[rows, cols], d_s, NT)
            if cols.start == 0:
                keys.append(part)
            else:
                keys[h] += part
            if cols.stop == tokens:
                put(0, h, jnp.concatenate(queries[h], axis=1) * HD**-0.5)
                put(1, h, keys[h])
                start = 2 * width + step * 2 * HD + h * HD
                d_proj[pl.ds(pl.multiple_of(start, HD), HD), :] = values[h].astype(BF)

        units = [(h, slice(t, t + tile)) for h in range(2) for t in range(0, tokens, tile)]
        coming = ahead(*units[0])
        for i, unit in enumerate(units):
            if i == len(units) // 2:
                do_due(1)
            here = coming
            if i + 1 < len(units):
                coming = ahead(*units[i + 1])
            d_s = centre(*unit, here)
            if i > 0:
                behind(*units[i - 1], held)
            held = d_s
        behind(*units[-1], held)


    def finish(tok, cols):
        d_act = mm(d_proj[:, cols], w_ref[...], TN)
        n, rstd = norm_parts(tok[...].astype(F32))
        grad = dx_ref[cols, :] + norm_pull(n, rstd, d_act * vec_ref[0:1, :])
        return grad, col_sum(d_act), col_sum(d_act * n)

    @pl.when(step == PAIRS)
    def _():
        for load in fetch[1:]:
            load().wait()
        weight_grad_of(2)
        grad, shift, pull = finish(tok_rem, slice(half, 2 * half))
        g_send[...] = grad.astype(BF)
        give_grad().start()
        q_core_done(2)
        q_to_y[2]().start()
        q_y_done(1)
        w_near_done(1)
        grad, shift_own, pull_own = finish(tok_own, slice(0, half))
        g_own[...] = grad
        keep_grad().start()
        shift += shift_own
        pull += pull_own
        lines = width // 128
        mine = mod_late.at[z, y, c, x]
        mine[2 * lines :, :] = jnp.zeros((mod_late.shape[4] - 2 * lines, 128), BF)
        put_rows(mine, 0, shift)
        put_rows(mine, lines, pull * vec_ref[2:3, :])
        sum_late[lines:, :] = jnp.zeros((sum_late.shape[0] - lines, 128), F32)
        put_rows(sum_late, 0, pull * (1.0 + vec_ref[3:4, :]))
        begin(late, 0)
        q_near_done(1)
        w_beyond_done(1)
        q_y_done(2)
        end(late, 0)
        begin(late, 1)
        u_done(2)
        w_done(0)
        q_done(0)
        end(late, 1)
        begin(late, 2)
        q_beyond_done(1)
        q_near_done(2)
        end(late, 2)
        begin(late, 3)
        d_to_facing().wait()
        mine, other = d_last[...].astype(F32), d_facing[...].astype(F32)
        rows_half = mine.shape[0]
        s_down[0:rows_half, :] = jnp.where(x == 0, mine, other)
        s_down[rows_half:, :] = jnp.where(x == 0, other, mine)
        q_beyond_done(2)
        cross_out().wait()
        w_done(1)
        q_done(1)
        end(late, 3)
        give_grad().wait()
        put_grad().start()
        keep_grad().wait()
        q_done(2)
        put_grad().wait()
        for out, value in zip(small_outs, (mod_early, mod_late, sum_early, sum_late)):
            out[...] = value[...]


def back(ins, zs, ff):
    q, att, d_att, e, linv, cos_t, sin_t = ins[:7]
    mod, sums, vec = ins[-8], ins[-7], ins[-1]
    width, tokens = att.shape
    half = tokens // 2
    cut = width // 2
    rows = width // (4 * zs)
    down_rows = ff // (4 * zs)
    down_half = (down_rows // 2, width)
    split = ((0, 4), (4, 8), (8, HEADS))
    sizes = [3 * (b - a) * HD for a, b in split]
    last = PAIRS - 1

    def part(k):
        return pl.BlockSpec((2 * HD, tokens), lambda i: (jnp.minimum(i, last) + k * PAIRS, 0))

    def vm(*shape, kind=BF):
        return pltpu.VMEM(shape, kind)

    lines = width // 128
    mod_early = (zs, 2, 2, 2) + mod.shape
    mod_late = (zs, 2, 2, 2, round_up(2 * lines, 16), 128)
    sum_late = (round_up(lines, 8), 128)
    outs = [
        ((half, width), F32),
        ((rows, 3 * width), F32),
        ((rows, width), F32),
        ((rows, ff), F32),
        ((down_rows, width), F32),
        (mod_early, BF),
        (mod_late, BF),
        (sums.shape, F32),
        (sum_late, F32),
    ]
    outs = [((half, width), F32), ((half, width), BF)] + outs[1:]
    fetched = ins[-6:-1]
    in_specs = (
        [part(0), part(1), part(2), part(0), part(0)]
        + [
            pl.BlockSpec((2, tokens, tokens), lambda i: (jnp.minimum(i, last), 0, 0)),
            pl.BlockSpec((1, 8, tokens), lambda i: (jnp.minimum(i, last), 0, 0)),
            once(cos_t.shape),
            once(sin_t.shape),
        ]
        + [ANY] * (len(ins) - 15)
        + [once(mod.shape), once(sums.shape)]
        + [ANY] * 5
        + [once(vec.shape)]
    )
    out_specs = [ANY, ANY, ANY] + [once(shape) for shape, _ in outs[2:]]
    out_shape = [jax.ShapeDtypeStruct((half, width), BF)] + [
        jax.ShapeDtypeStruct(*o) for o in outs
    ]
    scratch = [
        vm(2, 2 * HD, tokens),
        vm(3 * width, tokens),
        pltpu.SemaphoreType.DMA((250,)),
        vm(2, 2, 2, rows, cut),
        vm(2, 2, rows, cut),
        vm(2, 3, rows, cut),
        vm(3, rows, cut),
        vm(3, rows, cut),
        vm(2, 2, 2, 2, 2, rows, cut),
        vm(2, 2, 2, 2, 2, rows, cut),
        vm(2, 2, 2, 2, rows, cut),
        vm(2, 2, 2, rows, cut),
        vm(2, 2, rows, cut),
        vm(2, 2, rows, cut),
        vm(2, 2, rows, cut),
        vm(2, 2, *down_half),
        vm(2, 2, *down_half),
        vm(2, *down_half),
        vm(2, *down_half),
        vm(zs - 1, *down_half),
        vm(zs - 1, 2, *down_half),
        vm(*down_half),
        vm(*down_half),
        [vm(2, 2, 2, 2, rows, s) for s in sizes],
        [vm(2, 2, 2, rows, s) for s in sizes],
        [vm(2, 2, rows, s) for s in sizes],
        [vm(3, rows, s) for s in sizes],
        [vm(rows, s) for s in sizes],
        [vm(rows, s) for s in sizes],
        vm(half, width),
        vm(half, width),
        vm(3, *sums.shape, kind=F32),
        vm(zs, *sums.shape, kind=F32),
        vm(3, *sum_late, kind=F32),
        vm(zs, *sum_late, kind=F32),
        vm(*mod_early),
        vm(*mod_late),
        vm(*sums.shape, kind=F32),
        vm(*sum_late, kind=F32),
    ]
    scratch += [vm(*a.shape[-2:], kind=a.dtype) for a in fetched]
    scratch += [vm(half, width, kind=F32)]
    flat, tree = jax.tree.flatten(scratch)
    n_in, n_out = len(in_specs), len(out_specs)

    def kernel(*refs):
        back_kernel(
            zs,
            split,
            refs[:n_in],
            refs[n_in : n_in + n_out],
            jax.tree.unflatten(tree, refs[n_in + n_out :]),
        )

    return pl.pallas_call(
        kernel,
        grid=(PAIRS + 1,),
        in_specs=in_specs,
        out_specs=out_specs,
        out_shape=out_shape,
        scratch_shapes=flat,
        compiler_params=params(62, collective_id=5),
        cost_estimate=pl.CostEstimate(
            flops=32 * tokens * tokens * width + 12 * tokens * width * width,
            bytes_accessed=60 << 20,
            transcendentals=0,
        ),
        name="back",
    )(q, q, q, att, d_att, e, linv, cos_t, sin_t, *ins[7:])


def iota2(shape, axis):
    return lax.broadcasted_iota(jnp.int32, shape, axis)


def finish_kernel(pairs, early_ref, late_ref, sum_early_ref, sum_late_ref, *refs):
    sources, refs = refs[:8], refs[8:]
    output, grad, *shards, w_ada, b_ada, gain_one, gain_two, b_down, b_up = refs[:12]
    held, (wide, sems) = refs[12:20], refs[20:]
    x = lax.axis_index("seq")
    goals = [output.at[x], output.at[1 - x], grad.at[x], grad.at[1 - x], *shards]
    loads = [
        pltpu.make_async_copy(src, dst, sems.at[0, k])
        for k, (src, dst) in enumerate(zip(sources, held))
    ]
    stores = [
        pltpu.make_async_copy(wide if k == 3 else src, dst, sems.at[1, k])
        for k, (src, dst) in enumerate(zip(held, goals))
    ]
    for copy in loads:
        copy.start()
    for k in range(8):
        loads[k].wait()
        if k == 3:
            wide[...] = held[3][...].astype(F32)
        stores[k].start()
    dp = lax.axis_index("dp")
    rows, lines = w_ada.shape[0], early_ref.shape[1]
    width = gain_one.shape[0] * lax.axis_size("dp")
    per_line = width // 128
    stamp_line = 4 * per_line
    blocks = []
    for ref, first, count in ((late_ref, 0, 2 * per_line), (early_ref, 2 * per_line, 4 * per_line)):
        seqs, period = ref.shape[0], ref.shape[1]
        flat = ref[...].reshape(seqs * period, 128)
        stamps = early_ref[...].reshape(seqs * lines, 128)
        shape = (seqs * lines, seqs * period)
        line, col = iota2(shape, 0), iota2(shape, 1)
        pick = (line // lines == col // period) & (lax.rem(line, lines) == stamp_line)
        time = mm(stamps, jnp.where(pick, 1.0, 0.0).astype(BF), TN)
        time = 32.0 * time[0:1, :] + time[1:2, :]
        shape = (rows, seqs * period)
        index = dp * rows + iota2(shape, 0)
        place = jnp.where(index < pairs, index, index - pairs).astype(F32)
        angles = time * jnp.exp(-math.log(10000.0) * place / pairs)
        cond = features_of(angles, index >= pairs)
        shape = (period * rows, seqs * period)
        same = iota2(shape, 0) // rows == lax.rem(iota2(shape, 1), period)
        total = jnp.zeros((period * rows, 128), F32)
        for part in split_three(cond):
            spread = jnp.concatenate([part.astype(F32)] * period, axis=0)
            total += mm(jnp.where(same, spread, 0.0).astype(BF), flat)
        for k in range(count):
            start = (first + k) * 128
            w_ada[:, start : start + 128] = total[k * rows : (k + 1) * rows]
        shape = (period, seqs * period)
        same = iota2(shape, 0) == lax.rem(iota2(shape, 1), period)
        sums = mm(jnp.where(same, 1.0, 0.0).astype(BF), flat)
        blocks += [sums[k : k + 1] for k in range(count)]

    def mine(parts, out):
        row = jnp.concatenate(parts, axis=1)
        size, full = out.shape[0], row.shape[1]
        row = pltpu.roll(row, lax.rem(full - dp * size, full), 1)
        out[...] = row[0, 0:size]

    def lines_of(ref, first, count):
        return [ref[first + k : first + k + 1, :] for k in range(count)]

    mine(blocks, b_ada)
    mine(lines_of(sum_late_ref, 0, per_line), gain_one)
    mine(lines_of(sum_early_ref, 0, per_line), gain_two)
    mine(lines_of(sum_early_ref, per_line, per_line), b_down)
    mine(lines_of(sum_early_ref, 2 * per_line, b_up.shape[0] * lax.axis_size("dp") // 128), b_up)
    for copy in stores:
        copy.wait()


def finish_all(big, mod_early, mod_late, sum_early, sum_late, cond_width, width, ff, dps):
    seqs = 2 * dps
    mod_early = mod_early.reshape(seqs, *mod_early.shape[-2:])
    mod_late = mod_late.reshape(seqs, *mod_late.shape[-2:])
    smalls = (mod_early, mod_late, sum_early, sum_late)
    vmem = pl.BlockSpec(memory_space=pltpu.VMEM)
    half = big[0].shape[0]
    out_shape = [jax.ShapeDtypeStruct((2, half, width), kind) for kind in (BF, F32)]
    out_shape += [jax.ShapeDtypeStruct(a.shape, a.dtype) for a in big[4:]]
    out_shape += [jax.ShapeDtypeStruct((cond_width // dps, 6 * width), F32)]
    out_shape += [
        jax.ShapeDtypeStruct((n // dps,), F32) for n in (6 * width, width, width, width, ff)
    ]
    return pl.pallas_call(
        functools.partial(finish_kernel, cond_width // 2),
        in_specs=[vmem] * 4 + [ANY] * len(big),
        out_specs=[ANY] * 6 + [vmem] * 6,
        out_shape=out_shape,
        scratch_shapes=[pltpu.VMEM(a.shape, a.dtype) for a in big]
        + [pltpu.VMEM((half, width), F32), pltpu.SemaphoreType.DMA((2, len(big)))],
        compiler_params=params(),
        name="finish_all",
    )(*smalls, *big)


def time_features(time_steps, pair_count):
    frequency = jnp.exp(-math.log(10000.0) * jnp.arange(pair_count, dtype=F32) / pair_count)
    angles = time_steps.astype(F32)[:, None] * frequency[None, :]
    return jnp.concatenate([jnp.cos(angles), jnp.sin(angles)], axis=-1)


def per_device(
    tokens,
    cotangent,
    time_index,
    span_starts,
    span_lengths,
    w_ada,
    b_ada,
    gain_one,
    w_qkv,
    w_out,
    gain_two,
    w_up,
    b_up,
    w_down,
    b_down,
):
    seqs_dev, half, width = tokens.shape
    length = 2 * half
    rank = lax.axis_index("seq")
    swap = [(0, 1), (1, 0)]

    def pick(x, i):
        return lax.dynamic_index_in_dim(x, i, 0, keepdims=False)

    time_own = lax.dynamic_slice_in_dim(time_index, rank, 1)
    dp, dps = lax.axis_index("dp"), lax.axis_size("dp")
    ff = w_up.shape[1]
    zs = dps // 4
    linked = zs == 4 and dps == 16 and width % (64 * zs) == 0 and ff == zs * width

    act_t, qkv_t, w_qkv_t, tok_rem, vec_one, vec_two, span, cos_t, sin_t = project(
        tokens, time_index, span_starts, span_lengths, w_ada, b_ada, (gain_one, gain_two), b_down, w_qkv
    )
    att_t, e, linv, cot_rem = attend(qkv_t, cotangent)
    if linked:
        out_own, out_rem, dx, d_att_t, raw_out, raw_up, raw_down, *partial, mod, sums = middle_links(
            att_t, tokens, tok_rem, cotangent, cot_rem, span, vec_two, b_up[None], w_out, w_up, w_down, zs
        )
        ins = (qkv_t, att_t, d_att_t, e, linv, cos_t, sin_t, out_rem, *partial)
        ins += (raw_up, raw_out, raw_down, mod, sums, act_t, w_qkv_t, tokens, tok_rem, dx, vec_one)
        taken, g_own, g_take, *shards, mod_early, mod_late, sum_early, sum_late = back(ins, zs, ff)
        output, grad_tokens, *shards, s_w_ada, s_b_ada, s_gain_one, s_gain_two, s_b_down, s_b_up = (
            finish_all(
                (out_own, taken, g_own, g_take, *shards),
                mod_early,
                mod_late,
                sum_early,
                sum_late,
                w_ada.shape[0],
                width,
                ff,
                dps,
            )
        )
    else:
        tok_own, cot_own = pick(tokens, rank), pick(cotangent, rank)
        out_own, out_rem, dx, d_att_t, g_out, g_up, g_down, g_bup, sums_two = middle(
            att_t, tok_own, tok_rem, cot_own, cot_rem, span, vec_two, b_up[None], w_out, w_up, w_down
        )
        d_proj, out_back = attend_back(qkv_t, att_t, d_att_t, e, linv, cos_t, sin_t, out_rem)
        d_proj_t = d_proj.reshape(3 * width, length)
        g_own, g_rem, sums_one = tail(tok_own, tok_rem, d_proj_t, w_qkv_t, dx, vec_one)
        g_qkv = weight_grad(act_t, d_proj_t)

        def spread(own, other):
            first = jnp.where(rank == 0, own, other)
            second = jnp.where(rank == 0, other, own)
            return jnp.stack([first, second])

        output = spread(out_own, out_back)
        grad_tokens = spread(g_own, lax.ppermute(g_rem, "seq", swap).astype(F32))
        shards = [
            lax.psum(lax.psum_scatter(g, "dp", scatter_dimension=0, tiled=True), "seq").astype(F32)
            for g in (g_qkv, g_out, g_up, g_down)
        ]
        d_mod = jnp.concatenate([sums_one[:2].reshape(-1), sums_two[:4].reshape(-1)])
        small = jnp.concatenate([sums_one[2], sums_two[4], sums_two[5], g_bup[0]])
        d_mod_all = lax.all_gather(d_mod, ("dp", "seq"))
        time_all = lax.all_gather(time_own[0].astype(F32), ("dp", "seq"))
        small = lax.psum(small, ("dp", "seq"))

        def mine(x, axis=0):
            size = x.shape[axis] // dps
            return lax.dynamic_slice_in_dim(x, dp * size, size, axis)

        features = jax.nn.silu(time_features(time_all, w_ada.shape[0] // 2))
        s_w_ada = jnp.dot(mine(features, 1).T, d_mod_all, precision=lax.Precision.HIGHEST)
        s_b_ada = jnp.sum(mine(d_mod_all, 1), axis=0)
        s_gain_one = mine(small[:width])
        s_gain_two = mine(small[width : 2 * width])
        s_b_down = mine(small[2 * width : 3 * width])
        s_b_up = mine(small[3 * width :])

    s_qkv, s_out, s_up, s_down = shards

    return (
        output,
        grad_tokens,
        s_w_ada,
        s_b_ada,
        s_gain_one,
        s_qkv,
        s_out,
        s_gain_two,
        s_up,
        s_b_up,
        s_down,
        s_b_down,
    )


def solution(mesh):
    rows = P("dp", "seq", None)
    return jax.shard_map(
        per_device,
        mesh=mesh,
        in_specs=(rows, rows, P("dp"), P("dp"), P("dp")) + (P(),) * 10,
        out_specs=(
            rows,
            rows,
            P("dp", None),
            P("dp"),
            P("dp"),
            P("dp", None),
            P("dp", None),
            P("dp"),
            P("dp", None),
            P("dp"),
            P("dp", None),
            P("dp"),
        ),
        check_vma=False,
    )
```
